32 devices in a mesh: groups: 2 (over y), seq: 4 (over z), head: 4 (over x, core).
Axes of the slice: x: 2, y: 2, z: 4, core: 2. Of those that a mesh axis runs over, the one named last changes fastest.
Arguments:
- tokens: bfloat16 [8192, 1024], P(('groups', 'seq')), parts along dimension 0, may hold values from -16 to 16
- w_query: bfloat16 [1024, 1024], P(None, 'head'), may hold values from -0.1875 to 0.1875
- w_key: bfloat16 [1024, 1024], P(None, 'head'), may hold values from -0.1875 to 0.1875
- w_value: bfloat16 [1024, 1024], P(None, 'head'), may hold values from -0.1875 to 0.1875
- w_out: bfloat16 [1024, 1024], P(None, 'head'), may hold values from -0.1875 to 0.1875
- cotangent: bfloat16 [8192, 1024], P(('groups', 'seq')), parts along dimension 0, may hold values from -6 to 6
Outputs:
- mixed: bfloat16 [8192, 1024], P(('groups', 'seq'), 'head'), parts along dimension 0
- tokens_grad: bfloat16 [8192, 1024], P(('groups', 'seq'), 'head'), parts along dimension 0
- query_grad: bfloat16 [2048, 1024], P('groups', 'head'), parts along dimension 0
- key_grad: bfloat16 [2048, 1024], P('groups', 'head'), parts along dimension 0
- value_grad: bfloat16 [2048, 1024], P('groups', 'head'), parts along dimension 0
- out_grad: bfloat16 [2048, 1024], P('groups', 'head'), parts along dimension 0
The draws below stay inside these ranges and needn't reach their ends.
There are 2 independent parts, one for each index of `groups`. The reference program is written for one: setup_inputs(seed, part) draws one part's arguments, and reference() takes and returns one part's arrays. A program takes and returns all parts, laid end to end along the dimension named above; an argument that names none is the same for every part. Nothing has to cross between parts.
All inputs are finite; a program needn't handle non-finite values.
Results may differ from the reference program's by a relative error of at most 0.024.
The reference program's roundings to bfloat16 on the way count: a program that leaves them out, or rounds other values in their place, can miss the bound.
Values may be sent and summed in bfloat16 or wider, within the bound.
No kernel may reach another device: no remote copies, remote signals or barrier semaphores. Data moves between devices by JAX's collectives and lax.ppermute only.
A program may use at most 64 MiB of HBM per device.

```python
import math
import jax
import jax.numpy as jnp
from jax import lax

D = 1024
HEADS = 8
HEAD_DIM = 128
BLOCK = 128
TOKENS = 4096
N_HEAD = 4


def draw_tokens(key, part):
    key = jax.random.fold_in(key, 11)
    first = jax.random.fold_in(key, 0)
    result = jnp.clip(jax.random.normal(first, (TOKENS, D), jnp.float32), -4.0, 4.0)
    return result.astype(jnp.bfloat16)


def block_levels(stream_key, shape, cuts, smallest, top_value):
    def one(position, blocks):
        draws = jax.random.uniform(jax.random.fold_in(jax.random.fold_in(stream_key, 6), position), (blocks,), jnp.float32, smallest / len(cuts), top_value / len(cuts))
        return jnp.repeat(jnp.exp(draws), shape[position] // blocks).reshape((-1,) + (1,) * (len(shape) - position - 1))

    gain = one(*cuts[0])
    for cut in cuts[1:]:
        gain = gain * one(*cut)
    return gain


def normal_values(own_key, dims, width, bound, pieces=(), held_as=jnp.bfloat16):
    entries = width * jax.random.normal(own_key, dims, jnp.float32)
    if pieces:
        entries = entries * block_levels(own_key, dims, pieces, -0.22, 0.18)
    return jnp.clip(entries, -bound, bound).astype(held_as)


def setup_inputs(seed: int = 0, part: int = 0) -> dict:
    streams_of = jax.random.split(jax.random.key(seed), 7)
    part_keys = jax.random.split(jax.random.fold_in(streams_of[6], part), 7)
    return {
        "tokens": draw_tokens(jax.random.fold_in(jax.random.fold_in(streams_of[6], part), 71), part),
        "w_query": normal_values(streams_of[1], (D, HEADS * HEAD_DIM), D ** -0.5, 0.1875, ((1, 4),)),
        "w_key": normal_values(streams_of[2], (D, HEADS * HEAD_DIM), D ** -0.5, 0.1875, ((1, 4),)),
        "w_value": normal_values(streams_of[3], (D, HEADS * HEAD_DIM), D ** -0.5, 0.1875, ((1, 4),)),
        "w_out": normal_values(streams_of[4], (D, HEADS * HEAD_DIM), (HEADS * HEAD_DIM) ** -0.5, 0.1875, ((1, 4),)),
        "cotangent": normal_values(part_keys[5], (TOKENS, D), 1.0, 6.0, ((0, 4),)),
    }


def coarsen(values):
    wide = values.astype(jnp.float32)
    paired = wide.reshape(wide.shape[:-2] + (wide.shape[-2] // 2, 2, wide.shape[-1]))
    return ((paired[..., 0, :] + paired[..., 1, :]) * 0.5).astype(jnp.bfloat16)

def spread(grads):
    return jnp.repeat(grads, 2, axis=-2) * 0.5

def sibling_blocks(level, block_rows, reach):
    segments = level.shape[0] // block_rows
    flipped = level.reshape(segments // 2, 2, block_rows, level.shape[1])[:, ::-1]
    flipped = flipped.reshape(segments, block_rows, level.shape[1])
    return jnp.repeat(flipped, reach, axis=0)

def fold_back(grads, reach):
    blocks, block_rows, head_width = grads.shape
    segments = blocks // reach
    summed = grads.reshape(segments, reach, block_rows, head_width).sum(axis=1)
    summed = summed.reshape(segments // 2, 2, block_rows, head_width)[:, ::-1]
    return summed.reshape(segments * block_rows, head_width)

def project(left, weight):
    return lax.dot_general(left, weight, (((1,), (1,)), ((), ())), preferred_element_type=jnp.float32)

def contract_rows(left, right):
    return lax.dot_general(left, right, (((0,), (0,)), ((), ())), preferred_element_type=jnp.float32)

def one_head(operands):
    query, key, value, grad_attended = operands
    levels = (TOKENS // BLOCK).bit_length() - 1
    blocks = TOKENS // BLOCK
    score_scale = 1.0 / math.sqrt(HEAD_DIM)
    key_levels = [key]
    value_levels = [value]
    for level_index in range(levels - 1):
        key_levels.append(coarsen(key_levels[-1]))
        value_levels.append(coarsen(value_levels[-1]))
    key_set = jnp.concatenate([key.reshape(blocks, BLOCK, HEAD_DIM)] + [sibling_blocks(key_levels[i], BLOCK, 2 ** i) for i in range(levels)], axis=1)
    value_set = jnp.concatenate([value.reshape(blocks, BLOCK, HEAD_DIM)] + [sibling_blocks(value_levels[i], BLOCK, 2 ** i) for i in range(levels)], axis=1)
    bias = jnp.concatenate([jnp.zeros((BLOCK,), jnp.float32)] + [jnp.full((BLOCK,), i * math.log(2.0), jnp.float32) for i in range(levels)])
    q_blocks = query.reshape(blocks, BLOCK, HEAD_DIM).astype(jnp.float32)
    keys_wide = key_set.astype(jnp.float32)
    values_wide = value_set.astype(jnp.float32)
    scores = jnp.einsum('nqd,nkd->nqk', q_blocks, keys_wide) * score_scale + bias
    row_max = lax.optimization_barrier(jnp.max(scores, axis=-1, keepdims=True))
    expo = jnp.exp(scores - row_max)
    probs = expo / lax.optimization_barrier(jnp.sum(expo, axis=-1, keepdims=True))
    probs_b = probs.astype(jnp.bfloat16).astype(jnp.float32)
    attended = jnp.einsum('nqk,nkd->nqd', probs_b, values_wide).astype(jnp.bfloat16)
    g_blocks = grad_attended.reshape(blocks, BLOCK, HEAD_DIM).astype(jnp.float32)
    row_delta = lax.optimization_barrier(jnp.sum(g_blocks * attended.astype(jnp.float32), axis=-1))
    dprob = jnp.einsum('nqd,nkd->nqk', g_blocks, values_wide)
    score_grads = (probs * (dprob - row_delta[..., None]) * score_scale).astype(jnp.bfloat16).astype(jnp.float32)
    dquery = jnp.einsum('nqk,nkd->nqd', score_grads, keys_wide).astype(jnp.bfloat16)
    key_set_grads = jnp.einsum('nqk,nqd->nkd', score_grads, q_blocks)
    value_set_grads = jnp.einsum('nqk,nqd->nkd', probs_b, g_blocks)
    key_chain = None
    value_chain = None
    for i in reversed(range(levels)):
        key_part = fold_back(key_set_grads[:, (i + 1) * BLOCK:(i + 2) * BLOCK], 2 ** i)
        value_part = fold_back(value_set_grads[:, (i + 1) * BLOCK:(i + 2) * BLOCK], 2 ** i)
        if key_chain is None:
            key_chain, value_chain = (key_part, value_part)
        else:
            key_chain = key_part + spread(key_chain)
            value_chain = value_part + spread(value_chain)
    dkey = (key_set_grads[:, :BLOCK].reshape(TOKENS, HEAD_DIM) + key_chain).astype(jnp.bfloat16)
    dvalue = (value_set_grads[:, :BLOCK].reshape(TOKENS, HEAD_DIM) + value_chain).astype(jnp.bfloat16)
    return (attended.reshape(TOKENS, HEAD_DIM), dquery.reshape(TOKENS, HEAD_DIM), dkey, dvalue)

def reference(tokens, w_query, w_key, w_value, w_out, cotangent):
    inner_width = HEADS * HEAD_DIM
    query = jnp.dot(tokens, w_query, preferred_element_type=jnp.float32).astype(jnp.bfloat16)
    key = jnp.dot(tokens, w_key, preferred_element_type=jnp.float32).astype(jnp.bfloat16)
    value = jnp.dot(tokens, w_value, preferred_element_type=jnp.float32).astype(jnp.bfloat16)
    grad_attended = jnp.dot(cotangent, w_out, preferred_element_type=jnp.float32).astype(jnp.bfloat16)

    def split_heads(matrix):
        return matrix.reshape(TOKENS, HEADS, HEAD_DIM).transpose(1, 0, 2)

    def join_heads(stack):
        return stack.transpose(1, 0, 2).reshape(TOKENS, inner_width)
    attended, dquery, dkey, dvalue = lax.map(one_head, (split_heads(query), split_heads(key), split_heads(value), split_heads(grad_attended)))
    attended = join_heads(attended)
    dquery = join_heads(dquery)
    dkey = join_heads(dkey)
    dvalue = join_heads(dvalue)
    group_width = HEADS // N_HEAD * HEAD_DIM
    mixed_sum = jnp.zeros((TOKENS, D), jnp.float32)
    grad_sum = jnp.zeros((TOKENS, D), jnp.float32)
    for group in range(N_HEAD):
        low = group * group_width
        high = low + group_width
        part = project(attended[:, low:high], w_out[:, low:high]).astype(jnp.bfloat16)
        part = lax.optimization_barrier(part)
        mixed_sum = mixed_sum + part.astype(jnp.float32)
        grad_part = project(dquery[:, low:high], w_query[:, low:high]) + project(dkey[:, low:high], w_key[:, low:high]) + project(dvalue[:, low:high], w_value[:, low:high])
        grad_part = lax.optimization_barrier(grad_part.astype(jnp.bfloat16))
        grad_sum = grad_sum + grad_part.astype(jnp.float32)
    mixed = mixed_sum.astype(jnp.bfloat16)
    tokens_grad = grad_sum.astype(jnp.bfloat16)
    query_grad = contract_rows(tokens, dquery).astype(jnp.bfloat16)
    key_grad = contract_rows(tokens, dkey).astype(jnp.bfloat16)
    value_grad = contract_rows(tokens, dvalue).astype(jnp.bfloat16)
    out_grad = contract_rows(cotangent, attended).astype(jnp.bfloat16)
    return (mixed, tokens_grad, query_grad, key_grad, value_grad, out_grad)
```

```python
import functools
import math

import jax
import jax.numpy as jnp
from jax import lax
from jax.experimental import pallas as pl
from jax.experimental.pallas import tpu as pltpu
from jax.sharding import PartitionSpec as P

HEAD_DIM = 128
BLOCK = 128
BF16 = jnp.bfloat16
F32 = jnp.float32
MIB = 1024 * 1024

NN = (((1,), (0,)), ((), ()))
NT = (((1,), (1,)), ((), ()))
TN = (((0,), (0,)), ((), ()))


def dot(left, right, dims=NN):
    return lax.dot_general(left, right, dims, preferred_element_type=F32)


def params(mib):
    return pltpu.CompilerParams(vmem_limit_bytes=mib * MIB)


def cost(flops, moved, exps=0):
    return pl.CostEstimate(flops=int(flops), bytes_accessed=int(moved), transcendentals=int(exps))


def shape(rows, cols, dtype=BF16):
    return jax.ShapeDtypeStruct((rows, cols), dtype)


def whole(rows, cols):
    return pl.BlockSpec((rows, cols), lambda *_: (0, 0))


def pool_matrix(rows):
    row = lax.broadcasted_iota(jnp.int32, (rows // 2, rows), 0)
    col = lax.broadcasted_iota(jnp.int32, (rows // 2, rows), 1)
    return jnp.where(jnp.right_shift(col, 1) == row, 0.5, 0.0).astype(BF16)


def spread_matrix(rows, step_bits, offset, cols, weight):
    row = lax.broadcasted_iota(jnp.int32, (rows, cols), 0) + offset
    col = lax.broadcasted_iota(jnp.int32, (rows, cols), 1)
    return jnp.where(jnp.right_shift(row, step_bits) == col, weight, 0.0).astype(BF16)


def key_value_body(local_levels, far_levels, tok_ref, wk_ref, wv_ref, *outs):
    k_ref, v_ref = outs[:2]
    mid = outs[2 : 2 + 2 * (local_levels - 1)]
    far = outs[2 + 2 * (local_levels - 1) : -1]
    top_ref = outs[-1]
    step = pl.program_id(0)
    x = tok_ref[...]
    inner = wk_ref.shape[1]
    for which, (w_ref, out_ref) in enumerate(((wk_ref, k_ref), (wv_ref, v_ref))):
        rows = dot(x, w_ref[...]).astype(BF16)
        out_ref[...] = rows
        for i in range(local_levels - 1):
            rows = dot(pool_matrix(rows.shape[0]), rows).astype(BF16)
            mid[2 * i + which][...] = rows
        rows = dot(pool_matrix(rows.shape[0]), rows).astype(BF16)
        count = rows.shape[0]
        place = pl.ds(pl.multiple_of(step * count, count), count)
        top_ref[place, which * inner : (which + 1) * inner] = rows

    @pl.when(step == pl.num_programs(0) - 1)
    def _():
        rows = top_ref[...]
        for i in range(far_levels):
            if i:
                rows = dot(pool_matrix(rows.shape[0]), rows).astype(BF16)
            far[i][...] = rows


def key_value(tokens, w_key, w_value, local_levels, far_levels):
    tok_rows, width = tokens.shape
    inner = w_key.shape[1]
    tile = 2 * BLOCK
    steps = tok_rows // tile
    out_shape = [shape(tok_rows, inner)] * 2
    out_specs = [pl.BlockSpec((tile, inner), lambda i: (i, 0))] * 2
    for i in range(1, local_levels):
        out_shape += [shape(tok_rows >> i, inner)] * 2
        out_specs += [pl.BlockSpec((tile >> i, inner), lambda i: (i, 0))] * 2
    for i in range(far_levels):
        out_shape += [shape(BLOCK >> i, 2 * inner)]
        out_specs += [whole(BLOCK >> i, 2 * inner)]
    return pl.pallas_call(
        functools.partial(key_value_body, local_levels, far_levels),
        grid=(steps,),
        in_specs=[
            pl.BlockSpec((tile, width), lambda i: (i, 0)),
            whole(width, inner),
            whole(width, inner),
        ],
        out_specs=out_specs,
        out_shape=out_shape,
        scratch_shapes=[pltpu.VMEM((BLOCK, 2 * inner), BF16)],
        compiler_params=params(24),
        cost_estimate=cost(4 * tok_rows * width * inner, 2 * tok_rows * width + 8 * width * inner),
    )(tokens, w_key, w_value)


def pair_body(a_ref, b_ref, wa_ref, wb_ref, x_ref, y_ref):
    x_ref[...] = dot(a_ref[...], wa_ref[...]).astype(BF16)
    y_ref[...] = dot(b_ref[...], wb_ref[...]).astype(BF16)


def project_pair(a, b, wa, wb):
    tok_rows, width = a.shape
    inner = wa.shape[1]
    tile = 2 * BLOCK
    rows = pl.BlockSpec((tile, width), lambda i: (i, 0))
    outs = pl.BlockSpec((tile, inner), lambda i: (i, 0))
    return pl.pallas_call(
        pair_body,
        grid=(tok_rows // tile,),
        in_specs=[rows, rows, whole(width, inner), whole(width, inner)],
        out_specs=[outs, outs],
        out_shape=[shape(tok_rows, inner)] * 2,
        compiler_params=params(24),
        cost_estimate=cost(4 * tok_rows * width * inner, 4 * tok_rows * width + 8 * width * inner),
    )(a, b, wa, wb)


def attention_body(local_levels, far_bits, *refs):
    mids = local_levels - 1
    fars = len(far_bits)
    q_ref, g_ref, k_ref, v_ref = refs[:4]
    mid_refs = refs[4 : 4 + 2 * mids]
    far_refs = refs[4 + 2 * mids : 4 + 2 * mids + fars]
    outs = refs[4 + 2 * mids + fars :]
    att_ref, att_t_ref, dq_ref, dq_t_ref, dkv_ref = outs[:5]
    dmid_refs = outs[5 : 5 + mids]
    dfar_refs = outs[5 + mids : 5 + mids + fars]
    acc_ref = outs[-1]
    tok_rows, inner = q_ref.shape
    heads = inner // HEAD_DIM
    pair = 2 * BLOCK
    score_scale = 1.0 / math.sqrt(HEAD_DIM)
    sizes = [pair] + [BLOCK] * mids + [r.shape[0] for r in far_refs]
    biases = [0.0] + [i * math.log(2.0) for i in range(1, local_levels)]
    biases += [(local_levels + bit) * math.log(2.0) for bit in far_bits]
    starts = [sum(sizes[:i]) for i in range(len(sizes))]

    for ref in (*dmid_refs, acc_ref):
        ref[...] = jnp.zeros_like(ref)

    def unit(m, h):
        low = h * HEAD_DIM
        cols = slice(low, low + HEAD_DIM)
        vcols = slice(inner + low, inner + low + HEAD_DIM)
        here = pl.ds(pl.multiple_of(m * pair, pair), pair)
        seats = []
        for i in range(1, local_levels):
            sibling = jnp.bitwise_xor(jnp.right_shift(m, i - 1), 1)
            seats.append(pl.ds(pl.multiple_of(sibling * BLOCK, BLOCK), BLOCK))
        keys = [k_ref[here, cols]]
        values = [v_ref[here, cols]]
        for i in range(mids):
            keys.append(mid_refs[2 * i][seats[i], cols])
            values.append(mid_refs[2 * i + 1][seats[i], cols])
        for ref in far_refs:
            keys.append(ref[:, cols])
            values.append(ref[:, vcols])
        keys = jnp.concatenate(keys, axis=0)
        values = jnp.concatenate(values, axis=0)
        q = q_ref[here, cols]
        g = g_ref[here, cols]
        raw = dot(keys, q, NT)
        scores = jnp.concatenate(
            [
                raw[start : start + size] * score_scale + bias
                for start, size, bias in zip(starts, sizes, biases)
            ],
            axis=0,
        )
        expo = jnp.exp(scores - jnp.max(scores, axis=0, keepdims=True))
        probs = expo * (1.0 / jnp.sum(expo, axis=0, keepdims=True))
        probs_b = probs.astype(BF16)
        att_t = dot(values, probs_b, TN).astype(BF16)
        att_t_ref[cols, here] = att_t
        att_ref[here, cols] = att_t.T
        g_t = g.T
        delta = jnp.sum(g_t.astype(F32) * att_t.astype(F32), axis=0, keepdims=True)
        dprobs = dot(values, g, NT)
        grads = (probs * (dprobs - delta) * score_scale).astype(BF16)
        dq_t = dot(keys, grads, TN).astype(BF16)
        dq_t_ref[cols, here] = dq_t
        dq_ref[here, cols] = dq_t.T
        dk = dot(grads, q)
        dv = dot(probs_b, g)
        for part, where_to in ((dk, cols), (dv, vcols)):
            dkv_ref[here, where_to] = part[:pair]
            for i in range(mids):
                start = starts[1 + i]
                dmid_refs[i][seats[i], where_to] += part[start : start + BLOCK]
            acc_ref[:, where_to] += part[starts[1 + mids] :]

    def step(m, carry):
        for h in range(heads):
            unit(m, h)
        return carry

    lax.fori_loop(0, tok_rows // pair, step, 0)
    base = starts[1 + mids]
    for ref, start, size in zip(dfar_refs, starts[1 + mids :], sizes[1 + mids :]):
        ref[...] = acc_ref[start - base : start - base + size].astype(BF16)


def attention(query, grad, key, value, mids, fars, far_bits, local_levels):
    tok_rows, inner = query.shape
    far_rows = sum(f.shape[0] for f in fars)
    set_rows = (local_levels + 1) * BLOCK + far_rows
    out_shape = [
        shape(tok_rows, inner),
        shape(inner, tok_rows),
        shape(tok_rows, inner),
        shape(inner, tok_rows),
        shape(tok_rows, 2 * inner, F32),
    ]
    out_shape += [shape(tok_rows >> i, 2 * inner, F32) for i in range(1, local_levels)]
    out_shape += [shape(f.shape[0], 2 * inner) for f in fars]
    return pl.pallas_call(
        functools.partial(attention_body, local_levels, far_bits),
        out_shape=out_shape,
        scratch_shapes=[pltpu.VMEM((far_rows, 2 * inner), F32)],
        compiler_params=params(40),
        cost_estimate=cost(
            12 * tok_rows * set_rows * inner, 24 * tok_rows * inner, tok_rows * set_rows * 2
        ),
    )(query, grad, key, value, *mids, *fars)


def term_body(left_ref, right_ref, *out_refs):
    product = dot(left_ref[...], right_ref[...]).astype(BF16).T
    inner = product.shape[1] // len(out_refs)
    for i, ref in enumerate(out_refs):
        ref[...] = product[:, i * inner : (i + 1) * inner]


def weight_terms(left_t, right, count):
    rows, tok_rows = left_t.shape
    width = right.shape[1]
    tile = min(width, 256)
    inner = rows // count
    return pl.pallas_call(
        term_body,
        grid=(width // tile,),
        in_specs=[whole(rows, tok_rows), pl.BlockSpec((tok_rows, tile), lambda i: (0, i))],
        out_specs=[pl.BlockSpec((tile, inner), lambda i: (i, 0))] * count,
        out_shape=[shape(width, inner)] * count,
        compiler_params=params(24),
        cost_estimate=cost(2 * rows * tok_rows * width, 2 * tok_rows * width + 4 * rows * tok_rows),
    )(left_t, right)


def close_body(local_levels, far_bits, dkv_ref, *refs):
    mids = local_levels - 1
    dmid_refs = refs[:mids]
    back_refs = refs[mids : mids + len(far_bits)]
    dk_ref, dv_ref, dkv_t_ref = refs[mids + len(far_bits) :]
    tile = dkv_ref.shape[0]
    offset = pl.program_id(0) * tile
    inner = dk_ref.shape[1]
    total = dkv_ref[...]
    chain = None
    for i in reversed(range(mids)):
        chain = dmid_refs[i][...] if chain is None else dmid_refs[i][...] + chain
        high = chain.astype(BF16)
        low = (chain - high.astype(F32)).astype(BF16)
        rows = chain.shape[0]
        fan = spread_matrix(2 * rows, 1, 0, rows, 0.5)
        chain = dot(fan, high) + dot(fan, low)
    if chain is not None:
        total = total + chain
    for ref, bit in zip(back_refs, far_bits):
        weight = 0.5 ** (local_levels + bit)
        fan = spread_matrix(tile, local_levels + bit, offset, ref.shape[0], weight)
        total = total + dot(fan, ref[...])
    final = total.astype(BF16)
    dk_ref[...] = final[:, :inner]
    dv_ref[...] = final[:, inner:]
    dkv_t_ref[...] = final.T


def close_keys(dkv, dmids, backs, far_bits, local_levels):
    tok_rows, double = dkv.shape
    inner = double // 2
    tile = 2 * BLOCK
    in_specs = [pl.BlockSpec((tile, double), lambda i: (i, 0))]
    in_specs += [pl.BlockSpec((tile >> i, double), lambda i: (i, 0)) for i in range(1, local_levels)]
    in_specs += [whole(*b.shape) for b in backs]
    return pl.pallas_call(
        functools.partial(close_body, local_levels, far_bits),
        grid=(tok_rows // tile,),
        in_specs=in_specs,
        out_specs=[
            pl.BlockSpec((tile, inner), lambda i: (i, 0)),
            pl.BlockSpec((tile, inner), lambda i: (i, 0)),
            pl.BlockSpec((double, tile), lambda i: (0, i)),
        ],
        out_shape=[shape(tok_rows, inner), shape(tok_rows, inner), shape(double, tok_rows)],
        compiler_params=params(24),
        cost_estimate=cost(4 * tok_rows * 256 * double, 20 * tok_rows * double),
    )(dkv, *dmids, *backs)


def out_body(count, *refs):
    total = None
    for i in range(count):
        part = dot(refs[i][...], refs[count + i][...], NT)
        total = part if total is None else total + part
    refs[-1][...] = total.astype(BF16)


def project_out(lefts, weights):
    count = len(lefts)
    tok_rows, inner = lefts[0].shape
    width = weights[0].shape[0]
    tile = 2 * BLOCK
    return pl.pallas_call(
        functools.partial(out_body, count),
        grid=(tok_rows // tile,),
        in_specs=[pl.BlockSpec((tile, inner), lambda i: (i, 0))] * count
        + [whole(width, inner)] * count,
        out_specs=pl.BlockSpec((tile, width), lambda i: (i, 0)),
        out_shape=shape(tok_rows, width),
        compiler_params=params(24),
        cost_estimate=cost(2 * count * tok_rows * inner * width, 2 * tok_rows * width),
    )(*lefts, *weights)


def exchange(block, axis, distance):
    count = lax.axis_size(axis)
    return lax.ppermute(block, axis, [(i, i ^ distance) for i in range(count)])


def add(left, right):
    return (left.astype(F32) + right.astype(F32)).astype(BF16)


def line_sum(block, axis):
    count = lax.axis_size(axis)
    if count < 4:
        return add(block, exchange(block, axis, 1)) if count == 2 else block
    rank = jnp.bitwise_and(lax.axis_index(axis), 3)
    inward, across, outward = [], [], []
    for base in range(0, count, 4):
        inward += [(base, base + 1), (base + 3, base + 2)]
        across += [(base + 1, base + 2), (base + 2, base + 1)]
        outward += [(base + 1, base), (base + 2, base + 3)]
    half = add(block, lax.ppermute(block, axis, inward))
    total = add(half, lax.ppermute(half, axis, across))
    ends = lax.ppermute(total, axis, outward)
    total = jnp.where((rank == 0) | (rank == 3), ends, total)
    distance = 4
    while distance < count:
        total = add(total, exchange(total, axis, distance))
        distance *= 2
    return total


def per_device(tokens, w_query, w_key, w_value, w_out, cotangent):
    tok_rows = tokens.shape[0]
    local_levels = (tok_rows // BLOCK).bit_length() - 1
    count = lax.axis_size("seq")
    far_levels = count.bit_length() - 1
    far_bits = [d.bit_length() - 1 for d in range(1, count)]

    parts = key_value(tokens, w_key, w_value, local_levels, far_levels)
    key, value = parts[:2]
    mids = parts[2 : 2 + 2 * (local_levels - 1)]
    tops = parts[2 + 2 * (local_levels - 1) :]
    fars = [exchange(tops[bit], "seq", d) for d, bit in enumerate(far_bits, 1)]
    query, grad = project_pair(tokens, cotangent, w_query, w_out)
    results = attention(query, grad, key, value, mids, fars, far_bits, local_levels)
    attended, attended_t, dquery, dquery_t, dkv = results[:5]
    dmids = results[5 : 5 + local_levels - 1]
    dfars = results[5 + local_levels - 1 :]
    backs = [exchange(piece, "seq", d) for d, piece in enumerate(dfars, 1)]

    (out_term,) = weight_terms(attended_t, cotangent, 1)
    out_grad = line_sum(out_term, "seq")
    (query_term,) = weight_terms(dquery_t, tokens, 1)
    query_grad = line_sum(query_term, "seq")
    mixed_part = project_out([attended], [w_out])
    mixed = lax.psum_scatter(mixed_part, "head", scatter_dimension=1, tiled=True)

    dkey, dvalue, dkv_t = close_keys(dkv, dmids, backs, far_bits, local_levels)
    key_term, value_term = weight_terms(dkv_t, tokens, 2)
    key_grad = line_sum(key_term, "seq")
    value_grad = line_sum(value_term, "seq")
    grad_part = project_out([dquery, dkey, dvalue], [w_query, w_key, w_value])
    tokens_grad = lax.psum_scatter(grad_part, "head", scatter_dimension=1, tiled=True)
    return mixed, tokens_grad, query_grad, key_grad, value_grad, out_grad


def solution(mesh):
    return jax.shard_map(
        per_device,
        mesh=mesh,
        in_specs=(
            P(("groups", "seq"), None),
            P(None, "head"),
            P(None, "head"),
            P(None, "head"),
            P(None, "head"),
            P(("groups", "seq"), None),
        ),
        out_specs=(
            P(("groups", "seq"), "head"),
            P(("groups", "seq"), "head"),
            P("groups", "head"),
            P("groups", "head"),
            P("groups", "head"),
            P("groups", "head"),
        ),
        check_vma=False,
    )
```

```python
import functools
import math

import jax
import jax.numpy as jnp
from jax import lax
from jax.experimental import pallas as pl
from jax.experimental.pallas import tpu as pltpu
from jax.sharding import PartitionSpec as P

HEAD_DIM = 128
BLOCK = 128
BF16 = jnp.bfloat16
F32 = jnp.float32
MIB = 1024 * 1024

NN = (((1,), (0,)), ((), ()))
NT = (((1,), (1,)), ((), ()))
TN = (((0,), (0,)), ((), ()))


def dot(left, right, dims=NN):
    return lax.dot_general(left, right, dims, preferred_element_type=F32)


def params():
    return pltpu.CompilerParams(vmem_limit_bytes=56 * MIB)


def cost(flops, moved, exps=0):
    return pl.CostEstimate(flops=int(flops), bytes_accessed=int(moved), transcendentals=int(exps))


def shape(rows, cols, dtype=BF16):
    return jax.ShapeDtypeStruct((rows, cols), dtype)


def whole(rows, cols):
    return pl.BlockSpec((rows, cols), lambda *_: (0, 0))


def pool_matrix(rows):
    row = lax.broadcasted_iota(jnp.int32, (rows // 2, rows), 0)
    col = lax.broadcasted_iota(jnp.int32, (rows // 2, rows), 1)
    return jnp.where(jnp.right_shift(col, 1) == row, 0.5, 0.0).astype(BF16)


def spread_matrix(rows, step_bits, offset, cols, weight):
    row = lax.broadcasted_iota(jnp.int32, (rows, cols), 0) + offset
    col = lax.broadcasted_iota(jnp.int32, (rows, cols), 1)
    return jnp.where(jnp.right_shift(row, step_bits) == col, weight, 0.0).astype(BF16)


def key_value_body(local_levels, far_levels, tok_ref, wk_ref, wv_ref, *outs):
    kv_ref = outs[0]
    mid = outs[1:local_levels]
    far = outs[local_levels:-1]
    top_ref = outs[-1]
    step = pl.program_id(0)
    part = 2 * BLOCK
    parts = tok_ref.shape[0] // part
    for p in range(parts):
        x = tok_ref[p * part : (p + 1) * part, :]
        rows = jnp.concatenate([dot(x, wk_ref[...]), dot(x, wv_ref[...])], axis=1).astype(BF16)
        kv_ref[p * part : (p + 1) * part, :] = rows
        for ref in mid:
            rows = dot(pool_matrix(rows.shape[0]), rows).astype(BF16)
            ref[p * rows.shape[0] : (p + 1) * rows.shape[0], :] = rows
        rows = dot(pool_matrix(rows.shape[0]), rows).astype(BF16)
        count = rows.shape[0]
        top_ref[pl.ds(pl.multiple_of((step * parts + p) * count, count), count), :] = rows

    @pl.when(step == pl.num_programs(0) - 1)
    def _():
        rows = top_ref[...]
        for i in range(far_levels):
            if i:
                rows = dot(pool_matrix(rows.shape[0]), rows).astype(BF16)
            far[i][...] = rows


def key_value(tokens, w_key, w_value, local_levels, far_levels):
    tok_rows, width = tokens.shape
    inner = w_key.shape[1]
    tile = 4 * BLOCK
    out_shape, out_specs = [], []
    for i in range(local_levels):
        out_shape += [shape(tok_rows >> i, 2 * inner)]
        out_specs += [pl.BlockSpec((tile >> i, 2 * inner), lambda i: (i, 0))]
    for i in range(far_levels):
        out_shape += [shape(BLOCK >> i, 2 * inner)]
        out_specs += [whole(BLOCK >> i, 2 * inner)]
    return pl.pallas_call(
        functools.partial(key_value_body, local_levels, far_levels),
        grid=(tok_rows // tile,),
        in_specs=[
            pl.BlockSpec((tile, width), lambda i: (i, 0)),
            whole(width, inner),
            whole(width, inner),
        ],
        out_specs=out_specs,
        out_shape=out_shape,
        scratch_shapes=[pltpu.VMEM((BLOCK, 2 * inner), BF16)],
        compiler_params=params(),
        cost_estimate=cost(4 * tok_rows * width * inner, 2 * tok_rows * width + 8 * width * inner),
    )(tokens, w_key, w_value)


def pair_body(a_ref, b_ref, wa_ref, wb_ref, x_ref, y_ref):
    x_ref[...] = dot(a_ref[...], wa_ref[...]).astype(BF16)
    y_ref[...] = dot(b_ref[...], wb_ref[...]).astype(BF16)


def project_pair(a, b, wa, wb):
    tok_rows, width = a.shape
    inner = wa.shape[1]
    tile = 2 * BLOCK
    rows = pl.BlockSpec((tile, width), lambda i: (i, 0))
    outs = pl.BlockSpec((tile, inner), lambda i: (i, 0))
    return pl.pallas_call(
        pair_body,
        grid=(tok_rows // tile,),
        in_specs=[rows, rows, whole(width, inner), whole(width, inner)],
        out_specs=[outs, outs],
        out_shape=[shape(tok_rows, inner)] * 2,
        compiler_params=params(),
        cost_estimate=cost(4 * tok_rows * width * inner, 4 * tok_rows * width + 8 * width * inner),
    )(a, b, wa, wb)


def attention_body(local_levels, far_bits, *refs):
    mids = local_levels - 1
    fars = len(far_bits)
    q_ref, g_ref, kv_ref = refs[:3]
    mid_refs = refs[3 : 3 + mids]
    far_refs = refs[3 + mids : 3 + mids + fars]
    outs = refs[3 + mids + fars :]
    att_ref, att_t_ref, dq_ref, dq_t_ref, dkv_ref = outs[:5]
    dmid_refs = outs[5 : 5 + mids]
    dfar_refs = outs[5 + mids : 5 + mids + fars]
    acc_ref = outs[-1]
    inner = q_ref.shape[1]
    heads = inner // HEAD_DIM
    pair = 2 * BLOCK
    m = pl.program_id(0)
    score_scale = 1.0 / math.sqrt(HEAD_DIM)
    sizes = [pair] + [BLOCK] * mids + [r.shape[0] for r in far_refs]
    biases = [0.0] + [i * math.log(2.0) for i in range(1, local_levels)]
    biases += [(local_levels + bit) * math.log(2.0) for bit in far_bits]
    starts = [sum(sizes[:i]) for i in range(len(sizes))]
    seats = []
    for i in range(1, local_levels):
        sibling = jnp.bitwise_xor(jnp.right_shift(m, i - 1), 1)
        seats.append(pl.ds(pl.multiple_of(sibling * BLOCK, BLOCK), BLOCK))

    @pl.when(m == 0)
    def _():
        for ref in (*dmid_refs, acc_ref):
            ref[...] = jnp.zeros_like(ref)

    def rows_of(cols):
        rows = [kv_ref[:, cols]]
        rows += [ref[seat, cols] for ref, seat in zip(mid_refs, seats)]
        rows += [ref[:, cols] for ref in far_refs]
        return jnp.concatenate(rows, axis=0)

    for h in range(heads):
        low = h * HEAD_DIM
        cols = slice(low, low + HEAD_DIM)
        vcols = slice(inner + low, inner + low + HEAD_DIM)
        keys = rows_of(cols)
        values = rows_of(vcols)
        q = q_ref[:, cols]
        g = g_ref[:, cols]
        raw = dot(keys, q, NT)
        scores = jnp.concatenate(
            [
                raw[start : start + size] * score_scale + bias
                for start, size, bias in zip(starts, sizes, biases)
            ],
            axis=0,
        )
        expo = jnp.exp(scores - jnp.max(scores, axis=0, keepdims=True))
        probs = expo * (1.0 / jnp.sum(expo, axis=0, keepdims=True))
        probs_b = probs.astype(BF16)
        att_t = dot(values, probs_b, TN).astype(BF16)
        att_t_ref[cols, :] = att_t
        att_ref[:, cols] = att_t.T
        delta = jnp.sum(g.T.astype(F32) * att_t.astype(F32), axis=0, keepdims=True)
        dprobs = dot(values, g, NT)
        grads = (probs * (dprobs - delta) * score_scale).astype(BF16)
        dq_t = dot(keys, grads, TN).astype(BF16)
        dq_t_ref[cols, :] = dq_t
        dq_ref[:, cols] = dq_t.T
        for part, place in ((dot(grads, q), cols), (dot(probs_b, g), vcols)):
            dkv_ref[:, place] = part[:pair]
            for i in range(mids):
                start = starts[1 + i]
                dmid_refs[i][seats[i], place] += part[start : start + BLOCK]
            acc_ref[:, place] += part[starts[1 + mids] :]

    @pl.when(m == pl.num_programs(0) - 1)
    def _():
        base = starts[1 + mids]
        for ref, start, size in zip(dfar_refs, starts[1 + mids :], sizes[1 + mids :]):
            ref[...] = acc_ref[start - base : start - base + size].astype(BF16)


def attention(query, grad, levels, fars, far_bits):
    tok_rows, inner = query.shape
    local_levels = len(levels)
    far_rows = sum(f.shape[0] for f in fars)
    set_rows = (local_levels + 1) * BLOCK + far_rows
    pair = 2 * BLOCK
    rows = pl.BlockSpec((pair, inner), lambda i: (i, 0))
    cols = pl.BlockSpec((inner, pair), lambda i: (0, i))
    both = pl.BlockSpec((pair, 2 * inner), lambda i: (i, 0))
    others = [*levels[1:], *fars]
    out_shape = [
        shape(tok_rows, inner),
        shape(inner, tok_rows),
        shape(tok_rows, inner),
        shape(inner, tok_rows),
        shape(tok_rows, 2 * inner, F32),
    ]
    out_shape += [shape(*level.shape, F32) for level in levels[1:]]
    out_shape += [shape(*f.shape) for f in fars]
    return pl.pallas_call(
        functools.partial(attention_body, local_levels, far_bits),
        grid=(tok_rows // pair,),
        in_specs=[rows, rows, both] + [whole(*x.shape) for x in others],
        out_specs=[rows, cols, rows, cols, both] + [whole(*x.shape) for x in others],
        out_shape=out_shape,
        scratch_shapes=[pltpu.VMEM((far_rows, 2 * inner), F32)],
        compiler_params=params(),
        cost_estimate=cost(
            12 * tok_rows * set_rows * inner, 24 * tok_rows * inner, tok_rows * set_rows * 2
        ),
    )(query, grad, *levels, *fars)


def term_body(left_ref, right_ref, out_ref):
    out_ref[...] = dot(left_ref[...], right_ref[...]).astype(BF16).T


def weight_terms(left_t, right, inner, which, part, parts):
    tok_rows = left_t.shape[1]
    width = right.shape[1] // parts
    tile = 256
    steps = width // tile
    return pl.pallas_call(
        term_body,
        grid=(steps,),
        in_specs=[
            pl.BlockSpec((inner, tok_rows), lambda i: (which, 0)),
            pl.BlockSpec((tok_rows, tile), lambda i: (0, part * steps + i)),
        ],
        out_specs=pl.BlockSpec((tile, inner), lambda i: (i, 0)),
        out_shape=shape(width, inner),
        compiler_params=params(),
        cost_estimate=cost(2 * inner * tok_rows * width, 2 * tok_rows * (width + inner)),
    )(left_t, right)


def close_body(local_levels, far_bits, dkv_ref, *refs):
    mids = local_levels - 1
    dmid_refs = refs[:mids]
    back_refs = refs[mids : mids + len(far_bits)]
    dk_ref, dv_ref, dkv_t_ref = refs[mids + len(far_bits) :]
    tile = dkv_ref.shape[0]
    offset = pl.program_id(0) * tile
    inner = dk_ref.shape[1]
    total = dkv_ref[...]
    chain = None
    for i in reversed(range(mids)):
        chain = dmid_refs[i][...] if chain is None else dmid_refs[i][...] + chain
        high = chain.astype(BF16)
        low = (chain - high.astype(F32)).astype(BF16)
        rows = chain.shape[0]
        fan = spread_matrix(2 * rows, 1, 0, rows, 0.5)
        chain = dot(fan, high) + dot(fan, low)
    if chain is not None:
        total = total + chain
    for ref, bit in zip(back_refs, far_bits):
        weight = 0.5 ** (local_levels + bit)
        fan = spread_matrix(tile, local_levels + bit, offset, ref.shape[0], weight)
        total = total + dot(fan, ref[...])
    final = total.astype(BF16)
    dk_ref[...] = final[:, :inner]
    dv_ref[...] = final[:, inner:]
    dkv_t_ref[...] = final.T


def close_keys(dkv, dmids, backs, far_bits, local_levels):
    tok_rows, double = dkv.shape
    inner = double // 2
    tile = 2 * BLOCK
    in_specs = [pl.BlockSpec((tile, double), lambda i: (i, 0))]
    in_specs += [pl.BlockSpec((tile >> i, double), lambda i: (i, 0)) for i in range(1, local_levels)]
    in_specs += [whole(*b.shape) for b in backs]
    return pl.pallas_call(
        functools.partial(close_body, local_levels, far_bits),
        grid=(tok_rows // tile,),
        in_specs=in_specs,
        out_specs=[
            pl.BlockSpec((tile, inner), lambda i: (i, 0)),
            pl.BlockSpec((tile, inner), lambda i: (i, 0)),
            pl.BlockSpec((double, tile), lambda i: (0, i)),
        ],
        out_shape=[shape(tok_rows, inner), shape(tok_rows, inner), shape(double, tok_rows)],
        compiler_params=params(),
        cost_estimate=cost(4 * tok_rows * 256 * double, 20 * tok_rows * double),
    )(dkv, *dmids, *backs)


def out_body(count, *refs):
    total = None
    for i in range(count):
        part = dot(refs[i][...], refs[count + i][...], NT)
        total = part if total is None else total + part
    refs[-1][...] = total.astype(BF16)


def project_out(lefts, weights):
    count = len(lefts)
    tok_rows, inner = lefts[0].shape
    width = weights[0].shape[0]
    tile = 2 * BLOCK
    return pl.pallas_call(
        functools.partial(out_body, count),
        grid=(tok_rows // tile,),
        in_specs=[pl.BlockSpec((tile, inner), lambda i: (i, 0))] * count
        + [whole(width, inner)] * count,
        out_specs=pl.BlockSpec((tile, width), lambda i: (i, 0)),
        out_shape=shape(tok_rows, width),
        compiler_params=params(),
        cost_estimate=cost(2 * count * tok_rows * inner * width, 2 * tok_rows * width),
    )(*lefts, *weights)


def exchange(block, axis, distance):
    count = lax.axis_size(axis)
    return lax.ppermute(block, axis, [(i, i ^ distance) for i in range(count)])


def add(left, right):
    return (left.astype(F32) + right.astype(F32)).astype(BF16)


def combine_body(own_ref, into_ref, half_ref, across_ref, next_ref, total_ref):
    next_ref[...] = (own_ref[...].astype(F32) + into_ref[...].astype(F32)).astype(BF16)
    total_ref[...] = (half_ref[...].astype(F32) + across_ref[...].astype(F32)).astype(BF16)


def combine(own, into, half, across):
    return pl.pallas_call(
        combine_body,
        out_shape=[shape(*own.shape), shape(*half.shape)],
        compiler_params=pltpu.CompilerParams(vmem_limit_bytes=8 * MIB),
        cost_estimate=cost(2 * own.size, 12 * own.size),
    )(own, into, half, across)


def line_sums(chunks, axis):
    count = lax.axis_size(axis)
    if count < 4:
        return [add(c, exchange(c, axis, 1)) if count == 2 else c for c in chunks]
    rank = jnp.bitwise_and(lax.axis_index(axis), 3)
    at_end = (rank == 0) | (rank == 3)
    inward, across, outward = [], [], []
    for base in range(0, count, 4):
        inward += [(base, base + 1), (base + 3, base + 2)]
        across += [(base + 1, base + 2), (base + 2, base + 1)]
        outward += [(base + 1, base), (base + 2, base + 3)]
    lag = 2
    halves, crossed, totals, sums = [], [], [], []
    for k in range(len(chunks) + lag):
        if k < len(chunks):
            into = lax.ppermute(chunks[k], axis, inward)
        if k < lag:
            halves.append(add(chunks[k], into))
        elif k < len(chunks):
            half, total = combine(chunks[k], into, halves[k - lag], crossed[k - lag])
            halves.append(half)
            totals.append(total)
        else:
            totals.append(add(halves[k - lag], crossed[k - lag]))
        if k < len(chunks):
            crossed.append(lax.ppermute(halves[k], axis, across))
    for total in totals:
        ends = lax.ppermute(total, axis, outward)
        result = jnp.where(at_end, ends, total)
        distance = 4
        while distance < count:
            result = add(result, exchange(result, axis, distance))
            distance *= 2
        sums.append(result)
    return sums


def per_device(tokens, w_query, w_key, w_value, w_out, cotangent):
    tok_rows = tokens.shape[0]
    inner = w_query.shape[1]
    local_levels = (tok_rows // BLOCK).bit_length() - 1
    count = lax.axis_size("seq")
    far_levels = count.bit_length() - 1
    far_bits = [d.bit_length() - 1 for d in range(1, count)]

    parts = key_value(tokens, w_key, w_value, local_levels, far_levels)
    levels = parts[:local_levels]
    tops = parts[local_levels:]
    fars = [exchange(tops[bit], "seq", d) for d, bit in enumerate(far_bits, 1)]
    query, grad = project_pair(tokens, cotangent, w_query, w_out)
    results = attention(query, grad, levels, fars, far_bits)
    attended, attended_t, dquery, dquery_t, dkv = results[:5]
    dmids = results[5 : 5 + local_levels - 1]
    dfars = results[5 + local_levels - 1 :]
    backs = [exchange(piece, "seq", d) for d, piece in enumerate(dfars, 1)]
    mixed_part = project_out([attended], [w_out])
    mixed = lax.psum_scatter(mixed_part, "head", scatter_dimension=1, tiled=True)
    dkey, dvalue, dkv_t = close_keys(dkv, dmids, backs, far_bits, local_levels)
    grad_part = project_out([dquery, dkey, dvalue], [w_query, w_key, w_value])
    tokens_grad = lax.psum_scatter(grad_part, "head", scatter_dimension=1, tiled=True)

    pieces = 2
    chunks = []
    for left, which, right in (
        (attended_t, 0, cotangent),
        (dquery_t, 0, tokens),
        (dkv_t, 0, tokens),
        (dkv_t, 1, tokens),
    ):
        chunks += [weight_terms(left, right, inner, which, p, pieces) for p in range(pieces)]
    sums = line_sums(chunks, "seq")
    out_grad, query_grad, key_grad, value_grad = (
        jnp.concatenate(sums[i : i + pieces], axis=0) for i in range(0, len(sums), pieces)
    )
    return mixed, tokens_grad, query_grad, key_grad, value_grad, out_grad


def solution(mesh):
    return jax.shard_map(
        per_device,
        mesh=mesh,
        in_specs=(
            P(("groups", "seq"), None),
            P(None, "head"),
            P(None, "head"),
            P(None, "head"),
            P(None, "head"),
            P(("groups", "seq"), None),
        ),
        out_specs=(
            P(("groups", "seq"), "head"),
            P(("groups", "seq"), "head"),
            P("groups", "head"),
            P("groups", "head"),
            P("groups", "head"),
            P("groups", "head"),
        ),
        check_vma=False,
    )
```

```python
import functools
import math

import jax
import jax.numpy as jnp
from jax import lax
from jax.experimental import pallas as pl
from jax.experimental.pallas import tpu as pltpu
from jax.sharding import PartitionSpec as P

HEAD_DIM = 128
BLOCK = 128
BF16 = jnp.bfloat16
F32 = jnp.float32
MIB = 1024 * 1024

NN = (((1,), (0,)), ((), ()))
NT = (((1,), (1,)), ((), ()))
TN = (((0,), (0,)), ((), ()))


def dot(left, right, dims=NN):
    return lax.dot_general(left, right, dims, preferred_element_type=F32)


def params(mib):
    return pltpu.CompilerParams(vmem_limit_bytes=mib * MIB)


def cost(flops, moved, exps=0):
    return pl.CostEstimate(flops=int(flops), bytes_accessed=int(moved), transcendentals=int(exps))


def shape(rows, cols, dtype=BF16):
    return jax.ShapeDtypeStruct((rows, cols), dtype)


def whole(rows, cols):
    return pl.BlockSpec((rows, cols), lambda *_: (0, 0))


def pool_matrix(rows):
    row = lax.broadcasted_iota(jnp.int32, (rows // 2, rows), 0)
    col = lax.broadcasted_iota(jnp.int32, (rows // 2, rows), 1)
    return jnp.where(jnp.right_shift(col, 1) == row, 0.5, 0.0).astype(BF16)


def spread_matrix(rows, step_bits, offset, cols, weight):
    row = lax.broadcasted_iota(jnp.int32, (rows, cols), 0) + offset
    col = lax.broadcasted_iota(jnp.int32, (rows, cols), 1)
    return jnp.where(jnp.right_shift(row, step_bits) == col, weight, 0.0).astype(BF16)


def key_value_body(local_levels, far_levels, parts, tok_hbm, wk_hbm, wv_hbm, *refs):
    kv_ref = refs[0]
    mid = refs[1:local_levels]
    far = refs[local_levels : local_levels + far_levels]
    tok_ref, wk_ref, wv_ref, sems = refs[local_levels + far_levels :]
    part = tok_ref.shape[0] // parts
    copies = [
        pltpu.make_async_copy(wk_hbm, wk_ref, sems.at[0]),
        pltpu.make_async_copy(wv_hbm, wv_ref, sems.at[1]),
    ]
    for p in range(parts):
        rows = pl.ds(p * part, part)
        copies.append(pltpu.make_async_copy(tok_hbm.at[rows], tok_ref.at[rows], sems.at[2 + p]))
    for copy in (copies[2], *copies[:2], *copies[3:]):
        copy.start()
    copies[0].wait()
    copies[1].wait()
    tops = []
    for p in range(parts):
        copies[2 + p].wait()
        x = tok_ref[p * part : (p + 1) * part, :]
        rows = jnp.concatenate([dot(x, wk_ref[...]), dot(x, wv_ref[...])], axis=1).astype(BF16)
        kv_ref[p * part : (p + 1) * part, :] = rows
        for ref in mid:
            rows = dot(pool_matrix(rows.shape[0]), rows).astype(BF16)
            ref[p * rows.shape[0] : (p + 1) * rows.shape[0], :] = rows
        tops.append(dot(pool_matrix(rows.shape[0]), rows).astype(BF16))
    rows = jnp.concatenate(tops, axis=0)
    for i in range(far_levels):
        if i:
            rows = dot(pool_matrix(rows.shape[0]), rows).astype(BF16)
        far[i][...] = rows


def key_value(tokens, w_key, w_value, local_levels, far_levels):
    tok_rows, width = tokens.shape
    inner = w_key.shape[1]
    parts = tok_rows // (2 * BLOCK)
    out_shape = [shape(tok_rows >> i, 2 * inner) for i in range(local_levels)]
    out_shape += [shape(BLOCK >> i, 2 * inner) for i in range(far_levels)]
    return pl.pallas_call(
        functools.partial(key_value_body, local_levels, far_levels, parts),
        in_specs=[pl.BlockSpec(memory_space=pl.ANY)] * 3,
        out_shape=out_shape,
        scratch_shapes=[
            pltpu.VMEM((tok_rows, width), BF16),
            pltpu.VMEM((width, inner), BF16),
            pltpu.VMEM((width, inner), BF16),
            pltpu.SemaphoreType.DMA((parts + 2,)),
        ],
        compiler_params=params(56),
        cost_estimate=cost(4 * tok_rows * width * inner, 2 * tok_rows * width + 8 * width * inner),
    )(tokens, w_key, w_value)


def pair_body(a_ref, b_ref, wa_ref, wb_ref, x_ref, y_ref):
    x_ref[...] = dot(a_ref[...], wa_ref[...]).astype(BF16)
    y_ref[...] = dot(b_ref[...], wb_ref[...]).astype(BF16)


def project_pair(a, b, wa, wb):
    tok_rows, width = a.shape
    inner = wa.shape[1]
    return pl.pallas_call(
        pair_body,
        out_shape=[shape(tok_rows, inner)] * 2,
        compiler_params=params(8),
        cost_estimate=cost(4 * tok_rows * width * inner, 4 * tok_rows * width + 8 * width * inner),
    )(a, b, wa, wb)


class KeySet:
    def __init__(self, far_rows, far_bits, local_levels):
        mids = local_levels - 1
        self.sizes = [2 * BLOCK] + [BLOCK] * mids + list(far_rows)
        self.bounds = [sum(self.sizes[:i]) for i in range(len(self.sizes) + 1)]
        steps = [0] + list(range(1, local_levels)) + [local_levels + b for b in far_bits]
        self.biases = [float(step) for step in steps]
        self.mids = mids
        self.far_start = self.bounds[1 + mids]
        self.factor = math.log2(math.e) / math.sqrt(HEAD_DIM)

    def here(self, m):
        return pl.ds(pl.multiple_of(m * 2 * BLOCK, 2 * BLOCK), 2 * BLOCK)

    def seats(self, m):
        for i in range(self.mids):
            sibling = jnp.bitwise_xor(jnp.right_shift(m, i), 1)
            yield pl.ds(pl.multiple_of(sibling * BLOCK, BLOCK), BLOCK)

    def rows(self, m, kv_ref, mid_refs, far_refs, cols):
        rows = [kv_ref[self.here(m), cols]]
        rows += [ref[seat, cols] for ref, seat in zip(mid_refs, self.seats(m))]
        rows += [ref[:, cols] for ref in far_refs]
        return jnp.concatenate(rows, axis=0)

    def pieces(self, array):
        return [array[a:b] for a, b in zip(self.bounds, self.bounds[1:])]

    def top(self, raw):
        tops = [
            jnp.max(piece, axis=0, keepdims=True) * self.factor + bias
            for piece, bias in zip(self.pieces(raw), self.biases)
        ]
        return functools.reduce(jnp.maximum, tops)

    def powers(self, raw, top):
        return jnp.concatenate(
            [
                jnp.exp2(piece * self.factor + (bias - top))
                for piece, bias in zip(self.pieces(raw), self.biases)
            ],
            axis=0,
        )


def forward_body(local_levels, far_bits, *refs):
    mids = local_levels - 1
    fars = len(far_bits)
    q_ref, kv_ref = refs[:2]
    mid_refs = refs[2 : 2 + mids]
    far_refs = refs[2 + mids : 2 + mids + fars]
    att_ref, att_t_ref, stat_ref = refs[2 + mids + fars :]
    tok_rows, inner = q_ref.shape
    heads = inner // HEAD_DIM
    keyset = KeySet([r.shape[0] for r in far_refs], far_bits, local_levels)

    def step(m, carry):
        here = keyset.here(m)
        for h in range(heads):
            cols = slice(h * HEAD_DIM, (h + 1) * HEAD_DIM)
            vcols = slice(inner + h * HEAD_DIM, inner + (h + 1) * HEAD_DIM)
            keys = keyset.rows(m, kv_ref, mid_refs, far_refs, cols)
            values = keyset.rows(m, kv_ref, mid_refs, far_refs, vcols)
            raw = dot(keys, q_ref[here, cols], NT)
            top = keyset.top(raw)
            expo = keyset.powers(raw, top)
            inverse = 1.0 / jnp.sum(expo, axis=0, keepdims=True)
            att_t = dot(values, (expo * inverse).astype(BF16), TN).astype(BF16)
            att_t_ref[cols, here] = att_t
            att_ref[here, cols] = att_t.T
            stat_ref[h : h + 1, here] = top
            stat_ref[heads + h : heads + h + 1, here] = inverse
        return carry

    lax.fori_loop(0, tok_rows // (2 * BLOCK), step, 0)


def forward(query, levels, fars, far_bits):
    tok_rows, inner = query.shape
    heads = inner // HEAD_DIM
    set_rows = (len(levels) + 1) * BLOCK + sum(f.shape[0] for f in fars)
    return pl.pallas_call(
        functools.partial(forward_body, len(levels), far_bits),
        out_shape=[
            shape(tok_rows, inner),
            shape(inner, tok_rows),
            shape(2 * heads, tok_rows, F32),
        ],
        compiler_params=params(12),
        cost_estimate=cost(
            4 * tok_rows * set_rows * inner, 12 * tok_rows * inner, tok_rows * set_rows * 2
        ),
    )(query, *levels, *fars)


def backward_body(local_levels, far_bits, *refs):
    mids = local_levels - 1
    fars = len(far_bits)
    q_ref, g_ref, att_t_ref, stat_ref, kv_ref = refs[:5]
    mid_refs = refs[5 : 5 + mids]
    far_refs = refs[5 + mids : 5 + mids + fars]
    outs = refs[5 + mids + fars :]
    dq_ref, dq_t_ref, dkv_ref = outs[:3]
    dmid_refs = outs[3 : 3 + mids]
    dfar_refs = outs[3 + mids : 3 + mids + fars]
    acc_ref = outs[-1]
    tok_rows, inner = q_ref.shape
    heads = inner // HEAD_DIM
    score_scale = 1.0 / math.sqrt(HEAD_DIM)
    keyset = KeySet([r.shape[0] for r in far_refs], far_bits, local_levels)

    for ref in (*dmid_refs, acc_ref):
        ref[...] = jnp.zeros_like(ref)

    def step(m, carry):
        here = keyset.here(m)
        for h in range(heads):
            cols = slice(h * HEAD_DIM, (h + 1) * HEAD_DIM)
            vcols = slice(inner + h * HEAD_DIM, inner + (h + 1) * HEAD_DIM)
            keys = keyset.rows(m, kv_ref, mid_refs, far_refs, cols)
            values = keyset.rows(m, kv_ref, mid_refs, far_refs, vcols)
            q = q_ref[here, cols]
            g = g_ref[here, cols]
            top = stat_ref[h : h + 1, here]
            inverse = stat_ref[heads + h : heads + h + 1, here]
            probs = keyset.powers(dot(keys, q, NT), top) * inverse
            att_t = att_t_ref[cols, here].astype(F32)
            delta = jnp.sum(g.T.astype(F32) * att_t, axis=0, keepdims=True)
            grads = (probs * (dot(values, g, NT) - delta) * score_scale).astype(BF16)
            dq_t = dot(keys, grads, TN).astype(BF16)
            dq_t_ref[cols, here] = dq_t
            dq_ref[here, cols] = dq_t.T
            for part, place in ((dot(grads, q), cols), (dot(probs.astype(BF16), g), vcols)):
                own, *sides = keyset.pieces(part)
                dkv_ref[here, place] = own
                for ref, seat, side in zip(dmid_refs, keyset.seats(m), sides):
                    ref[seat, place] += side
                acc_ref[:, place] += part[keyset.far_start :]
        return carry

    lax.fori_loop(0, tok_rows // (2 * BLOCK), step, 0)
    low = 0
    for ref in dfar_refs:
        ref[...] = acc_ref[low : low + ref.shape[0]].astype(BF16)
        low += ref.shape[0]


def backward(query, grad, attended_t, stats, levels, fars, far_bits):
    tok_rows, inner = query.shape
    far_rows = sum(f.shape[0] for f in fars)
    set_rows = (len(levels) + 1) * BLOCK + far_rows
    return pl.pallas_call(
        functools.partial(backward_body, len(levels), far_bits),
        out_shape=[shape(tok_rows, inner), shape(inner, tok_rows)]
        + [shape(*level.shape, F32) for level in levels]
        + [shape(*f.shape) for f in fars],
        scratch_shapes=[pltpu.VMEM((far_rows, 2 * inner), F32)],
        compiler_params=params(16),
        cost_estimate=cost(
            10 * tok_rows * set_rows * inner, 24 * tok_rows * inner, tok_rows * set_rows * 2
        ),
    )(query, grad, attended_t, stats, *levels, *fars)


def term_body(which, low, left_ref, right_ref, out_ref):
    width, inner = out_ref.shape
    left = left_ref[which * inner : (which + 1) * inner, :]
    out_ref[...] = dot(left, right_ref[:, low : low + width]).astype(BF16).T


def weight_terms(left_t, right, inner, which, part, parts):
    tok_rows = left_t.shape[1]
    width = right.shape[1] // parts
    return pl.pallas_call(
        functools.partial(term_body, which, part * width),
        out_shape=shape(width, inner),
        compiler_params=params(6),
        cost_estimate=cost(2 * inner * tok_rows * width, 2 * tok_rows * (width + inner)),
    )(left_t, right)


def close_body(local_levels, far_bits, dkv_ref, *refs):
    mids = local_levels - 1
    dmid_refs = refs[:mids]
    back_refs = refs[mids : mids + len(far_bits)]
    dk_ref, dv_ref, dkv_t_ref = refs[mids + len(far_bits) :]
    inner = dk_ref.shape[1]
    tile = 2 * BLOCK
    for t in range(dkv_ref.shape[0] // tile):
        here = slice(t * tile, (t + 1) * tile)
        chain = None
        for i in reversed(range(mids)):
            rows = tile >> (i + 1)
            part = dmid_refs[i][t * rows : (t + 1) * rows, :]
            chain = part if chain is None else part + chain
            high = chain.astype(BF16)
            low = (chain - high.astype(F32)).astype(BF16)
            fan = spread_matrix(2 * rows, 1, 0, rows, 0.5)
            chain = dot(fan, high) + dot(fan, low)
        total = dkv_ref[here, :]
        if chain is not None:
            total = total + chain
        for ref, bit in zip(back_refs, far_bits):
            weight = 0.5 ** (local_levels + bit)
            fan = spread_matrix(tile, local_levels + bit, t * tile, ref.shape[0], weight)
            total = total + dot(fan, ref[...])
        final = total.astype(BF16)
        dk_ref[here, :] = final[:, :inner]
        dv_ref[here, :] = final[:, inner:]
        dkv_t_ref[:, here] = final.T


def close_keys(dkv, dmids, backs, far_bits, local_levels):
    tok_rows, double = dkv.shape
    inner = double // 2
    return pl.pallas_call(
        functools.partial(close_body, local_levels, far_bits),
        out_shape=[shape(tok_rows, inner), shape(tok_rows, inner), shape(double, tok_rows)],
        compiler_params=params(8),
        cost_estimate=cost(4 * tok_rows * 256 * double, 20 * tok_rows * double),
    )(dkv, *dmids, *backs)


def out_body(left_ref, weight_ref, out_ref):
    out_ref[...] = dot(left_ref[...], weight_ref[...], NT).astype(BF16)


def project_out(left, weight):
    tok_rows, inner = left.shape
    width = weight.shape[0]
    return pl.pallas_call(
        out_body,
        out_shape=shape(tok_rows, width),
        compiler_params=params(8),
        cost_estimate=cost(2 * tok_rows * inner * width, 2 * tok_rows * width),
    )(left, weight)


def split_body(count, parts, rank_ref, *refs):
    lefts, weights = refs[:count], refs[count : 2 * count]
    outs = refs[2 * count :]
    width = weights[0].shape[0] // parts
    for r in range(parts):
        owner = jnp.bitwise_xor(rank_ref[0], r)
        rows = pl.ds(pl.multiple_of(owner * width, width), width)
        total = None
        for left, weight in zip(lefts, weights):
            product = dot(left[...], weight[rows, :], NT)
            total = product if total is None else total + product
        place = r // 2 * width
        outs[r % 2][:, place : place + width] = total.astype(BF16)


def project_split(lefts, weights, axis):
    count = len(lefts)
    parts = lax.axis_size(axis)
    tok_rows, inner = lefts[0].shape
    width = weights[0].shape[0]
    rank = jnp.reshape(lax.axis_index(axis), (1,)).astype(jnp.int32)
    return pl.pallas_call(
        functools.partial(split_body, count, parts),
        in_specs=[pl.BlockSpec(memory_space=pltpu.SMEM)]
        + [pl.BlockSpec(memory_space=pltpu.VMEM)] * (2 * count),
        out_shape=[shape(tok_rows, width // 2)] * 2,
        compiler_params=params(8),
        cost_estimate=cost(2 * count * tok_rows * inner * width, 2 * tok_rows * width),
    )(rank, *lefts, *weights)


def exchange(block, axis, distance):
    count = lax.axis_size(axis)
    return lax.ppermute(block, axis, [(i, i ^ distance) for i in range(count)])


def add(left, right):
    return (left.astype(F32) + right.astype(F32)).astype(BF16)


def scatter_sum(keep, send, axis):
    parts = lax.axis_size(axis) // 2
    width = keep.shape[1] // parts
    pieces = [keep[:, i * width : (i + 1) * width] for i in range(parts)]
    distance = 1
    while True:
        into = exchange(send, axis, distance)
        for i in reversed(range(len(pieces))):
            pieces[i] = add(pieces[i], into[:, i * width : (i + 1) * width])
        if len(pieces) == 1:
            return pieces[0]
        away = pieces[1::2]
        send = away[0] if len(away) == 1 else jnp.concatenate(away, axis=1)
        pieces = pieces[0::2]
        distance *= 2


def combine_body(own_ref, into_ref, half_ref, across_ref, next_ref, total_ref):
    next_ref[...] = (own_ref[...].astype(F32) + into_ref[...].astype(F32)).astype(BF16)
    total_ref[...] = (half_ref[...].astype(F32) + across_ref[...].astype(F32)).astype(BF16)


def combine(own, into, half, across):
    return pl.pallas_call(
        combine_body,
        out_shape=[shape(*own.shape), shape(*half.shape)],
        compiler_params=pltpu.CompilerParams(vmem_limit_bytes=8 * MIB),
        cost_estimate=cost(2 * own.size, 12 * own.size),
    )(own, into, half, across)


def line_sums(chunks, axis):
    count = lax.axis_size(axis)
    if count < 4:
        return [add(c, exchange(c, axis, 1)) if count == 2 else c for c in chunks]
    rank = jnp.bitwise_and(lax.axis_index(axis), 3)
    at_end = (rank == 0) | (rank == 3)
    inward, across, outward = [], [], []
    for base in range(0, count, 4):
        inward += [(base, base + 1), (base + 3, base + 2)]
        across += [(base + 1, base + 2), (base + 2, base + 1)]
        outward += [(base + 1, base), (base + 2, base + 3)]
    lag = 2
    halves, crossed, totals, sums = [], [], [], []
    for k in range(len(chunks) + lag):
        if k < len(chunks):
            into = lax.ppermute(chunks[k], axis, inward)
        if k < lag:
            halves.append(add(chunks[k], into))
        elif k < len(chunks):
            half, total = combine(chunks[k], into, halves[k - lag], crossed[k - lag])
            halves.append(half)
            totals.append(total)
        else:
            totals.append(add(halves[k - lag], crossed[k - lag]))
        if k < len(chunks):
            crossed.append(lax.ppermute(halves[k], axis, across))
    for total in totals:
        ends = lax.ppermute(total, axis, outward)
        result = jnp.where(at_end, ends, total)
        distance = 4
        while distance < count:
            result = add(result, exchange(result, axis, distance))
            distance *= 2
        sums.append(result)
    return sums


def per_device(tokens, w_query, w_key, w_value, w_out, cotangent):
    tok_rows = tokens.shape[0]
    inner = w_query.shape[1]
    local_levels = (tok_rows // BLOCK).bit_length() - 1
    count = lax.axis_size("seq")
    far_levels = count.bit_length() - 1
    far_bits = [d.bit_length() - 1 for d in range(1, count)]

    parts = key_value(tokens, w_key, w_value, local_levels, far_levels)
    levels = parts[:local_levels]
    tops = parts[local_levels:]
    fars = [exchange(tops[bit], "seq", d) for d, bit in enumerate(far_bits, 1)]
    query, grad = project_pair(tokens, cotangent, w_query, w_out)
    attended, attended_t, stats = forward(query, levels, fars, far_bits)
    results = backward(query, grad, attended_t, stats, levels, fars, far_bits)
    dquery, dquery_t, dkv = results[:3]
    dmids = results[3 : 3 + local_levels - 1]
    dfars = results[3 + local_levels - 1 :]
    backs = [exchange(piece, "seq", d) for d, piece in enumerate(dfars, 1)]
    mixed_part = project_out(attended, w_out)
    mixed = lax.psum_scatter(mixed_part, "head", scatter_dimension=1, tiled=True)
    dkey, dvalue, dkv_t = close_keys(dkv, dmids, backs, far_bits, local_levels)
    keep, send = project_split([dquery, dkey, dvalue], [w_query, w_key, w_value], "head")
    tokens_grad = scatter_sum(keep, send, "head")

    pieces = 2
    chunks = []
    for left, which, right in (
        (attended_t, 0, cotangent),
        (dquery_t, 0, tokens),
        (dkv_t, 0, tokens),
        (dkv_t, 1, tokens),
    ):
        chunks += [weight_terms(left, right, inner, which, p, pieces) for p in range(pieces)]
    sums = line_sums(chunks, "seq")
    out_grad, query_grad, key_grad, value_grad = (
        jnp.concatenate(sums[i : i + pieces], axis=0) for i in range(0, len(sums), pieces)
    )
    return mixed, tokens_grad, query_grad, key_grad, value_grad, out_grad


def solution(mesh):
    return jax.shard_map(
        per_device,
        mesh=mesh,
        in_specs=(
            P(("groups", "seq"), None),
            P(None, "head"),
            P(None, "head"),
            P(None, "head"),
            P(None, "head"),
            P(("groups", "seq"), None),
        ),
        out_specs=(
            P(("groups", "seq"), "head"),
            P(("groups", "seq"), "head"),
            P("groups", "head"),
            P("groups", "head"),
            P("groups", "head"),
            P("groups", "head"),
        ),
        check_vma=False,
    )
```

```python
import functools
import math

import jax
import jax.numpy as jnp
from jax import lax
from jax.experimental import pallas as pl
from jax.experimental.pallas import tpu as pltpu
from jax.sharding import PartitionSpec as P

HEAD_DIM = 128
BLOCK = 128
BF16 = jnp.bfloat16
F32 = jnp.float32
MIB = 1024 * 1024

NN = (((1,), (0,)), ((), ()))
NT = (((1,), (1,)), ((), ()))
TN = (((0,), (0,)), ((), ()))


def dot(left, right, dims=NN):
    return lax.dot_general(left, right, dims, preferred_element_type=F32)


def params(mib):
    return pltpu.CompilerParams(vmem_limit_bytes=mib * MIB)


def cost(flops, moved, exps=0):
    return pl.CostEstimate(flops=int(flops), bytes_accessed=int(moved), transcendentals=int(exps))


def run(body, ready, after=(), in_specs=None, **options):
    count, extra = len(ready), len(after)

    def kernel(*refs):
        body(*refs[:count], *refs[count + extra :])

    in_specs = in_specs or [pl.BlockSpec(memory_space=pltpu.VMEM)] * count
    in_specs = in_specs + [pl.BlockSpec(memory_space=pl.ANY)] * extra
    return pl.pallas_call(kernel, in_specs=in_specs, **options)(*ready, *after)


def shape(rows, cols, dtype=BF16):
    return jax.ShapeDtypeStruct((rows, cols), dtype)


def whole(rows, cols):
    return pl.BlockSpec((rows, cols), lambda *_: (0, 0))


def pool_matrix(rows):
    row = lax.broadcasted_iota(jnp.int32, (rows // 2, rows), 0)
    col = lax.broadcasted_iota(jnp.int32, (rows // 2, rows), 1)
    return jnp.where(jnp.right_shift(col, 1) == row, 0.5, 0.0).astype(BF16)


def spread_matrix(rows, step_bits, offset, cols, weight):
    row = lax.broadcasted_iota(jnp.int32, (rows, cols), 0) + offset
    col = lax.broadcasted_iota(jnp.int32, (rows, cols), 1)
    return jnp.where(jnp.right_shift(row, step_bits) == col, weight, 0.0).astype(BF16)


def key_value_body(local_levels, far_levels, parts, tok_hbm, wk_hbm, wv_hbm, wq_hbm, *refs):
    count = local_levels + 1
    out_hbm = refs[:count]
    far = refs[count : count + far_levels]
    refs = refs[count + far_levels :]
    tok_ref, wk_ref, wv_ref, wq_ref = refs[:4]
    held = refs[4 : 4 + count]
    in_sems, out_sems = refs[4 + count :]
    part = tok_ref.shape[0] // parts

    def fetch(source, target, i):
        copy = pltpu.make_async_copy(source, target, in_sems.at[i])
        copy.start()
        return copy

    def flush(i):
        copy = pltpu.make_async_copy(held[i], out_hbm[i], out_sems.at[i])
        copy.start()
        return copy

    weights = [fetch(wk_hbm, wk_ref, 0), fetch(wv_hbm, wv_ref, 1)]
    tiles = []
    for p in range(parts):
        rows = pl.ds(p * part, part)
        tiles.append(fetch(tok_hbm.at[rows], tok_ref.at[rows], 3 + p))
    weights.append(fetch(wq_hbm, wq_ref, 2))
    kv_ref, q_ref = held[0], held[-1]
    weights[0].wait()
    weights[1].wait()
    for p in range(parts):
        tiles[p].wait()
        here = slice(p * part, (p + 1) * part)
        x = tok_ref[here, :]
        both = jnp.concatenate([dot(x, wk_ref[...]), dot(x, wv_ref[...])], axis=1)
        kv_ref[here, :] = both.astype(BF16)
    flushes = [flush(0)]
    weights[2].wait()
    q_ref[...] = dot(tok_ref[...], wq_ref[...]).astype(BF16)
    pool = pool_matrix(part)
    source = kv_ref
    for i in range(1, local_levels):
        rows = source.shape[0]
        for low in range(0, rows, part):
            held[i][low // 2 : (low + part) // 2, :] = dot(pool, source[low : low + part, :]).astype(BF16)
        flushes.append(flush(i))
        source = held[i]
    flushes.append(flush(count - 1))
    rows = dot(pool, source[...]).astype(BF16)
    for i in range(far_levels):
        if i:
            rows = dot(pool_matrix(rows.shape[0]), rows).astype(BF16)
        far[i][...] = rows
    for copy in flushes:
        copy.wait()


def key_value(tokens, w_key, w_value, w_query, local_levels, far_levels):
    tok_rows, width = tokens.shape
    inner = w_key.shape[1]
    parts = tok_rows // (2 * BLOCK)
    held = [(tok_rows >> i, 2 * inner) for i in range(local_levels)] + [(tok_rows, inner)]
    tops = [(BLOCK >> i, 2 * inner) for i in range(far_levels)]
    return pl.pallas_call(
        functools.partial(key_value_body, local_levels, far_levels, parts),
        in_specs=[pl.BlockSpec(memory_space=pl.ANY)] * 4,
        out_specs=[pl.BlockSpec(memory_space=pl.ANY)] * len(held)
        + [pl.BlockSpec(memory_space=pltpu.VMEM)] * len(tops),
        out_shape=[shape(*dims) for dims in held + tops],
        scratch_shapes=[pltpu.VMEM((tok_rows, width), BF16)]
        + [pltpu.VMEM((width, inner), BF16)] * 3
        + [pltpu.VMEM(dims, BF16) for dims in held]
        + [pltpu.SemaphoreType.DMA((parts + 3,)), pltpu.SemaphoreType.DMA((len(held),))],
        compiler_params=params(56),
        cost_estimate=cost(6 * tok_rows * width * inner, 2 * tok_rows * width + 12 * width * inner),
    )(tokens, w_key, w_value, w_query)


def project_body(left_ref, weight_ref, out_ref):
    out_ref[...] = dot(left_ref[...], weight_ref[...]).astype(BF16)


def project(left, weight):
    tok_rows, width = left.shape
    inner = weight.shape[1]
    return pl.pallas_call(
        project_body,
        out_shape=shape(tok_rows, inner),
        compiler_params=params(4),
        cost_estimate=cost(2 * tok_rows * width * inner, 2 * tok_rows * width + 4 * width * inner),
    )(left, weight)


class KeySet:
    def __init__(self, far_rows, far_bits, local_levels):
        mids = local_levels - 1
        self.sizes = [2 * BLOCK] + [BLOCK] * mids + list(far_rows)
        self.bounds = [sum(self.sizes[:i]) for i in range(len(self.sizes) + 1)]
        steps = [0] + list(range(1, local_levels)) + [local_levels + b for b in far_bits]
        self.biases = [float(step) for step in steps]
        self.mids = mids
        self.far_start = self.bounds[1 + mids]
        self.factor = math.log2(math.e) / math.sqrt(HEAD_DIM)

    def here(self, m):
        return pl.ds(pl.multiple_of(m * 2 * BLOCK, 2 * BLOCK), 2 * BLOCK)

    def seats(self, m):
        for i in range(self.mids):
            sibling = jnp.bitwise_xor(jnp.right_shift(m, i), 1)
            yield pl.ds(pl.multiple_of(sibling * BLOCK, BLOCK), BLOCK)

    def rows(self, m, kv_ref, mid_refs, far_refs, cols):
        rows = [kv_ref[self.here(m), cols]]
        rows += [ref[seat, cols] for ref, seat in zip(mid_refs, self.seats(m))]
        rows += [ref[:, cols] for ref in far_refs]
        return jnp.concatenate(rows, axis=0)

    def pieces(self, array):
        return [array[a:b] for a, b in zip(self.bounds, self.bounds[1:])]

    def top(self, raw):
        tops = [
            jnp.max(piece, axis=0, keepdims=True) * self.factor + bias
            for piece, bias in zip(self.pieces(raw), self.biases)
        ]
        return functools.reduce(jnp.maximum, tops)

    def powers(self, raw, top):
        return jnp.concatenate(
            [
                jnp.exp2(piece * self.factor + (bias - top))
                for piece, bias in zip(self.pieces(raw), self.biases)
            ],
            axis=0,
        )


def forward_body(local_levels, far_bits, *refs):
    mids = local_levels - 1
    fars = len(far_bits)
    q_ref, kv_ref = refs[:2]
    mid_refs = refs[2 : 2 + mids]
    far_refs = refs[2 + mids : 2 + mids + fars]
    att_ref, att_t_ref, stat_ref = refs[2 + mids + fars :]
    tok_rows, inner = q_ref.shape
    heads = inner // HEAD_DIM
    keyset = KeySet([r.shape[0] for r in far_refs], far_bits, local_levels)

    def step(m, carry):
        here = keyset.here(m)
        for h in range(heads):
            cols = slice(h * HEAD_DIM, (h + 1) * HEAD_DIM)
            vcols = slice(inner + h * HEAD_DIM, inner + (h + 1) * HEAD_DIM)
            keys = keyset.rows(m, kv_ref, mid_refs, far_refs, cols)
            values = keyset.rows(m, kv_ref, mid_refs, far_refs, vcols)
            raw = dot(keys, q_ref[here, cols], NT)
            top = keyset.top(raw)
            expo = keyset.powers(raw, top)
            inverse = 1.0 / jnp.sum(expo, axis=0, keepdims=True)
            att_t = dot(values, (expo * inverse).astype(BF16), TN).astype(BF16)
            att_t_ref[cols, here] = att_t
            att_ref[here, cols] = att_t.T
            stat_ref[h : h + 1, here] = top
            stat_ref[heads + h : heads + h + 1, here] = inverse
        return carry

    lax.fori_loop(0, tok_rows // (2 * BLOCK), step, 0)


def forward(query, levels, fars, far_bits):
    tok_rows, inner = query.shape
    heads = inner // HEAD_DIM
    set_rows = (len(levels) + 1) * BLOCK + sum(f.shape[0] for f in fars)
    return pl.pallas_call(
        functools.partial(forward_body, len(levels), far_bits),
        out_shape=[
            shape(tok_rows, inner),
            shape(inner, tok_rows),
            shape(2 * heads, tok_rows, F32),
        ],
        compiler_params=params(8),
        cost_estimate=cost(
            4 * tok_rows * set_rows * inner, 12 * tok_rows * inner, tok_rows * set_rows * 2
        ),
    )(query, *levels, *fars)


def backward_body(local_levels, far_bits, *refs):
    mids = local_levels - 1
    fars = len(far_bits)
    q_ref, g_ref, att_t_ref, stat_ref, kv_ref = refs[:5]
    mid_refs = refs[5 : 5 + mids]
    far_refs = refs[5 + mids : 5 + mids + fars]
    outs = refs[5 + mids + fars :]
    dq_ref, dq_t_ref, dkv_ref = outs[:3]
    dfar_refs = outs[3 : 3 + fars]
    dmid_refs = outs[3 + fars : 3 + fars + mids]
    acc_ref = outs[-1]
    tok_rows, inner = q_ref.shape
    heads = inner // HEAD_DIM
    score_scale = 1.0 / math.sqrt(HEAD_DIM)
    keyset = KeySet([r.shape[0] for r in far_refs], far_bits, local_levels)

    for ref in (*dmid_refs, acc_ref):
        ref[...] = jnp.zeros_like(ref)

    def step(m, carry):
        here = keyset.here(m)
        for h in range(heads):
            cols = slice(h * HEAD_DIM, (h + 1) * HEAD_DIM)
            vcols = slice(inner + h * HEAD_DIM, inner + (h + 1) * HEAD_DIM)
            keys = keyset.rows(m, kv_ref, mid_refs, far_refs, cols)
            values = keyset.rows(m, kv_ref, mid_refs, far_refs, vcols)
            q = q_ref[here, cols]
            g = g_ref[here, cols]
            top = stat_ref[h : h + 1, here]
            inverse = stat_ref[heads + h : heads + h + 1, here]
            probs = keyset.powers(dot(keys, q, NT), top) * inverse
            att_t = att_t_ref[cols, here].astype(F32)
            delta = jnp.sum(g.T.astype(F32) * att_t, axis=0, keepdims=True)
            grads = (probs * (dot(values, g, NT) - delta) * score_scale).astype(BF16)
            dq_t = dot(keys, grads, TN).astype(BF16)
            dq_t_ref[cols, here] = dq_t
            dq_ref[here, cols] = dq_t.T
            for part, place in ((dot(grads, q), cols), (dot(probs.astype(BF16), g), vcols)):
                own, *sides = keyset.pieces(part)
                dkv_ref[here, place] = own
                for ref, seat, side in zip(dmid_refs, keyset.seats(m), sides):
                    ref[seat, place] += side
                acc_ref[:, place] += part[keyset.far_start :]
        return carry

    lax.fori_loop(0, tok_rows // (2 * BLOCK), step, 0)
    low = 0
    for ref in dfar_refs:
        ref[...] = acc_ref[low : low + ref.shape[0]].astype(BF16)
        low += ref.shape[0]
    fan = spread_matrix(2 * BLOCK, 1, 0, BLOCK, 0.5)
    targets = (dkv_ref, *dmid_refs)
    for i in reversed(range(mids)):
        for t in range(dmid_refs[i].shape[0] // BLOCK):
            part = dmid_refs[i][t * BLOCK : (t + 1) * BLOCK, :]
            high = part.astype(BF16)
            low = (part - high.astype(F32)).astype(BF16)
            rows = slice(2 * t * BLOCK, 2 * (t + 1) * BLOCK)
            targets[i][rows, :] += dot(fan, high) + dot(fan, low)


def backward(query, grad, attended_t, stats, levels, fars, far_bits, after):
    tok_rows, inner = query.shape
    far_rows = sum(f.shape[0] for f in fars)
    set_rows = (len(levels) + 1) * BLOCK + far_rows
    return run(
        functools.partial(backward_body, len(levels), far_bits),
        [query, grad, attended_t, stats, *levels, *fars],
        after,
        out_shape=[shape(tok_rows, inner), shape(inner, tok_rows)]
        + [shape(tok_rows, 2 * inner, F32)]
        + [shape(*f.shape) for f in fars],
        scratch_shapes=[pltpu.VMEM(level.shape, F32) for level in levels[1:]]
        + [pltpu.VMEM((far_rows, 2 * inner), F32)],
        compiler_params=params(10),
        cost_estimate=cost(
            10 * tok_rows * set_rows * inner, 24 * tok_rows * inner, tok_rows * set_rows * 2
        ),
    )


def term_body(which, low, left_ref, right_ref, out_ref):
    width, inner = out_ref.shape
    left = left_ref[which * inner : (which + 1) * inner, :]
    out_ref[...] = dot(left, right_ref[:, low : low + width]).astype(BF16).T


def weight_terms(left_t, right, inner, which, part, parts, after):
    tok_rows = left_t.shape[1]
    width = right.shape[1] // parts
    return run(
        functools.partial(term_body, which, part * width),
        [left_t, right],
        after,
        out_shape=shape(width, inner),
        compiler_params=params(3),
        cost_estimate=cost(2 * inner * tok_rows * width, 2 * tok_rows * (width + inner)),
    )


def close_body(local_levels, far_bits, dkv_ref, *refs):
    back_refs = refs[: len(far_bits)]
    dk_ref, dv_ref, dkv_t_ref = refs[len(far_bits) :]
    inner = dk_ref.shape[1]
    tile = 2 * BLOCK
    for t in range(dkv_ref.shape[0] // tile):
        here = slice(t * tile, (t + 1) * tile)
        total = dkv_ref[here, :]
        for ref, bit in zip(back_refs, far_bits):
            weight = 0.5 ** (local_levels + bit)
            fan = spread_matrix(tile, local_levels + bit, t * tile, ref.shape[0], weight)
            total = total + dot(fan, ref[...])
        final = total.astype(BF16)
        dk_ref[here, :] = final[:, :inner]
        dv_ref[here, :] = final[:, inner:]
        dkv_t_ref[:, here] = final.T


def close_keys(dkv, backs, far_bits, local_levels, after):
    tok_rows, double = dkv.shape
    inner = double // 2
    return run(
        functools.partial(close_body, local_levels, far_bits),
        [dkv, *backs],
        after,
        out_shape=[shape(tok_rows, inner), shape(tok_rows, inner), shape(double, tok_rows)],
        compiler_params=params(5),
        cost_estimate=cost(2 * tok_rows * 256 * double, 12 * tok_rows * double),
    )


def split_body(count, parts, rank_ref, *refs):
    lefts, weights = refs[:count], refs[count : 2 * count]
    outs = refs[2 * count :]
    width = weights[0].shape[0] // parts
    for r in range(parts):
        owner = jnp.bitwise_xor(rank_ref[0], r)
        rows = pl.ds(pl.multiple_of(owner * width, width), width)
        total = None
        for left, weight in zip(lefts, weights):
            product = dot(left[...], weight[rows, :], NT)
            total = product if total is None else total + product
        place = r // 2 * width
        outs[r % 2][:, place : place + width] = total.astype(BF16)


def project_split(lefts, weights, axis, after):
    count = len(lefts)
    parts = lax.axis_size(axis)
    tok_rows, inner = lefts[0].shape
    width = weights[0].shape[0]
    rank = jnp.reshape(lax.axis_index(axis), (1,)).astype(jnp.int32)
    return run(
        functools.partial(split_body, count, parts),
        [rank, *lefts, *weights],
        after,
        in_specs=[pl.BlockSpec(memory_space=pltpu.SMEM)]
        + [pl.BlockSpec(memory_space=pltpu.VMEM)] * (2 * count),
        out_shape=[shape(tok_rows, width // 2)] * 2,
        compiler_params=params(5),
        cost_estimate=cost(2 * count * tok_rows * inner * width, 2 * tok_rows * width),
    )


def exchange(block, axis, distance):
    count = lax.axis_size(axis)
    return lax.ppermute(block, axis, [(i, i ^ distance) for i in range(count)])


def add(left, right):
    return (left.astype(F32) + right.astype(F32)).astype(BF16)


def scatter_sum(keep, send, axis):
    parts = lax.axis_size(axis) // 2
    width = keep.shape[1] // parts
    pieces = [keep[:, i * width : (i + 1) * width] for i in range(parts)]
    distance = 1
    while True:
        into = exchange(send, axis, distance)
        for i in reversed(range(len(pieces))):
            pieces[i] = add(pieces[i], into[:, i * width : (i + 1) * width])
        if len(pieces) == 1:
            return pieces[0]
        away = pieces[1::2]
        send = away[0] if len(away) == 1 else jnp.concatenate(away, axis=1)
        pieces = pieces[0::2]
        distance *= 2


class Line:
    lag = 3

    def __init__(self, axis):
        self.axis = axis
        self.count = lax.axis_size(axis)
        rank = jnp.bitwise_and(lax.axis_index(axis), 3)
        self.at_end = (rank == 0) | (rank == 3)
        self.across = []
        for low in range(0, self.count, 4):
            self.across += [(low, low), (low + 1, low + 2), (low + 2, low + 1), (low + 3, low + 3)]
        self.halves, self.totals, self.sums = [], [], []

    def push(self, chunk):
        if self.count < 4:
            total = add(chunk, exchange(chunk, self.axis, 1)) if self.count == 2 else chunk
            self.halves.append(total)
            self.totals.append(total)
            self.sums.append(total)
            return
        k = len(self.totals)
        send = chunk
        if k >= self.lag:
            send = jnp.where(self.at_end, chunk, self.totals[k - self.lag])
        into = exchange(send, self.axis, 1)
        if k >= self.lag:
            self.receive(into)
        half = add(chunk, into)
        self.halves.append(half)
        self.totals.append(add(half, lax.ppermute(half, self.axis, self.across)))

    def receive(self, into):
        result = jnp.where(self.at_end, into, self.totals[len(self.sums)])
        distance = 4
        while distance < self.count:
            result = add(result, exchange(result, self.axis, distance))
            distance *= 2
        self.sums.append(result)

    def finish(self):
        while len(self.sums) < len(self.totals):
            self.receive(exchange(self.totals[len(self.sums)], self.axis, 1))
        return self.sums


def per_device(tokens, w_query, w_key, w_value, w_out, cotangent):
    tok_rows = tokens.shape[0]
    inner = w_query.shape[1]
    local_levels = (tok_rows // BLOCK).bit_length() - 1
    count = lax.axis_size("seq")
    far_levels = count.bit_length() - 1
    far_bits = [d.bit_length() - 1 for d in range(1, count)]

    parts = key_value(tokens, w_key, w_value, w_query, local_levels, far_levels)
    levels, query, tops = parts[:local_levels], parts[local_levels], parts[local_levels + 1 :]
    fars = [exchange(tops[bit], "seq", d) for d, bit in enumerate(far_bits, 1)]
    grad = project(cotangent, w_out)
    attended, attended_t, stats = forward(query, levels, fars, far_bits)
    pieces = 2
    line = Line("seq")

    def push_terms(left, which, right, after):
        for p in range(pieces):
            chunk = weight_terms(left, right, inner, which, p, pieces, after)
            line.push(chunk)
            after = [chunk]
        return after

    after = push_terms(attended_t, 0, cotangent, [])
    dquery, dquery_t, dkv, *dfars = backward(
        query, grad, attended_t, stats, levels, fars, far_bits, after
    )
    backs = [exchange(piece, "seq", d) for d, piece in enumerate(dfars, 1)]
    after = push_terms(dquery_t, 0, tokens, [line.halves[0]])
    parts = project_split([attended], [w_out], "head", after)
    mixed = scatter_sum(*parts, "head")
    dkey, dvalue, dkv_t = close_keys(
        dkv, backs, far_bits, local_levels, [parts[0], line.halves[1]]
    )
    after = push_terms(dkv_t, 0, tokens, [line.totals[0]])
    after = push_terms(dkv_t, 1, tokens, after)
    parts = project_split([dquery, dkey, dvalue], [w_query, w_key, w_value], "head", after)
    tokens_grad = scatter_sum(*parts, "head")
    sums = line.finish()
    out_grad, query_grad, key_grad, value_grad = (
        jnp.concatenate(sums[i : i + pieces], axis=0) for i in range(0, len(sums), pieces)
    )
    return mixed, tokens_grad, query_grad, key_grad, value_grad, out_grad


def solution(mesh):
    return jax.shard_map(
        per_device,
        mesh=mesh,
        in_specs=(
            P(("groups", "seq"), None),
            P(None, "head"),
            P(None, "head"),
            P(None, "head"),
            P(None, "head"),
            P(("groups", "seq"), None),
        ),
        out_specs=(
            P(("groups", "seq"), "head"),
            P(("groups", "seq"), "head"),
            P("groups", "head"),
            P("groups", "head"),
            P("groups", "head"),
            P("groups", "head"),
        ),
        check_vma=False,
    )
```

```python
import functools
import math

import jax
import jax.numpy as jnp
from jax import lax
from jax.experimental import pallas as pl
from jax.experimental.pallas import tpu as pltpu
from jax.sharding import PartitionSpec as P

HEAD_DIM = 128
BLOCK = 128
BF16 = jnp.bfloat16
F32 = jnp.float32
MIB = 1024 * 1024

NN = (((1,), (0,)), ((), ()))
NT = (((1,), (1,)), ((), ()))
TN = (((0,), (0,)), ((), ()))


def dot(left, right, dims=NN):
    return lax.dot_general(left, right, dims, preferred_element_type=F32)


def params(mib):
    return pltpu.CompilerParams(vmem_limit_bytes=mib * MIB)


def cost(flops, moved, exps=0):
    return pl.CostEstimate(flops=int(flops), bytes_accessed=int(moved), transcendentals=int(exps))


def run(body, ready, after=(), in_specs=None, **options):
    count, extra = len(ready), len(after)

    def kernel(*refs):
        body(*refs[:count], *refs[count + extra :])

    in_specs = in_specs or [pl.BlockSpec(memory_space=pltpu.VMEM)] * count
    in_specs = in_specs + [pl.BlockSpec(memory_space=pl.ANY)] * extra
    return pl.pallas_call(kernel, in_specs=in_specs, **options)(*ready, *after)


def shape(rows, cols, dtype=BF16):
    return jax.ShapeDtypeStruct((rows, cols), dtype)


def whole(rows, cols):
    return pl.BlockSpec((rows, cols), lambda *_: (0, 0))


def pool_matrix(rows):
    row = lax.broadcasted_iota(jnp.int32, (rows // 2, rows), 0)
    col = lax.broadcasted_iota(jnp.int32, (rows // 2, rows), 1)
    return jnp.where(jnp.right_shift(col, 1) == row, 0.5, 0.0).astype(BF16)


def spread_matrix(rows, step_bits, offset, cols, weight):
    row = lax.broadcasted_iota(jnp.int32, (rows, cols), 0) + offset
    col = lax.broadcasted_iota(jnp.int32, (rows, cols), 1)
    return jnp.where(jnp.right_shift(row, step_bits) == col, weight, 0.0).astype(BF16)


def key_value_body(local_levels, far_levels, parts, tok_hbm, wk_hbm, wv_hbm, *refs):
    out_hbm = refs[:local_levels]
    far = refs[local_levels : local_levels + far_levels]
    refs = refs[local_levels + far_levels :]
    tok_ref, wk_ref, wv_ref = refs[:3]
    levels = refs[3 : 3 + local_levels]
    in_sems, out_sems = refs[3 + local_levels :]
    part = tok_ref.shape[0] // parts

    def fetch(source, target, i):
        copy = pltpu.make_async_copy(source, target, in_sems.at[i])
        copy.start()
        return copy

    def flush(i):
        copy = pltpu.make_async_copy(levels[i], out_hbm[i], out_sems.at[i])
        copy.start()
        return copy

    weights = [fetch(wk_hbm, wk_ref, 0), fetch(wv_hbm, wv_ref, 1)]
    tiles = []
    for p in range(parts):
        rows = pl.ds(p * part, part)
        tiles.append(fetch(tok_hbm.at[rows], tok_ref.at[rows], 2 + p))
    for copy in weights:
        copy.wait()
    for p in range(parts):
        tiles[p].wait()
        here = slice(p * part, (p + 1) * part)
        x = tok_ref[here, :]
        both = jnp.concatenate([dot(x, wk_ref[...]), dot(x, wv_ref[...])], axis=1)
        levels[0][here, :] = both.astype(BF16)
    flushes = [flush(0)]
    pool = pool_matrix(part)
    for i in range(1, local_levels):
        source = levels[i - 1]
        for low in range(0, source.shape[0], part):
            mean = dot(pool, source[low : low + part, :])
            levels[i][low // 2 : (low + part) // 2, :] = mean.astype(BF16)
        flushes.append(flush(i))
    rows = dot(pool, levels[-1][...]).astype(BF16)
    for i in range(far_levels):
        if i:
            rows = dot(pool_matrix(rows.shape[0]), rows).astype(BF16)
        far[i][...] = rows
    for copy in flushes:
        copy.wait()


def key_value(tokens, w_key, w_value, local_levels, far_levels):
    tok_rows, width = tokens.shape
    inner = w_key.shape[1]
    parts = tok_rows // (2 * BLOCK)
    held = [(tok_rows >> i, 2 * inner) for i in range(local_levels)]
    tops = [(BLOCK >> i, 2 * inner) for i in range(far_levels)]
    return pl.pallas_call(
        functools.partial(key_value_body, local_levels, far_levels, parts),
        in_specs=[pl.BlockSpec(memory_space=pl.ANY)] * 3,
        out_specs=[pl.BlockSpec(memory_space=pl.ANY)] * len(held)
        + [pl.BlockSpec(memory_space=pltpu.VMEM)] * len(tops),
        out_shape=[shape(*dims) for dims in held + tops],
        scratch_shapes=[pltpu.VMEM((tok_rows, width), BF16)]
        + [pltpu.VMEM((width, inner), BF16)] * 2
        + [pltpu.VMEM(dims, BF16) for dims in held]
        + [pltpu.SemaphoreType.DMA((parts + 2,)), pltpu.SemaphoreType.DMA((len(held),))],
        compiler_params=params(56),
        cost_estimate=cost(4 * tok_rows * width * inner, 2 * tok_rows * width + 8 * width * inner),
    )(tokens, w_key, w_value)


def project_body(left_ref, weight_ref, out_ref):
    out_ref[...] = dot(left_ref[...], weight_ref[...]).astype(BF16)


def project(left, weight, after=()):
    tok_rows, width = left.shape
    inner = weight.shape[1]
    return run(
        project_body,
        [left, weight],
        after,
        out_shape=shape(tok_rows, inner),
        compiler_params=params(4),
        cost_estimate=cost(2 * tok_rows * width * inner, 2 * tok_rows * width + 4 * width * inner),
    )


class KeySet:
    def __init__(self, far_rows, far_bits, local_levels):
        mids = local_levels - 1
        self.sizes = [2 * BLOCK] + [BLOCK] * mids + list(far_rows)
        self.bounds = [sum(self.sizes[:i]) for i in range(len(self.sizes) + 1)]
        steps = [0] + list(range(1, local_levels)) + [local_levels + b for b in far_bits]
        self.biases = [float(step) for step in steps]
        self.mids = mids
        self.far_start = self.bounds[1 + mids]
        self.factor = math.log2(math.e) / math.sqrt(HEAD_DIM)

    def here(self, m):
        return pl.ds(pl.multiple_of(m * 2 * BLOCK, 2 * BLOCK), 2 * BLOCK)

    def seats(self, m):
        for i in range(self.mids):
            sibling = jnp.bitwise_xor(jnp.right_shift(m, i), 1)
            yield pl.ds(pl.multiple_of(sibling * BLOCK, BLOCK), BLOCK)

    def near(self, m, level_refs, cols):
        rows = [level_refs[0][self.here(m), cols]]
        rows += [ref[seat, cols] for ref, seat in zip(level_refs[1:], self.seats(m))]
        return rows

    def far(self, far_refs, cols):
        return [ref[:, cols] for ref in far_refs]

    def pieces(self, array, first=0, count=None):
        base = self.bounds[first]
        ends = self.bounds[first:] if count is None else self.bounds[first : first + count + 1]
        return [array[a - base : b - base] for a, b in zip(ends, ends[1:])]

    def top(self, pieces, first=0):
        tops = [
            jnp.max(piece, axis=0, keepdims=True) * self.factor + bias
            for piece, bias in zip(pieces, self.biases[first:])
        ]
        return functools.reduce(jnp.maximum, tops)

    def powers(self, pieces, top, first=0):
        return jnp.concatenate(
            [
                jnp.exp2(piece * self.factor + (bias - top))
                for piece, bias in zip(pieces, self.biases[first:])
            ],
            axis=0,
        )


def head_columns(h, inner):
    low = h * HEAD_DIM
    return slice(low, low + HEAD_DIM), slice(inner + low, inner + low + HEAD_DIM)


def near_body(local_levels, q_ref, *refs):
    level_refs = refs[:local_levels]
    power_ref, stat_ref = refs[local_levels:]
    tok_rows, inner = q_ref.shape
    heads = inner // HEAD_DIM
    keyset = KeySet([], [], local_levels)
    rows = keyset.far_start

    def step(m, carry):
        here = keyset.here(m)
        for h in range(heads):
            cols, _ = head_columns(h, inner)
            keys = jnp.concatenate(keyset.near(m, level_refs, cols), axis=0)
            pieces = keyset.pieces(dot(keys, q_ref[here, cols], NT))
            top = keyset.top(pieces)
            powers = keyset.powers(pieces, top)
            stat_ref[h : h + 1, here] = top
            stat_ref[heads + h : heads + h + 1, here] = jnp.sum(powers, axis=0, keepdims=True)
            power_ref[pl.ds(pl.multiple_of((m * heads + h) * rows, rows), rows), :] = powers
        return carry

    lax.fori_loop(0, tok_rows // (2 * BLOCK), step, 0)


def near_powers(query, levels):
    tok_rows, inner = query.shape
    heads = inner // HEAD_DIM
    pairs = tok_rows // (2 * BLOCK)
    rows = (len(levels) + 1) * BLOCK
    return run(
        functools.partial(near_body, len(levels)),
        [query, *levels],
        out_shape=[shape(pairs * heads * rows, 2 * BLOCK, F32), shape(2 * heads, tok_rows, F32)],
        compiler_params=params(6),
        cost_estimate=cost(2 * tok_rows * rows * inner, 12 * tok_rows * inner, tok_rows * rows * 2),
    )


def forward_body(local_levels, far_bits, *refs):
    fars = len(far_bits)
    q_ref, power_ref, near_ref = refs[:3]
    level_refs = refs[3 : 3 + local_levels]
    far_refs = refs[3 + local_levels : 3 + local_levels + fars]
    att_ref, att_t_ref, stat_ref = refs[3 + local_levels + fars :]
    tok_rows, inner = q_ref.shape
    heads = inner // HEAD_DIM
    keyset = KeySet([r.shape[0] for r in far_refs], far_bits, local_levels)
    rows = keyset.far_start

    def step(m, carry):
        here = keyset.here(m)
        for h in range(heads):
            cols, vcols = head_columns(h, inner)
            second = heads + h
            keys = jnp.concatenate(keyset.far(far_refs, cols), axis=0)
            values = keyset.near(m, level_refs, vcols) + keyset.far(far_refs, vcols)
            values = jnp.concatenate(values, axis=0)
            first = local_levels
            pieces = keyset.pieces(dot(keys, q_ref[here, cols], NT), first)
            near_top = near_ref[h : h + 1, here]
            top = jnp.maximum(near_top, keyset.top(pieces, first))
            shrink = jnp.exp2(near_top - top)
            powers = keyset.powers(pieces, top, first)
            total = near_ref[second : second + 1, here] * shrink
            total = total + jnp.sum(powers, axis=0, keepdims=True)
            inverse = 1.0 / total
            place = pl.ds(pl.multiple_of((m * heads + h) * rows, rows), rows)
            near_probs = (power_ref[place, :] * (shrink * inverse)).astype(BF16)
            far_probs = (powers * inverse).astype(BF16)
            probs_b = jnp.concatenate([near_probs, far_probs], axis=0)
            att_t = dot(values, probs_b, TN).astype(BF16)
            att_t_ref[cols, here] = att_t
            att_ref[here, cols] = att_t.T
            stat_ref[h : h + 1, here] = top
            stat_ref[second : second + 1, here] = inverse
        return carry

    lax.fori_loop(0, tok_rows // (2 * BLOCK), step, 0)


def forward(query, powers, near, levels, fars, far_bits, after):
    tok_rows, inner = query.shape
    heads = inner // HEAD_DIM
    set_rows = (len(levels) + 1) * BLOCK + sum(f.shape[0] for f in fars)
    return run(
        functools.partial(forward_body, len(levels), far_bits),
        [query, powers, near, *levels, *fars],
        after,
        out_shape=[
            shape(tok_rows, inner),
            shape(inner, tok_rows),
            shape(2 * heads, tok_rows, F32),
        ],
        compiler_params=params(6),
        cost_estimate=cost(
            3 * tok_rows * set_rows * inner, 12 * tok_rows * inner, tok_rows * set_rows
        ),
    )


def backward_body(local_levels, far_bits, *refs):
    mids = local_levels - 1
    fars = len(far_bits)
    q_ref, g_ref, att_t_ref, stat_ref = refs[:4]
    level_refs = refs[4 : 4 + local_levels]
    far_refs = refs[4 + local_levels : 4 + local_levels + fars]
    outs = refs[4 + local_levels + fars :]
    dq_ref, dq_t_ref, dkv_ref = outs[:3]
    dfar_refs = outs[3 : 3 + fars]
    dmid_refs = outs[3 + fars : 3 + fars + mids]
    acc_ref = outs[-1]
    tok_rows, inner = q_ref.shape
    heads = inner // HEAD_DIM
    score_scale = 1.0 / math.sqrt(HEAD_DIM)
    keyset = KeySet([r.shape[0] for r in far_refs], far_bits, local_levels)

    for ref in (*dmid_refs, acc_ref):
        ref[...] = jnp.zeros_like(ref)

    def step(m, carry):
        here = keyset.here(m)
        for h in range(heads):
            cols, vcols = head_columns(h, inner)
            keys, values = (
                jnp.concatenate(keyset.near(m, level_refs, c) + keyset.far(far_refs, c), axis=0)
                for c in (cols, vcols)
            )
            q = q_ref[here, cols]
            g = g_ref[here, cols]
            top = stat_ref[h : h + 1, here]
            inverse = stat_ref[heads + h : heads + h + 1, here]
            probs = keyset.powers(keyset.pieces(dot(keys, q, NT)), top) * inverse
            att_t = att_t_ref[cols, here].astype(F32)
            delta = jnp.sum(g.T.astype(F32) * att_t, axis=0, keepdims=True)
            grads = (probs * (dot(values, g, NT) - delta) * score_scale).astype(BF16)
            dq_t = dot(keys, grads, TN).astype(BF16)
            dq_t_ref[cols, here] = dq_t
            dq_ref[here, cols] = dq_t.T
            for part, place in ((dot(grads, q), cols), (dot(probs.astype(BF16), g), vcols)):
                own, *sides = keyset.pieces(part)
                dkv_ref[here, place] = own
                for ref, seat, side in zip(dmid_refs, keyset.seats(m), sides):
                    ref[seat, place] += side
                acc_ref[:, place] += part[keyset.far_start :]
        return carry

    lax.fori_loop(0, tok_rows // (2 * BLOCK), step, 0)
    low = 0
    for ref in dfar_refs:
        ref[...] = acc_ref[low : low + ref.shape[0]].astype(BF16)
        low += ref.shape[0]
    fan = spread_matrix(2 * BLOCK, 1, 0, BLOCK, 0.5)
    targets = (dkv_ref, *dmid_refs)
    for i in reversed(range(mids)):
        for t in range(dmid_refs[i].shape[0] // BLOCK):
            part = dmid_refs[i][t * BLOCK : (t + 1) * BLOCK, :]
            high = part.astype(BF16)
            low = (part - high.astype(F32)).astype(BF16)
            rows = slice(2 * t * BLOCK, 2 * (t + 1) * BLOCK)
            targets[i][rows, :] += dot(fan, high) + dot(fan, low)


def backward(query, grad, attended_t, stats, levels, fars, far_bits, after):
    tok_rows, inner = query.shape
    far_rows = sum(f.shape[0] for f in fars)
    set_rows = (len(levels) + 1) * BLOCK + far_rows
    return run(
        functools.partial(backward_body, len(levels), far_bits),
        [query, grad, attended_t, stats, *levels, *fars],
        after,
        out_shape=[shape(tok_rows, inner), shape(inner, tok_rows)]
        + [shape(tok_rows, 2 * inner, F32)]
        + [shape(*f.shape) for f in fars],
        scratch_shapes=[pltpu.VMEM(level.shape, F32) for level in levels[1:]]
        + [pltpu.VMEM((far_rows, 2 * inner), F32)],
        compiler_params=params(10),
        cost_estimate=cost(
            10 * tok_rows * set_rows * inner, 24 * tok_rows * inner, tok_rows * set_rows * 2
        ),
    )


def term_body(which, low, left_ref, right_ref, out_ref):
    width, inner = out_ref.shape
    left = left_ref[which * inner : (which + 1) * inner, :]
    out_ref[...] = dot(left, right_ref[:, low : low + width]).astype(BF16).T


def weight_terms(left_t, right, inner, which, part, parts, after):
    tok_rows = left_t.shape[1]
    width = right.shape[1] // parts
    return run(
        functools.partial(term_body, which, part * width),
        [left_t, right],
        after,
        out_shape=shape(width, inner),
        compiler_params=params(3),
        cost_estimate=cost(2 * inner * tok_rows * width, 2 * tok_rows * (width + inner)),
    )


def close_body(local_levels, far_bits, dkv_ref, *refs):
    back_refs = refs[: len(far_bits)]
    dk_ref, dv_ref, dkv_t_ref = refs[len(far_bits) :]
    inner = dk_ref.shape[1]
    tile = 2 * BLOCK
    for t in range(dkv_ref.shape[0] // tile):
        here = slice(t * tile, (t + 1) * tile)
        total = dkv_ref[here, :]
        for ref, bit in zip(back_refs, far_bits):
            weight = 0.5 ** (local_levels + bit)
            fan = spread_matrix(tile, local_levels + bit, t * tile, ref.shape[0], weight)
            total = total + dot(fan, ref[...])
        final = total.astype(BF16)
        dk_ref[here, :] = final[:, :inner]
        dv_ref[here, :] = final[:, inner:]
        dkv_t_ref[:, here] = final.T


def close_keys(dkv, backs, far_bits, local_levels, after):
    tok_rows, double = dkv.shape
    inner = double // 2
    return run(
        functools.partial(close_body, local_levels, far_bits),
        [dkv, *backs],
        after,
        out_shape=[shape(tok_rows, inner), shape(tok_rows, inner), shape(double, tok_rows)],
        compiler_params=params(5),
        cost_estimate=cost(2 * tok_rows * 256 * double, 12 * tok_rows * double),
    )


def split_body(count, parts, rank_ref, *refs):
    lefts, weights = refs[:count], refs[count : 2 * count]
    outs = refs[2 * count :]
    width = weights[0].shape[0] // parts
    for r in range(parts):
        owner = jnp.bitwise_xor(rank_ref[0], r)
        rows = pl.ds(pl.multiple_of(owner * width, width), width)
        total = None
        for left, weight in zip(lefts, weights):
            product = dot(left[...], weight[rows, :], NT)
            total = product if total is None else total + product
        place = r // 2 * width
        outs[r % 2][:, place : place + width] = total.astype(BF16)


def project_split(lefts, weights, axis, after):
    count = len(lefts)
    parts = lax.axis_size(axis)
    tok_rows, inner = lefts[0].shape
    width = weights[0].shape[0]
    rank = jnp.reshape(lax.axis_index(axis), (1,)).astype(jnp.int32)
    return run(
        functools.partial(split_body, count, parts),
        [rank, *lefts, *weights],
        after,
        in_specs=[pl.BlockSpec(memory_space=pltpu.SMEM)]
        + [pl.BlockSpec(memory_space=pltpu.VMEM)] * (2 * count),
        out_shape=[shape(tok_rows, width // 2)] * 2,
        compiler_params=params(5),
        cost_estimate=cost(2 * count * tok_rows * inner * width, 2 * tok_rows * width),
    )


def exchange(block, axis, distance):
    count = lax.axis_size(axis)
    return lax.ppermute(block, axis, [(i, i ^ distance) for i in range(count)])


def add(left, right):
    return (left.astype(F32) + right.astype(F32)).astype(BF16)


def scatter_sum(keep, send, axis):
    parts = lax.axis_size(axis) // 2
    width = keep.shape[1] // parts
    pieces = [keep[:, i * width : (i + 1) * width] for i in range(parts)]
    distance = 1
    while True:
        into = exchange(send, axis, distance)
        for i in reversed(range(len(pieces))):
            pieces[i] = add(pieces[i], into[:, i * width : (i + 1) * width])
        if len(pieces) == 1:
            return pieces[0]
        away = pieces[1::2]
        send = away[0] if len(away) == 1 else jnp.concatenate(away, axis=1)
        pieces = pieces[0::2]
        distance *= 2


def half_body(chunk_ref, into_ref, out_ref):
    out_ref[...] = (chunk_ref[...].astype(F32) + into_ref[...].astype(F32)).astype(BF16)


def half_sum(chunk, into, after=()):
    return run(
        half_body,
        [chunk, into],
        after,
        out_shape=shape(*chunk.shape),
        compiler_params=params(2),
        cost_estimate=cost(chunk.size, 6 * chunk.size),
    )


def turn_body(end_ref, half_ref, across_ref, chunk_ref, total_ref, send_ref):
    total = (half_ref[...].astype(F32) + across_ref[...].astype(F32)).astype(BF16)
    total_ref[...] = total

    @pl.when(end_ref[0] == 1)
    def _():
        send_ref[...] = chunk_ref[...]

    @pl.when(end_ref[0] == 0)
    def _():
        send_ref[...] = total


def turn(end, half, across, chunk, after=()):
    return run(
        turn_body,
        [end, half, across, chunk],
        after,
        in_specs=[pl.BlockSpec(memory_space=pltpu.SMEM)]
        + [pl.BlockSpec(memory_space=pltpu.VMEM)] * 3,
        out_shape=[shape(*half.shape)] * 2,
        compiler_params=params(2),
        cost_estimate=cost(half.size, 10 * half.size),
    )


class Line:
    lag = 3

    def __init__(self, axis, other):
        self.axes = (axis, other)
        self.axis = axis
        self.count = lax.axis_size(axis)
        rank = jnp.bitwise_and(lax.axis_index(axis), 3)
        self.at_end = (rank == 0) | (rank == 3)
        self.end = jnp.reshape(self.at_end, (1,)).astype(jnp.int32)
        width = lax.axis_size(other)
        self.across = []
        for place in range(self.count):
            for seat in range(width):
                target = (place, seat ^ 1 if width > 1 else seat)
                if place & 3 in (1, 2):
                    target = (place ^ 3, seat)
                self.across.append((place * width + seat, target[0] * width + target[1]))
        self.chunks, self.halves, self.crossed, self.totals, self.sums = [], [], [], [], []

    def push(self, chunk, after=(), later=()):
        k = len(self.chunks)
        self.chunks.append(chunk)
        if self.count < 4:
            total = add(chunk, exchange(chunk, self.axis, 1)) if self.count == 2 else chunk
            self.halves.append(total)
            self.sums.append(total)
            return
        send = chunk
        if k >= self.lag:
            old = k - self.lag
            total, send = turn(self.end, self.halves[old], self.crossed[old], chunk, later)
            self.totals.append(total)
        into = exchange(send, self.axis, 1)
        if k >= self.lag:
            self.receive(into)
        half = half_sum(chunk, into, after)
        self.halves.append(half)
        self.crossed.append(lax.ppermute(half, self.axes, self.across))

    def receive(self, into):
        result = jnp.where(self.at_end, into, self.totals[len(self.sums)])
        distance = 4
        while distance < self.count:
            result = add(result, exchange(result, self.axis, distance))
            distance *= 2
        self.sums.append(result)

    def finish(self, last):
        while len(self.sums) < len(self.chunks):
            old = len(self.sums)
            after = last if old == len(self.chunks) - 1 else ()
            self.totals.append(half_sum(self.halves[old], self.crossed[old], after))
            self.receive(exchange(self.totals[old], self.axis, 1))
        return self.sums


def per_device(tokens, w_query, w_key, w_value, w_out, cotangent):
    tok_rows = tokens.shape[0]
    inner = w_query.shape[1]
    local_levels = (tok_rows // BLOCK).bit_length() - 1
    count = lax.axis_size("seq")
    far_levels = count.bit_length() - 1
    far_bits = [d.bit_length() - 1 for d in range(1, count)]

    parts = key_value(tokens, w_key, w_value, local_levels, far_levels)
    levels, tops = parts[:local_levels], parts[local_levels:]
    fars = [exchange(tops[bit], "seq", d) for d, bit in enumerate(far_bits, 1)]
    query = project(tokens, w_query)
    powers, near = near_powers(query, levels)
    grad = project(cotangent, w_out, [near])
    attended, attended_t, stats = forward(query, powers, near, levels, fars, far_bits, [grad])
    pieces = 2
    line = Line("seq", "head")

    def terms(left, which, right, after):
        chunks = []
        for p in range(pieces):
            chunks.append(weight_terms(left, right, inner, which, p, pieces, after))
            after = chunks[-1:]
        return chunks

    chunks = terms(attended_t, 0, cotangent, [])
    line.push(chunks[0])
    line.push(chunks[1])
    dquery, dquery_t, dkv, *dfars = backward(
        query, grad, attended_t, stats, levels, fars, far_bits, chunks
    )
    backs = [exchange(piece, "seq", d) for d, piece in enumerate(dfars, 1)]
    chunks = terms(dquery_t, 0, tokens, line.halves[:1])
    line.push(chunks[0])
    keep, send = project_split([attended], [w_out], "head", chunks)
    mixed = scatter_sum(keep, send, "head")
    dkey, dvalue, dkv_t = close_keys(
        dkv, backs, far_bits, local_levels, [keep, line.halves[1]]
    )
    line.push(chunks[1])
    chunks = terms(dkv_t, 0, tokens, [])
    line.push(chunks[0])
    line.push(chunks[1])
    chunks = terms(dkv_t, 1, tokens, chunks)
    line.push(chunks[0], [mixed])
    keep, send = project_split([dquery, dkey, dvalue], [w_query, w_key, w_value], "head", chunks)
    tokens_grad = scatter_sum(keep, send, "head")
    line.push(chunks[1])
    sums = line.finish([tokens_grad])
    out_grad, query_grad, key_grad, value_grad = (
        jnp.concatenate(sums[i : i + pieces], axis=0) for i in range(0, len(sums), pieces)
    )
    return mixed, tokens_grad, query_grad, key_grad, value_grad, out_grad


def solution(mesh):
    return jax.shard_map(
        per_device,
        mesh=mesh,
        in_specs=(
            P(("groups", "seq"), None),
            P(None, "head"),
            P(None, "head"),
            P(None, "head"),
            P(None, "head"),
            P(("groups", "seq"), None),
        ),
        out_specs=(
            P(("groups", "seq"), "head"),
            P(("groups", "seq"), "head"),
            P("groups", "head"),
            P("groups", "head"),
            P("groups", "head"),
            P("groups", "head"),
        ),
        check_vma=False,
    )
```

```python
import functools
import math

import jax
import jax.numpy as jnp
from jax import lax
from jax.experimental import pallas as pl
from jax.experimental.pallas import tpu as pltpu
from jax.sharding import PartitionSpec as P

HEAD_DIM = 128
BLOCK = 128
BF16 = jnp.bfloat16
F32 = jnp.float32
MIB = 1024 * 1024

NN = (((1,), (0,)), ((), ()))
NT = (((1,), (1,)), ((), ()))
TN = (((0,), (0,)), ((), ()))


def dot(left, right, dims=NN):
    return lax.dot_general(left, right, dims, preferred_element_type=F32)


def params(mib):
    return pltpu.CompilerParams(vmem_limit_bytes=mib * MIB)


def cost(microseconds):
    return pl.CostEstimate(flops=int(microseconds * 1150e6) + 1, bytes_accessed=1, transcendentals=0)


def run(body, ready, after=(), in_specs=None, **options):
    count, extra = len(ready), len(after)

    def kernel(*refs):
        body(*refs[:count], *refs[count + extra :])

    in_specs = in_specs or [pl.BlockSpec(memory_space=pltpu.VMEM)] * count
    in_specs = in_specs + [pl.BlockSpec(memory_space=pl.ANY)] * extra
    return pl.pallas_call(kernel, in_specs=in_specs, **options)(*ready, *after)


def shape(rows, cols, dtype=BF16):
    return jax.ShapeDtypeStruct((rows, cols), dtype)


def whole(rows, cols):
    return pl.BlockSpec((rows, cols), lambda *_: (0, 0))


def pool_matrix(rows):
    row = lax.broadcasted_iota(jnp.int32, (rows // 2, rows), 0)
    col = lax.broadcasted_iota(jnp.int32, (rows // 2, rows), 1)
    return jnp.where(jnp.right_shift(col, 1) == row, 0.5, 0.0).astype(BF16)


def spread_matrix(rows, step_bits, offset, cols, weight):
    row = lax.broadcasted_iota(jnp.int32, (rows, cols), 0) + offset
    col = lax.broadcasted_iota(jnp.int32, (rows, cols), 1)
    return jnp.where(jnp.right_shift(row, step_bits) == col, weight, 0.0).astype(BF16)


def key_value_body(local_levels, far_levels, parts, tok_hbm, wk_hbm, wv_hbm, *refs):
    out_hbm = refs[:local_levels]
    far = refs[local_levels : local_levels + far_levels]
    refs = refs[local_levels + far_levels :]
    tok_ref, wk_ref, wv_ref = refs[:3]
    levels = refs[3 : 3 + local_levels]
    in_sems, out_sems = refs[3 + local_levels :]
    part = tok_ref.shape[0] // parts

    def fetch(source, target, i):
        copy = pltpu.make_async_copy(source, target, in_sems.at[i])
        copy.start()
        return copy

    def flush(i):
        copy = pltpu.make_async_copy(levels[i], out_hbm[i], out_sems.at[i])
        copy.start()
        return copy

    weights = [fetch(wk_hbm, wk_ref, 0), fetch(wv_hbm, wv_ref, 1)]
    tiles = []
    for p in range(parts):
        rows = pl.ds(p * part, part)
        tiles.append(fetch(tok_hbm.at[rows], tok_ref.at[rows], 2 + p))
    for copy in weights:
        copy.wait()
    for p in range(parts):
        tiles[p].wait()
        here = slice(p * part, (p + 1) * part)
        x = tok_ref[here, :]
        both = jnp.concatenate([dot(x, wk_ref[...]), dot(x, wv_ref[...])], axis=1)
        levels[0][here, :] = both.astype(BF16)
    flushes = [flush(0)]
    pool = pool_matrix(part)
    for i in range(1, local_levels):
        source = levels[i - 1]
        for low in range(0, source.shape[0], part):
            mean = dot(pool, source[low : low + part, :])
            levels[i][low // 2 : (low + part) // 2, :] = mean.astype(BF16)
        flushes.append(flush(i))
    rows = dot(pool, levels[-1][...]).astype(BF16)
    for i in range(far_levels):
        if i:
            rows = dot(pool_matrix(rows.shape[0]), rows).astype(BF16)
        far[i][...] = rows
    for copy in flushes:
        copy.wait()


def key_value(tokens, w_key, w_value, local_levels, far_levels):
    tok_rows, width = tokens.shape
    inner = w_key.shape[1]
    parts = tok_rows // (2 * BLOCK)
    held = [(tok_rows >> i, 2 * inner) for i in range(local_levels)]
    tops = [(BLOCK >> i, 2 * inner) for i in range(far_levels)]
    return pl.pallas_call(
        functools.partial(key_value_body, local_levels, far_levels, parts),
        in_specs=[pl.BlockSpec(memory_space=pl.ANY)] * 3,
        out_specs=[pl.BlockSpec(memory_space=pl.ANY)] * len(held)
        + [pl.BlockSpec(memory_space=pltpu.VMEM)] * len(tops),
        out_shape=[shape(*dims) for dims in held + tops],
        scratch_shapes=[pltpu.VMEM((tok_rows, width), BF16)]
        + [pltpu.VMEM((width, inner), BF16)] * 2
        + [pltpu.VMEM(dims, BF16) for dims in held]
        + [pltpu.SemaphoreType.DMA((parts + 2,)), pltpu.SemaphoreType.DMA((len(held),))],
        compiler_params=params(56),
        cost_estimate=cost(5.0),
    )(tokens, w_key, w_value)


def project_body(left_ref, weight_ref, out_ref):
    out_ref[...] = dot(left_ref[...], weight_ref[...]).astype(BF16)


def project(left, weight, after):
    tok_rows, width = left.shape
    inner = weight.shape[1]
    return run(
        project_body,
        [left, weight],
        after,
        out_shape=shape(tok_rows, inner),
        compiler_params=params(4),
        cost_estimate=cost(0.7),
    )


class KeySet:
    def __init__(self, far_rows, far_bits, local_levels):
        mids = local_levels - 1
        self.sizes = [2 * BLOCK] + [BLOCK] * mids + list(far_rows)
        self.bounds = [sum(self.sizes[:i]) for i in range(len(self.sizes) + 1)]
        steps = [0] + list(range(1, local_levels)) + [local_levels + b for b in far_bits]
        self.biases = [float(step) for step in steps]
        self.mids = mids
        self.far_start = self.bounds[1 + mids]
        self.factor = math.log2(math.e) / math.sqrt(HEAD_DIM)

    def here(self, m):
        return pl.ds(pl.multiple_of(m * 2 * BLOCK, 2 * BLOCK), 2 * BLOCK)

    def seats(self, m):
        for i in range(self.mids):
            sibling = jnp.bitwise_xor(jnp.right_shift(m, i), 1)
            yield pl.ds(pl.multiple_of(sibling * BLOCK, BLOCK), BLOCK)

    def near(self, m, level_refs, cols):
        rows = [level_refs[0][self.here(m), cols]]
        rows += [ref[seat, cols] for ref, seat in zip(level_refs[1:], self.seats(m))]
        return rows

    def far(self, far_refs, cols):
        return [ref[:, cols] for ref in far_refs]

    def pieces(self, array, first=0, count=None):
        base = self.bounds[first]
        ends = self.bounds[first:] if count is None else self.bounds[first : first + count + 1]
        return [array[a - base : b - base] for a, b in zip(ends, ends[1:])]

    def top(self, pieces, first=0):
        tops = [
            jnp.max(piece, axis=0, keepdims=True) * self.factor + bias
            for piece, bias in zip(pieces, self.biases[first:])
        ]
        return functools.reduce(jnp.maximum, tops)

    def powers(self, pieces, top, first=0):
        return jnp.concatenate(
            [
                jnp.exp2(piece * self.factor + (bias - top))
                for piece, bias in zip(pieces, self.biases[first:])
            ],
            axis=0,
        )


def head_columns(h, inner):
    low = h * HEAD_DIM
    return slice(low, low + HEAD_DIM), slice(inner + low, inner + low + HEAD_DIM)


def near_body(local_levels, q_ref, *refs):
    level_refs = refs[:local_levels]
    power_ref, stat_ref = refs[local_levels:]
    tok_rows, inner = q_ref.shape
    heads = inner // HEAD_DIM
    keyset = KeySet([], [], local_levels)
    rows = keyset.far_start

    def step(m, carry):
        here = keyset.here(m)
        for h in range(heads):
            cols, _ = head_columns(h, inner)
            keys = jnp.concatenate(keyset.near(m, level_refs, cols), axis=0)
            pieces = keyset.pieces(dot(keys, q_ref[here, cols], NT))
            top = keyset.top(pieces)
            powers = keyset.powers(pieces, top)
            stat_ref[h : h + 1, here] = top
            stat_ref[heads + h : heads + h + 1, here] = jnp.sum(powers, axis=0, keepdims=True)
            power_ref[pl.ds(pl.multiple_of((m * heads + h) * rows, rows), rows), :] = powers
        return carry

    lax.fori_loop(0, tok_rows // (2 * BLOCK), step, 0)


def near_powers(query, levels, after):
    tok_rows, inner = query.shape
    heads = inner // HEAD_DIM
    pairs = tok_rows // (2 * BLOCK)
    rows = (len(levels) + 1) * BLOCK
    return run(
        functools.partial(near_body, len(levels)),
        [query, *levels],
        after,
        out_shape=[shape(pairs * heads * rows, 2 * BLOCK, F32), shape(2 * heads, tok_rows, F32)],
        compiler_params=params(6),
        cost_estimate=cost(2.3),
    )


def forward_body(local_levels, far_bits, *refs):
    fars = len(far_bits)
    q_ref, power_ref, near_ref = refs[:3]
    level_refs = refs[3 : 3 + local_levels]
    far_refs = refs[3 + local_levels : 3 + local_levels + fars]
    att_ref, att_t_ref, stat_ref = refs[3 + local_levels + fars :]
    tok_rows, inner = q_ref.shape
    heads = inner // HEAD_DIM
    keyset = KeySet([r.shape[0] for r in far_refs], far_bits, local_levels)
    rows = keyset.far_start

    def step(m, carry):
        here = keyset.here(m)
        for h in range(heads):
            cols, vcols = head_columns(h, inner)
            second = heads + h
            keys = jnp.concatenate(keyset.far(far_refs, cols), axis=0)
            values = keyset.near(m, level_refs, vcols) + keyset.far(far_refs, vcols)
            values = jnp.concatenate(values, axis=0)
            first = local_levels
            pieces = keyset.pieces(dot(keys, q_ref[here, cols], NT), first)
            near_top = near_ref[h : h + 1, here]
            top = jnp.maximum(near_top, keyset.top(pieces, first))
            shrink = jnp.exp2(near_top - top)
            powers = keyset.powers(pieces, top, first)
            total = near_ref[second : second + 1, here] * shrink
            total = total + jnp.sum(powers, axis=0, keepdims=True)
            inverse = 1.0 / total
            place = pl.ds(pl.multiple_of((m * heads + h) * rows, rows), rows)
            near_probs = (power_ref[place, :] * (shrink * inverse)).astype(BF16)
            far_probs = (powers * inverse).astype(BF16)
            probs_b = jnp.concatenate([near_probs, far_probs], axis=0)
            att_t = dot(values, probs_b, TN).astype(BF16)
            att_t_ref[cols, here] = att_t
            att_ref[here, cols] = att_t.T
            stat_ref[h : h + 1, here] = top
            stat_ref[second : second + 1, here] = inverse
        return carry

    lax.fori_loop(0, tok_rows // (2 * BLOCK), step, 0)


def forward(query, powers, near, levels, fars, far_bits, after):
    tok_rows, inner = query.shape
    heads = inner // HEAD_DIM
    set_rows = (len(levels) + 1) * BLOCK + sum(f.shape[0] for f in fars)
    return run(
        functools.partial(forward_body, len(levels), far_bits),
        [query, powers, near, *levels, *fars],
        after,
        out_shape=[
            shape(tok_rows, inner),
            shape(inner, tok_rows),
            shape(2 * heads, tok_rows, F32),
        ],
        compiler_params=params(6),
        cost_estimate=cost(4.0),
    )


def backward_body(local_levels, far_bits, pieces, *refs):
    mids = local_levels - 1
    fars = len(far_bits)
    q_ref, g_ref, att_t_ref, stat_ref, tok_ref = refs[:5]
    level_refs = refs[5 : 5 + local_levels]
    far_refs = refs[5 + local_levels : 5 + local_levels + fars]
    outs = refs[5 + local_levels + fars :]
    dq_ref, dkv_ref = outs[:2]
    term_refs = outs[2 : 2 + pieces]
    dfar_refs = outs[2 + pieces : 1 + pieces + fars]
    dmid_refs = outs[1 + pieces + fars : 1 + pieces + fars + mids]
    dq_t_ref, acc_ref = outs[-2:]
    tok_rows, inner = q_ref.shape
    heads = inner // HEAD_DIM
    score_scale = 1.0 / math.sqrt(HEAD_DIM)
    keyset = KeySet([r.shape[0] for r in far_refs], far_bits, local_levels)

    for ref in (*dmid_refs, acc_ref):
        ref[...] = jnp.zeros_like(ref)

    def step(m, carry):
        here = keyset.here(m)
        for h in range(heads):
            cols, vcols = head_columns(h, inner)
            keys, values = (
                jnp.concatenate(keyset.near(m, level_refs, c) + keyset.far(far_refs, c), axis=0)
                for c in (cols, vcols)
            )
            q = q_ref[here, cols]
            g = g_ref[here, cols]
            top = stat_ref[h : h + 1, here]
            inverse = stat_ref[heads + h : heads + h + 1, here]
            probs = keyset.powers(keyset.pieces(dot(keys, q, NT)), top) * inverse
            att_t = att_t_ref[cols, here].astype(F32)
            delta = jnp.sum(g.T.astype(F32) * att_t, axis=0, keepdims=True)
            grads = (probs * (dot(values, g, NT) - delta) * score_scale).astype(BF16)
            dq_t = dot(keys, grads, TN).astype(BF16)
            dq_t_ref[cols, here] = dq_t
            dq_ref[here, cols] = dq_t.T
            for part, place in ((dot(grads, q), cols), (dot(probs.astype(BF16), g), vcols)):
                own, *sides = keyset.pieces(part)
                dkv_ref[here, place] = own
                for ref, seat, side in zip(dmid_refs, keyset.seats(m), sides):
                    ref[seat, place] += side
                acc_ref[:, place] += part[keyset.far_start :]
        return carry

    lax.fori_loop(0, tok_rows // (2 * BLOCK), step, 0)
    width = term_refs[-1].shape[0]
    first = acc_ref[:BLOCK].astype(BF16)
    term_refs[0][width : width + BLOCK, :] = first[:, :inner]
    term_refs[0][width + BLOCK :, :] = first[:, inner:]
    low = BLOCK
    for ref in dfar_refs:
        ref[...] = acc_ref[low : low + ref.shape[0]].astype(BF16)
        low += ref.shape[0]
    for i, ref in enumerate(term_refs):
        part = dot(dq_t_ref[...], tok_ref[:, i * width : (i + 1) * width])
        ref[:width, :] = part.astype(BF16).T
    fan = spread_matrix(2 * BLOCK, 1, 0, BLOCK, 0.5)
    targets = (dkv_ref, *dmid_refs)
    for i in reversed(range(mids)):
        for t in range(dmid_refs[i].shape[0] // BLOCK):
            part = dmid_refs[i][t * BLOCK : (t + 1) * BLOCK, :]
            high = part.astype(BF16)
            low = (part - high.astype(F32)).astype(BF16)
            rows = slice(2 * t * BLOCK, 2 * (t + 1) * BLOCK)
            targets[i][rows, :] += dot(fan, high) + dot(fan, low)


def backward(query, grad, attended_t, stats, tokens, levels, fars, far_bits, pieces, after):
    tok_rows, inner = query.shape
    far_rows = sum(f.shape[0] for f in fars)
    set_rows = (len(levels) + 1) * BLOCK + far_rows
    return run(
        functools.partial(backward_body, len(levels), far_bits, pieces),
        [query, grad, attended_t, stats, tokens, *levels, *fars],
        after,
        out_shape=[shape(tok_rows, inner), shape(tok_rows, 2 * inner, F32)]
        + [shape(tokens.shape[1] // pieces + 2 * BLOCK, inner)]
        + [shape(tokens.shape[1] // pieces, inner)] * (pieces - 1)
        + [shape(*f.shape) for f in fars[1:]],
        scratch_shapes=[pltpu.VMEM(level.shape, F32) for level in levels[1:]]
        + [pltpu.VMEM((inner, tok_rows), BF16), pltpu.VMEM((far_rows, 2 * inner), F32)],
        compiler_params=params(10),
        cost_estimate=cost(8.0),
    )


def term_body(which, low, left_ref, right_ref, out_ref):
    width, inner = out_ref.shape
    left = left_ref[which * inner : (which + 1) * inner, :]
    out_ref[...] = dot(left, right_ref[:, low : low + width]).astype(BF16).T


def weight_terms(left_t, right, inner, which, part, parts, after):
    tok_rows = left_t.shape[1]
    width = right.shape[1] // parts
    return run(
        functools.partial(term_body, which, part * width),
        [left_t, right],
        after,
        out_shape=shape(width, inner),
        compiler_params=params(3),
        cost_estimate=cost(0.5),
    )


def close_body(local_levels, far_bits, dkv_ref, *refs):
    joined_ref, *back_refs = refs[: len(far_bits)]
    dk_ref, dv_ref, dkv_t_ref = refs[len(far_bits) :]
    inner = dk_ref.shape[1]
    tile = 2 * BLOCK
    low = joined_ref.shape[0] - 2 * BLOCK
    joined = [joined_ref[low : low + BLOCK, :], joined_ref[low + BLOCK :, :]]
    backs = [jnp.concatenate(joined, axis=1)] + [ref[...] for ref in back_refs]
    for t in range(dkv_ref.shape[0] // tile):
        here = slice(t * tile, (t + 1) * tile)
        total = dkv_ref[here, :]
        for back, bit in zip(backs, far_bits):
            weight = 0.5 ** (local_levels + bit)
            fan = spread_matrix(tile, local_levels + bit, t * tile, back.shape[0], weight)
            total = total + dot(fan, back)
        final = total.astype(BF16)
        dk_ref[here, :] = final[:, :inner]
        dv_ref[here, :] = final[:, inner:]
        dkv_t_ref[:, here] = final.T


def close_keys(dkv, backs, far_bits, local_levels, after):
    tok_rows, double = dkv.shape
    inner = double // 2
    return run(
        functools.partial(close_body, local_levels, far_bits),
        [dkv, *backs],
        after,
        out_shape=[shape(tok_rows, inner), shape(tok_rows, inner), shape(double, tok_rows)],
        compiler_params=params(5),
        cost_estimate=cost(1.8),
    )


def split_body(count, parts, rank_ref, *refs):
    lefts, weights = refs[:count], refs[count : 2 * count]
    outs = refs[2 * count :]
    width = weights[0].shape[0] // parts
    for r in range(parts):
        owner = jnp.bitwise_xor(rank_ref[0], r)
        rows = pl.ds(pl.multiple_of(owner * width, width), width)
        total = None
        for left, weight in zip(lefts, weights):
            product = dot(left[...], weight[rows, :], NT)
            total = product if total is None else total + product
        place = r // 2 * width
        outs[r % 2][:, place : place + width] = total.astype(BF16)


def project_split(lefts, weights, axis, after):
    count = len(lefts)
    parts = lax.axis_size(axis)
    tok_rows, inner = lefts[0].shape
    width = weights[0].shape[0]
    rank = jnp.reshape(lax.axis_index(axis), (1,)).astype(jnp.int32)
    return run(
        functools.partial(split_body, count, parts),
        [rank, *lefts, *weights],
        after,
        in_specs=[pl.BlockSpec(memory_space=pltpu.SMEM)]
        + [pl.BlockSpec(memory_space=pltpu.VMEM)] * (2 * count),
        out_shape=[shape(tok_rows, width // 2)] * 2,
        compiler_params=params(5),
        cost_estimate=cost(1.0),
    )


def exchange(block, axis, distance):
    count = lax.axis_size(axis)
    return lax.ppermute(block, axis, [(i, i ^ distance) for i in range(count)])


def add(left, right):
    return (left.astype(F32) + right.astype(F32)).astype(BF16)


def term_half_body(chunk_ref, into_ref, out_ref):
    rows = slice(0, out_ref.shape[0])
    out_ref[...] = (chunk_ref[rows, :].astype(F32) + into_ref[rows, :].astype(F32)).astype(BF16)


def half_sum(chunk, into, rows, after):
    return run(
        term_half_body,
        [chunk, into],
        after,
        out_shape=shape(rows, chunk.shape[1]),
        compiler_params=params(3),
        cost_estimate=cost(0.1),
    )


def pair_half_body(chunk_ref, into_ref, *out_refs):
    rows = out_refs[0].shape[0]
    for i, ref in enumerate(out_refs):
        here = slice(i * rows, (i + 1) * rows)
        ref[...] = (chunk_ref[here, :].astype(F32) + into_ref[here, :].astype(F32)).astype(BF16)


def half_sums(chunk, into, count, after):
    rows = chunk.shape[0] // count
    return run(
        pair_half_body,
        [chunk, into],
        after,
        out_shape=[shape(rows, chunk.shape[1])] * count,
        compiler_params=params(3),
        cost_estimate=cost(0.2),
    )


def scatter_body(pieces, keep_ref, into_ref, even_ref, odd_ref):
    width = keep_ref.shape[1] // pieces
    for i in range(pieces):
        here = slice(i * width, (i + 1) * width)
        place = slice(i // 2 * width, (i // 2 + 1) * width)
        total = keep_ref[:, here].astype(F32) + into_ref[:, here].astype(F32)
        (even_ref, odd_ref)[i % 2][:, place] = total.astype(BF16)


def scatter_step(keep, into, pieces, after):
    rows, width = keep.shape
    return run(
        functools.partial(scatter_body, pieces),
        [keep, into],
        after,
        out_shape=[shape(rows, width // 2)] * 2,
        compiler_params=params(4),
        cost_estimate=cost(0.2),
    )


def turn_body(end_ref, half_ref, across_ref, chunk_ref, total_ref, send_ref):
    total = (half_ref[...].astype(F32) + across_ref[...].astype(F32)).astype(BF16)
    total_ref[...] = total

    @pl.when(end_ref[0] == 1)
    def _():
        send_ref[...] = chunk_ref[...]

    @pl.when(end_ref[0] == 0)
    def _():
        send_ref[...] = total


def turn(end, half, across, chunk, after):
    return run(
        turn_body,
        [end, half, across, chunk],
        after,
        in_specs=[pl.BlockSpec(memory_space=pltpu.SMEM)]
        + [pl.BlockSpec(memory_space=pltpu.VMEM)] * 3,
        out_shape=[shape(*half.shape)] * 2,
        compiler_params=params(2),
        cost_estimate=cost(0.1),
    )


def output_body(count, end_ref, *refs):
    totals, ends, out_ref = refs[:count], refs[count : 2 * count], refs[-1]
    rows = totals[0].shape[0]

    for flag, sources in ((0, totals), (1, ends)):

        @pl.when(end_ref[0] == flag)
        def _():
            for i, ref in enumerate(sources):
                out_ref[i * rows : (i + 1) * rows, :] = ref[...]


def output(end, totals, ends, after):
    count = len(totals)
    rows, width = totals[0].shape
    return run(
        functools.partial(output_body, count),
        [end, *totals, *ends],
        after,
        in_specs=[pl.BlockSpec(memory_space=pltpu.SMEM)]
        + [pl.BlockSpec(memory_space=pltpu.VMEM)] * (2 * count),
        out_shape=shape(count * rows, width),
        compiler_params=params(4),
        cost_estimate=cost(0.9),
    )


def relay_body(source_ref, target_ref):
    target_ref[...] = source_ref[...]


def relay(block, after):
    return run(
        relay_body,
        [block],
        after,
        out_shape=shape(*block.shape),
        compiler_params=params(3),
        cost_estimate=cost(0.2),
    )


class Line:
    lag = 3

    def __init__(self, axis, other, step):
        self.axis, self.axes, self.step = axis, (axis, other), step
        self.count = lax.axis_size(axis)
        rank = jnp.bitwise_and(lax.axis_index(axis), 3)
        self.end = jnp.reshape((rank == 0) | (rank == 3), (1,)).astype(jnp.int32)
        width = lax.axis_size(other)
        self.across = []
        for place in range(self.count):
            for seat in range(width):
                target = (place, seat ^ 1 if width > 1 else seat)
                if place & 3 in (1, 2):
                    target = (place ^ 3, seat)
                self.across.append((place * width + seat, target[0] * width + target[1]))
        self.chunks, self.into, self.halves, self.crossed, self.totals = [], [], [], [], []

    def enter(self, chunk):
        self.chunks.append(chunk)
        self.into.append(exchange(chunk, self.axis, 1))

    def enter_whole(self, whole, count):
        self.whole = whole, exchange(whole, self.axis, 1), count
        self.chunks += [None] * count
        self.into += [None] * count

    def meet_whole(self):
        for half in self.step(half_sums, *self.whole):
            self.halves.append(half)
            self.crossed.append(lax.ppermute(half, self.axes, self.across))

    def meet(self, rows):
        k = len(self.halves)
        half = self.step(half_sum, self.chunks[k], self.into[k], rows)
        self.halves.append(half)
        self.crossed.append(lax.ppermute(half, self.axes, self.across))

    def turn(self, chunk):
        old = len(self.totals)
        total, send = self.step(turn, self.end, self.halves[old], self.crossed[old], chunk)
        self.totals.append(total)
        self.chunks.append(chunk)
        self.into.append(exchange(send, self.axis, 1))

    def leave(self):
        old = len(self.totals)
        half = self.halves[old]
        total = self.step(half_sum, half, self.crossed[old], half.shape[0])
        self.totals.append(total)
        self.into.append(exchange(total, self.axis, 1))

    def output(self, first, count):
        ends = self.into[first + self.lag : first + self.lag + count]
        result = self.step(output, self.end, self.totals[first : first + count], ends)
        distance = 4
        while distance < self.count:
            result = add(result, exchange(result, self.axis, distance))
            distance *= 2
        return result


class Scatter:
    def __init__(self, parts, axis, step):
        self.axis, self.step = axis, step
        self.pieces = lax.axis_size(axis) // 2
        self.keep, send = parts
        self.distance = 1
        self.into = exchange(send, axis, 1)

    def advance(self):
        while self.pieces > 1:
            self.keep, send = self.step(scatter_step, self.keep, self.into, self.pieces)
            self.distance *= 2
            self.pieces //= 2
            self.into = exchange(send, self.axis, self.distance)

    def result(self):
        return self.step(half_sum, self.keep, self.into, self.keep.shape[0])


def per_device(tokens, w_query, w_key, w_value, w_out, cotangent):
    tok_rows = tokens.shape[0]
    inner = w_query.shape[1]
    local_levels = (tok_rows // BLOCK).bit_length() - 1
    count = lax.axis_size("seq")
    far_levels = count.bit_length() - 1
    far_bits = [d.bit_length() - 1 for d in range(1, count)]

    last = []

    def step(kernel, *operands):
        made = kernel(*operands, list(last))
        last[:] = made[:1] if isinstance(made, (list, tuple)) else [made]
        return made

    parts = key_value(tokens, w_key, w_value, local_levels, far_levels)
    levels, tops = parts[:local_levels], parts[local_levels:]
    fars = [exchange(tops[bit], "seq", d) for d, bit in enumerate(far_bits, 1)]
    query = step(project, tokens, w_query)
    powers, near = step(near_powers, query, levels)
    grad = step(project, cotangent, w_out)
    attended, attended_t, stats = step(forward, query, powers, near, levels, fars, far_bits)

    line = Line("seq", "head", step)
    pieces = 2
    rows = tokens.shape[1] // pieces
    line.enter_whole(step(weight_terms, attended_t, cotangent, inner, 0, 0, 1), pieces)
    dquery, dkv, query_first, query_second, *away = step(
        backward, query, grad, attended_t, stats, tokens, levels, fars, far_bits, pieces
    )
    line.enter(query_first)
    backs = [exchange(piece, "seq", d) for d, piece in enumerate(away, 2)]
    line.meet_whole()
    line.turn(query_second)
    dkey, dvalue, dkv_t = step(
        close_keys, dkv, [line.into[2], *backs], far_bits, local_levels
    )
    key_first = step(weight_terms, dkv_t, tokens, inner, 0, 0, pieces)
    line.meet(rows)
    line.turn(key_first)
    line.meet(rows)
    parts = step(project_split, [attended], [w_out], "head")
    mixed = Scatter(parts, "head", step)
    key_second = step(weight_terms, dkv_t, tokens, inner, 0, 1, pieces)
    value_first = step(weight_terms, dkv_t, tokens, inner, 1, 0, pieces)
    value_second = step(weight_terms, dkv_t, tokens, inner, 1, 1, pieces)
    keep, send = step(project_split, [dquery, dkey, dvalue], [w_query, w_key, w_value], "head")
    line.turn(key_second)
    line.meet(rows)
    tokens_grad = Scatter([keep, step(relay, send)], "head", step)
    line.turn(value_first)
    line.meet(rows)
    mixed.advance()
    line.turn(value_second)
    tokens_grad.advance()
    out_grad = line.output(0, pieces)
    line.meet(rows)
    line.leave()
    query_grad = line.output(2, pieces)
    line.meet(rows)
    mixed = mixed.result()
    line.leave()
    line.leave()
    tokens_grad = tokens_grad.result()
    key_grad = line.output(4, pieces)
    value_grad = line.output(6, pieces)
    return mixed, tokens_grad, query_grad, key_grad, value_grad, out_grad


def solution(mesh):
    return jax.shard_map(
        per_device,
        mesh=mesh,
        in_specs=(
            P(("groups", "seq"), None),
            P(None, "head"),
            P(None, "head"),
            P(None, "head"),
            P(None, "head"),
            P(("groups", "seq"), None),
        ),
        out_specs=(
            P(("groups", "seq"), "head"),
            P(("groups", "seq"), "head"),
            P("groups", "head"),
            P("groups", "head"),
            P("groups", "head"),
            P("groups", "head"),
        ),
        check_vma=False,
    )
```

```python
import functools
import math

import jax
import jax.numpy as jnp
from jax import lax
from jax.experimental import pallas as pl
from jax.experimental.pallas import tpu as pltpu
from jax.sharding import PartitionSpec as P

HEAD_DIM = 128
BLOCK = 128
BF16 = jnp.bfloat16
F32 = jnp.float32
MIB = 1024 * 1024

NN = (((1,), (0,)), ((), ()))
NT = (((1,), (1,)), ((), ()))
TN = (((0,), (0,)), ((), ()))


def dot(left, right, dims=NN):
    return lax.dot_general(left, right, dims, preferred_element_type=F32)


def params(mib):
    return pltpu.CompilerParams(vmem_limit_bytes=mib * MIB)


def cost(microseconds):
    return pl.CostEstimate(flops=int(microseconds * 1150e6) + 1, bytes_accessed=1, transcendentals=0)


def run(body, ready, after=(), in_specs=None, **options):
    count, extra = len(ready), len(after)

    def kernel(*refs):
        body(*refs[:count], *refs[count + extra :])

    in_specs = in_specs or [pl.BlockSpec(memory_space=pltpu.VMEM)] * count
    in_specs = in_specs + [pl.BlockSpec(memory_space=pl.ANY)] * extra
    return pl.pallas_call(kernel, in_specs=in_specs, **options)(*ready, *after)


def shape(rows, cols, dtype=BF16):
    return jax.ShapeDtypeStruct((rows, cols), dtype)


def whole(rows, cols):
    return pl.BlockSpec((rows, cols), lambda *_: (0, 0))


def pool_matrix(rows):
    row = lax.broadcasted_iota(jnp.int32, (rows // 2, rows), 0)
    col = lax.broadcasted_iota(jnp.int32, (rows // 2, rows), 1)
    return jnp.where(jnp.right_shift(col, 1) == row, 0.5, 0.0).astype(BF16)


def spread_matrix(rows, step_bits, offset, cols, weight):
    row = lax.broadcasted_iota(jnp.int32, (rows, cols), 0) + offset
    col = lax.broadcasted_iota(jnp.int32, (rows, cols), 1)
    return jnp.where(jnp.right_shift(row, step_bits) == col, weight, 0.0).astype(BF16)


def key_value_body(local_levels, far_levels, parts, tok_hbm, wk_hbm, wv_hbm, *refs):
    out_hbm = refs[:local_levels]
    far = refs[local_levels : local_levels + far_levels]
    refs = refs[local_levels + far_levels :]
    tok_ref, wk_ref, wv_ref = refs[:3]
    levels = refs[3 : 3 + local_levels]
    in_sems, out_sems = refs[3 + local_levels :]
    part = tok_ref.shape[0] // parts

    def fetch(source, target, i):
        copy = pltpu.make_async_copy(source, target, in_sems.at[i])
        copy.start()
        return copy

    def flush(i):
        copy = pltpu.make_async_copy(levels[i], out_hbm[i], out_sems.at[i])
        copy.start()
        return copy

    weights = [fetch(wk_hbm, wk_ref, 0), fetch(wv_hbm, wv_ref, 1)]
    tiles = []
    for p in range(parts):
        rows = pl.ds(p * part, part)
        tiles.append(fetch(tok_hbm.at[rows], tok_ref.at[rows], 2 + p))
    for copy in weights:
        copy.wait()
    for p in range(parts):
        tiles[p].wait()
        here = slice(p * part, (p + 1) * part)
        x = tok_ref[here, :]
        both = jnp.concatenate([dot(x, wk_ref[...]), dot(x, wv_ref[...])], axis=1)
        levels[0][here, :] = both.astype(BF16)
    flushes = [flush(0)]
    pool = pool_matrix(part)
    for i in range(1, local_levels):
        source = levels[i - 1]
        for low in range(0, source.shape[0], part):
            mean = dot(pool, source[low : low + part, :])
            levels[i][low // 2 : (low + part) // 2, :] = mean.astype(BF16)
        flushes.append(flush(i))
    rows = dot(pool, levels[-1][...]).astype(BF16)
    for i in range(far_levels):
        if i:
            rows = dot(pool_matrix(rows.shape[0]), rows).astype(BF16)
        far[i][...] = rows
    for copy in flushes:
        copy.wait()


def key_value(tokens, w_key, w_value, local_levels, far_levels, after):
    tok_rows, width = tokens.shape
    inner = w_key.shape[1]
    parts = tok_rows // (2 * BLOCK)
    held = [(tok_rows >> i, 2 * inner) for i in range(local_levels)]
    tops = [(BLOCK >> i, 2 * inner) for i in range(far_levels)]
    return run(
        functools.partial(key_value_body, local_levels, far_levels, parts),
        [tokens, w_key, w_value],
        after,
        in_specs=[pl.BlockSpec(memory_space=pl.ANY)] * 3,
        out_specs=[pl.BlockSpec(memory_space=pl.ANY)] * len(held)
        + [pl.BlockSpec(memory_space=pltpu.VMEM)] * len(tops),
        out_shape=[shape(*dims) for dims in held + tops],
        scratch_shapes=[pltpu.VMEM((tok_rows, width), BF16)]
        + [pltpu.VMEM((width, inner), BF16)] * 2
        + [pltpu.VMEM(dims, BF16) for dims in held]
        + [pltpu.SemaphoreType.DMA((parts + 2,)), pltpu.SemaphoreType.DMA((len(held),))],
        compiler_params=params(56),
        cost_estimate=cost(5.0),
    )


def project_body(left_ref, weight_ref, out_ref):
    out_ref[...] = dot(left_ref[...], weight_ref[...]).astype(BF16)


def project(left, weight, after):
    tok_rows, width = left.shape
    inner = weight.shape[1]
    return run(
        project_body,
        [left, weight],
        after,
        out_shape=shape(tok_rows, inner),
        compiler_params=params(4),
        cost_estimate=cost(0.7),
    )


class KeySet:
    def __init__(self, far_rows, far_bits, local_levels):
        mids = local_levels - 1
        self.sizes = [2 * BLOCK] + [BLOCK] * mids + list(far_rows)
        self.bounds = [sum(self.sizes[:i]) for i in range(len(self.sizes) + 1)]
        steps = [0] + list(range(1, local_levels)) + [local_levels + b for b in far_bits]
        self.biases = [float(step) for step in steps]
        self.mids = mids
        self.far_start = self.bounds[1 + mids]
        self.factor = math.log2(math.e) / math.sqrt(HEAD_DIM)

    def here(self, m):
        return pl.ds(pl.multiple_of(m * 2 * BLOCK, 2 * BLOCK), 2 * BLOCK)

    def seats(self, m):
        for i in range(self.mids):
            sibling = jnp.bitwise_xor(jnp.right_shift(m, i), 1)
            yield pl.ds(pl.multiple_of(sibling * BLOCK, BLOCK), BLOCK)

    def near(self, m, level_refs, cols):
        rows = [level_refs[0][self.here(m), cols]]
        rows += [ref[seat, cols] for ref, seat in zip(level_refs[1:], self.seats(m))]
        return rows

    def far(self, far_refs, cols):
        return [ref[:, cols] for ref in far_refs]

    def pieces(self, array, first=0, count=None):
        base = self.bounds[first]
        ends = self.bounds[first:] if count is None else self.bounds[first : first + count + 1]
        return [array[a - base : b - base] for a, b in zip(ends, ends[1:])]

    def top(self, pieces, first=0):
        tops = [
            jnp.max(piece, axis=0, keepdims=True) * self.factor + bias
            for piece, bias in zip(pieces, self.biases[first:])
        ]
        return functools.reduce(jnp.maximum, tops)

    def powers(self, pieces, top, first=0):
        return jnp.concatenate(
            [
                jnp.exp2(piece * self.factor + (bias - top))
                for piece, bias in zip(pieces, self.biases[first:])
            ],
            axis=0,
        )


def head_columns(h, inner):
    low = h * HEAD_DIM
    return slice(low, low + HEAD_DIM), slice(inner + low, inner + low + HEAD_DIM)


def near_body(local_levels, q_ref, *refs):
    level_refs = refs[:local_levels]
    power_ref, stat_ref = refs[local_levels:]
    tok_rows, inner = q_ref.shape
    heads = inner // HEAD_DIM
    keyset = KeySet([], [], local_levels)
    rows = keyset.far_start

    def step(m, carry):
        here = keyset.here(m)
        for h in range(heads):
            cols, _ = head_columns(h, inner)
            keys = jnp.concatenate(keyset.near(m, level_refs, cols), axis=0)
            pieces = keyset.pieces(dot(keys, q_ref[here, cols], NT))
            top = keyset.top(pieces)
            powers = keyset.powers(pieces, top)
            stat_ref[h : h + 1, here] = top
            stat_ref[heads + h : heads + h + 1, here] = jnp.sum(powers, axis=0, keepdims=True)
            power_ref[pl.ds(pl.multiple_of((m * heads + h) * rows, rows), rows), :] = powers
        return carry

    lax.fori_loop(0, tok_rows // (2 * BLOCK), step, 0)


def near_powers(query, levels, after):
    tok_rows, inner = query.shape
    heads = inner // HEAD_DIM
    pairs = tok_rows // (2 * BLOCK)
    rows = (len(levels) + 1) * BLOCK
    return run(
        functools.partial(near_body, len(levels)),
        [query, *levels],
        after,
        out_shape=[shape(pairs * heads * rows, 2 * BLOCK, F32), shape(2 * heads, tok_rows, F32)],
        compiler_params=params(6),
        cost_estimate=cost(2.3),
    )


def forward_body(local_levels, far_bits, *refs):
    fars = len(far_bits)
    q_ref, power_ref, near_ref = refs[:3]
    level_refs = refs[3 : 3 + local_levels]
    far_refs = refs[3 + local_levels : 3 + local_levels + fars]
    att_ref, att_t_ref, stat_ref = refs[3 + local_levels + fars :]
    tok_rows, inner = q_ref.shape
    heads = inner // HEAD_DIM
    keyset = KeySet([r.shape[0] for r in far_refs], far_bits, local_levels)
    rows = keyset.far_start

    def step(m, carry):
        here = keyset.here(m)
        for h in range(heads):
            cols, vcols = head_columns(h, inner)
            second = heads + h
            keys = jnp.concatenate(keyset.far(far_refs, cols), axis=0)
            values = keyset.near(m, level_refs, vcols) + keyset.far(far_refs, vcols)
            values = jnp.concatenate(values, axis=0)
            first = local_levels
            pieces = keyset.pieces(dot(keys, q_ref[here, cols], NT), first)
            near_top = near_ref[h : h + 1, here]
            top = jnp.maximum(near_top, keyset.top(pieces, first))
            shrink = jnp.exp2(near_top - top)
            powers = keyset.powers(pieces, top, first)
            total = near_ref[second : second + 1, here] * shrink
            total = total + jnp.sum(powers, axis=0, keepdims=True)
            inverse = 1.0 / total
            place = pl.ds(pl.multiple_of((m * heads + h) * rows, rows), rows)
            near_probs = (power_ref[place, :] * (shrink * inverse)).astype(BF16)
            far_probs = (powers * inverse).astype(BF16)
            probs_b = jnp.concatenate([near_probs, far_probs], axis=0)
            att_t = dot(values, probs_b, TN).astype(BF16)
            att_t_ref[cols, here] = att_t
            att_ref[here, cols] = att_t.T
            stat_ref[h : h + 1, here] = top
            stat_ref[second : second + 1, here] = inverse
        return carry

    lax.fori_loop(0, tok_rows // (2 * BLOCK), step, 0)


def forward(query, powers, near, levels, fars, far_bits, after):
    tok_rows, inner = query.shape
    heads = inner // HEAD_DIM
    set_rows = (len(levels) + 1) * BLOCK + sum(f.shape[0] for f in fars)
    return run(
        functools.partial(forward_body, len(levels), far_bits),
        [query, powers, near, *levels, *fars],
        after,
        out_shape=[
            shape(tok_rows, inner),
            shape(inner, tok_rows),
            shape(2 * heads, tok_rows, F32),
        ],
        compiler_params=params(6),
        cost_estimate=cost(4.0),
    )


def backward_body(local_levels, far_bits, pieces, *refs):
    mids = local_levels - 1
    fars = len(far_bits)
    q_ref, g_ref, att_t_ref, stat_ref, tok_ref = refs[:5]
    level_refs = refs[5 : 5 + local_levels]
    far_refs = refs[5 + local_levels : 5 + local_levels + fars]
    outs = refs[5 + local_levels + fars :]
    dq_ref, dkv_ref = outs[:2]
    term_refs = outs[2 : 2 + pieces]
    dfar_refs = outs[2 + pieces : 1 + pieces + fars]
    dmid_refs = outs[1 + pieces + fars : 1 + pieces + fars + mids]
    dq_t_ref, acc_ref = outs[-2:]
    tok_rows, inner = q_ref.shape
    heads = inner // HEAD_DIM
    score_scale = 1.0 / math.sqrt(HEAD_DIM)
    keyset = KeySet([r.shape[0] for r in far_refs], far_bits, local_levels)

    for ref in (*dmid_refs, acc_ref):
        ref[...] = jnp.zeros_like(ref)

    def step(m, carry):
        here = keyset.here(m)
        for h in range(heads):
            cols, vcols = head_columns(h, inner)
            keys, values = (
                jnp.concatenate(keyset.near(m, level_refs, c) + keyset.far(far_refs, c), axis=0)
                for c in (cols, vcols)
            )
            q = q_ref[here, cols]
            g = g_ref[here, cols]
            top = stat_ref[h : h + 1, here]
            inverse = stat_ref[heads + h : heads + h + 1, here]
            probs = keyset.powers(keyset.pieces(dot(keys, q, NT)), top) * inverse
            att_t = att_t_ref[cols, here].astype(F32)
            delta = jnp.sum(g.T.astype(F32) * att_t, axis=0, keepdims=True)
            grads = (probs * (dot(values, g, NT) - delta) * score_scale).astype(BF16)
            dq_t = dot(keys, grads, TN).astype(BF16)
            dq_t_ref[cols, here] = dq_t
            dq_ref[here, cols] = dq_t.T
            for part, place in ((dot(grads, q), cols), (dot(probs.astype(BF16), g), vcols)):
                own, *sides = keyset.pieces(part)
                dkv_ref[here, place] = own
                for ref, seat, side in zip(dmid_refs, keyset.seats(m), sides):
                    ref[seat, place] += side
                acc_ref[:, place] += part[keyset.far_start :]
        return carry

    lax.fori_loop(0, tok_rows // (2 * BLOCK), step, 0)
    width = term_refs[-1].shape[0]
    first = acc_ref[:BLOCK].astype(BF16)
    term_refs[0][width : width + BLOCK, :] = first[:, :inner]
    term_refs[0][width + BLOCK :, :] = first[:, inner:]
    low = BLOCK
    for ref in dfar_refs:
        ref[...] = acc_ref[low : low + ref.shape[0]].astype(BF16)
        low += ref.shape[0]
    for i, ref in enumerate(term_refs):
        part = dot(dq_t_ref[...], tok_ref[:, i * width : (i + 1) * width])
        ref[:width, :] = part.astype(BF16).T
    fan = spread_matrix(2 * BLOCK, 1, 0, BLOCK, 0.5)
    targets = (dkv_ref, *dmid_refs)
    for i in reversed(range(mids)):
        for t in range(dmid_refs[i].shape[0] // BLOCK):
            part = dmid_refs[i][t * BLOCK : (t + 1) * BLOCK, :]
            high = part.astype(BF16)
            low = (part - high.astype(F32)).astype(BF16)
            rows = slice(2 * t * BLOCK, 2 * (t + 1) * BLOCK)
            targets[i][rows, :] += dot(fan, high) + dot(fan, low)


def backward(query, grad, attended_t, stats, tokens, levels, fars, far_bits, pieces, after):
    tok_rows, inner = query.shape
    far_rows = sum(f.shape[0] for f in fars)
    set_rows = (len(levels) + 1) * BLOCK + far_rows
    return run(
        functools.partial(backward_body, len(levels), far_bits, pieces),
        [query, grad, attended_t, stats, tokens, *levels, *fars],
        after,
        out_shape=[shape(tok_rows, inner), shape(tok_rows, 2 * inner, F32)]
        + [shape(tokens.shape[1] // pieces + 2 * BLOCK, inner)]
        + [shape(tokens.shape[1] // pieces, inner)] * (pieces - 1)
        + [shape(*f.shape) for f in fars[1:]],
        scratch_shapes=[pltpu.VMEM(level.shape, F32) for level in levels[1:]]
        + [pltpu.VMEM((inner, tok_rows), BF16), pltpu.VMEM((far_rows, 2 * inner), F32)],
        compiler_params=params(10),
        cost_estimate=cost(8.0),
    )


def term_body(which, low, left_ref, right_ref, out_ref):
    width, inner = out_ref.shape
    left = left_ref[which * inner : (which + 1) * inner, :]
    out_ref[...] = dot(left, right_ref[:, low : low + width]).astype(BF16).T


def weight_terms(left_t, right, inner, which, part, parts, after):
    tok_rows = left_t.shape[1]
    width = right.shape[1] // parts
    return run(
        functools.partial(term_body, which, part * width),
        [left_t, right],
        after,
        out_shape=shape(width, inner),
        compiler_params=params(3),
        cost_estimate=cost(0.5),
    )


def close_body(local_levels, far_bits, dkv_ref, *refs):
    joined_ref, *back_refs = refs[: len(far_bits)]
    dk_ref, dv_ref, dkv_t_ref = refs[len(far_bits) :]
    inner = dk_ref.shape[1]
    tile = 2 * BLOCK
    low = joined_ref.shape[0] - 2 * BLOCK
    joined = [joined_ref[low : low + BLOCK, :], joined_ref[low + BLOCK :, :]]
    backs = [jnp.concatenate(joined, axis=1)] + [ref[...] for ref in back_refs]
    for t in range(dkv_ref.shape[0] // tile):
        here = slice(t * tile, (t + 1) * tile)
        total = dkv_ref[here, :]
        for back, bit in zip(backs, far_bits):
            weight = 0.5 ** (local_levels + bit)
            fan = spread_matrix(tile, local_levels + bit, t * tile, back.shape[0], weight)
            total = total + dot(fan, back)
        final = total.astype(BF16)
        dk_ref[here, :] = final[:, :inner]
        dv_ref[here, :] = final[:, inner:]
        dkv_t_ref[:, here] = final.T


def close_keys(dkv, backs, far_bits, local_levels, after):
    tok_rows, double = dkv.shape
    inner = double // 2
    return run(
        functools.partial(close_body, local_levels, far_bits),
        [dkv, *backs],
        after,
        out_shape=[shape(tok_rows, inner), shape(tok_rows, inner), shape(double, tok_rows)],
        compiler_params=params(5),
        cost_estimate=cost(1.8),
    )


def split_body(count, parts, rank_ref, *refs):
    lefts, weights = refs[:count], refs[count : 2 * count]
    outs = refs[2 * count :]
    width = weights[0].shape[0] // parts
    for r in range(parts):
        owner = jnp.bitwise_xor(rank_ref[0], r)
        rows = pl.ds(pl.multiple_of(owner * width, width), width)
        total = None
        for left, weight in zip(lefts, weights):
            product = dot(left[...], weight[rows, :], NT)
            total = product if total is None else total + product
        place = r // 2 * width
        outs[r % 2][:, place : place + width] = total.astype(BF16)


def project_split(rank, lefts, weights, axis, after):
    count = len(lefts)
    parts = lax.axis_size(axis)
    tok_rows, inner = lefts[0].shape
    width = weights[0].shape[0]
    return run(
        functools.partial(split_body, count, parts),
        [rank, *lefts, *weights],
        after,
        in_specs=[pl.BlockSpec(memory_space=pltpu.SMEM)]
        + [pl.BlockSpec(memory_space=pltpu.VMEM)] * (2 * count),
        out_shape=[shape(tok_rows, width // 2)] * 2,
        compiler_params=params(5),
        cost_estimate=cost(1.0),
    )


def exchange(block, axis, distance):
    count = lax.axis_size(axis)
    return lax.ppermute(block, axis, [(i, i ^ distance) for i in range(count)])


def add(left, right):
    return (left.astype(F32) + right.astype(F32)).astype(BF16)


def term_half_body(chunk_ref, into_ref, out_ref):
    rows = slice(0, out_ref.shape[0])
    out_ref[...] = (chunk_ref[rows, :].astype(F32) + into_ref[rows, :].astype(F32)).astype(BF16)


def half_sum(chunk, into, rows, after):
    return run(
        term_half_body,
        [chunk, into],
        after,
        out_shape=shape(rows, chunk.shape[1]),
        compiler_params=params(3),
        cost_estimate=cost(0.1),
    )


def pair_half_body(chunk_ref, into_ref, *out_refs):
    rows = out_refs[0].shape[0]
    for i, ref in enumerate(out_refs):
        here = slice(i * rows, (i + 1) * rows)
        ref[...] = (chunk_ref[here, :].astype(F32) + into_ref[here, :].astype(F32)).astype(BF16)


def half_sums(chunk, into, count, after):
    rows = chunk.shape[0] // count
    return run(
        pair_half_body,
        [chunk, into],
        after,
        out_shape=[shape(rows, chunk.shape[1])] * count,
        compiler_params=params(3),
        cost_estimate=cost(0.2),
    )


def scatter_body(pieces, keep_ref, into_ref, even_ref, odd_ref):
    width = keep_ref.shape[1] // pieces
    for i in range(pieces):
        here = slice(i * width, (i + 1) * width)
        place = slice(i // 2 * width, (i // 2 + 1) * width)
        total = keep_ref[:, here].astype(F32) + into_ref[:, here].astype(F32)
        (even_ref, odd_ref)[i % 2][:, place] = total.astype(BF16)


def last_body(left_ref, right_ref, token_ref, out_ref):
    token_ref[...] = jnp.zeros_like(token_ref)
    out_ref[...] = (left_ref[...].astype(F32) + right_ref[...].astype(F32)).astype(BF16)


def last_sum(left, right, after):
    return run(
        last_body,
        [left, right],
        after,
        out_shape=[shape(8, 128, F32), shape(*left.shape)],
        compiler_params=params(3),
        cost_estimate=cost(0.9),
    )


def scatter_step(keep, into, pieces, after):
    rows, width = keep.shape
    return run(
        functools.partial(scatter_body, pieces),
        [keep, into],
        after,
        out_shape=[shape(rows, width // 2)] * 2,
        compiler_params=params(4),
        cost_estimate=cost(0.2),
    )


def turn_body(end_ref, half_ref, across_ref, chunk_ref, total_ref, send_ref):
    total = (half_ref[...].astype(F32) + across_ref[...].astype(F32)).astype(BF16)
    total_ref[...] = total

    @pl.when(end_ref[0] == 1)
    def _():
        send_ref[...] = chunk_ref[...]

    @pl.when(end_ref[0] == 0)
    def _():
        send_ref[...] = total


def turn(end, half, across, chunk, after):
    return run(
        turn_body,
        [end, half, across, chunk],
        after,
        in_specs=[pl.BlockSpec(memory_space=pltpu.SMEM)]
        + [pl.BlockSpec(memory_space=pltpu.VMEM)] * 3,
        out_shape=[shape(*half.shape)] * 2,
        compiler_params=params(2),
        cost_estimate=cost(0.1),
    )


def output_body(count, end_ref, *refs):
    totals, ends, (token_ref, out_ref) = refs[:count], refs[count : 2 * count], refs[2 * count :]
    token_ref[...] = jnp.zeros_like(token_ref)
    rows = totals[0].shape[0]

    for flag, sources in ((0, totals), (1, ends)):

        @pl.when(end_ref[0] == flag)
        def _():
            for i, ref in enumerate(sources):
                out_ref[i * rows : (i + 1) * rows, :] = ref[...]


def output(end, totals, ends, after):
    count = len(totals)
    rows, width = totals[0].shape
    return run(
        functools.partial(output_body, count),
        [end, *totals, *ends],
        after,
        in_specs=[pl.BlockSpec(memory_space=pltpu.SMEM)]
        + [pl.BlockSpec(memory_space=pltpu.VMEM)] * (2 * count),
        out_shape=[shape(8, 128, F32), shape(count * rows, width)],
        compiler_params=params(4),
        cost_estimate=cost(0.9),
    )


def relay_body(source_ref, target_ref):
    target_ref[...] = source_ref[...]


def relay(block, after):
    return run(
        relay_body,
        [block],
        after,
        out_shape=shape(*block.shape),
        compiler_params=params(3),
        cost_estimate=cost(0.2),
    )


class Line:
    lag = 3

    def __init__(self, axis, other, end, step):
        self.axis, self.axes, self.step = axis, (axis, other), step
        self.count = lax.axis_size(axis)
        self.end = end
        width = lax.axis_size(other)
        self.across = []
        for place in range(self.count):
            for seat in range(width):
                target = (place, seat ^ 1 if width > 1 else seat)
                if place & 3 in (1, 2):
                    target = (place ^ 3, seat)
                self.across.append((place * width + seat, target[0] * width + target[1]))
        self.chunks, self.into, self.halves, self.crossed, self.totals = [], [], [], [], []

    def enter(self, chunk):
        self.chunks.append(chunk)
        self.into.append(exchange(chunk, self.axis, 1))

    def enter_whole(self, whole, count):
        self.whole = whole, exchange(whole, self.axis, 1), count
        self.chunks += [None] * count
        self.into += [None] * count

    def meet_whole(self):
        for half in self.step(half_sums, *self.whole):
            self.halves.append(half)
            self.crossed.append(lax.ppermute(half, self.axes, self.across))

    def meet(self, rows):
        k = len(self.halves)
        half = self.step(half_sum, self.chunks[k], self.into[k], rows)
        self.halves.append(half)
        self.crossed.append(lax.ppermute(half, self.axes, self.across))

    def turn(self, chunk):
        old = len(self.totals)
        total, send = self.step(turn, self.end, self.halves[old], self.crossed[old], chunk)
        self.totals.append(total)
        self.chunks.append(chunk)
        self.into.append(exchange(send, self.axis, 1))

    def leave(self):
        old = len(self.totals)
        half = self.halves[old]
        total = self.step(half_sum, half, self.crossed[old], half.shape[0])
        self.totals.append(total)
        self.into.append(exchange(total, self.axis, 1))

    def output(self, first, count):
        ends = self.into[first + self.lag : first + self.lag + count]
        _, result = self.step(output, self.end, self.totals[first : first + count], ends)
        distance = 4
        while distance < self.count:
            result = add(result, exchange(result, self.axis, distance))
            distance *= 2
        return result


class Scatter:
    def __init__(self, parts, axis, step):
        self.axis, self.step = axis, step
        self.pieces = lax.axis_size(axis) // 2
        self.keep, send = parts
        self.distance = 1
        self.into = exchange(send, axis, 1)

    def advance(self):
        while self.pieces > 1:
            self.keep, send = self.step(scatter_step, self.keep, self.into, self.pieces)
            self.distance *= 2
            self.pieces //= 2
            self.into = exchange(send, self.axis, self.distance)

    def result(self):
        return self.step(last_sum, self.keep, self.into)[1]


def per_device(tokens, w_query, w_key, w_value, w_out, cotangent):
    tok_rows = tokens.shape[0]
    inner = w_query.shape[1]
    local_levels = (tok_rows // BLOCK).bit_length() - 1
    count = lax.axis_size("seq")
    far_levels = count.bit_length() - 1
    far_bits = [d.bit_length() - 1 for d in range(1, count)]

    last = []

    def step(kernel, *operands):
        made = kernel(*operands, list(last))
        last[:] = made[:1] if isinstance(made, (list, tuple)) else [made]
        return made

    place = jnp.bitwise_and(lax.axis_index("seq"), 3)
    end = jnp.reshape((place == 0) | (place == 3), (1,)).astype(jnp.int32)
    rank = jnp.reshape(lax.axis_index("head"), (1,)).astype(jnp.int32)
    parts = key_value(tokens, w_key, w_value, local_levels, far_levels, [end, rank])
    levels, tops = parts[:local_levels], parts[local_levels:]
    fars = [exchange(tops[bit], "seq", d) for d, bit in enumerate(far_bits, 1)]
    query = step(project, tokens, w_query)
    powers, near = step(near_powers, query, levels)
    grad = step(project, cotangent, w_out)
    attended, attended_t, stats = step(forward, query, powers, near, levels, fars, far_bits)

    line = Line("seq", "head", end, step)
    pieces = 2
    rows = tokens.shape[1] // pieces
    line.enter_whole(step(weight_terms, attended_t, cotangent, inner, 0, 0, 1), pieces)
    dquery, dkv, query_first, query_second, *away = step(
        backward, query, grad, attended_t, stats, tokens, levels, fars, far_bits, pieces
    )
    line.enter(query_first)
    backs = [exchange(piece, "seq", d) for d, piece in enumerate(away, 2)]
    line.meet_whole()
    line.turn(query_second)
    dkey, dvalue, dkv_t = step(
        close_keys, dkv, [line.into[2], *backs], far_bits, local_levels
    )
    key_first = step(weight_terms, dkv_t, tokens, inner, 0, 0, pieces)
    line.meet(rows)
    line.turn(key_first)
    line.meet(rows)
    parts = step(project_split, rank, [attended], [w_out], "head")
    mixed = Scatter(parts, "head", step)
    key_second = step(weight_terms, dkv_t, tokens, inner, 0, 1, pieces)
    value_first = step(weight_terms, dkv_t, tokens, inner, 1, 0, pieces)
    value_second = step(weight_terms, dkv_t, tokens, inner, 1, 1, pieces)
    keep, send = step(project_split, rank, [dquery, dkey, dvalue], [w_query, w_key, w_value], "head")
    line.turn(key_second)
    line.meet(rows)
    tokens_grad = Scatter([keep, step(relay, send)], "head", step)
    line.turn(value_first)
    mixed.advance()
    line.meet(rows)
    line.turn(value_second)
    tokens_grad.advance()
    line.meet(rows)
    out_grad = line.output(0, pieces)
    line.leave()
    line.meet(rows)
    query_grad = line.output(2, pieces)
    line.leave()
    mixed = mixed.result()
    key_grad = line.output(4, pieces)
    line.leave()
    tokens_grad = tokens_grad.result()
    value_grad = line.output(6, pieces)
    return mixed, tokens_grad, query_grad, key_grad, value_grad, out_grad


def solution(mesh):
    return jax.shard_map(
        per_device,
        mesh=mesh,
        in_specs=(
            P(("groups", "seq"), None),
            P(None, "head"),
            P(None, "head"),
            P(None, "head"),
            P(None, "head"),
            P(("groups", "seq"), None),
        ),
        out_specs=(
            P(("groups", "seq"), "head"),
            P(("groups", "seq"), "head"),
            P("groups", "head"),
            P("groups", "head"),
            P("groups", "head"),
            P("groups", "head"),
        ),
        check_vma=False,
    )
```

```python
import functools
import math

import jax
import jax.numpy as jnp
from jax import lax
from jax.experimental import pallas as pl
from jax.experimental.pallas import tpu as pltpu
from jax.sharding import PartitionSpec as P

HEAD_DIM = 128
BLOCK = 128
BF16 = jnp.bfloat16
F32 = jnp.float32
MIB = 1024 * 1024

NN = (((1,), (0,)), ((), ()))
NT = (((1,), (1,)), ((), ()))
TN = (((0,), (0,)), ((), ()))


def dot(left, right, dims=NN):
    return lax.dot_general(left, right, dims, preferred_element_type=F32)


def params(mib):
    return pltpu.CompilerParams(vmem_limit_bytes=mib * MIB)


def cost(microseconds):
    return pl.CostEstimate(flops=int(microseconds * 1150e6) + 1, bytes_accessed=1, transcendentals=0)


def run(body, ready, after=(), in_specs=None, **options):
    count, extra = len(ready), len(after)

    def kernel(*refs):
        body(*refs[:count], *refs[count + extra :])

    in_specs = in_specs or [pl.BlockSpec(memory_space=pltpu.VMEM)] * count
    in_specs = in_specs + [pl.BlockSpec(memory_space=pl.ANY)] * extra
    return pl.pallas_call(kernel, in_specs=in_specs, **options)(*ready, *after)


def shape(rows, cols, dtype=BF16):
    return jax.ShapeDtypeStruct((rows, cols), dtype)


def whole(rows, cols):
    return pl.BlockSpec((rows, cols), lambda *_: (0, 0))


def pool_matrix(rows):
    row = lax.broadcasted_iota(jnp.int32, (rows // 2, rows), 0)
    col = lax.broadcasted_iota(jnp.int32, (rows // 2, rows), 1)
    return jnp.where(jnp.right_shift(col, 1) == row, 0.5, 0.0).astype(BF16)


def spread_matrix(rows, step_bits, offset, cols, weight):
    row = lax.broadcasted_iota(jnp.int32, (rows, cols), 0) + offset
    col = lax.broadcasted_iota(jnp.int32, (rows, cols), 1)
    return jnp.where(jnp.right_shift(row, step_bits) == col, weight, 0.0).astype(BF16)


def key_value_body(local_levels, far_levels, parts, tok_hbm, wk_hbm, wv_hbm, *refs):
    out_hbm = refs[:local_levels]
    far = refs[local_levels : local_levels + far_levels]
    refs = refs[local_levels + far_levels :]
    tok_ref, wk_ref, wv_ref = refs[:3]
    levels = refs[3 : 3 + local_levels]
    in_sems, out_sems = refs[3 + local_levels :]
    part = tok_ref.shape[0] // parts

    def fetch(source, target, i):
        copy = pltpu.make_async_copy(source, target, in_sems.at[i])
        copy.start()
        return copy

    def flush(i):
        copy = pltpu.make_async_copy(levels[i], out_hbm[i], out_sems.at[i])
        copy.start()
        return copy

    weights = [fetch(wk_hbm, wk_ref, 0), fetch(wv_hbm, wv_ref, 1)]
    tiles = []
    for p in range(parts):
        rows = pl.ds(p * part, part)
        tiles.append(fetch(tok_hbm.at[rows], tok_ref.at[rows], 2 + p))
    for copy in weights:
        copy.wait()
    for p in range(parts):
        tiles[p].wait()
        here = slice(p * part, (p + 1) * part)
        x = tok_ref[here, :]
        both = jnp.concatenate([dot(x, wk_ref[...]), dot(x, wv_ref[...])], axis=1)
        levels[0][here, :] = both.astype(BF16)
    flushes = [flush(0)]
    pool = pool_matrix(part)
    for i in range(1, local_levels):
        source = levels[i - 1]
        for low in range(0, source.shape[0], part):
            mean = dot(pool, source[low : low + part, :])
            levels[i][low // 2 : (low + part) // 2, :] = mean.astype(BF16)
        flushes.append(flush(i))
    rows = dot(pool, levels[-1][...]).astype(BF16)
    for i in range(far_levels):
        if i:
            rows = dot(pool_matrix(rows.shape[0]), rows).astype(BF16)
        far[i][...] = rows
    for copy in flushes:
        copy.wait()


def key_value(tokens, w_key, w_value, local_levels, far_levels, after):
    tok_rows, width = tokens.shape
    inner = w_key.shape[1]
    parts = tok_rows // (2 * BLOCK)
    held = [(tok_rows >> i, 2 * inner) for i in range(local_levels)]
    tops = [(BLOCK >> i, 2 * inner) for i in range(far_levels)]
    return run(
        functools.partial(key_value_body, local_levels, far_levels, parts),
        [tokens, w_key, w_value],
        after,
        in_specs=[pl.BlockSpec(memory_space=pl.ANY)] * 3,
        out_specs=[pl.BlockSpec(memory_space=pl.ANY)] * len(held)
        + [pl.BlockSpec(memory_space=pltpu.VMEM)] * len(tops),
        out_shape=[shape(*dims) for dims in held + tops],
        scratch_shapes=[pltpu.VMEM((tok_rows, width), BF16)]
        + [pltpu.VMEM((width, inner), BF16)] * 2
        + [pltpu.VMEM(dims, BF16) for dims in held]
        + [pltpu.SemaphoreType.DMA((parts + 2,)), pltpu.SemaphoreType.DMA((len(held),))],
        compiler_params=params(56),
        cost_estimate=cost(5.0),
    )


def project_body(left_ref, weight_ref, out_ref):
    out_ref[...] = dot(left_ref[...], weight_ref[...]).astype(BF16)


def project(left, weight, after):
    tok_rows, width = left.shape
    inner = weight.shape[1]
    return run(
        project_body,
        [left, weight],
        after,
        out_shape=shape(tok_rows, inner),
        compiler_params=params(4),
        cost_estimate=cost(0.7),
    )


class KeySet:
    def __init__(self, far_rows, far_bits, local_levels):
        mids = local_levels - 1
        self.sizes = [2 * BLOCK] + [BLOCK] * mids + list(far_rows)
        self.bounds = [sum(self.sizes[:i]) for i in range(len(self.sizes) + 1)]
        steps = [0] + list(range(1, local_levels)) + [local_levels + b for b in far_bits]
        self.biases = [float(step) for step in steps]
        self.mids = mids
        self.far_start = self.bounds[1 + mids]
        self.factor = math.log2(math.e) / math.sqrt(HEAD_DIM)

    def here(self, m):
        return pl.ds(pl.multiple_of(m * 2 * BLOCK, 2 * BLOCK), 2 * BLOCK)

    def seats(self, m):
        for i in range(self.mids):
            sibling = jnp.bitwise_xor(jnp.right_shift(m, i), 1)
            yield pl.ds(pl.multiple_of(sibling * BLOCK, BLOCK), BLOCK)

    def near(self, m, level_refs, cols):
        rows = [level_refs[0][self.here(m), cols]]
        rows += [ref[seat, cols] for ref, seat in zip(level_refs[1:], self.seats(m))]
        return rows

    def far(self, far_refs, cols):
        return [ref[:, cols] for ref in far_refs]

    def pieces(self, array, first=0, count=None):
        base = self.bounds[first]
        ends = self.bounds[first:] if count is None else self.bounds[first : first + count + 1]
        return [array[a - base : b - base] for a, b in zip(ends, ends[1:])]

    def top(self, pieces, first=0):
        tops = [
            jnp.max(piece, axis=0, keepdims=True) * self.factor + bias
            for piece, bias in zip(pieces, self.biases[first:])
        ]
        return functools.reduce(jnp.maximum, tops)

    def powers(self, pieces, top, first=0):
        return jnp.concatenate(
            [
                jnp.exp2(piece * self.factor + (bias - top))
                for piece, bias in zip(pieces, self.biases[first:])
            ],
            axis=0,
        )


def head_columns(h, inner):
    low = h * HEAD_DIM
    return slice(low, low + HEAD_DIM), slice(inner + low, inner + low + HEAD_DIM)


def near_body(local_levels, q_ref, *refs):
    level_refs = refs[:local_levels]
    power_ref, stat_ref = refs[local_levels:]
    tok_rows, inner = q_ref.shape
    heads = inner // HEAD_DIM
    keyset = KeySet([], [], local_levels)
    rows = keyset.far_start

    def step(m, carry):
        here = keyset.here(m)
        for h in range(heads):
            cols, _ = head_columns(h, inner)
            keys = jnp.concatenate(keyset.near(m, level_refs, cols), axis=0)
            pieces = keyset.pieces(dot(keys, q_ref[here, cols], NT))
            top = keyset.top(pieces)
            powers = keyset.powers(pieces, top)
            stat_ref[h : h + 1, here] = top
            stat_ref[heads + h : heads + h + 1, here] = jnp.sum(powers, axis=0, keepdims=True)
            power_ref[pl.ds(pl.multiple_of((m * heads + h) * rows, rows), rows), :] = powers
        return carry

    lax.fori_loop(0, tok_rows // (2 * BLOCK), step, 0)


def near_powers(query, levels, after):
    tok_rows, inner = query.shape
    heads = inner // HEAD_DIM
    pairs = tok_rows // (2 * BLOCK)
    rows = (len(levels) + 1) * BLOCK
    return run(
        functools.partial(near_body, len(levels)),
        [query, *levels],
        after,
        out_shape=[shape(pairs * heads * rows, 2 * BLOCK, F32), shape(2 * heads, tok_rows, F32)],
        compiler_params=params(6),
        cost_estimate=cost(2.3),
    )


def forward_body(local_levels, far_bits, *refs):
    fars = len(far_bits)
    q_ref, power_ref, near_ref = refs[:3]
    level_refs = refs[3 : 3 + local_levels]
    far_refs = refs[3 + local_levels : 3 + local_levels + fars]
    att_ref, att_t_ref, stat_ref = refs[3 + local_levels + fars :]
    tok_rows, inner = q_ref.shape
    heads = inner // HEAD_DIM
    keyset = KeySet([r.shape[0] for r in far_refs], far_bits, local_levels)
    rows = keyset.far_start

    def step(m, carry):
        here = keyset.here(m)
        for h in range(heads):
            cols, vcols = head_columns(h, inner)
            second = heads + h
            keys = jnp.concatenate(keyset.far(far_refs, cols), axis=0)
            values = keyset.near(m, level_refs, vcols) + keyset.far(far_refs, vcols)
            values = jnp.concatenate(values, axis=0)
            first = local_levels
            pieces = keyset.pieces(dot(keys, q_ref[here, cols], NT), first)
            near_top = near_ref[h : h + 1, here]
            top = jnp.maximum(near_top, keyset.top(pieces, first))
            shrink = jnp.exp2(near_top - top)
            powers = keyset.powers(pieces, top, first)
            total = near_ref[second : second + 1, here] * shrink
            total = total + jnp.sum(powers, axis=0, keepdims=True)
            inverse = 1.0 / total
            place = pl.ds(pl.multiple_of((m * heads + h) * rows, rows), rows)
            near_probs = (power_ref[place, :] * (shrink * inverse)).astype(BF16)
            far_probs = (powers * inverse).astype(BF16)
            probs_b = jnp.concatenate([near_probs, far_probs], axis=0)
            att_t = dot(values, probs_b, TN).astype(BF16)
            att_t_ref[cols, here] = att_t
            att_ref[here, cols] = att_t.T
            stat_ref[h : h + 1, here] = top
            stat_ref[second : second + 1, here] = inverse
        return carry

    lax.fori_loop(0, tok_rows // (2 * BLOCK), step, 0)


def forward(query, powers, near, levels, fars, far_bits, after):
    tok_rows, inner = query.shape
    heads = inner // HEAD_DIM
    set_rows = (len(levels) + 1) * BLOCK + sum(f.shape[0] for f in fars)
    return run(
        functools.partial(forward_body, len(levels), far_bits),
        [query, powers, near, *levels, *fars],
        after,
        out_shape=[
            shape(tok_rows, inner),
            shape(inner, tok_rows),
            shape(2 * heads, tok_rows, F32),
        ],
        compiler_params=params(6),
        cost_estimate=cost(4.0),
    )


def backward_body(local_levels, far_bits, pieces, *refs):
    mids = local_levels - 1
    fars = len(far_bits)
    q_ref, g_ref, att_t_ref, stat_ref, tok_ref = refs[:5]
    level_refs = refs[5 : 5 + local_levels]
    far_refs = refs[5 + local_levels : 5 + local_levels + fars]
    outs = refs[5 + local_levels + fars :]
    dq_ref, dkv_ref = outs[:2]
    term_refs = outs[2 : 2 + pieces]
    dfar_refs = outs[2 + pieces : 1 + pieces + fars]
    dmid_refs = outs[1 + pieces + fars : 1 + pieces + fars + mids]
    dq_t_ref, acc_ref = outs[-2:]
    tok_rows, inner = q_ref.shape
    heads = inner // HEAD_DIM
    score_scale = 1.0 / math.sqrt(HEAD_DIM)
    keyset = KeySet([r.shape[0] for r in far_refs], far_bits, local_levels)

    for ref in (*dmid_refs, acc_ref):
        ref[...] = jnp.zeros_like(ref)

    def step(m, carry):
        here = keyset.here(m)
        for h in range(heads):
            cols, vcols = head_columns(h, inner)
            keys, values = (
                jnp.concatenate(keyset.near(m, level_refs, c) + keyset.far(far_refs, c), axis=0)
                for c in (cols, vcols)
            )
            q = q_ref[here, cols]
            g = g_ref[here, cols]
            top = stat_ref[h : h + 1, here]
            inverse = stat_ref[heads + h : heads + h + 1, here]
            probs = keyset.powers(keyset.pieces(dot(keys, q, NT)), top) * inverse
            att_t = att_t_ref[cols, here].astype(F32)
            delta = jnp.sum(g.T.astype(F32) * att_t, axis=0, keepdims=True)
            grads = (probs * (dot(values, g, NT) - delta) * score_scale).astype(BF16)
            dq_t = dot(keys, grads, TN).astype(BF16)
            dq_t_ref[cols, here] = dq_t
            dq_ref[here, cols] = dq_t.T
            for part, place in ((dot(grads, q), cols), (dot(probs.astype(BF16), g), vcols)):
                own, *sides = keyset.pieces(part)
                dkv_ref[here, place] = own
                for ref, seat, side in zip(dmid_refs, keyset.seats(m), sides):
                    ref[seat, place] += side
                acc_ref[:, place] += part[keyset.far_start :]
        return carry

    lax.fori_loop(0, tok_rows // (2 * BLOCK), step, 0)
    width = term_refs[-1].shape[0]
    first = acc_ref[:BLOCK].astype(BF16)
    term_refs[0][width : width + BLOCK, :] = first[:, :inner]
    term_refs[0][width + BLOCK :, :] = first[:, inner:]
    low = BLOCK
    for ref in dfar_refs:
        ref[...] = acc_ref[low : low + ref.shape[0]].astype(BF16)
        low += ref.shape[0]
    for i, ref in enumerate(term_refs):
        part = dot(dq_t_ref[...], tok_ref[:, i * width : (i + 1) * width])
        ref[:width, :] = part.astype(BF16).T
    fan = spread_matrix(2 * BLOCK, 1, 0, BLOCK, 0.5)
    targets = (dkv_ref, *dmid_refs)
    for i in reversed(range(mids)):
        for t in range(dmid_refs[i].shape[0] // BLOCK):
            part = dmid_refs[i][t * BLOCK : (t + 1) * BLOCK, :]
            high = part.astype(BF16)
            low = (part - high.astype(F32)).astype(BF16)
            rows = slice(2 * t * BLOCK, 2 * (t + 1) * BLOCK)
            targets[i][rows, :] += dot(fan, high) + dot(fan, low)


def backward(query, grad, attended_t, stats, tokens, levels, fars, far_bits, pieces, after):
    tok_rows, inner = query.shape
    far_rows = sum(f.shape[0] for f in fars)
    set_rows = (len(levels) + 1) * BLOCK + far_rows
    return run(
        functools.partial(backward_body, len(levels), far_bits, pieces),
        [query, grad, attended_t, stats, tokens, *levels, *fars],
        after,
        out_shape=[shape(tok_rows, inner), shape(tok_rows, 2 * inner, F32)]
        + [shape(tokens.shape[1] // pieces + 2 * BLOCK, inner)]
        + [shape(tokens.shape[1] // pieces, inner)] * (pieces - 1)
        + [shape(*f.shape) for f in fars[1:]],
        scratch_shapes=[pltpu.VMEM(level.shape, F32) for level in levels[1:]]
        + [pltpu.VMEM((inner, tok_rows), BF16), pltpu.VMEM((far_rows, 2 * inner), F32)],
        compiler_params=params(10),
        cost_estimate=cost(8.0),
    )


def term_body(which, low, left_ref, right_ref, out_ref):
    width, inner = out_ref.shape
    left = left_ref[which * inner : (which + 1) * inner, :]
    out_ref[...] = dot(left, right_ref[:, low : low + width]).astype(BF16).T


def weight_terms(left_t, right, inner, which, part, parts, after):
    tok_rows = left_t.shape[1]
    width = right.shape[1] // parts
    return run(
        functools.partial(term_body, which, part * width),
        [left_t, right],
        after,
        out_shape=shape(width, inner),
        compiler_params=params(3),
        cost_estimate=cost(0.5),
    )


def close_body(local_levels, far_bits, dkv_ref, *refs):
    joined_ref, *back_refs = refs[: len(far_bits)]
    dk_ref, dv_ref, dkv_t_ref = refs[len(far_bits) :]
    inner = dk_ref.shape[1]
    tile = 2 * BLOCK
    low = joined_ref.shape[0] - 2 * BLOCK
    joined = [joined_ref[low : low + BLOCK, :], joined_ref[low + BLOCK :, :]]
    backs = [jnp.concatenate(joined, axis=1)] + [ref[...] for ref in back_refs]
    for t in range(dkv_ref.shape[0] // tile):
        here = slice(t * tile, (t + 1) * tile)
        total = dkv_ref[here, :]
        for back, bit in zip(backs, far_bits):
            weight = 0.5 ** (local_levels + bit)
            fan = spread_matrix(tile, local_levels + bit, t * tile, back.shape[0], weight)
            total = total + dot(fan, back)
        final = total.astype(BF16)
        dk_ref[here, :] = final[:, :inner]
        dv_ref[here, :] = final[:, inner:]
        dkv_t_ref[:, here] = final.T


def close_keys(dkv, backs, far_bits, local_levels, after):
    tok_rows, double = dkv.shape
    inner = double // 2
    return run(
        functools.partial(close_body, local_levels, far_bits),
        [dkv, *backs],
        after,
        out_shape=[shape(tok_rows, inner), shape(tok_rows, inner), shape(double, tok_rows)],
        compiler_params=params(5),
        cost_estimate=cost(1.8),
    )


def split_body(count, parts, rank_ref, *refs):
    lefts, weights = refs[:count], refs[count : 2 * count]
    outs = refs[2 * count :]
    width = weights[0].shape[0] // parts
    for r in range(parts):
        owner = jnp.bitwise_xor(rank_ref[0], r)
        rows = pl.ds(pl.multiple_of(owner * width, width), width)
        total = None
        for left, weight in zip(lefts, weights):
            product = dot(left[...], weight[rows, :], NT)
            total = product if total is None else total + product
        place = r // 2 * width
        outs[r % 2][:, place : place + width] = total.astype(BF16)


def project_split(rank, lefts, weights, axis, after):
    count = len(lefts)
    parts = lax.axis_size(axis)
    tok_rows, inner = lefts[0].shape
    width = weights[0].shape[0]
    return run(
        functools.partial(split_body, count, parts),
        [rank, *lefts, *weights],
        after,
        in_specs=[pl.BlockSpec(memory_space=pltpu.SMEM)]
        + [pl.BlockSpec(memory_space=pltpu.VMEM)] * (2 * count),
        out_shape=[shape(tok_rows, width // 2)] * 2,
        compiler_params=params(5),
        cost_estimate=cost(1.0),
    )


def exchange(block, axis, distance):
    count = lax.axis_size(axis)
    return lax.ppermute(block, axis, [(i, i ^ distance) for i in range(count)])


def add(left, right):
    return (left.astype(F32) + right.astype(F32)).astype(BF16)


def term_half_body(chunk_ref, into_ref, out_ref):
    rows = slice(0, out_ref.shape[0])
    out_ref[...] = (chunk_ref[rows, :].astype(F32) + into_ref[rows, :].astype(F32)).astype(BF16)


def half_sum(chunk, into, rows, after):
    return run(
        term_half_body,
        [chunk, into],
        after,
        out_shape=shape(rows, chunk.shape[1]),
        compiler_params=params(3),
        cost_estimate=cost(0.1),
    )


def scatter_body(pieces, keep_ref, into_ref, even_ref, odd_ref):
    width = keep_ref.shape[1] // pieces
    for i in range(pieces):
        here = slice(i * width, (i + 1) * width)
        place = slice(i // 2 * width, (i // 2 + 1) * width)
        total = keep_ref[:, here].astype(F32) + into_ref[:, here].astype(F32)
        (even_ref, odd_ref)[i % 2][:, place] = total.astype(BF16)


def last_body(left_ref, right_ref, token_ref, out_ref):
    token_ref[...] = jnp.zeros_like(token_ref)
    out_ref[...] = (left_ref[...].astype(F32) + right_ref[...].astype(F32)).astype(BF16)


def last_sum(left, right, after):
    return run(
        last_body,
        [left, right],
        after,
        out_shape=[shape(8, 128, F32), shape(*left.shape)],
        compiler_params=params(3),
        cost_estimate=cost(0.9),
    )


def scatter_step(keep, into, pieces, after):
    rows, width = keep.shape
    return run(
        functools.partial(scatter_body, pieces),
        [keep, into],
        after,
        out_shape=[shape(rows, width // 2)] * 2,
        compiler_params=params(4),
        cost_estimate=cost(0.2),
    )


def turn_body(end_ref, half_ref, across_ref, chunk_ref, total_ref, send_ref):
    total = (half_ref[...].astype(F32) + across_ref[...].astype(F32)).astype(BF16)
    total_ref[...] = total

    @pl.when(end_ref[0] == 1)
    def _():
        send_ref[...] = chunk_ref[...]

    @pl.when(end_ref[0] == 0)
    def _():
        send_ref[...] = total


def turn(end, half, across, chunk, after):
    return run(
        turn_body,
        [end, half, across, chunk],
        after,
        in_specs=[pl.BlockSpec(memory_space=pltpu.SMEM)]
        + [pl.BlockSpec(memory_space=pltpu.VMEM)] * 3,
        out_shape=[shape(*half.shape)] * 2,
        compiler_params=params(2),
        cost_estimate=cost(0.1),
    )


def output_body(count, end_ref, *refs):
    totals, ends, (token_ref, out_ref) = refs[:count], refs[count : 2 * count], refs[2 * count :]
    token_ref[...] = jnp.zeros_like(token_ref)
    rows = totals[0].shape[0]

    for flag, sources in ((0, totals), (1, ends)):

        @pl.when(end_ref[0] == flag)
        def _():
            for i, ref in enumerate(sources):
                out_ref[i * rows : (i + 1) * rows, :] = ref[...]


def output(end, totals, ends, after):
    count = len(totals)
    rows, width = totals[0].shape
    return run(
        functools.partial(output_body, count),
        [end, *totals, *ends],
        after,
        in_specs=[pl.BlockSpec(memory_space=pltpu.SMEM)]
        + [pl.BlockSpec(memory_space=pltpu.VMEM)] * (2 * count),
        out_shape=[shape(8, 128, F32), shape(count * rows, width)],
        compiler_params=params(4),
        cost_estimate=cost(0.9),
    )


def relay_body(source_ref, target_ref):
    target_ref[...] = source_ref[...]


def relay(block, after):
    return run(
        relay_body,
        [block],
        after,
        out_shape=shape(*block.shape),
        compiler_params=params(3),
        cost_estimate=cost(0.2),
    )


class Line:
    lag = 3

    def __init__(self, axis, other, end, step):
        self.axis, self.axes, self.step = axis, (axis, other), step
        self.count = lax.axis_size(axis)
        self.end = end
        width = lax.axis_size(other)
        self.across = []
        for place in range(self.count):
            for seat in range(width):
                target = (place, seat ^ 1 if width > 1 else seat)
                if place & 3 in (1, 2):
                    target = (place ^ 3, seat)
                self.across.append((place * width + seat, target[0] * width + target[1]))
        self.chunks, self.into, self.halves, self.crossed, self.totals = [], [], [], [], []

    def enter(self, chunk):
        self.chunks.append(chunk)
        self.into.append(exchange(chunk, self.axis, 1))

    def meet(self, rows):
        k = len(self.halves)
        half = self.step(half_sum, self.chunks[k], self.into[k], rows)
        self.halves.append(half)
        self.crossed.append(lax.ppermute(half, self.axes, self.across))

    def turn(self, chunk):
        old = len(self.totals)
        total, send = self.step(turn, self.end, self.halves[old], self.crossed[old], chunk)
        self.totals.append(total)
        self.chunks.append(chunk)
        self.into.append(exchange(send, self.axis, 1))

    def leave(self):
        old = len(self.totals)
        half = self.halves[old]
        total = self.step(half_sum, half, self.crossed[old], half.shape[0])
        self.totals.append(total)
        self.into.append(exchange(total, self.axis, 1))

    def output(self, first, count):
        ends = self.into[first + self.lag : first + self.lag + count]
        _, result = self.step(output, self.end, self.totals[first : first + count], ends)
        distance = 4
        while distance < self.count:
            result = add(result, exchange(result, self.axis, distance))
            distance *= 2
        return result


class Scatter:
    def __init__(self, parts, axis, step):
        self.axis, self.step = axis, step
        self.pieces = lax.axis_size(axis) // 2
        self.keep, send = parts
        self.distance = 1
        self.into = exchange(send, axis, 1)

    def advance(self):
        while self.pieces > 1:
            self.keep, send = self.step(scatter_step, self.keep, self.into, self.pieces)
            self.distance *= 2
            self.pieces //= 2
            self.into = exchange(send, self.axis, self.distance)

    def result(self):
        return self.step(last_sum, self.keep, self.into)[1]


def per_device(tokens, w_query, w_key, w_value, w_out, cotangent):
    tok_rows = tokens.shape[0]
    inner = w_query.shape[1]
    local_levels = (tok_rows // BLOCK).bit_length() - 1
    count = lax.axis_size("seq")
    far_levels = count.bit_length() - 1
    far_bits = [d.bit_length() - 1 for d in range(1, count)]

    last = []

    def step(kernel, *operands):
        made = kernel(*operands, list(last))
        last[:] = made[:1] if isinstance(made, (list, tuple)) else [made]
        return made

    place = jnp.bitwise_and(lax.axis_index("seq"), 3)
    end = jnp.reshape((place == 0) | (place == 3), (1,)).astype(jnp.int32)
    rank = jnp.reshape(lax.axis_index("head"), (1,)).astype(jnp.int32)
    parts = key_value(tokens, w_key, w_value, local_levels, far_levels, [end, rank])
    levels, tops = parts[:local_levels], parts[local_levels:]
    fars = [exchange(tops[bit], "seq", d) for d, bit in enumerate(far_bits, 1)]
    query = step(project, tokens, w_query)
    powers, near = step(near_powers, query, levels)
    grad = step(project, cotangent, w_out)
    attended, attended_t, stats = step(forward, query, powers, near, levels, fars, far_bits)

    line = Line("seq", "head", end, step)
    pieces = 2
    rows = tokens.shape[1] // pieces
    line.enter(step(weight_terms, attended_t, cotangent, inner, 0, 0, pieces))
    line.enter(step(weight_terms, attended_t, cotangent, inner, 0, 1, pieces))
    dquery, dkv, query_first, query_second, *away = step(
        backward, query, grad, attended_t, stats, tokens, levels, fars, far_bits, pieces
    )
    line.enter(query_first)
    backs = [exchange(piece, "seq", d) for d, piece in enumerate(away, 2)]
    line.meet(rows)
    line.meet(rows)
    line.turn(query_second)
    dkey, dvalue, dkv_t = step(
        close_keys, dkv, [line.into[2], *backs], far_bits, local_levels
    )
    key_first = step(weight_terms, dkv_t, tokens, inner, 0, 0, pieces)
    line.meet(rows)
    line.turn(key_first)
    line.meet(rows)
    parts = step(project_split, rank, [attended], [w_out], "head")
    mixed = Scatter(parts, "head", step)
    key_second = step(weight_terms, dkv_t, tokens, inner, 0, 1, pieces)
    value_first = step(weight_terms, dkv_t, tokens, inner, 1, 0, pieces)
    value_second = step(weight_terms, dkv_t, tokens, inner, 1, 1, pieces)
    keep, send = step(project_split, rank, [dquery, dkey, dvalue], [w_query, w_key, w_value], "head")
    line.turn(key_second)
    line.meet(rows)
    line.turn(value_first)
    tokens_grad = Scatter([keep, step(relay, send)], "head", step)
    mixed.advance()
    line.meet(rows)
    line.turn(value_second)
    tokens_grad.advance()
    line.meet(rows)
    out_grad = line.output(0, pieces)
    line.leave()
    line.meet(rows)
    query_grad = line.output(2, pieces)
    line.leave()
    mixed = mixed.result()
    key_grad = line.output(4, pieces)
    line.leave()
    tokens_grad = tokens_grad.result()
    value_grad = line.output(6, pieces)
    return mixed, tokens_grad, query_grad, key_grad, value_grad, out_grad


def solution(mesh):
    return jax.shard_map(
        per_device,
        mesh=mesh,
        in_specs=(
            P(("groups", "seq"), None),
            P(None, "head"),
            P(None, "head"),
            P(None, "head"),
            P(None, "head"),
            P(("groups", "seq"), None),
        ),
        out_specs=(
            P(("groups", "seq"), "head"),
            P(("groups", "seq"), "head"),
            P("groups", "head"),
            P("groups", "head"),
            P("groups", "head"),
            P("groups", "head"),
        ),
        check_vma=False,
    )
```

```python
import functools
import math

import jax
import jax.numpy as jnp
from jax import lax
from jax.experimental import pallas as pl
from jax.experimental.pallas import tpu as pltpu
from jax.sharding import PartitionSpec as P

HEAD_DIM = 128
BLOCK = 128
BF16 = jnp.bfloat16
F32 = jnp.float32
MIB = 1024 * 1024

NN = (((1,), (0,)), ((), ()))
NT = (((1,), (1,)), ((), ()))
TN = (((0,), (0,)), ((), ()))


def dot(left, right, dims=NN):
    return lax.dot_general(left, right, dims, preferred_element_type=F32)


def params(mib):
    return pltpu.CompilerParams(vmem_limit_bytes=mib * MIB)


def cost(microseconds):
    return pl.CostEstimate(flops=int(microseconds * 1150e6) + 1, bytes_accessed=1, transcendentals=0)


def run(body, ready, after=(), in_specs=None, **options):
    count, extra = len(ready), len(after)

    def kernel(*refs):
        body(*refs[:count], *refs[count + extra :])

    in_specs = in_specs or [pl.BlockSpec(memory_space=pltpu.VMEM)] * count
    in_specs = in_specs + [pl.BlockSpec(memory_space=pl.ANY)] * extra
    return pl.pallas_call(kernel, in_specs=in_specs, **options)(*ready, *after)


def shape(rows, cols, dtype=BF16):
    return jax.ShapeDtypeStruct((rows, cols), dtype)


def whole(rows, cols):
    return pl.BlockSpec((rows, cols), lambda *_: (0, 0))


def pool_matrix(rows):
    row = lax.broadcasted_iota(jnp.int32, (rows // 2, rows), 0)
    col = lax.broadcasted_iota(jnp.int32, (rows // 2, rows), 1)
    return jnp.where(jnp.right_shift(col, 1) == row, 0.5, 0.0).astype(BF16)


def spread_matrix(rows, step_bits, offset, cols, weight):
    row = lax.broadcasted_iota(jnp.int32, (rows, cols), 0) + offset
    col = lax.broadcasted_iota(jnp.int32, (rows, cols), 1)
    return jnp.where(jnp.right_shift(row, step_bits) == col, weight, 0.0).astype(BF16)


def key_value_body(local_levels, far_levels, parts, tok_hbm, wk_hbm, wv_hbm, *refs):
    out_hbm = refs[:local_levels]
    far = refs[local_levels : local_levels + far_levels]
    refs = refs[local_levels + far_levels :]
    tok_ref, wk_ref, wv_ref = refs[:3]
    levels = refs[3 : 3 + local_levels]
    in_sems, out_sems = refs[3 + local_levels :]
    part = tok_ref.shape[0] // parts

    def fetch(source, target, i):
        copy = pltpu.make_async_copy(source, target, in_sems.at[i])
        copy.start()
        return copy

    def flush(i):
        copy = pltpu.make_async_copy(levels[i], out_hbm[i], out_sems.at[i])
        copy.start()
        return copy

    weights = [fetch(wk_hbm, wk_ref, 0), fetch(wv_hbm, wv_ref, 1)]
    tiles = []
    for p in range(parts):
        rows = pl.ds(p * part, part)
        tiles.append(fetch(tok_hbm.at[rows], tok_ref.at[rows], 2 + p))
    for copy in weights:
        copy.wait()
    for p in range(parts):
        tiles[p].wait()
        here = slice(p * part, (p + 1) * part)
        x = tok_ref[here, :]
        both = jnp.concatenate([dot(x, wk_ref[...]), dot(x, wv_ref[...])], axis=1)
        levels[0][here, :] = both.astype(BF16)
    flushes = [flush(0)]
    pool = pool_matrix(part)
    for i in range(1, local_levels):
        source = levels[i - 1]
        for low in range(0, source.shape[0], part):
            mean = dot(pool, source[low : low + part, :])
            levels[i][low // 2 : (low + part) // 2, :] = mean.astype(BF16)
        flushes.append(flush(i))
    rows = dot(pool, levels[-1][...]).astype(BF16)
    for i in range(far_levels):
        if i:
            rows = dot(pool_matrix(rows.shape[0]), rows).astype(BF16)
        far[i][...] = rows
    for copy in flushes:
        copy.wait()


def key_value(tokens, w_key, w_value, local_levels, far_levels, after):
    tok_rows, width = tokens.shape
    inner = w_key.shape[1]
    parts = tok_rows // (2 * BLOCK)
    held = [(tok_rows >> i, 2 * inner) for i in range(local_levels)]
    tops = [(BLOCK >> i, 2 * inner) for i in range(far_levels)]
    return run(
        functools.partial(key_value_body, local_levels, far_levels, parts),
        [tokens, w_key, w_value],
        after,
        in_specs=[pl.BlockSpec(memory_space=pl.ANY)] * 3,
        out_specs=[pl.BlockSpec(memory_space=pl.ANY)] * len(held)
        + [pl.BlockSpec(memory_space=pltpu.VMEM)] * len(tops),
        out_shape=[shape(*dims) for dims in held + tops],
        scratch_shapes=[pltpu.VMEM((tok_rows, width), BF16)]
        + [pltpu.VMEM((width, inner), BF16)] * 2
        + [pltpu.VMEM(dims, BF16) for dims in held]
        + [pltpu.SemaphoreType.DMA((parts + 2,)), pltpu.SemaphoreType.DMA((len(held),))],
        compiler_params=params(56),
        cost_estimate=cost(5.0),
    )


def project_body(left_ref, weight_ref, out_ref):
    out_ref[...] = dot(left_ref[...], weight_ref[...]).astype(BF16)


def project(left, weight, after):
    tok_rows, width = left.shape
    inner = weight.shape[1]
    return run(
        project_body,
        [left, weight],
        after,
        out_shape=shape(tok_rows, inner),
        compiler_params=params(4),
        cost_estimate=cost(0.7),
    )


class KeySet:
    def __init__(self, far_rows, far_bits, local_levels):
        mids = local_levels - 1
        self.sizes = [2 * BLOCK] + [BLOCK] * mids + list(far_rows)
        self.bounds = [sum(self.sizes[:i]) for i in range(len(self.sizes) + 1)]
        steps = [0] + list(range(1, local_levels)) + [local_levels + b for b in far_bits]
        self.biases = [float(step) for step in steps]
        self.mids = mids
        self.far_start = self.bounds[1 + mids]
        self.factor = math.log2(math.e) / math.sqrt(HEAD_DIM)

    def here(self, m):
        return pl.ds(pl.multiple_of(m * 2 * BLOCK, 2 * BLOCK), 2 * BLOCK)

    def seats(self, m):
        for i in range(self.mids):
            sibling = jnp.bitwise_xor(jnp.right_shift(m, i), 1)
            yield pl.ds(pl.multiple_of(sibling * BLOCK, BLOCK), BLOCK)

    def near(self, m, level_refs, cols):
        rows = [level_refs[0][self.here(m), cols]]
        rows += [ref[seat, cols] for ref, seat in zip(level_refs[1:], self.seats(m))]
        return rows

    def far(self, far_refs, cols):
        return [ref[:, cols] for ref in far_refs]

    def pieces(self, array, first=0, count=None):
        base = self.bounds[first]
        ends = self.bounds[first:] if count is None else self.bounds[first : first + count + 1]
        return [array[a - base : b - base] for a, b in zip(ends, ends[1:])]

    def top(self, pieces, first=0):
        tops = [
            jnp.max(piece, axis=0, keepdims=True) * self.factor + bias
            for piece, bias in zip(pieces, self.biases[first:])
        ]
        return functools.reduce(jnp.maximum, tops)

    def powers(self, pieces, top, first=0):
        return jnp.concatenate(
            [
                jnp.exp2(piece * self.factor + (bias - top))
                for piece, bias in zip(pieces, self.biases[first:])
            ],
            axis=0,
        )


def head_columns(h, inner):
    low = h * HEAD_DIM
    return slice(low, low + HEAD_DIM), slice(inner + low, inner + low + HEAD_DIM)


def near_body(local_levels, q_ref, *refs):
    level_refs = refs[:local_levels]
    power_ref, stat_ref = refs[local_levels:]
    tok_rows, inner = q_ref.shape
    heads = inner // HEAD_DIM
    keyset = KeySet([], [], local_levels)
    rows = keyset.far_start

    def step(m, carry):
        here = keyset.here(m)
        for h in range(heads):
            cols, _ = head_columns(h, inner)
            keys = jnp.concatenate(keyset.near(m, level_refs, cols), axis=0)
            pieces = keyset.pieces(dot(keys, q_ref[here, cols], NT))
            top = keyset.top(pieces)
            powers = keyset.powers(pieces, top)
            stat_ref[h : h + 1, here] = top
            stat_ref[heads + h : heads + h + 1, here] = jnp.sum(powers, axis=0, keepdims=True)
            power_ref[pl.ds(pl.multiple_of((m * heads + h) * rows, rows), rows), :] = powers
        return carry

    lax.fori_loop(0, tok_rows // (2 * BLOCK), step, 0)


def near_powers(query, levels, after):
    tok_rows, inner = query.shape
    heads = inner // HEAD_DIM
    pairs = tok_rows // (2 * BLOCK)
    rows = (len(levels) + 1) * BLOCK
    return run(
        functools.partial(near_body, len(levels)),
        [query, *levels],
        after,
        out_shape=[shape(pairs * heads * rows, 2 * BLOCK, F32), shape(2 * heads, tok_rows, F32)],
        compiler_params=params(6),
        cost_estimate=cost(2.3),
    )


def forward_body(local_levels, far_bits, *refs):
    fars = len(far_bits)
    q_ref, power_ref, near_ref = refs[:3]
    level_refs = refs[3 : 3 + local_levels]
    far_refs = refs[3 + local_levels : 3 + local_levels + fars]
    att_ref, att_t_ref, stat_ref = refs[3 + local_levels + fars :]
    tok_rows, inner = q_ref.shape
    heads = inner // HEAD_DIM
    keyset = KeySet([r.shape[0] for r in far_refs], far_bits, local_levels)
    rows = keyset.far_start

    def step(m, carry):
        here = keyset.here(m)
        for h in range(heads):
            cols, vcols = head_columns(h, inner)
            second = heads + h
            keys = jnp.concatenate(keyset.far(far_refs, cols), axis=0)
            values = keyset.near(m, level_refs, vcols) + keyset.far(far_refs, vcols)
            values = jnp.concatenate(values, axis=0)
            first = local_levels
            pieces = keyset.pieces(dot(keys, q_ref[here, cols], NT), first)
            near_top = near_ref[h : h + 1, here]
            top = jnp.maximum(near_top, keyset.top(pieces, first))
            shrink = jnp.exp2(near_top - top)
            powers = keyset.powers(pieces, top, first)
            total = near_ref[second : second + 1, here] * shrink
            total = total + jnp.sum(powers, axis=0, keepdims=True)
            inverse = 1.0 / total
            place = pl.ds(pl.multiple_of((m * heads + h) * rows, rows), rows)
            near_probs = (power_ref[place, :] * (shrink * inverse)).astype(BF16)
            far_probs = (powers * inverse).astype(BF16)
            probs_b = jnp.concatenate([near_probs, far_probs], axis=0)
            att_t = dot(values, probs_b, TN).astype(BF16)
            att_t_ref[cols, here] = att_t
            att_ref[here, cols] = att_t.T
            stat_ref[h : h + 1, here] = top
            stat_ref[second : second + 1, here] = inverse
        return carry

    lax.fori_loop(0, tok_rows // (2 * BLOCK), step, 0)


def forward(query, powers, near, levels, fars, far_bits, after):
    tok_rows, inner = query.shape
    heads = inner // HEAD_DIM
    set_rows = (len(levels) + 1) * BLOCK + sum(f.shape[0] for f in fars)
    return run(
        functools.partial(forward_body, len(levels), far_bits),
        [query, powers, near, *levels, *fars],
        after,
        out_shape=[
            shape(tok_rows, inner),
            shape(inner, tok_rows),
            shape(2 * heads, tok_rows, F32),
        ],
        compiler_params=params(6),
        cost_estimate=cost(4.0),
    )


def backward_body(local_levels, far_bits, pieces, *refs):
    mids = local_levels - 1
    fars = len(far_bits)
    q_ref, g_ref, att_t_ref, stat_ref, tok_ref = refs[:5]
    level_refs = refs[5 : 5 + local_levels]
    far_refs = refs[5 + local_levels : 5 + local_levels + fars]
    outs = refs[5 + local_levels + fars :]
    dq_ref, dkv_ref = outs[:2]
    term_refs = outs[2 : 2 + pieces]
    dfar_refs = outs[2 + pieces : 1 + pieces + fars]
    dmid_refs = outs[1 + pieces + fars : 1 + pieces + fars + mids]
    dq_t_ref, acc_ref = outs[-2:]
    tok_rows, inner = q_ref.shape
    heads = inner // HEAD_DIM
    score_scale = 1.0 / math.sqrt(HEAD_DIM)
    keyset = KeySet([r.shape[0] for r in far_refs], far_bits, local_levels)

    for ref in (*dmid_refs, acc_ref):
        ref[...] = jnp.zeros_like(ref)

    def step(m, carry):
        here = keyset.here(m)
        for h in range(heads):
            cols, vcols = head_columns(h, inner)
            keys, values = (
                jnp.concatenate(keyset.near(m, level_refs, c) + keyset.far(far_refs, c), axis=0)
                for c in (cols, vcols)
            )
            q = q_ref[here, cols]
            g = g_ref[here, cols]
            top = stat_ref[h : h + 1, here]
            inverse = stat_ref[heads + h : heads + h + 1, here]
            probs = keyset.powers(keyset.pieces(dot(keys, q, NT)), top) * inverse
            att_t = att_t_ref[cols, here].astype(F32)
            delta = jnp.sum(g.T.astype(F32) * att_t, axis=0, keepdims=True)
            grads = (probs * (dot(values, g, NT) - delta) * score_scale).astype(BF16)
            dq_t = dot(keys, grads, TN).astype(BF16)
            dq_t_ref[cols, here] = dq_t
            dq_ref[here, cols] = dq_t.T
            for part, place in ((dot(grads, q), cols), (dot(probs.astype(BF16), g), vcols)):
                own, *sides = keyset.pieces(part)
                dkv_ref[here, place] = own
                for ref, seat, side in zip(dmid_refs, keyset.seats(m), sides):
                    ref[seat, place] += side
                acc_ref[:, place] += part[keyset.far_start :]
        return carry

    lax.fori_loop(0, tok_rows // (2 * BLOCK), step, 0)
    width = term_refs[-1].shape[0]
    first = acc_ref[:BLOCK].astype(BF16)
    term_refs[0][width : width + BLOCK, :] = first[:, :inner]
    term_refs[0][width + BLOCK :, :] = first[:, inner:]
    low = BLOCK
    for ref in dfar_refs:
        ref[...] = acc_ref[low : low + ref.shape[0]].astype(BF16)
        low += ref.shape[0]
    for i, ref in enumerate(term_refs):
        part = dot(dq_t_ref[...], tok_ref[:, i * width : (i + 1) * width])
        ref[:width, :] = part.astype(BF16).T
    fan = spread_matrix(2 * BLOCK, 1, 0, BLOCK, 0.5)
    targets = (dkv_ref, *dmid_refs)
    for i in reversed(range(mids)):
        for t in range(dmid_refs[i].shape[0] // BLOCK):
            part = dmid_refs[i][t * BLOCK : (t + 1) * BLOCK, :]
            high = part.astype(BF16)
            low = (part - high.astype(F32)).astype(BF16)
            rows = slice(2 * t * BLOCK, 2 * (t + 1) * BLOCK)
            targets[i][rows, :] += dot(fan, high) + dot(fan, low)


def backward(query, grad, attended_t, stats, tokens, levels, fars, far_bits, pieces, after):
    tok_rows, inner = query.shape
    far_rows = sum(f.shape[0] for f in fars)
    set_rows = (len(levels) + 1) * BLOCK + far_rows
    return run(
        functools.partial(backward_body, len(levels), far_bits, pieces),
        [query, grad, attended_t, stats, tokens, *levels, *fars],
        after,
        out_shape=[shape(tok_rows, inner), shape(tok_rows, 2 * inner, F32)]
        + [shape(tokens.shape[1] // pieces + 2 * BLOCK, inner)]
        + [shape(tokens.shape[1] // pieces, inner)] * (pieces - 1)
        + [shape(*f.shape) for f in fars[1:]],
        scratch_shapes=[pltpu.VMEM(level.shape, F32) for level in levels[1:]]
        + [pltpu.VMEM((inner, tok_rows), BF16), pltpu.VMEM((far_rows, 2 * inner), F32)],
        compiler_params=params(10),
        cost_estimate=cost(8.0),
    )


def term_body(which, low, left_ref, right_ref, out_ref):
    width, inner = out_ref.shape
    left = left_ref[which * inner : (which + 1) * inner, :]
    out_ref[...] = dot(left, right_ref[:, low : low + width]).astype(BF16).T


def weight_terms(left_t, right, inner, which, part, parts, after):
    tok_rows = left_t.shape[1]
    width = right.shape[1] // parts
    return run(
        functools.partial(term_body, which, part * width),
        [left_t, right],
        after,
        out_shape=shape(width, inner),
        compiler_params=params(3),
        cost_estimate=cost(0.2),
    )


def close_body(local_levels, far_bits, dkv_ref, *refs):
    joined_ref, *back_refs = refs[: len(far_bits)]
    dk_ref, dv_ref, dkv_t_ref = refs[len(far_bits) :]
    inner = dk_ref.shape[1]
    tile = 2 * BLOCK
    low = joined_ref.shape[0] - 2 * BLOCK
    joined = [joined_ref[low : low + BLOCK, :], joined_ref[low + BLOCK :, :]]
    backs = [jnp.concatenate(joined, axis=1)] + [ref[...] for ref in back_refs]
    for t in range(dkv_ref.shape[0] // tile):
        here = slice(t * tile, (t + 1) * tile)
        total = dkv_ref[here, :]
        for back, bit in zip(backs, far_bits):
            weight = 0.5 ** (local_levels + bit)
            fan = spread_matrix(tile, local_levels + bit, t * tile, back.shape[0], weight)
            total = total + dot(fan, back)
        final = total.astype(BF16)
        dk_ref[here, :] = final[:, :inner]
        dv_ref[here, :] = final[:, inner:]
        dkv_t_ref[:, here] = final.T


def close_keys(dkv, backs, far_bits, local_levels, after):
    tok_rows, double = dkv.shape
    inner = double // 2
    return run(
        functools.partial(close_body, local_levels, far_bits),
        [dkv, *backs],
        after,
        out_shape=[shape(tok_rows, inner), shape(tok_rows, inner), shape(double, tok_rows)],
        compiler_params=params(5),
        cost_estimate=cost(0.2),
    )


def split_body(count, parts, rank_ref, *refs):
    lefts, weights = refs[:count], refs[count : 2 * count]
    outs = refs[2 * count :]
    width = weights[0].shape[0] // parts
    for r in range(parts):
        owner = jnp.bitwise_xor(rank_ref[0], r)
        rows = pl.ds(pl.multiple_of(owner * width, width), width)
        total = None
        for left, weight in zip(lefts, weights):
            product = dot(left[...], weight[rows, :], NT)
            total = product if total is None else total + product
        place = r // 2 * width
        outs[r % 2][:, place : place + width] = total.astype(BF16)


def project_split(rank, lefts, weights, axis, after):
    count = len(lefts)
    parts = lax.axis_size(axis)
    tok_rows, inner = lefts[0].shape
    width = weights[0].shape[0]
    return run(
        functools.partial(split_body, count, parts),
        [rank, *lefts, *weights],
        after,
        in_specs=[pl.BlockSpec(memory_space=pltpu.SMEM)]
        + [pl.BlockSpec(memory_space=pltpu.VMEM)] * (2 * count),
        out_shape=[shape(tok_rows, width // 2)] * 2,
        compiler_params=params(5),
        cost_estimate=cost(1.0),
    )


def exchange(block, axis, distance):
    count = lax.axis_size(axis)
    return lax.ppermute(block, axis, [(i, i ^ distance) for i in range(count)])


def add(left, right):
    return (left.astype(F32) + right.astype(F32)).astype(BF16)


def term_half_body(chunk_ref, into_ref, out_ref):
    rows = slice(0, out_ref.shape[0])
    out_ref[...] = (chunk_ref[rows, :].astype(F32) + into_ref[rows, :].astype(F32)).astype(BF16)


def half_sum(chunk, into, rows, after):
    return run(
        term_half_body,
        [chunk, into],
        after,
        out_shape=shape(rows, chunk.shape[1]),
        compiler_params=params(3),
        cost_estimate=cost(3),
    )


def scatter_body(pieces, keep_ref, into_ref, even_ref, odd_ref):
    width = keep_ref.shape[1] // pieces
    for i in range(pieces):
        here = slice(i * width, (i + 1) * width)
        place = slice(i // 2 * width, (i // 2 + 1) * width)
        total = keep_ref[:, here].astype(F32) + into_ref[:, here].astype(F32)
        (even_ref, odd_ref)[i % 2][:, place] = total.astype(BF16)


def last_body(left_ref, right_ref, token_ref, out_ref):
    token_ref[...] = jnp.zeros_like(token_ref)
    out_ref[...] = (left_ref[...].astype(F32) + right_ref[...].astype(F32)).astype(BF16)


def last_sum(left, right, after):
    return run(
        last_body,
        [left, right],
        after,
        out_shape=[shape(8, 128, F32), shape(*left.shape)],
        compiler_params=params(3),
        cost_estimate=cost(0.9),
    )


def scatter_step(keep, into, pieces, after):
    rows, width = keep.shape
    return run(
        functools.partial(scatter_body, pieces),
        [keep, into],
        after,
        out_shape=[shape(rows, width // 2)] * 2,
        compiler_params=params(4),
        cost_estimate=cost(0.2),
    )


def turn_body(end_ref, half_ref, across_ref, chunk_ref, total_ref, send_ref):
    total = (half_ref[...].astype(F32) + across_ref[...].astype(F32)).astype(BF16)
    total_ref[...] = total

    @pl.when(end_ref[0] == 1)
    def _():
        send_ref[...] = chunk_ref[...]

    @pl.when(end_ref[0] == 0)
    def _():
        send_ref[...] = total


def turn(end, half, across, chunk, after):
    return run(
        turn_body,
        [end, half, across, chunk],
        after,
        in_specs=[pl.BlockSpec(memory_space=pltpu.SMEM)]
        + [pl.BlockSpec(memory_space=pltpu.VMEM)] * 3,
        out_shape=[shape(*half.shape)] * 2,
        compiler_params=params(2),
        cost_estimate=cost(3),
    )


def output_body(count, end_ref, *refs):
    totals, ends, (token_ref, out_ref) = refs[:count], refs[count : 2 * count], refs[2 * count :]
    token_ref[...] = jnp.zeros_like(token_ref)
    rows = totals[0].shape[0]

    for flag, sources in ((0, totals), (1, ends)):

        @pl.when(end_ref[0] == flag)
        def _():
            for i, ref in enumerate(sources):
                out_ref[i * rows : (i + 1) * rows, :] = ref[...]


def output(end, totals, ends, after):
    count = len(totals)
    rows, width = totals[0].shape
    return run(
        functools.partial(output_body, count),
        [end, *totals, *ends],
        after,
        in_specs=[pl.BlockSpec(memory_space=pltpu.SMEM)]
        + [pl.BlockSpec(memory_space=pltpu.VMEM)] * (2 * count),
        out_shape=[shape(8, 128, F32), shape(count * rows, width)],
        compiler_params=params(4),
        cost_estimate=cost(0.9),
    )


def relay_body(source_ref, target_ref):
    target_ref[...] = source_ref[...]


def relay(block, after):
    return run(
        relay_body,
        [block],
        after,
        out_shape=shape(*block.shape),
        compiler_params=params(3),
        cost_estimate=cost(0.2),
    )


class Line:
    lag = 3

    def __init__(self, axis, other, end, step):
        self.axis, self.axes, self.step = axis, (axis, other), step
        self.count = lax.axis_size(axis)
        self.end = end
        width = lax.axis_size(other)
        self.across = []
        for place in range(self.count):
            for seat in range(width):
                target = (place, seat ^ 1 if width > 1 else seat)
                if place & 3 in (1, 2):
                    target = (place ^ 3, seat)
                self.across.append((place * width + seat, target[0] * width + target[1]))
        self.chunks, self.into, self.halves, self.crossed, self.totals = [], [], [], [], []

    def enter(self, chunk):
        self.chunks.append(chunk)
        self.into.append(exchange(chunk, self.axis, 1))

    def meet(self, rows):
        k = len(self.halves)
        half = self.step(half_sum, self.chunks[k], self.into[k], rows)
        self.halves.append(half)
        self.crossed.append(lax.ppermute(half, self.axes, self.across))

    def turn(self, chunk):
        old = len(self.totals)
        total, send = self.step(turn, self.end, self.halves[old], self.crossed[old], chunk)
        self.totals.append(total)
        self.chunks.append(chunk)
        self.into.append(exchange(send, self.axis, 1))

    def leave(self):
        old = len(self.totals)
        half = self.halves[old]
        total = self.step(half_sum, half, self.crossed[old], half.shape[0])
        self.totals.append(total)
        self.into.append(exchange(total, self.axis, 1))

    def output(self, first, count):
        ends = self.into[first + self.lag : first + self.lag + count]
        _, result = self.step(output, self.end, self.totals[first : first + count], ends)
        distance = 4
        while distance < self.count:
            result = add(result, exchange(result, self.axis, distance))
            distance *= 2
        return result


class Scatter:
    def __init__(self, parts, axis, step):
        self.axis, self.step = axis, step
        self.pieces = lax.axis_size(axis) // 2
        self.keep, send = parts
        self.distance = 1
        self.into = exchange(send, axis, 1)

    def advance(self):
        while self.pieces > 1:
            self.keep, send = self.step(scatter_step, self.keep, self.into, self.pieces)
            self.distance *= 2
            self.pieces //= 2
            self.into = exchange(send, self.axis, self.distance)

    def result(self):
        return self.step(last_sum, self.keep, self.into)[1]


def per_device(tokens, w_query, w_key, w_value, w_out, cotangent):
    tok_rows = tokens.shape[0]
    inner = w_query.shape[1]
    local_levels = (tok_rows // BLOCK).bit_length() - 1
    count = lax.axis_size("seq")
    far_levels = count.bit_length() - 1
    far_bits = [d.bit_length() - 1 for d in range(1, count)]

    last = []

    def step(kernel, *operands):
        made = kernel(*operands, list(last))
        last[:] = made[:1] if isinstance(made, (list, tuple)) else [made]
        return made

    place = jnp.bitwise_and(lax.axis_index("seq"), 3)
    end = jnp.reshape((place == 0) | (place == 3), (1,)).astype(jnp.int32)
    rank = jnp.reshape(lax.axis_index("head"), (1,)).astype(jnp.int32)
    parts = key_value(tokens, w_key, w_value, local_levels, far_levels, [end, rank])
    levels, tops = parts[:local_levels], parts[local_levels:]
    fars = [exchange(tops[bit], "seq", d) for d, bit in enumerate(far_bits, 1)]
    query = step(project, tokens, w_query)
    powers, near = step(near_powers, query, levels)
    grad = step(project, cotangent, w_out)
    attended, attended_t, stats = step(forward, query, powers, near, levels, fars, far_bits)

    line = Line("seq", "head", end, step)
    pieces = 2
    rows = tokens.shape[1] // pieces
    line.enter(step(weight_terms, attended_t, cotangent, inner, 0, 0, pieces))
    line.enter(step(weight_terms, attended_t, cotangent, inner, 0, 1, pieces))
    dquery, dkv, query_first, query_second, *away = step(
        backward, query, grad, attended_t, stats, tokens, levels, fars, far_bits, pieces
    )
    line.enter(query_first)
    backs = [exchange(piece, "seq", d) for d, piece in enumerate(away, 2)]
    line.meet(rows)
    line.meet(rows)
    line.turn(query_second)
    dkey, dvalue, dkv_t = step(
        close_keys, dkv, [line.into[2], *backs], far_bits, local_levels
    )
    key_first = step(weight_terms, dkv_t, tokens, inner, 0, 0, pieces)
    line.meet(rows)
    parts = step(project_split, rank, [attended], [w_out], "head")
    mixed = Scatter(parts, "head", step)
    line.turn(key_first)
    line.meet(rows)
    key_second = step(weight_terms, dkv_t, tokens, inner, 0, 1, pieces)
    line.turn(key_second)
    value_first = step(weight_terms, dkv_t, tokens, inner, 1, 0, pieces)
    keep, send = step(project_split, rank, [dquery, dkey, dvalue], [w_query, w_key, w_value], "head")
    line.meet(rows)
    tokens_grad = Scatter([keep, step(relay, send)], "head", step)
    line.turn(value_first)
    mixed.advance()
    value_second = step(weight_terms, dkv_t, tokens, inner, 1, 1, pieces)
    line.meet(rows)
    line.turn(value_second)
    out_grad = line.output(0, pieces)
    line.meet(rows)
    mixed = mixed.result()
    line.leave()
    tokens_grad.advance()
    line.meet(rows)
    query_grad = line.output(2, pieces)
    line.leave()
    key_grad = line.output(4, pieces)
    tokens_grad = tokens_grad.result()
    line.leave()
    value_grad = line.output(6, pieces)
    return mixed, tokens_grad, query_grad, key_grad, value_grad, out_grad


def solution(mesh):
    return jax.shard_map(
        per_device,
        mesh=mesh,
        in_specs=(
            P(("groups", "seq"), None),
            P(None, "head"),
            P(None, "head"),
            P(None, "head"),
            P(None, "head"),
            P(("groups", "seq"), None),
        ),
        out_specs=(
            P(("groups", "seq"), "head"),
            P(("groups", "seq"), "head"),
            P("groups", "head"),
            P("groups", "head"),
            P("groups", "head"),
            P("groups", "head"),
        ),
        check_vma=False,
    )
```

```python
import functools
import math

import jax
import jax.numpy as jnp
from jax import lax
from jax.experimental import pallas as pl
from jax.experimental.pallas import tpu as pltpu
from jax.sharding import PartitionSpec as P

HEAD_DIM = 128
BLOCK = 128
BF16 = jnp.bfloat16
F32 = jnp.float32
MIB = 1024 * 1024

NN = (((1,), (0,)), ((), ()))
NT = (((1,), (1,)), ((), ()))
TN = (((0,), (0,)), ((), ()))


def dot(left, right, dims=NN):
    return lax.dot_general(left, right, dims, preferred_element_type=F32)


def params(mib):
    return pltpu.CompilerParams(vmem_limit_bytes=mib * MIB)


def cost(microseconds):
    return pl.CostEstimate(flops=int(microseconds * 1150e6) + 1, bytes_accessed=1, transcendentals=0)


def run(body, ready, after=(), in_specs=None, **options):
    count, extra = len(ready), len(after)

    def kernel(*refs):
        body(*refs[:count], *refs[count + extra :])

    in_specs = in_specs or [pl.BlockSpec(memory_space=pltpu.VMEM)] * count
    in_specs = in_specs + [pl.BlockSpec(memory_space=pl.ANY)] * extra
    return pl.pallas_call(kernel, in_specs=in_specs, **options)(*ready, *after)


def shape(rows, cols, dtype=BF16):
    return jax.ShapeDtypeStruct((rows, cols), dtype)


def whole(rows, cols):
    return pl.BlockSpec((rows, cols), lambda *_: (0, 0))


def pool_matrix(rows):
    row = lax.broadcasted_iota(jnp.int32, (rows // 2, rows), 0)
    col = lax.broadcasted_iota(jnp.int32, (rows // 2, rows), 1)
    return jnp.where(jnp.right_shift(col, 1) == row, 0.5, 0.0).astype(BF16)


def spread_matrix(rows, step_bits, offset, cols, weight):
    row = lax.broadcasted_iota(jnp.int32, (rows, cols), 0) + offset
    col = lax.broadcasted_iota(jnp.int32, (rows, cols), 1)
    return jnp.where(jnp.right_shift(row, step_bits) == col, weight, 0.0).astype(BF16)


def key_value_body(local_levels, far_levels, parts, tok_hbm, wk_hbm, wv_hbm, *refs):
    out_hbm = refs[:local_levels]
    far = refs[local_levels : local_levels + far_levels]
    refs = refs[local_levels + far_levels :]
    tok_ref, wk_ref, wv_ref = refs[:3]
    levels = refs[3 : 3 + local_levels]
    in_sems, out_sems = refs[3 + local_levels :]
    part = tok_ref.shape[0] // parts

    def fetch(source, target, i):
        copy = pltpu.make_async_copy(source, target, in_sems.at[i])
        copy.start()
        return copy

    def flush(i):
        copy = pltpu.make_async_copy(levels[i], out_hbm[i], out_sems.at[i])
        copy.start()
        return copy

    weights = [fetch(wk_hbm, wk_ref, 0), fetch(wv_hbm, wv_ref, 1)]
    tiles = []
    for p in range(parts):
        rows = pl.ds(p * part, part)
        tiles.append(fetch(tok_hbm.at[rows], tok_ref.at[rows], 2 + p))
    for copy in weights:
        copy.wait()
    for p in range(parts):
        tiles[p].wait()
        here = slice(p * part, (p + 1) * part)
        x = tok_ref[here, :]
        both = jnp.concatenate([dot(x, wk_ref[...]), dot(x, wv_ref[...])], axis=1)
        levels[0][here, :] = both.astype(BF16)
    flushes = [flush(0)]
    pool = pool_matrix(part)
    for i in range(1, local_levels):
        source = levels[i - 1]
        for low in range(0, source.shape[0], part):
            mean = dot(pool, source[low : low + part, :])
            levels[i][low // 2 : (low + part) // 2, :] = mean.astype(BF16)
        flushes.append(flush(i))
    rows = dot(pool, levels[-1][...]).astype(BF16)
    for i in range(far_levels):
        if i:
            rows = dot(pool_matrix(rows.shape[0]), rows).astype(BF16)
        far[i][...] = rows
    for copy in flushes:
        copy.wait()


def key_value(tokens, w_key, w_value, local_levels, far_levels, after):
    tok_rows, width = tokens.shape
    inner = w_key.shape[1]
    parts = tok_rows // (2 * BLOCK)
    held = [(tok_rows >> i, 2 * inner) for i in range(local_levels)]
    tops = [(BLOCK >> i, 2 * inner) for i in range(far_levels)]
    return run(
        functools.partial(key_value_body, local_levels, far_levels, parts),
        [tokens, w_key, w_value],
        after,
        in_specs=[pl.BlockSpec(memory_space=pl.ANY)] * 3,
        out_specs=[pl.BlockSpec(memory_space=pl.ANY)] * len(held)
        + [pl.BlockSpec(memory_space=pltpu.VMEM)] * len(tops),
        out_shape=[shape(*dims) for dims in held + tops],
        scratch_shapes=[pltpu.VMEM((tok_rows, width), BF16)]
        + [pltpu.VMEM((width, inner), BF16)] * 2
        + [pltpu.VMEM(dims, BF16) for dims in held]
        + [pltpu.SemaphoreType.DMA((parts + 2,)), pltpu.SemaphoreType.DMA((len(held),))],
        compiler_params=params(56),
        cost_estimate=cost(5.0),
    )


def project_body(left_ref, weight_ref, out_ref):
    out_ref[...] = dot(left_ref[...], weight_ref[...]).astype(BF16)


def project(left, weight, after):
    tok_rows, width = left.shape
    inner = weight.shape[1]
    return run(
        project_body,
        [left, weight],
        after,
        out_shape=shape(tok_rows, inner),
        compiler_params=params(4),
        cost_estimate=cost(0.7),
    )


class KeySet:
    def __init__(self, far_rows, far_bits, local_levels):
        mids = local_levels - 1
        self.sizes = [2 * BLOCK] + [BLOCK] * mids + list(far_rows)
        self.bounds = [sum(self.sizes[:i]) for i in range(len(self.sizes) + 1)]
        steps = [0] + list(range(1, local_levels)) + [local_levels + b for b in far_bits]
        self.biases = [float(step) for step in steps]
        self.mids = mids
        self.far_start = self.bounds[1 + mids]
        self.factor = math.log2(math.e) / math.sqrt(HEAD_DIM)

    def here(self, m):
        return pl.ds(pl.multiple_of(m * 2 * BLOCK, 2 * BLOCK), 2 * BLOCK)

    def seats(self, m):
        for i in range(self.mids):
            sibling = jnp.bitwise_xor(jnp.right_shift(m, i), 1)
            yield pl.ds(pl.multiple_of(sibling * BLOCK, BLOCK), BLOCK)

    def near(self, m, level_refs, cols):
        rows = [level_refs[0][self.here(m), cols]]
        rows += [ref[seat, cols] for ref, seat in zip(level_refs[1:], self.seats(m))]
        return rows

    def far(self, far_refs, cols):
        return [ref[:, cols] for ref in far_refs]

    def pieces(self, array, first=0, count=None):
        base = self.bounds[first]
        ends = self.bounds[first:] if count is None else self.bounds[first : first + count + 1]
        return [array[a - base : b - base] for a, b in zip(ends, ends[1:])]

    def top(self, pieces, first=0):
        tops = [
            jnp.max(piece, axis=0, keepdims=True) * self.factor + bias
            for piece, bias in zip(pieces, self.biases[first:])
        ]
        return functools.reduce(jnp.maximum, tops)

    def powers(self, pieces, top, first=0):
        return jnp.concatenate(
            [
                jnp.exp2(piece * self.factor + (bias - top))
                for piece, bias in zip(pieces, self.biases[first:])
            ],
            axis=0,
        )


def head_columns(h, inner):
    low = h * HEAD_DIM
    return slice(low, low + HEAD_DIM), slice(inner + low, inner + low + HEAD_DIM)


def near_body(local_levels, q_ref, *refs):
    level_refs = refs[:local_levels]
    power_ref, stat_ref = refs[local_levels:]
    tok_rows, inner = q_ref.shape
    heads = inner // HEAD_DIM
    keyset = KeySet([], [], local_levels)
    rows = keyset.far_start

    def step(m, carry):
        here = keyset.here(m)
        for h in range(heads):
            cols, _ = head_columns(h, inner)
            keys = jnp.concatenate(keyset.near(m, level_refs, cols), axis=0)
            pieces = keyset.pieces(dot(keys, q_ref[here, cols], NT))
            top = keyset.top(pieces)
            powers = keyset.powers(pieces, top)
            stat_ref[h : h + 1, here] = top
            stat_ref[heads + h : heads + h + 1, here] = jnp.sum(powers, axis=0, keepdims=True)
            power_ref[pl.ds(pl.multiple_of((m * heads + h) * rows, rows), rows), :] = powers
        return carry

    lax.fori_loop(0, tok_rows // (2 * BLOCK), step, 0)


def near_powers(query, levels, after):
    tok_rows, inner = query.shape
    heads = inner // HEAD_DIM
    pairs = tok_rows // (2 * BLOCK)
    rows = (len(levels) + 1) * BLOCK
    return run(
        functools.partial(near_body, len(levels)),
        [query, *levels],
        after,
        out_shape=[shape(pairs * heads * rows, 2 * BLOCK, F32), shape(2 * heads, tok_rows, F32)],
        compiler_params=params(6),
        cost_estimate=cost(2.3),
    )


def forward_body(local_levels, far_bits, *refs):
    fars = len(far_bits)
    q_ref, power_ref, near_ref = refs[:3]
    level_refs = refs[3 : 3 + local_levels]
    far_refs = refs[3 + local_levels : 3 + local_levels + fars]
    att_ref, att_t_ref, stat_ref = refs[3 + local_levels + fars :]
    tok_rows, inner = q_ref.shape
    heads = inner // HEAD_DIM
    keyset = KeySet([r.shape[0] for r in far_refs], far_bits, local_levels)
    rows = keyset.far_start

    def step(m, carry):
        here = keyset.here(m)
        for h in range(heads):
            cols, vcols = head_columns(h, inner)
            second = heads + h
            keys = jnp.concatenate(keyset.far(far_refs, cols), axis=0)
            values = keyset.near(m, level_refs, vcols) + keyset.far(far_refs, vcols)
            values = jnp.concatenate(values, axis=0)
            first = local_levels
            pieces = keyset.pieces(dot(keys, q_ref[here, cols], NT), first)
            near_top = near_ref[h : h + 1, here]
            top = jnp.maximum(near_top, keyset.top(pieces, first))
            shrink = jnp.exp2(near_top - top)
            powers = keyset.powers(pieces, top, first)
            total = near_ref[second : second + 1, here] * shrink
            total = total + jnp.sum(powers, axis=0, keepdims=True)
            inverse = 1.0 / total
            place = pl.ds(pl.multiple_of((m * heads + h) * rows, rows), rows)
            near_probs = (power_ref[place, :] * (shrink * inverse)).astype(BF16)
            far_probs = (powers * inverse).astype(BF16)
            probs_b = jnp.concatenate([near_probs, far_probs], axis=0)
            att_t = dot(values, probs_b, TN).astype(BF16)
            att_t_ref[cols, here] = att_t
            att_ref[here, cols] = att_t.T
            stat_ref[h : h + 1, here] = top
            stat_ref[second : second + 1, here] = inverse
        return carry

    lax.fori_loop(0, tok_rows // (2 * BLOCK), step, 0)


def forward(query, powers, near, levels, fars, far_bits, after):
    tok_rows, inner = query.shape
    heads = inner // HEAD_DIM
    set_rows = (len(levels) + 1) * BLOCK + sum(f.shape[0] for f in fars)
    return run(
        functools.partial(forward_body, len(levels), far_bits),
        [query, powers, near, *levels, *fars],
        after,
        out_shape=[
            shape(tok_rows, inner),
            shape(inner, tok_rows),
            shape(2 * heads, tok_rows, F32),
        ],
        compiler_params=params(6),
        cost_estimate=cost(4.0),
    )


def backward_body(local_levels, far_bits, pieces, *refs):
    mids = local_levels - 1
    fars = len(far_bits)
    q_ref, g_ref, att_t_ref, stat_ref, tok_ref = refs[:5]
    level_refs = refs[5 : 5 + local_levels]
    far_refs = refs[5 + local_levels : 5 + local_levels + fars]
    outs = refs[5 + local_levels + fars :]
    dq_ref, dkv_ref = outs[:2]
    term_refs = outs[2 : 2 + pieces]
    dfar_refs = outs[2 + pieces : 1 + pieces + fars]
    dmid_refs = outs[1 + pieces + fars : 1 + pieces + fars + mids]
    dq_t_ref, acc_ref = outs[-2:]
    tok_rows, inner = q_ref.shape
    heads = inner // HEAD_DIM
    score_scale = 1.0 / math.sqrt(HEAD_DIM)
    keyset = KeySet([r.shape[0] for r in far_refs], far_bits, local_levels)

    for ref in (*dmid_refs, acc_ref):
        ref[...] = jnp.zeros_like(ref)

    def step(m, carry):
        here = keyset.here(m)
        for h in range(heads):
            cols, vcols = head_columns(h, inner)
            keys, values = (
                jnp.concatenate(keyset.near(m, level_refs, c) + keyset.far(far_refs, c), axis=0)
                for c in (cols, vcols)
            )
            q = q_ref[here, cols]
            g = g_ref[here, cols]
            top = stat_ref[h : h + 1, here]
            inverse = stat_ref[heads + h : heads + h + 1, here]
            probs = keyset.powers(keyset.pieces(dot(keys, q, NT)), top) * inverse
            att_t = att_t_ref[cols, here].astype(F32)
            delta = jnp.sum(g.T.astype(F32) * att_t, axis=0, keepdims=True)
            grads = (probs * (dot(values, g, NT) - delta) * score_scale).astype(BF16)
            dq_t = dot(keys, grads, TN).astype(BF16)
            dq_t_ref[cols, here] = dq_t
            dq_ref[here, cols] = dq_t.T
            for part, place in ((dot(grads, q), cols), (dot(probs.astype(BF16), g), vcols)):
                own, *sides = keyset.pieces(part)
                dkv_ref[here, place] = own
                for ref, seat, side in zip(dmid_refs, keyset.seats(m), sides):
                    ref[seat, place] += side
                acc_ref[:, place] += part[keyset.far_start :]
        return carry

    lax.fori_loop(0, tok_rows // (2 * BLOCK), step, 0)
    width = term_refs[-1].shape[0]
    first = acc_ref[:BLOCK].astype(BF16)
    term_refs[0][width : width + BLOCK, :] = first[:, :inner]
    term_refs[0][width + BLOCK :, :] = first[:, inner:]
    low = BLOCK
    for ref in dfar_refs:
        ref[...] = acc_ref[low : low + ref.shape[0]].astype(BF16)
        low += ref.shape[0]
    for i, ref in enumerate(term_refs):
        part = dot(dq_t_ref[...], tok_ref[:, i * width : (i + 1) * width])
        ref[:width, :] = part.astype(BF16).T
    fan = spread_matrix(2 * BLOCK, 1, 0, BLOCK, 0.5)
    targets = (dkv_ref, *dmid_refs)
    for i in reversed(range(mids)):
        for t in range(dmid_refs[i].shape[0] // BLOCK):
            part = dmid_refs[i][t * BLOCK : (t + 1) * BLOCK, :]
            high = part.astype(BF16)
            low = (part - high.astype(F32)).astype(BF16)
            rows = slice(2 * t * BLOCK, 2 * (t + 1) * BLOCK)
            targets[i][rows, :] += dot(fan, high) + dot(fan, low)


def backward(query, grad, attended_t, stats, tokens, levels, fars, far_bits, pieces, after):
    tok_rows, inner = query.shape
    far_rows = sum(f.shape[0] for f in fars)
    set_rows = (len(levels) + 1) * BLOCK + far_rows
    return run(
        functools.partial(backward_body, len(levels), far_bits, pieces),
        [query, grad, attended_t, stats, tokens, *levels, *fars],
        after,
        out_shape=[shape(tok_rows, inner), shape(tok_rows, 2 * inner, F32)]
        + [shape(tokens.shape[1] // pieces + 2 * BLOCK, inner)]
        + [shape(tokens.shape[1] // pieces, inner)] * (pieces - 1)
        + [shape(*f.shape) for f in fars[1:]],
        scratch_shapes=[pltpu.VMEM(level.shape, F32) for level in levels[1:]]
        + [pltpu.VMEM((inner, tok_rows), BF16), pltpu.VMEM((far_rows, 2 * inner), F32)],
        compiler_params=params(10),
        cost_estimate=cost(8.0),
    )


def term_body(which, low, left_ref, right_ref, out_ref):
    width, inner = out_ref.shape
    left = left_ref[which * inner : (which + 1) * inner, :]
    out_ref[...] = dot(left, right_ref[:, low : low + width]).astype(BF16).T


def weight_terms(left_t, right, inner, which, part, parts, after):
    tok_rows = left_t.shape[1]
    width = right.shape[1] // parts
    return run(
        functools.partial(term_body, which, part * width),
        [left_t, right],
        after,
        out_shape=shape(width, inner),
        compiler_params=params(3),
        cost_estimate=cost(0.2),
    )


def close_body(local_levels, far_bits, dkv_ref, *refs):
    joined_ref, *back_refs = refs[: len(far_bits)]
    dk_ref, dv_ref, dkv_t_ref = refs[len(far_bits) :]
    inner = dk_ref.shape[1]
    tile = 2 * BLOCK
    low = joined_ref.shape[0] - 2 * BLOCK
    joined = [joined_ref[low : low + BLOCK, :], joined_ref[low + BLOCK :, :]]
    backs = [jnp.concatenate(joined, axis=1)] + [ref[...] for ref in back_refs]
    for t in range(dkv_ref.shape[0] // tile):
        here = slice(t * tile, (t + 1) * tile)
        total = dkv_ref[here, :]
        for back, bit in zip(backs, far_bits):
            weight = 0.5 ** (local_levels + bit)
            fan = spread_matrix(tile, local_levels + bit, t * tile, back.shape[0], weight)
            total = total + dot(fan, back)
        final = total.astype(BF16)
        dk_ref[here, :] = final[:, :inner]
        dv_ref[here, :] = final[:, inner:]
        dkv_t_ref[:, here] = final.T


def close_keys(dkv, backs, far_bits, local_levels, after):
    tok_rows, double = dkv.shape
    inner = double // 2
    return run(
        functools.partial(close_body, local_levels, far_bits),
        [dkv, *backs],
        after,
        out_shape=[shape(tok_rows, inner), shape(tok_rows, inner), shape(double, tok_rows)],
        compiler_params=params(5),
        cost_estimate=cost(0.2),
    )


def split_body(count, parts, rank_ref, *refs):
    lefts, weights = refs[:count], refs[count : 2 * count]
    outs = refs[2 * count :]
    width = weights[0].shape[0] // parts
    for r in range(parts):
        owner = jnp.bitwise_xor(rank_ref[0], r)
        rows = pl.ds(pl.multiple_of(owner * width, width), width)
        total = None
        for left, weight in zip(lefts, weights):
            product = dot(left[...], weight[rows, :], NT)
            total = product if total is None else total + product
        place = r // 2 * width
        outs[r % 2][:, place : place + width] = total.astype(BF16)


def project_split(rank, lefts, weights, axis, after):
    count = len(lefts)
    parts = lax.axis_size(axis)
    tok_rows, inner = lefts[0].shape
    width = weights[0].shape[0]
    return run(
        functools.partial(split_body, count, parts),
        [rank, *lefts, *weights],
        after,
        in_specs=[pl.BlockSpec(memory_space=pltpu.SMEM)]
        + [pl.BlockSpec(memory_space=pltpu.VMEM)] * (2 * count),
        out_shape=[shape(tok_rows, width // 2)] * 2,
        compiler_params=params(5),
        cost_estimate=cost(1.0),
    )


def exchange(block, axis, distance):
    count = lax.axis_size(axis)
    return lax.ppermute(block, axis, [(i, i ^ distance) for i in range(count)])


def add(left, right):
    return (left.astype(F32) + right.astype(F32)).astype(BF16)


def term_half_body(chunk_ref, into_ref, out_ref):
    rows = slice(0, out_ref.shape[0])
    out_ref[...] = (chunk_ref[rows, :].astype(F32) + into_ref[rows, :].astype(F32)).astype(BF16)


def half_sum(chunk, into, rows, weight, after):
    return run(
        term_half_body,
        [chunk, into],
        after,
        out_shape=shape(rows, chunk.shape[1]),
        compiler_params=params(3),
        cost_estimate=cost(weight),
    )


def scatter_body(pieces, keep_ref, into_ref, even_ref, odd_ref):
    width = keep_ref.shape[1] // pieces
    for i in range(pieces):
        here = slice(i * width, (i + 1) * width)
        place = slice(i // 2 * width, (i // 2 + 1) * width)
        total = keep_ref[:, here].astype(F32) + into_ref[:, here].astype(F32)
        (even_ref, odd_ref)[i % 2][:, place] = total.astype(BF16)


def last_body(left_ref, right_ref, token_ref, out_ref):
    token_ref[...] = jnp.zeros_like(token_ref)
    out_ref[...] = (left_ref[...].astype(F32) + right_ref[...].astype(F32)).astype(BF16)


def last_sum(left, right, after):
    return run(
        last_body,
        [left, right],
        after,
        out_shape=[shape(8, 128, F32), shape(*left.shape)],
        compiler_params=params(3),
        cost_estimate=cost(0.9),
    )


def scatter_step(keep, into, pieces, after):
    rows, width = keep.shape
    return run(
        functools.partial(scatter_body, pieces),
        [keep, into],
        after,
        out_shape=[shape(rows, width // 2)] * 2,
        compiler_params=params(4),
        cost_estimate=cost(0.2),
    )


def turn_body(end_ref, half_ref, across_ref, chunk_ref, total_ref, send_ref):
    total = (half_ref[...].astype(F32) + across_ref[...].astype(F32)).astype(BF16)
    total_ref[...] = total

    @pl.when(end_ref[0] == 1)
    def _():
        send_ref[...] = chunk_ref[...]

    @pl.when(end_ref[0] == 0)
    def _():
        send_ref[...] = total


def turn(end, half, across, chunk, weight, after):
    return run(
        turn_body,
        [end, half, across, chunk],
        after,
        in_specs=[pl.BlockSpec(memory_space=pltpu.SMEM)]
        + [pl.BlockSpec(memory_space=pltpu.VMEM)] * 3,
        out_shape=[shape(*half.shape)] * 2,
        compiler_params=params(2),
        cost_estimate=cost(weight),
    )


def output_body(count, end_ref, *refs):
    totals, ends, (token_ref, out_ref) = refs[:count], refs[count : 2 * count], refs[2 * count :]
    token_ref[...] = jnp.zeros_like(token_ref)
    rows = totals[0].shape[0]

    for flag, sources in ((0, totals), (1, ends)):

        @pl.when(end_ref[0] == flag)
        def _():
            for i, ref in enumerate(sources):
                out_ref[i * rows : (i + 1) * rows, :] = ref[...]


def output(end, totals, ends, after):
    count = len(totals)
    rows, width = totals[0].shape
    return run(
        functools.partial(output_body, count),
        [end, *totals, *ends],
        after,
        in_specs=[pl.BlockSpec(memory_space=pltpu.SMEM)]
        + [pl.BlockSpec(memory_space=pltpu.VMEM)] * (2 * count),
        out_shape=[shape(8, 128, F32), shape(count * rows, width)],
        compiler_params=params(4),
        cost_estimate=cost(0.9),
    )


def relay_body(source_ref, target_ref):
    target_ref[...] = source_ref[...]


def relay(block, after):
    return run(
        relay_body,
        [block],
        after,
        out_shape=shape(*block.shape),
        compiler_params=params(3),
        cost_estimate=cost(0.2),
    )


class Line:
    lag = 3
    half_weights = (3.0, 3.0, 3.0, 2.5, 2.5, 3.0, 3.0, 3.0)
    turn_weights = (3.0, 2.5, 2.5, 3.0, 3.0, 3.0, 3.0, 3.0)

    def __init__(self, axis, other, end, step):
        self.axis, self.axes, self.step = axis, (axis, other), step
        self.count = lax.axis_size(axis)
        self.end = end
        width = lax.axis_size(other)
        self.across = []
        for place in range(self.count):
            for seat in range(width):
                target = (place, seat ^ 1 if width > 1 else seat)
                if place & 3 in (1, 2):
                    target = (place ^ 3, seat)
                self.across.append((place * width + seat, target[0] * width + target[1]))
        self.chunks, self.into, self.halves, self.crossed, self.totals = [], [], [], [], []

    def enter(self, chunk):
        self.chunks.append(chunk)
        self.into.append(exchange(chunk, self.axis, 1))

    def meet(self, rows):
        k = len(self.halves)
        weight = self.half_weights[k]
        half = self.step(half_sum, self.chunks[k], self.into[k], rows, weight)
        self.halves.append(half)
        self.crossed.append(lax.ppermute(half, self.axes, self.across))

    def turn(self, chunk):
        old = len(self.totals)
        half, crossed = self.halves[old], self.crossed[old]
        weight = self.turn_weights[old]
        total, send = self.step(turn, self.end, half, crossed, chunk, weight)
        self.totals.append(total)
        self.chunks.append(chunk)
        self.into.append(exchange(send, self.axis, 1))

    def leave(self):
        old = len(self.totals)
        half = self.halves[old]
        weight = self.turn_weights[old]
        total = self.step(half_sum, half, self.crossed[old], half.shape[0], weight)
        self.totals.append(total)
        self.into.append(exchange(total, self.axis, 1))

    def output(self, first, count):
        ends = self.into[first + self.lag : first + self.lag + count]
        _, result = self.step(output, self.end, self.totals[first : first + count], ends)
        distance = 4
        while distance < self.count:
            result = add(result, exchange(result, self.axis, distance))
            distance *= 2
        return result


class Scatter:
    def __init__(self, parts, axis, step):
        self.axis, self.step = axis, step
        self.pieces = lax.axis_size(axis) // 2
        self.keep, send = parts
        self.distance = 1
        self.into = exchange(send, axis, 1)

    def advance(self):
        while self.pieces > 1:
            self.keep, send = self.step(scatter_step, self.keep, self.into, self.pieces)
            self.distance *= 2
            self.pieces //= 2
            self.into = exchange(send, self.axis, self.distance)

    def result(self):
        return self.step(last_sum, self.keep, self.into)[1]


def per_device(tokens, w_query, w_key, w_value, w_out, cotangent):
    tok_rows = tokens.shape[0]
    inner = w_query.shape[1]
    local_levels = (tok_rows // BLOCK).bit_length() - 1
    count = lax.axis_size("seq")
    far_levels = count.bit_length() - 1
    far_bits = [d.bit_length() - 1 for d in range(1, count)]

    last = []

    def step(kernel, *operands):
        made = kernel(*operands, list(last))
        last[:] = made[:1] if isinstance(made, (list, tuple)) else [made]
        return made

    place = jnp.bitwise_and(lax.axis_index("seq"), 3)
    end = jnp.reshape((place == 0) | (place == 3), (1,)).astype(jnp.int32)
    rank = jnp.reshape(lax.axis_index("head"), (1,)).astype(jnp.int32)
    parts = key_value(tokens, w_key, w_value, local_levels, far_levels, [end, rank])
    levels, tops = parts[:local_levels], parts[local_levels:]
    fars = [exchange(tops[bit], "seq", d) for d, bit in enumerate(far_bits, 1)]
    query = step(project, tokens, w_query)
    powers, near = step(near_powers, query, levels)
    grad = step(project, cotangent, w_out)
    attended, attended_t, stats = step(forward, query, powers, near, levels, fars, far_bits)

    line = Line("seq", "head", end, step)
    pieces = 2
    rows = tokens.shape[1] // pieces
    line.enter(step(weight_terms, attended_t, cotangent, inner, 0, 0, pieces))
    line.enter(step(weight_terms, attended_t, cotangent, inner, 0, 1, pieces))
    parts = step(project_split, rank, [attended], [w_out], "head")
    mixed = Scatter(parts, "head", step)
    dquery, dkv, query_first, query_second, *away = step(
        backward, query, grad, attended_t, stats, tokens, levels, fars, far_bits, pieces
    )
    line.enter(query_first)
    backs = [exchange(piece, "seq", d) for d, piece in enumerate(away, 2)]
    line.meet(rows)
    mixed.advance()
    line.meet(rows)
    line.turn(query_second)
    dkey, dvalue, dkv_t = step(
        close_keys, dkv, [line.into[2], *backs], far_bits, local_levels
    )
    key_first = step(weight_terms, dkv_t, tokens, inner, 0, 0, pieces)
    line.meet(rows)
    line.turn(key_first)
    line.meet(rows)
    key_second = step(weight_terms, dkv_t, tokens, inner, 0, 1, pieces)
    line.turn(key_second)
    value_first = step(weight_terms, dkv_t, tokens, inner, 1, 0, pieces)
    keep, send = step(project_split, rank, [dquery, dkey, dvalue], [w_query, w_key, w_value], "head")
    line.meet(rows)
    tokens_grad = Scatter([keep, step(relay, send)], "head", step)
    line.turn(value_first)
    mixed = mixed.result()
    value_second = step(weight_terms, dkv_t, tokens, inner, 1, 1, pieces)
    line.meet(rows)
    line.turn(value_second)
    out_grad = line.output(0, pieces)
    line.meet(rows)
    tokens_grad.advance()
    line.leave()
    line.meet(rows)
    query_grad = line.output(2, pieces)
    line.leave()
    key_grad = line.output(4, pieces)
    line.leave()
    tokens_grad = tokens_grad.result()
    value_grad = line.output(6, pieces)
    return mixed, tokens_grad, query_grad, key_grad, value_grad, out_grad


def solution(mesh):
    return jax.shard_map(
        per_device,
        mesh=mesh,
        in_specs=(
            P(("groups", "seq"), None),
            P(None, "head"),
            P(None, "head"),
            P(None, "head"),
            P(None, "head"),
            P(("groups", "seq"), None),
        ),
        out_specs=(
            P(("groups", "seq"), "head"),
            P(("groups", "seq"), "head"),
            P("groups", "head"),
            P("groups", "head"),
            P("groups", "head"),
            P("groups", "head"),
        ),
        check_vma=False,
    )
```

```python
import functools
import math

import jax
import jax.numpy as jnp
from jax import lax
from jax.experimental import pallas as pl
from jax.experimental.pallas import tpu as pltpu
from jax.sharding import PartitionSpec as P

HEAD_DIM = 128
BLOCK = 128
BF16 = jnp.bfloat16
F32 = jnp.float32
MIB = 1024 * 1024

NN = (((1,), (0,)), ((), ()))
NT = (((1,), (1,)), ((), ()))
TN = (((0,), (0,)), ((), ()))


def dot(left, right, dims=NN):
    return lax.dot_general(left, right, dims, preferred_element_type=F32)


def params(mib):
    return pltpu.CompilerParams(vmem_limit_bytes=mib * MIB)


def cost(microseconds):
    return pl.CostEstimate(flops=int(microseconds * 1150e6) + 1, bytes_accessed=1, transcendentals=0)


def run(body, ready, after=(), in_specs=None, **options):
    count, extra = len(ready), len(after)

    def kernel(*refs):
        body(*refs[:count], *refs[count + extra :])

    in_specs = in_specs or [pl.BlockSpec(memory_space=pltpu.VMEM)] * count
    in_specs = in_specs + [pl.BlockSpec(memory_space=pl.ANY)] * extra
    return pl.pallas_call(kernel, in_specs=in_specs, **options)(*ready, *after)


def shape(rows, cols, dtype=BF16):
    return jax.ShapeDtypeStruct((rows, cols), dtype)


def whole(rows, cols):
    return pl.BlockSpec((rows, cols), lambda *_: (0, 0))


def pool_matrix(rows):
    row = lax.broadcasted_iota(jnp.int32, (rows // 2, rows), 0)
    col = lax.broadcasted_iota(jnp.int32, (rows // 2, rows), 1)
    return jnp.where(jnp.right_shift(col, 1) == row, 0.5, 0.0).astype(BF16)


def spread_matrix(rows, step_bits, offset, cols, weight):
    row = lax.broadcasted_iota(jnp.int32, (rows, cols), 0) + offset
    col = lax.broadcasted_iota(jnp.int32, (rows, cols), 1)
    return jnp.where(jnp.right_shift(row, step_bits) == col, weight, 0.0).astype(BF16)


def key_value_body(local_levels, far_levels, parts, tok_hbm, wk_hbm, wv_hbm, *refs):
    out_hbm = refs[:local_levels]
    far = refs[local_levels : local_levels + far_levels]
    refs = refs[local_levels + far_levels :]
    tok_ref, wk_ref, wv_ref = refs[:3]
    levels = refs[3 : 3 + local_levels]
    in_sems, out_sems = refs[3 + local_levels :]
    part = tok_ref.shape[0] // parts

    def fetch(source, target, i):
        copy = pltpu.make_async_copy(source, target, in_sems.at[i])
        copy.start()
        return copy

    def flush(i):
        copy = pltpu.make_async_copy(levels[i], out_hbm[i], out_sems.at[i])
        copy.start()
        return copy

    weights = [fetch(wk_hbm, wk_ref, 0), fetch(wv_hbm, wv_ref, 1)]
    tiles = []
    for p in range(parts):
        rows = pl.ds(p * part, part)
        tiles.append(fetch(tok_hbm.at[rows], tok_ref.at[rows], 2 + p))
    for copy in weights:
        copy.wait()
    for p in range(parts):
        tiles[p].wait()
        here = slice(p * part, (p + 1) * part)
        x = tok_ref[here, :]
        both = jnp.concatenate([dot(x, wk_ref[...]), dot(x, wv_ref[...])], axis=1)
        levels[0][here, :] = both.astype(BF16)
    flushes = [flush(0)]
    pool = pool_matrix(part)
    for i in range(1, local_levels):
        source = levels[i - 1]
        for low in range(0, source.shape[0], part):
            mean = dot(pool, source[low : low + part, :])
            levels[i][low // 2 : (low + part) // 2, :] = mean.astype(BF16)
        flushes.append(flush(i))
    rows = dot(pool, levels[-1][...]).astype(BF16)
    for i in range(far_levels):
        if i:
            rows = dot(pool_matrix(rows.shape[0]), rows).astype(BF16)
        far[i][...] = rows
    for copy in flushes:
        copy.wait()


def key_value(tokens, w_key, w_value, local_levels, far_levels, after):
    tok_rows, width = tokens.shape
    inner = w_key.shape[1]
    parts = tok_rows // (2 * BLOCK)
    held = [(tok_rows >> i, 2 * inner) for i in range(local_levels)]
    tops = [(BLOCK >> i, 2 * inner) for i in range(far_levels)]
    return run(
        functools.partial(key_value_body, local_levels, far_levels, parts),
        [tokens, w_key, w_value],
        after,
        in_specs=[pl.BlockSpec(memory_space=pl.ANY)] * 3,
        out_specs=[pl.BlockSpec(memory_space=pl.ANY)] * len(held)
        + [pl.BlockSpec(memory_space=pltpu.VMEM)] * len(tops),
        out_shape=[shape(*dims) for dims in held + tops],
        scratch_shapes=[pltpu.VMEM((tok_rows, width), BF16)]
        + [pltpu.VMEM((width, inner), BF16)] * 2
        + [pltpu.VMEM(dims, BF16) for dims in held]
        + [pltpu.SemaphoreType.DMA((parts + 2,)), pltpu.SemaphoreType.DMA((len(held),))],
        compiler_params=params(56),
        cost_estimate=cost(5.0),
    )


def project_body(left_ref, weight_ref, out_ref):
    out_ref[...] = dot(left_ref[...], weight_ref[...]).astype(BF16)


def project(left, weight, after):
    tok_rows, width = left.shape
    inner = weight.shape[1]
    return run(
        project_body,
        [left, weight],
        after,
        out_shape=shape(tok_rows, inner),
        compiler_params=params(4),
        cost_estimate=cost(0.7),
    )


class KeySet:
    def __init__(self, far_rows, far_bits, local_levels):
        mids = local_levels - 1
        self.sizes = [2 * BLOCK] + [BLOCK] * mids + list(far_rows)
        self.bounds = [sum(self.sizes[:i]) for i in range(len(self.sizes) + 1)]
        steps = [0] + list(range(1, local_levels)) + [local_levels + b for b in far_bits]
        self.biases = [float(step) for step in steps]
        self.mids = mids
        self.far_start = self.bounds[1 + mids]
        self.factor = math.log2(math.e) / math.sqrt(HEAD_DIM)

    def here(self, m):
        return pl.ds(pl.multiple_of(m * 2 * BLOCK, 2 * BLOCK), 2 * BLOCK)

    def seats(self, m):
        for i in range(self.mids):
            sibling = jnp.bitwise_xor(jnp.right_shift(m, i), 1)
            yield pl.ds(pl.multiple_of(sibling * BLOCK, BLOCK), BLOCK)

    def near(self, m, level_refs, cols):
        rows = [level_refs[0][self.here(m), cols]]
        rows += [ref[seat, cols] for ref, seat in zip(level_refs[1:], self.seats(m))]
        return rows

    def far(self, far_refs, cols):
        return [ref[:, cols] for ref in far_refs]

    def pieces(self, array, first=0, count=None):
        base = self.bounds[first]
        ends = self.bounds[first:] if count is None else self.bounds[first : first + count + 1]
        return [array[a - base : b - base] for a, b in zip(ends, ends[1:])]

    def top(self, pieces, first=0):
        tops = [
            jnp.max(piece, axis=0, keepdims=True) * self.factor + bias
            for piece, bias in zip(pieces, self.biases[first:])
        ]
        return functools.reduce(jnp.maximum, tops)

    def powers(self, pieces, top, first=0):
        return jnp.concatenate(
            [
                jnp.exp2(piece * self.factor + (bias - top))
                for piece, bias in zip(pieces, self.biases[first:])
            ],
            axis=0,
        )


def head_columns(h, inner):
    low = h * HEAD_DIM
    return slice(low, low + HEAD_DIM), slice(inner + low, inner + low + HEAD_DIM)


def near_body(local_levels, q_ref, *refs):
    level_refs = refs[:local_levels]
    power_ref, stat_ref = refs[local_levels:]
    tok_rows, inner = q_ref.shape
    heads = inner // HEAD_DIM
    keyset = KeySet([], [], local_levels)
    rows = keyset.far_start

    def step(m, carry):
        here = keyset.here(m)
        for h in range(heads):
            cols, _ = head_columns(h, inner)
            keys = jnp.concatenate(keyset.near(m, level_refs, cols), axis=0)
            pieces = keyset.pieces(dot(keys, q_ref[here, cols], NT))
            top = keyset.top(pieces)
            powers = keyset.powers(pieces, top)
            stat_ref[h : h + 1, here] = top
            stat_ref[heads + h : heads + h + 1, here] = jnp.sum(powers, axis=0, keepdims=True)
            power_ref[pl.ds(pl.multiple_of((m * heads + h) * rows, rows), rows), :] = powers
        return carry

    lax.fori_loop(0, tok_rows // (2 * BLOCK), step, 0)


def near_powers(query, levels, after):
    tok_rows, inner = query.shape
    heads = inner // HEAD_DIM
    pairs = tok_rows // (2 * BLOCK)
    rows = (len(levels) + 1) * BLOCK
    return run(
        functools.partial(near_body, len(levels)),
        [query, *levels],
        after,
        out_shape=[shape(pairs * heads * rows, 2 * BLOCK, F32), shape(2 * heads, tok_rows, F32)],
        compiler_params=params(6),
        cost_estimate=cost(2.3),
    )


def forward_body(local_levels, far_bits, *refs):
    fars = len(far_bits)
    q_ref, power_ref, near_ref = refs[:3]
    level_refs = refs[3 : 3 + local_levels]
    far_refs = refs[3 + local_levels : 3 + local_levels + fars]
    att_ref, att_t_ref, stat_ref = refs[3 + local_levels + fars :]
    tok_rows, inner = q_ref.shape
    heads = inner // HEAD_DIM
    keyset = KeySet([r.shape[0] for r in far_refs], far_bits, local_levels)
    rows = keyset.far_start

    def step(m, carry):
        here = keyset.here(m)
        for h in range(heads):
            cols, vcols = head_columns(h, inner)
            second = heads + h
            keys = jnp.concatenate(keyset.far(far_refs, cols), axis=0)
            values = keyset.near(m, level_refs, vcols) + keyset.far(far_refs, vcols)
            values = jnp.concatenate(values, axis=0)
            first = local_levels
            pieces = keyset.pieces(dot(keys, q_ref[here, cols], NT), first)
            near_top = near_ref[h : h + 1, here]
            top = jnp.maximum(near_top, keyset.top(pieces, first))
            shrink = jnp.exp2(near_top - top)
            powers = keyset.powers(pieces, top, first)
            total = near_ref[second : second + 1, here] * shrink
            total = total + jnp.sum(powers, axis=0, keepdims=True)
            inverse = 1.0 / total
            place = pl.ds(pl.multiple_of((m * heads + h) * rows, rows), rows)
            near_probs = (power_ref[place, :] * (shrink * inverse)).astype(BF16)
            far_probs = (powers * inverse).astype(BF16)
            probs_b = jnp.concatenate([near_probs, far_probs], axis=0)
            att_t = dot(values, probs_b, TN).astype(BF16)
            att_t_ref[cols, here] = att_t
            att_ref[here, cols] = att_t.T
            stat_ref[h : h + 1, here] = top
            stat_ref[second : second + 1, here] = inverse
        return carry

    lax.fori_loop(0, tok_rows // (2 * BLOCK), step, 0)


def forward(query, powers, near, levels, fars, far_bits, after):
    tok_rows, inner = query.shape
    heads = inner // HEAD_DIM
    set_rows = (len(levels) + 1) * BLOCK + sum(f.shape[0] for f in fars)
    return run(
        functools.partial(forward_body, len(levels), far_bits),
        [query, powers, near, *levels, *fars],
        after,
        out_shape=[
            shape(tok_rows, inner),
            shape(inner, tok_rows),
            shape(2 * heads, tok_rows, F32),
        ],
        compiler_params=params(6),
        cost_estimate=cost(4.0),
    )


def backward_body(h, heads, local_levels, far_bits, pieces, *refs):
    mids = local_levels - 1
    fars = len(far_bits)
    closing = h == heads - 1
    q_ref, g_ref, att_t_ref, stat_ref = refs[:4]
    level_refs = refs[4 : 4 + local_levels]
    far_refs = refs[4 + local_levels : 4 + local_levels + fars]
    refs = refs[4 + local_levels + fars :]
    if closing:
        tok_ref, *earlier = refs[: 1 + 3 * h]
        refs = refs[1 + 3 * h :]
        dq_ref, dkv_ref = refs[:2]
        term_refs = refs[2 : 2 + pieces]
        dfar_refs = refs[2 + pieces : 1 + pieces + fars]
        scratch = refs[1 + pieces + fars :]
        dq_t_ref = scratch[-1]
        place = slice(h * HEAD_DIM, (h + 1) * HEAD_DIM)
    else:
        dq_ref, dkv_ref, dq_t_ref, out_ref = refs[:4]
        scratch = refs[4:]
        place = slice(0, HEAD_DIM)
    dmid_refs = scratch[:mids]
    acc_ref = scratch[mids]
    tok_rows, inner = q_ref.shape
    score_scale = 1.0 / math.sqrt(HEAD_DIM)
    keyset = KeySet([r.shape[0] for r in far_refs], far_bits, local_levels)
    cols, vcols = head_columns(h, inner)
    parts = (slice(0, HEAD_DIM), slice(HEAD_DIM, 2 * HEAD_DIM))

    for ref in (*dmid_refs, acc_ref):
        ref[...] = jnp.zeros_like(ref)

    def unit(m):
        here = keyset.here(m)
        keys, values = (
            jnp.concatenate(keyset.near(m, level_refs, c) + keyset.far(far_refs, c), axis=0)
            for c in (cols, vcols)
        )
        q = q_ref[here, cols]
        g = g_ref[here, cols]
        top = stat_ref[h : h + 1, here]
        inverse = stat_ref[heads + h : heads + h + 1, here]
        probs = keyset.powers(keyset.pieces(dot(keys, q, NT)), top) * inverse
        att_t = att_t_ref[cols, here].astype(F32)
        delta = jnp.sum(g.T.astype(F32) * att_t, axis=0, keepdims=True)
        grads = (probs * (dot(values, g, NT) - delta) * score_scale).astype(BF16)
        dq_t = dot(keys, grads, TN).astype(BF16)
        dq_t_ref[place, here] = dq_t
        dq_ref[here, place] = dq_t.T
        for part, half in zip((dot(grads, q), dot(probs.astype(BF16), g)), parts):
            own, *sides = keyset.pieces(part)
            dkv_ref[here, half] = own
            for ref, seat, side in zip(dmid_refs, keyset.seats(m), sides):
                ref[seat, half] += side
            acc_ref[:, half] += part[keyset.far_start :]

    pairs = tok_rows // (2 * BLOCK)
    stride = 2 if pairs % 2 == 0 else 1

    def step(i, carry):
        for u in range(stride):
            unit(i * stride + u)
        return carry

    lax.fori_loop(0, pairs // stride, step, 0)
    fan = spread_matrix(2 * BLOCK, 1, 0, BLOCK, 0.5)
    targets = (dkv_ref, *dmid_refs)
    for i in reversed(range(mids)):
        for t in range(dmid_refs[i].shape[0] // BLOCK):
            part = dmid_refs[i][t * BLOCK : (t + 1) * BLOCK, :]
            high = part.astype(BF16)
            low = (part - high.astype(F32)).astype(BF16)
            rows = slice(2 * t * BLOCK, 2 * (t + 1) * BLOCK)
            targets[i][rows, :] += dot(fan, high) + dot(fan, low)
    away = acc_ref[...].astype(BF16)
    if not closing:
        out_ref[...] = away
        return
    aways = []
    for e in range(h):
        dq_e, dq_t_e, away_e = earlier[3 * e : 3 * e + 3]
        here = slice(e * HEAD_DIM, (e + 1) * HEAD_DIM)
        dq_ref[:, here] = dq_e[...]
        dq_t_ref[here, :] = dq_t_e[...]
        aways.append(away_e[...])
    aways.append(away)
    away = jnp.concatenate([x[:, half] for half in parts for x in aways], axis=1)
    width = term_refs[-1].shape[0]
    term_refs[0][width : width + BLOCK, :] = away[:BLOCK, :inner]
    term_refs[0][width + BLOCK :, :] = away[:BLOCK, inner:]
    low = BLOCK
    for ref in dfar_refs:
        ref[...] = away[low : low + ref.shape[0]]
        low += ref.shape[0]
    for i, ref in enumerate(term_refs):
        part = dot(dq_t_ref[...], tok_ref[:, i * width : (i + 1) * width])
        ref[:width, :] = part.astype(BF16).T


def backward_scratch(levels, fars):
    mids = [pltpu.VMEM((level.shape[0], 2 * HEAD_DIM), F32) for level in levels[1:]]
    return mids + [pltpu.VMEM((sum(f.shape[0] for f in fars), 2 * HEAD_DIM), F32)]


def backward_first(h, query, grad, attended_t, stats, levels, fars, far_bits, after):
    tok_rows, inner = query.shape
    return run(
        functools.partial(
            backward_body, h, inner // HEAD_DIM, len(levels), far_bits, 0
        ),
        [query, grad, attended_t, stats, *levels, *fars],
        after,
        out_shape=[
            shape(tok_rows, HEAD_DIM),
            shape(tok_rows, 2 * HEAD_DIM, F32),
            shape(HEAD_DIM, tok_rows),
            shape(sum(f.shape[0] for f in fars), 2 * HEAD_DIM),
        ],
        scratch_shapes=backward_scratch(levels, fars),
        compiler_params=params(10),
        cost_estimate=cost(4.0),
    )


def backward_last(earlier, query, grad, attended_t, stats, tokens, levels, fars, far_bits, pieces, after):
    tok_rows, inner = query.shape
    h = len(earlier)
    ready = [query, grad, attended_t, stats, *levels, *fars, tokens]
    for dq, _, dq_t, away in earlier:
        ready += [dq, dq_t, away]
    return run(
        functools.partial(
            backward_body, h, inner // HEAD_DIM, len(levels), far_bits, pieces
        ),
        ready,
        after,
        out_shape=[shape(tok_rows, inner), shape(tok_rows, 2 * HEAD_DIM, F32)]
        + [shape(tokens.shape[1] // pieces + 2 * BLOCK, inner)]
        + [shape(tokens.shape[1] // pieces, inner)] * (pieces - 1)
        + [shape(*f.shape) for f in fars[1:]],
        scratch_shapes=backward_scratch(levels, fars) + [pltpu.VMEM((inner, tok_rows), BF16)],
        compiler_params=params(10),
        cost_estimate=cost(4.0),
    )


def term_body(which, low, left_ref, right_ref, out_ref):
    width, inner = out_ref.shape
    left = left_ref[which * inner : (which + 1) * inner, :]
    out_ref[...] = dot(left, right_ref[:, low : low + width]).astype(BF16).T


def weight_terms(left_t, right, inner, which, part, parts, after):
    tok_rows = left_t.shape[1]
    width = right.shape[1] // parts
    return run(
        functools.partial(term_body, which, part * width),
        [left_t, right],
        after,
        out_shape=shape(width, inner),
        compiler_params=params(3),
        cost_estimate=cost(0.2),
    )


def close_body(local_levels, far_bits, heads, *refs):
    dkv_refs = refs[:heads]
    joined_ref, *back_refs = refs[heads : heads + len(far_bits)]
    dk_ref, dv_ref, dkv_t_ref = refs[heads + len(far_bits) :]
    inner = dk_ref.shape[1]
    tile = 2 * BLOCK
    low = joined_ref.shape[0] - 2 * BLOCK
    joined = [joined_ref[low : low + BLOCK, :], joined_ref[low + BLOCK :, :]]
    backs = [jnp.concatenate(joined, axis=1)] + [ref[...] for ref in back_refs]
    halves = (slice(0, HEAD_DIM), slice(HEAD_DIM, 2 * HEAD_DIM))
    for t in range(dk_ref.shape[0] // tile):
        here = slice(t * tile, (t + 1) * tile)
        total = jnp.concatenate([ref[here, half] for half in halves for ref in dkv_refs], axis=1)
        for back, bit in zip(backs, far_bits):
            weight = 0.5 ** (local_levels + bit)
            fan = spread_matrix(tile, local_levels + bit, t * tile, back.shape[0], weight)
            total = total + dot(fan, back)
        final = total.astype(BF16)
        dk_ref[here, :] = final[:, :inner]
        dv_ref[here, :] = final[:, inner:]
        dkv_t_ref[:, here] = final.T


def close_keys(dkvs, backs, far_bits, local_levels, after):
    tok_rows = dkvs[0].shape[0]
    inner = len(dkvs) * HEAD_DIM
    double = 2 * inner
    return run(
        functools.partial(close_body, local_levels, far_bits, len(dkvs)),
        [*dkvs, *backs],
        after,
        out_shape=[shape(tok_rows, inner), shape(tok_rows, inner), shape(double, tok_rows)],
        compiler_params=params(5),
        cost_estimate=cost(0.2),
    )


def split_body(count, parts, rank_ref, *refs):
    lefts, weights = refs[:count], refs[count : 2 * count]
    outs = refs[2 * count :]
    width = weights[0].shape[0] // parts
    for r in range(parts):
        owner = jnp.bitwise_xor(rank_ref[0], r)
        rows = pl.ds(pl.multiple_of(owner * width, width), width)
        total = None
        for left, weight in zip(lefts, weights):
            product = dot(left[...], weight[rows, :], NT)
            total = product if total is None else total + product
        place = r // 2 * width
        outs[r % 2][:, place : place + width] = total.astype(BF16)


def project_split(rank, lefts, weights, axis, after):
    count = len(lefts)
    parts = lax.axis_size(axis)
    tok_rows, inner = lefts[0].shape
    width = weights[0].shape[0]
    return run(
        functools.partial(split_body, count, parts),
        [rank, *lefts, *weights],
        after,
        in_specs=[pl.BlockSpec(memory_space=pltpu.SMEM)]
        + [pl.BlockSpec(memory_space=pltpu.VMEM)] * (2 * count),
        out_shape=[shape(tok_rows, width // 2)] * 2,
        compiler_params=params(5),
        cost_estimate=cost(1.0),
    )


def exchange(block, axis, distance):
    count = lax.axis_size(axis)
    return lax.ppermute(block, axis, [(i, i ^ distance) for i in range(count)])


def add(left, right):
    return (left.astype(F32) + right.astype(F32)).astype(BF16)


def term_half_body(chunk_ref, into_ref, out_ref):
    rows = slice(0, out_ref.shape[0])
    out_ref[...] = (chunk_ref[rows, :].astype(F32) + into_ref[rows, :].astype(F32)).astype(BF16)


def half_sum(chunk, into, rows, weight, after):
    return run(
        term_half_body,
        [chunk, into],
        after,
        out_shape=shape(rows, chunk.shape[1]),
        compiler_params=params(3),
        cost_estimate=cost(weight),
    )


def scatter_body(pieces, keep_ref, into_ref, even_ref, odd_ref):
    width = keep_ref.shape[1] // pieces
    for i in range(pieces):
        here = slice(i * width, (i + 1) * width)
        place = slice(i // 2 * width, (i // 2 + 1) * width)
        total = keep_ref[:, here].astype(F32) + into_ref[:, here].astype(F32)
        (even_ref, odd_ref)[i % 2][:, place] = total.astype(BF16)


def last_body(left_ref, right_ref, token_ref, out_ref):
    token_ref[...] = jnp.zeros_like(token_ref)
    out_ref[...] = (left_ref[...].astype(F32) + right_ref[...].astype(F32)).astype(BF16)


def last_sum(left, right, after):
    return run(
        last_body,
        [left, right],
        after,
        out_shape=[shape(8, 128, F32), shape(*left.shape)],
        compiler_params=params(3),
        cost_estimate=cost(0.9),
    )


def scatter_step(keep, into, pieces, after):
    rows, width = keep.shape
    return run(
        functools.partial(scatter_body, pieces),
        [keep, into],
        after,
        out_shape=[shape(rows, width // 2)] * 2,
        compiler_params=params(4),
        cost_estimate=cost(0.2),
    )


def turn_body(end_ref, half_ref, across_ref, chunk_ref, total_ref, send_ref):
    total = (half_ref[...].astype(F32) + across_ref[...].astype(F32)).astype(BF16)
    total_ref[...] = total

    @pl.when(end_ref[0] == 1)
    def _():
        send_ref[...] = chunk_ref[...]

    @pl.when(end_ref[0] == 0)
    def _():
        send_ref[...] = total


def turn(end, half, across, chunk, weight, after):
    return run(
        turn_body,
        [end, half, across, chunk],
        after,
        in_specs=[pl.BlockSpec(memory_space=pltpu.SMEM)]
        + [pl.BlockSpec(memory_space=pltpu.VMEM)] * 3,
        out_shape=[shape(*half.shape)] * 2,
        compiler_params=params(2),
        cost_estimate=cost(weight),
    )


def output_body(count, end_ref, *refs):
    totals, ends, (token_ref, out_ref) = refs[:count], refs[count : 2 * count], refs[2 * count :]
    token_ref[...] = jnp.zeros_like(token_ref)
    rows = totals[0].shape[0]

    for flag, sources in ((0, totals), (1, ends)):

        @pl.when(end_ref[0] == flag)
        def _():
            for i, ref in enumerate(sources):
                out_ref[i * rows : (i + 1) * rows, :] = ref[...]


def output(end, totals, ends, after):
    count = len(totals)
    rows, width = totals[0].shape
    return run(
        functools.partial(output_body, count),
        [end, *totals, *ends],
        after,
        in_specs=[pl.BlockSpec(memory_space=pltpu.SMEM)]
        + [pl.BlockSpec(memory_space=pltpu.VMEM)] * (2 * count),
        out_shape=[shape(8, 128, F32), shape(count * rows, width)],
        compiler_params=params(4),
        cost_estimate=cost(0.9),
    )


def relay_body(source_ref, target_ref):
    target_ref[...] = source_ref[...]


def relay(block, after):
    return run(
        relay_body,
        [block],
        after,
        out_shape=shape(*block.shape),
        compiler_params=params(3),
        cost_estimate=cost(0.2),
    )


class Line:
    lag = 3
    half_weights = (3.0, 3.0, 2.5, 2.0, 2.5, 3.0, 3.0, 2.0)
    turn_weights = (3.0, 2.0, 2.0, 3.0, 3.0, 2.0, 2.0, 2.0)

    def __init__(self, axis, other, end, step):
        self.axis, self.axes, self.step = axis, (axis, other), step
        self.count = lax.axis_size(axis)
        self.end = end
        width = lax.axis_size(other)
        self.across = []
        for place in range(self.count):
            for seat in range(width):
                target = (place, seat ^ 1 if width > 1 else seat)
                if place & 3 in (1, 2):
                    target = (place ^ 3, seat)
                self.across.append((place * width + seat, target[0] * width + target[1]))
        self.chunks, self.into, self.halves, self.crossed, self.totals = [], [], [], [], []

    def enter(self, chunk):
        self.chunks.append(chunk)
        self.into.append(exchange(chunk, self.axis, 1))

    def meet(self, rows):
        k = len(self.halves)
        weight = self.half_weights[k]
        half = self.step(half_sum, self.chunks[k], self.into[k], rows, weight)
        self.halves.append(half)
        self.crossed.append(lax.ppermute(half, self.axes, self.across))

    def turn(self, chunk):
        old = len(self.totals)
        half, crossed = self.halves[old], self.crossed[old]
        weight = self.turn_weights[old]
        total, send = self.step(turn, self.end, half, crossed, chunk, weight)
        self.totals.append(total)
        self.chunks.append(chunk)
        self.into.append(exchange(send, self.axis, 1))

    def leave(self):
        old = len(self.totals)
        half = self.halves[old]
        weight = self.turn_weights[old]
        total = self.step(half_sum, half, self.crossed[old], half.shape[0], weight)
        self.totals.append(total)
        self.into.append(exchange(total, self.axis, 1))

    def output(self, first, count):
        ends = self.into[first + self.lag : first + self.lag + count]
        _, result = self.step(output, self.end, self.totals[first : first + count], ends)
        distance = 4
        while distance < self.count:
            result = add(result, exchange(result, self.axis, distance))
            distance *= 2
        return result


class Scatter:
    def __init__(self, parts, axis, step):
        self.axis, self.step = axis, step
        self.pieces = lax.axis_size(axis) // 2
        self.keep, send = parts
        self.distance = 1
        self.into = exchange(send, axis, 1)

    def advance(self):
        while self.pieces > 1:
            self.keep, send = self.step(scatter_step, self.keep, self.into, self.pieces)
            self.distance *= 2
            self.pieces //= 2
            self.into = exchange(send, self.axis, self.distance)

    def result(self):
        return self.step(last_sum, self.keep, self.into)[1]


def per_device(tokens, w_query, w_key, w_value, w_out, cotangent):
    tok_rows = tokens.shape[0]
    inner = w_query.shape[1]
    local_levels = (tok_rows // BLOCK).bit_length() - 1
    count = lax.axis_size("seq")
    far_levels = count.bit_length() - 1
    far_bits = [d.bit_length() - 1 for d in range(1, count)]

    last = []

    def step(kernel, *operands):
        made = kernel(*operands, list(last))
        last[:] = made[:1] if isinstance(made, (list, tuple)) else [made]
        return made

    place = jnp.bitwise_and(lax.axis_index("seq"), 3)
    end = jnp.reshape((place == 0) | (place == 3), (1,)).astype(jnp.int32)
    rank = jnp.reshape(lax.axis_index("head"), (1,)).astype(jnp.int32)
    parts = key_value(tokens, w_key, w_value, local_levels, far_levels, [end, rank])
    levels, tops = parts[:local_levels], parts[local_levels:]
    fars = [exchange(tops[bit], "seq", d) for d, bit in enumerate(far_bits, 1)]
    query = step(project, tokens, w_query)
    powers, near = step(near_powers, query, levels)
    grad = step(project, cotangent, w_out)
    attended, attended_t, stats = step(forward, query, powers, near, levels, fars, far_bits)

    line = Line("seq", "head", end, step)
    pieces = 2
    rows = tokens.shape[1] // pieces
    line.enter(step(weight_terms, attended_t, cotangent, inner, 0, 0, pieces))
    parts = step(project_split, rank, [attended], [w_out], "head")
    mixed = Scatter(parts, "head", step)
    earlier = [
        step(backward_first, h, query, grad, attended_t, stats, levels, fars, far_bits)
        for h in range(inner // HEAD_DIM - 1)
    ]
    line.enter(step(weight_terms, attended_t, cotangent, inner, 0, 1, pieces))
    line.meet(rows)
    mixed.advance()
    dquery, dkv, query_first, query_second, *away = step(
        backward_last, earlier, query, grad, attended_t, stats, tokens, levels, fars, far_bits, pieces
    )
    line.enter(query_first)
    backs = [exchange(piece, "seq", d) for d, piece in enumerate(away, 2)]
    line.meet(rows)
    line.turn(query_second)
    dkey, dvalue, dkv_t = step(
        close_keys, [made[1] for made in earlier] + [dkv], [line.into[2], *backs], far_bits, local_levels
    )
    key_first = step(weight_terms, dkv_t, tokens, inner, 0, 0, pieces)
    line.meet(rows)
    line.turn(key_first)
    line.meet(rows)
    key_second = step(weight_terms, dkv_t, tokens, inner, 0, 1, pieces)
    line.turn(key_second)
    value_first = step(weight_terms, dkv_t, tokens, inner, 1, 0, pieces)
    keep, send = step(project_split, rank, [dquery, dkey, dvalue], [w_query, w_key, w_value], "head")
    line.meet(rows)
    tokens_grad = Scatter([keep, step(relay, send)], "head", step)
    line.turn(value_first)
    mixed = mixed.result()
    value_second = step(weight_terms, dkv_t, tokens, inner, 1, 1, pieces)
    line.meet(rows)
    line.turn(value_second)
    out_grad = line.output(0, pieces)
    line.meet(rows)
    tokens_grad.advance()
    line.leave()
    line.meet(rows)
    query_grad = line.output(2, pieces)
    line.leave()
    key_grad = line.output(4, pieces)
    line.leave()
    tokens_grad = tokens_grad.result()
    value_grad = line.output(6, pieces)
    return mixed, tokens_grad, query_grad, key_grad, value_grad, out_grad


def solution(mesh):
    return jax.shard_map(
        per_device,
        mesh=mesh,
        in_specs=(
            P(("groups", "seq"), None),
            P(None, "head"),
            P(None, "head"),
            P(None, "head"),
            P(None, "head"),
            P(("groups", "seq"), None),
        ),
        out_specs=(
            P(("groups", "seq"), "head"),
            P(("groups", "seq"), "head"),
            P("groups", "head"),
            P("groups", "head"),
            P("groups", "head"),
            P("groups", "head"),
        ),
        check_vma=False,
    )
```

```python
import functools
import math

import jax
import jax.numpy as jnp
from jax import lax
from jax.experimental import pallas as pl
from jax.experimental.pallas import tpu as pltpu
from jax.sharding import PartitionSpec as P

HEAD_DIM = 128
BLOCK = 128
BF16 = jnp.bfloat16
F32 = jnp.float32
MIB = 1024 * 1024

NN = (((1,), (0,)), ((), ()))
NT = (((1,), (1,)), ((), ()))
TN = (((0,), (0,)), ((), ()))


def dot(left, right, dims=NN):
    return lax.dot_general(left, right, dims, preferred_element_type=F32)


def params(mib):
    return pltpu.CompilerParams(vmem_limit_bytes=mib * MIB)


def cost(microseconds):
    return pl.CostEstimate(flops=int(microseconds * 1150e6) + 1, bytes_accessed=1, transcendentals=0)


def run(body, ready, after=(), in_specs=None, **options):
    count, extra = len(ready), len(after)

    def kernel(*refs):
        body(*refs[:count], *refs[count + extra :])

    in_specs = in_specs or [pl.BlockSpec(memory_space=pltpu.VMEM)] * count
    in_specs = in_specs + [pl.BlockSpec(memory_space=pl.ANY)] * extra
    return pl.pallas_call(kernel, in_specs=in_specs, **options)(*ready, *after)


def shape(rows, cols, dtype=BF16):
    return jax.ShapeDtypeStruct((rows, cols), dtype)


def whole(rows, cols):
    return pl.BlockSpec((rows, cols), lambda *_: (0, 0))


def pool_matrix(rows):
    row = lax.broadcasted_iota(jnp.int32, (rows // 2, rows), 0)
    col = lax.broadcasted_iota(jnp.int32, (rows // 2, rows), 1)
    return jnp.where(jnp.right_shift(col, 1) == row, 0.5, 0.0).astype(BF16)


def spread_matrix(rows, step_bits, offset, cols, weight):
    row = lax.broadcasted_iota(jnp.int32, (rows, cols), 0) + offset
    col = lax.broadcasted_iota(jnp.int32, (rows, cols), 1)
    return jnp.where(jnp.right_shift(row, step_bits) == col, weight, 0.0).astype(BF16)


def key_value_body(local_levels, far_levels, parts, tok_hbm, wk_hbm, wv_hbm, *refs):
    out_hbm = refs[:local_levels]
    far = refs[local_levels : local_levels + far_levels]
    refs = refs[local_levels + far_levels :]
    tok_ref, wk_ref, wv_ref = refs[:3]
    levels = refs[3 : 3 + local_levels]
    in_sems, out_sems = refs[3 + local_levels :]
    part = tok_ref.shape[0] // parts

    def fetch(source, target, i):
        copy = pltpu.make_async_copy(source, target, in_sems.at[i])
        copy.start()
        return copy

    def flush(i):
        copy = pltpu.make_async_copy(levels[i], out_hbm[i], out_sems.at[i])
        copy.start()
        return copy

    weights = [fetch(wk_hbm, wk_ref, 0), fetch(wv_hbm, wv_ref, 1)]
    tiles = []
    for p in range(parts):
        rows = pl.ds(p * part, part)
        tiles.append(fetch(tok_hbm.at[rows], tok_ref.at[rows], 2 + p))
    for copy in weights:
        copy.wait()
    for p in range(parts):
        tiles[p].wait()
        here = slice(p * part, (p + 1) * part)
        x = tok_ref[here, :]
        both = jnp.concatenate([dot(x, wk_ref[...]), dot(x, wv_ref[...])], axis=1)
        levels[0][here, :] = both.astype(BF16)
    flushes = [flush(0)]
    pool = pool_matrix(part)
    for i in range(1, local_levels):
        source = levels[i - 1]
        for low in range(0, source.shape[0], part):
            mean = dot(pool, source[low : low + part, :])
            levels[i][low // 2 : (low + part) // 2, :] = mean.astype(BF16)
        flushes.append(flush(i))
    rows = dot(pool, levels[-1][...]).astype(BF16)
    for i in range(far_levels):
        if i:
            rows = dot(pool_matrix(rows.shape[0]), rows).astype(BF16)
        far[i][...] = rows
    for copy in flushes:
        copy.wait()


def key_value(tokens, w_key, w_value, local_levels, far_levels, after):
    tok_rows, width = tokens.shape
    inner = w_key.shape[1]
    parts = tok_rows // (2 * BLOCK)
    held = [(tok_rows >> i, 2 * inner) for i in range(local_levels)]
    tops = [(BLOCK >> i, 2 * inner) for i in range(far_levels)]
    return run(
        functools.partial(key_value_body, local_levels, far_levels, parts),
        [tokens, w_key, w_value],
        after,
        in_specs=[pl.BlockSpec(memory_space=pl.ANY)] * 3,
        out_specs=[pl.BlockSpec(memory_space=pl.ANY)] * len(held)
        + [pl.BlockSpec(memory_space=pltpu.VMEM)] * len(tops),
        out_shape=[shape(*dims) for dims in held + tops],
        scratch_shapes=[pltpu.VMEM((tok_rows, width), BF16)]
        + [pltpu.VMEM((width, inner), BF16)] * 2
        + [pltpu.VMEM(dims, BF16) for dims in held]
        + [pltpu.SemaphoreType.DMA((parts + 2,)), pltpu.SemaphoreType.DMA((len(held),))],
        compiler_params=params(56),
        cost_estimate=cost(5.0),
    )


def project_body(left_ref, weight_ref, out_ref):
    out_ref[...] = dot(left_ref[...], weight_ref[...]).astype(BF16)


def project(left, weight, after):
    tok_rows, width = left.shape
    inner = weight.shape[1]
    return run(
        project_body,
        [left, weight],
        after,
        out_shape=shape(tok_rows, inner),
        compiler_params=params(4),
        cost_estimate=cost(0.7),
    )


class KeySet:
    def __init__(self, far_rows, far_bits, local_levels):
        mids = local_levels - 1
        self.sizes = [2 * BLOCK] + [BLOCK] * mids + list(far_rows)
        self.bounds = [sum(self.sizes[:i]) for i in range(len(self.sizes) + 1)]
        steps = [0] + list(range(1, local_levels)) + [local_levels + b for b in far_bits]
        self.biases = [float(step) for step in steps]
        self.mids = mids
        self.far_start = self.bounds[1 + mids]
        self.factor = math.log2(math.e) / math.sqrt(HEAD_DIM)

    def here(self, m):
        return pl.ds(pl.multiple_of(m * 2 * BLOCK, 2 * BLOCK), 2 * BLOCK)

    def seats(self, m):
        for i in range(self.mids):
            sibling = jnp.bitwise_xor(jnp.right_shift(m, i), 1)
            yield pl.ds(pl.multiple_of(sibling * BLOCK, BLOCK), BLOCK)

    def near(self, m, level_refs, cols):
        rows = [level_refs[0][self.here(m), cols]]
        rows += [ref[seat, cols] for ref, seat in zip(level_refs[1:], self.seats(m))]
        return rows

    def far(self, far_refs, cols):
        return [ref[:, cols] for ref in far_refs]

    def pieces(self, array, first=0, count=None):
        base = self.bounds[first]
        ends = self.bounds[first:] if count is None else self.bounds[first : first + count + 1]
        return [array[a - base : b - base] for a, b in zip(ends, ends[1:])]

    def top(self, pieces, first=0):
        tops = [
            jnp.max(piece, axis=0, keepdims=True) * self.factor + bias
            for piece, bias in zip(pieces, self.biases[first:])
        ]
        return functools.reduce(jnp.maximum, tops)

    def powers(self, pieces, top, first=0):
        return jnp.concatenate(
            [
                jnp.exp2(piece * self.factor + (bias - top))
                for piece, bias in zip(pieces, self.biases[first:])
            ],
            axis=0,
        )


def head_columns(h, inner):
    low = h * HEAD_DIM
    return slice(low, low + HEAD_DIM), slice(inner + low, inner + low + HEAD_DIM)


def near_body(local_levels, q_ref, *refs):
    level_refs = refs[:local_levels]
    power_ref, stat_ref = refs[local_levels:]
    tok_rows, inner = q_ref.shape
    heads = inner // HEAD_DIM
    keyset = KeySet([], [], local_levels)
    rows = keyset.far_start

    def step(m, carry):
        here = keyset.here(m)
        for h in range(heads):
            cols, _ = head_columns(h, inner)
            keys = jnp.concatenate(keyset.near(m, level_refs, cols), axis=0)
            pieces = keyset.pieces(dot(keys, q_ref[here, cols], NT))
            top = keyset.top(pieces)
            powers = keyset.powers(pieces, top)
            stat_ref[h : h + 1, here] = top
            stat_ref[heads + h : heads + h + 1, here] = jnp.sum(powers, axis=0, keepdims=True)
            power_ref[pl.ds(pl.multiple_of((m * heads + h) * rows, rows), rows), :] = powers
        return carry

    lax.fori_loop(0, tok_rows // (2 * BLOCK), step, 0)


def near_powers(query, levels, after):
    tok_rows, inner = query.shape
    heads = inner // HEAD_DIM
    pairs = tok_rows // (2 * BLOCK)
    rows = (len(levels) + 1) * BLOCK
    return run(
        functools.partial(near_body, len(levels)),
        [query, *levels],
        after,
        out_shape=[shape(pairs * heads * rows, 2 * BLOCK, F32), shape(2 * heads, tok_rows, F32)],
        compiler_params=params(6),
        cost_estimate=cost(2.3),
    )


def forward_body(local_levels, far_bits, *refs):
    fars = len(far_bits)
    q_ref, power_ref, near_ref = refs[:3]
    level_refs = refs[3 : 3 + local_levels]
    far_refs = refs[3 + local_levels : 3 + local_levels + fars]
    att_ref, att_t_ref, stat_ref = refs[3 + local_levels + fars :]
    tok_rows, inner = q_ref.shape
    heads = inner // HEAD_DIM
    keyset = KeySet([r.shape[0] for r in far_refs], far_bits, local_levels)
    rows = keyset.far_start

    def step(m, carry):
        here = keyset.here(m)
        for h in range(heads):
            cols, vcols = head_columns(h, inner)
            second = heads + h
            keys = jnp.concatenate(keyset.far(far_refs, cols), axis=0)
            values = keyset.near(m, level_refs, vcols) + keyset.far(far_refs, vcols)
            values = jnp.concatenate(values, axis=0)
            first = local_levels
            pieces = keyset.pieces(dot(keys, q_ref[here, cols], NT), first)
            near_top = near_ref[h : h + 1, here]
            top = jnp.maximum(near_top, keyset.top(pieces, first))
            shrink = jnp.exp2(near_top - top)
            powers = keyset.powers(pieces, top, first)
            total = near_ref[second : second + 1, here] * shrink
            total = total + jnp.sum(powers, axis=0, keepdims=True)
            inverse = 1.0 / total
            place = pl.ds(pl.multiple_of((m * heads + h) * rows, rows), rows)
            near_probs = (power_ref[place, :] * (shrink * inverse)).astype(BF16)
            far_probs = (powers * inverse).astype(BF16)
            probs_b = jnp.concatenate([near_probs, far_probs], axis=0)
            att_t = dot(values, probs_b, TN).astype(BF16)
            att_t_ref[cols, here] = att_t
            att_ref[here, cols] = att_t.T
            stat_ref[h : h + 1, here] = top
            stat_ref[second : second + 1, here] = inverse
        return carry

    lax.fori_loop(0, tok_rows // (2 * BLOCK), step, 0)


def forward(query, powers, near, levels, fars, far_bits, after):
    tok_rows, inner = query.shape
    heads = inner // HEAD_DIM
    set_rows = (len(levels) + 1) * BLOCK + sum(f.shape[0] for f in fars)
    return run(
        functools.partial(forward_body, len(levels), far_bits),
        [query, powers, near, *levels, *fars],
        after,
        out_shape=[
            shape(tok_rows, inner),
            shape(inner, tok_rows),
            shape(2 * heads, tok_rows, F32),
        ],
        compiler_params=params(6),
        cost_estimate=cost(4.0),
    )


def backward_body(local_levels, far_bits, pieces, *refs):
    mids = local_levels - 1
    fars = len(far_bits)
    q_ref, g_ref, att_t_ref, stat_ref, tok_ref = refs[:5]
    level_refs = refs[5 : 5 + local_levels]
    far_refs = refs[5 + local_levels : 5 + local_levels + fars]
    outs = refs[5 + local_levels + fars :]
    dq_ref, dkv_ref = outs[:2]
    term_refs = outs[2 : 2 + pieces]
    dfar_refs = outs[2 + pieces : 2 + pieces + fars]
    dmid_refs = outs[2 + pieces + fars : 2 + pieces + fars + mids]
    dq_t_ref, acc_ref = outs[-2:]
    tok_rows, inner = q_ref.shape
    heads = inner // HEAD_DIM
    score_scale = 1.0 / math.sqrt(HEAD_DIM)
    keyset = KeySet([r.shape[0] for r in far_refs], far_bits, local_levels)

    for ref in (*dmid_refs, acc_ref):
        ref[...] = jnp.zeros_like(ref)

    def step(m, carry):
        here = keyset.here(m)
        for h in range(heads):
            cols, vcols = head_columns(h, inner)
            keys, values = (
                jnp.concatenate(keyset.near(m, level_refs, c) + keyset.far(far_refs, c), axis=0)
                for c in (cols, vcols)
            )
            q = q_ref[here, cols]
            g = g_ref[here, cols]
            top = stat_ref[h : h + 1, here]
            inverse = stat_ref[heads + h : heads + h + 1, here]
            probs = keyset.powers(keyset.pieces(dot(keys, q, NT)), top) * inverse
            att_t = att_t_ref[cols, here].astype(F32)
            delta = jnp.sum(g.T.astype(F32) * att_t, axis=0, keepdims=True)
            grads = (probs * (dot(values, g, NT) - delta) * score_scale).astype(BF16)
            dq_t = dot(keys, grads, TN).astype(BF16)
            dq_t_ref[cols, here] = dq_t
            dq_ref[here, cols] = dq_t.T
            for part, place in ((dot(grads, q), cols), (dot(probs.astype(BF16), g), vcols)):
                own, *sides = keyset.pieces(part)
                dkv_ref[here, place] = own
                for ref, seat, side in zip(dmid_refs, keyset.seats(m), sides):
                    ref[seat, place] += side
                acc_ref[:, place] += part[keyset.far_start :]
        return carry

    lax.fori_loop(0, tok_rows // (2 * BLOCK), step, 0)
    width = term_refs[-1].shape[0]
    low = 0
    for ref in dfar_refs:
        ref[...] = acc_ref[low : low + ref.shape[0]].astype(BF16)
        low += ref.shape[0]
    for i, ref in enumerate(term_refs):
        part = dot(dq_t_ref[...], tok_ref[:, i * width : (i + 1) * width])
        ref[...] = part.astype(BF16).T
    fan = spread_matrix(2 * BLOCK, 1, 0, BLOCK, 0.5)
    targets = (dkv_ref, *dmid_refs)
    for i in reversed(range(mids)):
        for t in range(dmid_refs[i].shape[0] // BLOCK):
            part = dmid_refs[i][t * BLOCK : (t + 1) * BLOCK, :]
            high = part.astype(BF16)
            low = (part - high.astype(F32)).astype(BF16)
            rows = slice(2 * t * BLOCK, 2 * (t + 1) * BLOCK)
            targets[i][rows, :] += dot(fan, high) + dot(fan, low)


def backward(query, grad, attended_t, stats, tokens, levels, fars, far_bits, pieces, after):
    tok_rows, inner = query.shape
    far_rows = sum(f.shape[0] for f in fars)
    set_rows = (len(levels) + 1) * BLOCK + far_rows
    return run(
        functools.partial(backward_body, len(levels), far_bits, pieces),
        [query, grad, attended_t, stats, tokens, *levels, *fars],
        after,
        out_shape=[shape(tok_rows, inner), shape(tok_rows, 2 * inner, F32)]
        + [shape(tokens.shape[1] // pieces, inner)] * pieces
        + [shape(*f.shape) for f in fars],
        scratch_shapes=[pltpu.VMEM(level.shape, F32) for level in levels[1:]]
        + [pltpu.VMEM((inner, tok_rows), BF16), pltpu.VMEM((far_rows, 2 * inner), F32)],
        compiler_params=params(10),
        cost_estimate=cost(8.0),
    )


def term_body(which, low, left_ref, right_ref, out_ref):
    width, inner = out_ref.shape
    left = left_ref[which * inner : (which + 1) * inner, :]
    out_ref[...] = dot(left, right_ref[:, low : low + width]).astype(BF16).T


def weight_terms(left_t, right, inner, which, part, parts, after):
    tok_rows = left_t.shape[1]
    width = right.shape[1] // parts
    return run(
        functools.partial(term_body, which, part * width),
        [left_t, right],
        after,
        out_shape=shape(width, inner),
        compiler_params=params(3),
        cost_estimate=cost(0.2),
    )


def close_body(local_levels, far_bits, dkv_ref, *refs):
    backs = [ref[...] for ref in refs[: len(far_bits)]]
    dk_ref, dv_ref, dkv_t_ref = refs[len(far_bits) :]
    inner = dk_ref.shape[1]
    tile = 2 * BLOCK
    for t in range(dkv_ref.shape[0] // tile):
        here = slice(t * tile, (t + 1) * tile)
        total = dkv_ref[here, :]
        for back, bit in zip(backs, far_bits):
            weight = 0.5 ** (local_levels + bit)
            fan = spread_matrix(tile, local_levels + bit, t * tile, back.shape[0], weight)
            total = total + dot(fan, back)
        final = total.astype(BF16)
        dk_ref[here, :] = final[:, :inner]
        dv_ref[here, :] = final[:, inner:]
        dkv_t_ref[:, here] = final.T


def close_keys(dkv, backs, far_bits, local_levels, after):
    tok_rows, double = dkv.shape
    inner = double // 2
    return run(
        functools.partial(close_body, local_levels, far_bits),
        [dkv, *backs],
        after,
        out_shape=[shape(tok_rows, inner), shape(tok_rows, inner), shape(double, tok_rows)],
        compiler_params=params(5),
        cost_estimate=cost(0.2),
    )


def split_body(count, parts, rank_ref, *refs):
    lefts, weights = refs[:count], refs[count : 2 * count]
    outs = refs[2 * count :]
    width = weights[0].shape[0] // parts
    for r in range(parts):
        owner = jnp.bitwise_xor(rank_ref[0], r)
        rows = pl.ds(pl.multiple_of(owner * width, width), width)
        total = None
        for left, weight in zip(lefts, weights):
            product = dot(left[...], weight[rows, :], NT)
            total = product if total is None else total + product
        place = r // 2 * width
        outs[r % 2][:, place : place + width] = total.astype(BF16)


def project_split(rank, lefts, weights, axis, after):
    count = len(lefts)
    parts = lax.axis_size(axis)
    tok_rows, inner = lefts[0].shape
    width = weights[0].shape[0]
    return run(
        functools.partial(split_body, count, parts),
        [rank, *lefts, *weights],
        after,
        in_specs=[pl.BlockSpec(memory_space=pltpu.SMEM)]
        + [pl.BlockSpec(memory_space=pltpu.VMEM)] * (2 * count),
        out_shape=[shape(tok_rows, width // 2)] * 2,
        compiler_params=params(5),
        cost_estimate=cost(1.0),
    )


def exchange(block, axis, distance):
    count = lax.axis_size(axis)
    return lax.ppermute(block, axis, [(i, i ^ distance) for i in range(count)])


def add(left, right):
    return (left.astype(F32) + right.astype(F32)).astype(BF16)


def term_half_body(chunk_ref, into_ref, out_ref):
    rows = slice(0, out_ref.shape[0])
    out_ref[...] = (chunk_ref[rows, :].astype(F32) + into_ref[rows, :].astype(F32)).astype(BF16)


def half_sum(chunk, into, rows, weight, after):
    return run(
        term_half_body,
        [chunk, into],
        after,
        out_shape=shape(rows, chunk.shape[1]),
        compiler_params=params(3),
        cost_estimate=cost(weight),
    )


def scatter_body(pieces, keep_ref, into_ref, even_ref, odd_ref):
    width = keep_ref.shape[1] // pieces
    for i in range(pieces):
        here = slice(i * width, (i + 1) * width)
        place = slice(i // 2 * width, (i // 2 + 1) * width)
        total = keep_ref[:, here].astype(F32) + into_ref[:, here].astype(F32)
        (even_ref, odd_ref)[i % 2][:, place] = total.astype(BF16)


def last_body(left_ref, right_ref, token_ref, out_ref):
    token_ref[...] = jnp.zeros_like(token_ref)
    out_ref[...] = (left_ref[...].astype(F32) + right_ref[...].astype(F32)).astype(BF16)


def last_sum(left, right, after):
    return run(
        last_body,
        [left, right],
        after,
        out_shape=[shape(8, 128, F32), shape(*left.shape)],
        compiler_params=params(3),
        cost_estimate=cost(0.9),
    )


def scatter_step(keep, into, pieces, after):
    rows, width = keep.shape
    return run(
        functools.partial(scatter_body, pieces),
        [keep, into],
        after,
        out_shape=[shape(rows, width // 2)] * 2,
        compiler_params=params(4),
        cost_estimate=cost(0.2),
    )


def turn_body(end_ref, half_ref, across_ref, chunk_ref, total_ref, send_ref):
    total = (half_ref[...].astype(F32) + across_ref[...].astype(F32)).astype(BF16)
    total_ref[...] = total

    @pl.when(end_ref[0] == 1)
    def _():
        send_ref[...] = chunk_ref[...]

    @pl.when(end_ref[0] == 0)
    def _():
        send_ref[...] = total


def turn(end, half, across, chunk, weight, after):
    return run(
        turn_body,
        [end, half, across, chunk],
        after,
        in_specs=[pl.BlockSpec(memory_space=pltpu.SMEM)]
        + [pl.BlockSpec(memory_space=pltpu.VMEM)] * 3,
        out_shape=[shape(*half.shape)] * 2,
        compiler_params=params(2),
        cost_estimate=cost(weight),
    )


def output_body(count, end_ref, *refs):
    totals, ends, (token_ref, out_ref) = refs[:count], refs[count : 2 * count], refs[2 * count :]
    token_ref[...] = jnp.zeros_like(token_ref)
    rows = totals[0].shape[0]

    for flag, sources in ((0, totals), (1, ends)):

        @pl.when(end_ref[0] == flag)
        def _():
            for i, ref in enumerate(sources):
                out_ref[i * rows : (i + 1) * rows, :] = ref[...]


def output(end, totals, ends, after):
    count = len(totals)
    rows, width = totals[0].shape
    return run(
        functools.partial(output_body, count),
        [end, *totals, *ends],
        after,
        in_specs=[pl.BlockSpec(memory_space=pltpu.SMEM)]
        + [pl.BlockSpec(memory_space=pltpu.VMEM)] * (2 * count),
        out_shape=[shape(8, 128, F32), shape(count * rows, width)],
        compiler_params=params(4),
        cost_estimate=cost(0.9),
    )


def relay_body(source_ref, target_ref):
    target_ref[...] = source_ref[...]


def relay(block, after):
    return run(
        relay_body,
        [block],
        after,
        out_shape=shape(*block.shape),
        compiler_params=params(3),
        cost_estimate=cost(0.2),
    )


class Line:
    lag = 3
    half_weights = (3.0, 3.0, 3.0, 1.0, 1.0, 3.0, 3.0, 0.5)
    turn_weights = (6.0, 1.0, 1.0, 1.0, 4.0, 2.0, 0.5, 0.5)

    def __init__(self, axis, other, end, step):
        self.axis, self.axes, self.step = axis, (axis, other), step
        self.count = lax.axis_size(axis)
        self.end = end
        width = lax.axis_size(other)
        self.across = []
        for place in range(self.count):
            for seat in range(width):
                target = (place, seat ^ 1 if width > 1 else seat)
                if place & 3 in (1, 2):
                    target = (place ^ 3, seat)
                self.across.append((place * width + seat, target[0] * width + target[1]))
        self.chunks, self.into, self.halves, self.crossed, self.totals = [], [], [], [], []

    def enter(self, chunk):
        self.chunks.append(chunk)
        self.into.append(exchange(chunk, self.axis, 1))

    def meet(self, rows):
        k = len(self.halves)
        weight = self.half_weights[k]
        half = self.step(half_sum, self.chunks[k], self.into[k], rows, weight)
        self.halves.append(half)
        self.crossed.append(lax.ppermute(half, self.axes, self.across))

    def turn(self, chunk):
        old = len(self.totals)
        half, crossed = self.halves[old], self.crossed[old]
        weight = self.turn_weights[old]
        total, send = self.step(turn, self.end, half, crossed, chunk, weight)
        self.totals.append(total)
        self.chunks.append(chunk)
        self.into.append(exchange(send, self.axis, 1))

    def leave(self):
        old = len(self.totals)
        half = self.halves[old]
        weight = self.turn_weights[old]
        total = self.step(half_sum, half, self.crossed[old], half.shape[0], weight)
        self.totals.append(total)
        self.into.append(exchange(total, self.axis, 1))

    def output(self, first, count):
        ends = self.into[first + self.lag : first + self.lag + count]
        _, result = self.step(output, self.end, self.totals[first : first + count], ends)
        distance = 4
        while distance < self.count:
            result = add(result, exchange(result, self.axis, distance))
            distance *= 2
        return result


class Scatter:
    def __init__(self, parts, axis, step):
        self.axis, self.step = axis, step
        self.pieces = lax.axis_size(axis) // 2
        self.keep, send = parts
        self.distance = 1
        self.into = exchange(send, axis, 1)

    def advance(self):
        while self.pieces > 1:
            self.keep, send = self.step(scatter_step, self.keep, self.into, self.pieces)
            self.distance *= 2
            self.pieces //= 2
            self.into = exchange(send, self.axis, self.distance)

    def result(self):
        return self.step(last_sum, self.keep, self.into)[1]


def per_device(tokens, w_query, w_key, w_value, w_out, cotangent):
    tok_rows = tokens.shape[0]
    inner = w_query.shape[1]
    local_levels = (tok_rows // BLOCK).bit_length() - 1
    count = lax.axis_size("seq")
    far_levels = count.bit_length() - 1
    far_bits = [d.bit_length() - 1 for d in range(1, count)]

    last = []

    def step(kernel, *operands):
        made = kernel(*operands, list(last))
        last[:] = made[:1] if isinstance(made, (list, tuple)) else [made]
        return made

    place = jnp.bitwise_and(lax.axis_index("seq"), 3)
    end = jnp.reshape((place == 0) | (place == 3), (1,)).astype(jnp.int32)
    rank = jnp.reshape(lax.axis_index("head"), (1,)).astype(jnp.int32)
    parts = key_value(tokens, w_key, w_value, local_levels, far_levels, [end, rank])
    levels, tops = parts[:local_levels], parts[local_levels:]
    fars = [exchange(tops[bit], "seq", d) for d, bit in enumerate(far_bits, 1)]
    query = step(project, tokens, w_query)
    powers, near = step(near_powers, query, levels)
    grad = step(project, cotangent, w_out)
    attended, attended_t, stats = step(forward, query, powers, near, levels, fars, far_bits)

    line = Line("seq", "head", end, step)
    pieces = 2
    rows = tokens.shape[1] // pieces
    line.enter(step(weight_terms, attended_t, cotangent, inner, 0, 0, pieces))
    line.enter(step(weight_terms, attended_t, cotangent, inner, 0, 1, pieces))
    dquery, dkv, query_first, query_second, *away = step(
        backward, query, grad, attended_t, stats, tokens, levels, fars, far_bits, pieces
    )
    backs = [exchange(piece, "seq", d) for d, piece in enumerate(away, 1)]
    line.meet(rows)
    line.meet(rows)
    dkey, dvalue, dkv_t = step(close_keys, dkv, backs, far_bits, local_levels)
    line.enter(step(relay, query_first))
    parts = step(project_split, rank, [attended], [w_out], "head")
    mixed = Scatter(parts, "head", step)
    line.turn(query_second)
    key_first = step(weight_terms, dkv_t, tokens, inner, 0, 0, pieces)
    key_second = step(weight_terms, dkv_t, tokens, inner, 0, 1, pieces)
    keep, send = step(project_split, rank, [dquery, dkey, dvalue], [w_query, w_key, w_value], "head")
    line.meet(rows)
    mixed.advance()
    line.turn(key_first)
    line.meet(rows)
    value_first = step(weight_terms, dkv_t, tokens, inner, 1, 0, pieces)
    line.turn(key_second)
    line.meet(rows)
    tokens_grad = Scatter([keep, step(relay, send)], "head", step)
    line.turn(value_first)
    mixed = mixed.result()
    value_second = step(weight_terms, dkv_t, tokens, inner, 1, 1, pieces)
    line.meet(rows)
    line.turn(value_second)
    out_grad = line.output(0, pieces)
    line.meet(rows)
    tokens_grad.advance()
    line.leave()
    line.meet(rows)
    query_grad = line.output(2, pieces)
    line.leave()
    key_grad = line.output(4, pieces)
    line.leave()
    tokens_grad = tokens_grad.result()
    value_grad = line.output(6, pieces)
    return mixed, tokens_grad, query_grad, key_grad, value_grad, out_grad


def solution(mesh):
    return jax.shard_map(
        per_device,
        mesh=mesh,
        in_specs=(
            P(("groups", "seq"), None),
            P(None, "head"),
            P(None, "head"),
            P(None, "head"),
            P(None, "head"),
            P(("groups", "seq"), None),
        ),
        out_specs=(
            P(("groups", "seq"), "head"),
            P(("groups", "seq"), "head"),
            P("groups", "head"),
            P("groups", "head"),
            P("groups", "head"),
            P("groups", "head"),
        ),
        check_vma=False,
    )
```

```python
import functools
import math

import jax
import jax.numpy as jnp
from jax import lax
from jax.experimental import pallas as pl
from jax.experimental.pallas import tpu as pltpu
from jax.sharding import PartitionSpec as P

HEAD_DIM = 128
BLOCK = 128
BF16 = jnp.bfloat16
F32 = jnp.float32
MIB = 1024 * 1024

NN = (((1,), (0,)), ((), ()))
NT = (((1,), (1,)), ((), ()))
TN = (((0,), (0,)), ((), ()))


def dot(left, right, dims=NN):
    return lax.dot_general(left, right, dims, preferred_element_type=F32)


def params(mib):
    return pltpu.CompilerParams(vmem_limit_bytes=mib * MIB)


def cost(microseconds):
    return pl.CostEstimate(flops=int(microseconds * 1150e6) + 1, bytes_accessed=1, transcendentals=0)


def run(body, ready, after=(), in_specs=None, **options):
    count, extra = len(ready), len(after)

    def kernel(*refs):
        body(*refs[:count], *refs[count + extra :])

    in_specs = in_specs or [pl.BlockSpec(memory_space=pltpu.VMEM)] * count
    in_specs = in_specs + [pl.BlockSpec(memory_space=pl.ANY)] * extra
    return pl.pallas_call(kernel, in_specs=in_specs, **options)(*ready, *after)


def shape(rows, cols, dtype=BF16):
    return jax.ShapeDtypeStruct((rows, cols), dtype)


def whole(rows, cols):
    return pl.BlockSpec((rows, cols), lambda *_: (0, 0))


def pool_matrix(rows):
    row = lax.broadcasted_iota(jnp.int32, (rows // 2, rows), 0)
    col = lax.broadcasted_iota(jnp.int32, (rows // 2, rows), 1)
    return jnp.where(jnp.right_shift(col, 1) == row, 0.5, 0.0).astype(BF16)


def spread_matrix(rows, step_bits, offset, cols, weight):
    row = lax.broadcasted_iota(jnp.int32, (rows, cols), 0) + offset
    col = lax.broadcasted_iota(jnp.int32, (rows, cols), 1)
    return jnp.where(jnp.right_shift(row, step_bits) == col, weight, 0.0).astype(BF16)


def key_value_body(local_levels, far_levels, parts, tok_hbm, wk_hbm, wv_hbm, *refs):
    out_hbm = refs[:local_levels]
    far = refs[local_levels : local_levels + far_levels]
    refs = refs[local_levels + far_levels :]
    tok_ref, wk_ref, wv_ref = refs[:3]
    levels = refs[3 : 3 + local_levels]
    in_sems, out_sems = refs[3 + local_levels :]
    part = tok_ref.shape[0] // parts

    def fetch(source, target, i):
        copy = pltpu.make_async_copy(source, target, in_sems.at[i])
        copy.start()
        return copy

    def flush(i):
        copy = pltpu.make_async_copy(levels[i], out_hbm[i], out_sems.at[i])
        copy.start()
        return copy

    weights = [fetch(wk_hbm, wk_ref, 0), fetch(wv_hbm, wv_ref, 1)]
    tiles = []
    for p in range(parts):
        rows = pl.ds(p * part, part)
        tiles.append(fetch(tok_hbm.at[rows], tok_ref.at[rows], 2 + p))
    for copy in weights:
        copy.wait()
    for p in range(parts):
        tiles[p].wait()
        here = slice(p * part, (p + 1) * part)
        x = tok_ref[here, :]
        both = jnp.concatenate([dot(x, wk_ref[...]), dot(x, wv_ref[...])], axis=1)
        levels[0][here, :] = both.astype(BF16)
    flushes = [flush(0)]
    pool = pool_matrix(part)
    for i in range(1, local_levels):
        source = levels[i - 1]
        for low in range(0, source.shape[0], part):
            mean = dot(pool, source[low : low + part, :])
            levels[i][low // 2 : (low + part) // 2, :] = mean.astype(BF16)
        flushes.append(flush(i))
    rows = dot(pool, levels[-1][...]).astype(BF16)
    for i in range(far_levels):
        if i:
            rows = dot(pool_matrix(rows.shape[0]), rows).astype(BF16)
        far[i][...] = rows
    for copy in flushes:
        copy.wait()


def key_value(tokens, w_key, w_value, local_levels, far_levels, after):
    tok_rows, width = tokens.shape
    inner = w_key.shape[1]
    parts = tok_rows // (2 * BLOCK)
    held = [(tok_rows >> i, 2 * inner) for i in range(local_levels)]
    tops = [(BLOCK >> i, 2 * inner) for i in range(far_levels)]
    return run(
        functools.partial(key_value_body, local_levels, far_levels, parts),
        [tokens, w_key, w_value],
        after,
        in_specs=[pl.BlockSpec(memory_space=pl.ANY)] * 3,
        out_specs=[pl.BlockSpec(memory_space=pl.ANY)] * len(held)
        + [pl.BlockSpec(memory_space=pltpu.VMEM)] * len(tops),
        out_shape=[shape(*dims) for dims in held + tops],
        scratch_shapes=[pltpu.VMEM((tok_rows, width), BF16)]
        + [pltpu.VMEM((width, inner), BF16)] * 2
        + [pltpu.VMEM(dims, BF16) for dims in held]
        + [pltpu.SemaphoreType.DMA((parts + 2,)), pltpu.SemaphoreType.DMA((len(held),))],
        compiler_params=params(56),
        cost_estimate=cost(5.0),
    )


def project_body(left_ref, weight_ref, out_ref):
    out_ref[...] = dot(left_ref[...], weight_ref[...]).astype(BF16)


def project(left, weight, after):
    tok_rows, width = left.shape
    inner = weight.shape[1]
    return run(
        project_body,
        [left, weight],
        after,
        out_shape=shape(tok_rows, inner),
        compiler_params=params(4),
        cost_estimate=cost(0.7),
    )


class KeySet:
    def __init__(self, far_rows, far_bits, local_levels):
        mids = local_levels - 1
        self.sizes = [2 * BLOCK] + [BLOCK] * mids + list(far_rows)
        self.bounds = [sum(self.sizes[:i]) for i in range(len(self.sizes) + 1)]
        steps = [0] + list(range(1, local_levels)) + [local_levels + b for b in far_bits]
        self.biases = [float(step) for step in steps]
        self.mids = mids
        self.far_start = self.bounds[1 + mids]
        self.factor = math.log2(math.e) / math.sqrt(HEAD_DIM)

    def here(self, m):
        return pl.ds(pl.multiple_of(m * 2 * BLOCK, 2 * BLOCK), 2 * BLOCK)

    def seats(self, m):
        for i in range(self.mids):
            sibling = jnp.bitwise_xor(jnp.right_shift(m, i), 1)
            yield pl.ds(pl.multiple_of(sibling * BLOCK, BLOCK), BLOCK)

    def near(self, m, level_refs, cols):
        rows = [level_refs[0][self.here(m), cols]]
        rows += [ref[seat, cols] for ref, seat in zip(level_refs[1:], self.seats(m))]
        return rows

    def far(self, far_refs, cols):
        return [ref[:, cols] for ref in far_refs]

    def pieces(self, array, first=0, count=None):
        base = self.bounds[first]
        ends = self.bounds[first:] if count is None else self.bounds[first : first + count + 1]
        return [array[a - base : b - base] for a, b in zip(ends, ends[1:])]

    def top(self, pieces, first=0):
        tops = [
            jnp.max(piece, axis=0, keepdims=True) * self.factor + bias
            for piece, bias in zip(pieces, self.biases[first:])
        ]
        return functools.reduce(jnp.maximum, tops)

    def powers(self, pieces, top, first=0):
        return jnp.concatenate(
            [
                jnp.exp2(piece * self.factor + (bias - top))
                for piece, bias in zip(pieces, self.biases[first:])
            ],
            axis=0,
        )


def head_columns(h, inner):
    low = h * HEAD_DIM
    return slice(low, low + HEAD_DIM), slice(inner + low, inner + low + HEAD_DIM)


def near_body(local_levels, q_ref, *refs):
    level_refs = refs[:local_levels]
    power_ref, stat_ref = refs[local_levels:]
    tok_rows, inner = q_ref.shape
    heads = inner // HEAD_DIM
    keyset = KeySet([], [], local_levels)
    rows = keyset.far_start

    def step(m, carry):
        here = keyset.here(m)
        for h in range(heads):
            cols, _ = head_columns(h, inner)
            keys = jnp.concatenate(keyset.near(m, level_refs, cols), axis=0)
            pieces = keyset.pieces(dot(keys, q_ref[here, cols], NT))
            top = keyset.top(pieces)
            powers = keyset.powers(pieces, top)
            stat_ref[h : h + 1, here] = top
            stat_ref[heads + h : heads + h + 1, here] = jnp.sum(powers, axis=0, keepdims=True)
            power_ref[pl.ds(pl.multiple_of((m * heads + h) * rows, rows), rows), :] = powers
        return carry

    lax.fori_loop(0, tok_rows // (2 * BLOCK), step, 0)


def near_powers(query, levels, after):
    tok_rows, inner = query.shape
    heads = inner // HEAD_DIM
    pairs = tok_rows // (2 * BLOCK)
    rows = (len(levels) + 1) * BLOCK
    return run(
        functools.partial(near_body, len(levels)),
        [query, *levels],
        after,
        out_shape=[shape(pairs * heads * rows, 2 * BLOCK, F32), shape(2 * heads, tok_rows, F32)],
        compiler_params=params(6),
        cost_estimate=cost(2.3),
    )


def forward_body(local_levels, far_bits, *refs):
    fars = len(far_bits)
    q_ref, power_ref, near_ref = refs[:3]
    level_refs = refs[3 : 3 + local_levels]
    far_refs = refs[3 + local_levels : 3 + local_levels + fars]
    att_ref, att_t_ref, stat_ref = refs[3 + local_levels + fars :]
    tok_rows, inner = q_ref.shape
    heads = inner // HEAD_DIM
    keyset = KeySet([r.shape[0] for r in far_refs], far_bits, local_levels)
    rows = keyset.far_start

    def step(m, carry):
        here = keyset.here(m)
        for h in range(heads):
            cols, vcols = head_columns(h, inner)
            second = heads + h
            keys = jnp.concatenate(keyset.far(far_refs, cols), axis=0)
            values = keyset.near(m, level_refs, vcols) + keyset.far(far_refs, vcols)
            values = jnp.concatenate(values, axis=0)
            first = local_levels
            pieces = keyset.pieces(dot(keys, q_ref[here, cols], NT), first)
            near_top = near_ref[h : h + 1, here]
            top = jnp.maximum(near_top, keyset.top(pieces, first))
            shrink = jnp.exp2(near_top - top)
            powers = keyset.powers(pieces, top, first)
            total = near_ref[second : second + 1, here] * shrink
            total = total + jnp.sum(powers, axis=0, keepdims=True)
            inverse = 1.0 / total
            place = pl.ds(pl.multiple_of((m * heads + h) * rows, rows), rows)
            near_probs = (power_ref[place, :] * (shrink * inverse)).astype(BF16)
            far_probs = (powers * inverse).astype(BF16)
            probs_b = jnp.concatenate([near_probs, far_probs], axis=0)
            att_t = dot(values, probs_b, TN).astype(BF16)
            att_t_ref[cols, here] = att_t
            att_ref[here, cols] = att_t.T
            stat_ref[h : h + 1, here] = top
            stat_ref[second : second + 1, here] = inverse
        return carry

    lax.fori_loop(0, tok_rows // (2 * BLOCK), step, 0)


def forward(query, powers, near, levels, fars, far_bits, after):
    tok_rows, inner = query.shape
    heads = inner // HEAD_DIM
    set_rows = (len(levels) + 1) * BLOCK + sum(f.shape[0] for f in fars)
    return run(
        functools.partial(forward_body, len(levels), far_bits),
        [query, powers, near, *levels, *fars],
        after,
        out_shape=[
            shape(tok_rows, inner),
            shape(inner, tok_rows),
            shape(2 * heads, tok_rows, F32),
        ],
        compiler_params=params(6),
        cost_estimate=cost(4.0),
    )


def backward_body(local_levels, far_bits, pieces, *refs):
    mids = local_levels - 1
    fars = len(far_bits)
    q_ref, g_ref, att_t_ref, stat_ref, tok_ref = refs[:5]
    level_refs = refs[5 : 5 + local_levels]
    far_refs = refs[5 + local_levels : 5 + local_levels + fars]
    outs = refs[5 + local_levels + fars :]
    dq_ref, dkv_ref = outs[:2]
    term_refs = outs[2 : 2 + pieces]
    dfar_refs = outs[2 + pieces : 2 + pieces + fars]
    dmid_refs = outs[2 + pieces + fars : 2 + pieces + fars + mids]
    dq_t_ref, acc_ref = outs[-2:]
    tok_rows, inner = q_ref.shape
    heads = inner // HEAD_DIM
    score_scale = 1.0 / math.sqrt(HEAD_DIM)
    keyset = KeySet([r.shape[0] for r in far_refs], far_bits, local_levels)

    for ref in (*dmid_refs, acc_ref):
        ref[...] = jnp.zeros_like(ref)

    def step(m, carry):
        here = keyset.here(m)
        for h in range(heads):
            cols, vcols = head_columns(h, inner)
            keys, values = (
                jnp.concatenate(keyset.near(m, level_refs, c) + keyset.far(far_refs, c), axis=0)
                for c in (cols, vcols)
            )
            q = q_ref[here, cols]
            g = g_ref[here, cols]
            top = stat_ref[h : h + 1, here]
            inverse = stat_ref[heads + h : heads + h + 1, here]
            probs = keyset.powers(keyset.pieces(dot(keys, q, NT)), top) * inverse
            att_t = att_t_ref[cols, here].astype(F32)
            delta = jnp.sum(g.T.astype(F32) * att_t, axis=0, keepdims=True)
            grads = (probs * (dot(values, g, NT) - delta) * score_scale).astype(BF16)
            dq_t = dot(keys, grads, TN).astype(BF16)
            dq_t_ref[cols, here] = dq_t
            dq_ref[here, cols] = dq_t.T
            for part, place in ((dot(grads, q), cols), (dot(probs.astype(BF16), g), vcols)):
                own, *sides = keyset.pieces(part)
                dkv_ref[here, place] = own
                for ref, seat, side in zip(dmid_refs, keyset.seats(m), sides):
                    ref[seat, place] += side
                acc_ref[:, place] += part[keyset.far_start :]
        return carry

    lax.fori_loop(0, tok_rows // (2 * BLOCK), step, 0)
    width = term_refs[-1].shape[0]
    low = 0
    for ref in dfar_refs:
        ref[...] = acc_ref[low : low + ref.shape[0]].astype(BF16)
        low += ref.shape[0]
    for i, ref in enumerate(term_refs):
        part = dot(dq_t_ref[...], tok_ref[:, i * width : (i + 1) * width])
        ref[...] = part.astype(BF16).T
    fan = spread_matrix(2 * BLOCK, 1, 0, BLOCK, 0.5)
    targets = (dkv_ref, *dmid_refs)
    for i in reversed(range(mids)):
        for t in range(dmid_refs[i].shape[0] // BLOCK):
            part = dmid_refs[i][t * BLOCK : (t + 1) * BLOCK, :]
            high = part.astype(BF16)
            low = (part - high.astype(F32)).astype(BF16)
            rows = slice(2 * t * BLOCK, 2 * (t + 1) * BLOCK)
            targets[i][rows, :] += dot(fan, high) + dot(fan, low)


def backward(query, grad, attended_t, stats, tokens, levels, fars, far_bits, pieces, after):
    tok_rows, inner = query.shape
    far_rows = sum(f.shape[0] for f in fars)
    set_rows = (len(levels) + 1) * BLOCK + far_rows
    return run(
        functools.partial(backward_body, len(levels), far_bits, pieces),
        [query, grad, attended_t, stats, tokens, *levels, *fars],
        after,
        out_shape=[shape(tok_rows, inner), shape(tok_rows, 2 * inner, F32)]
        + [shape(tokens.shape[1] // pieces, inner)] * pieces
        + [shape(*f.shape) for f in fars],
        scratch_shapes=[pltpu.VMEM(level.shape, F32) for level in levels[1:]]
        + [pltpu.VMEM((inner, tok_rows), BF16), pltpu.VMEM((far_rows, 2 * inner), F32)],
        compiler_params=params(10),
        cost_estimate=cost(8.0),
    )


def term_body(which, low, left_ref, right_ref, out_ref):
    width, inner = out_ref.shape
    left = left_ref[which * inner : (which + 1) * inner, :]
    out_ref[...] = dot(left, right_ref[:, low : low + width]).astype(BF16).T


def weight_terms(left_t, right, inner, which, part, parts, after):
    tok_rows = left_t.shape[1]
    width = right.shape[1] // parts
    return run(
        functools.partial(term_body, which, part * width),
        [left_t, right],
        after,
        out_shape=shape(width, inner),
        compiler_params=params(3),
        cost_estimate=cost(0.2),
    )


def close_body(local_levels, far_bits, dkv_ref, *refs):
    backs = [ref[...] for ref in refs[: len(far_bits)]]
    dk_ref, dv_ref, dkv_t_ref = refs[len(far_bits) :]
    inner = dk_ref.shape[1]
    tile = 2 * BLOCK
    for t in range(dkv_ref.shape[0] // tile):
        here = slice(t * tile, (t + 1) * tile)
        total = dkv_ref[here, :]
        for back, bit in zip(backs, far_bits):
            weight = 0.5 ** (local_levels + bit)
            fan = spread_matrix(tile, local_levels + bit, t * tile, back.shape[0], weight)
            total = total + dot(fan, back)
        final = total.astype(BF16)
        dk_ref[here, :] = final[:, :inner]
        dv_ref[here, :] = final[:, inner:]
        dkv_t_ref[:, here] = final.T


def close_keys(dkv, backs, far_bits, local_levels, after):
    tok_rows, double = dkv.shape
    inner = double // 2
    return run(
        functools.partial(close_body, local_levels, far_bits),
        [dkv, *backs],
        after,
        out_shape=[shape(tok_rows, inner), shape(tok_rows, inner), shape(double, tok_rows)],
        compiler_params=params(5),
        cost_estimate=cost(0.2),
    )


def split_body(count, parts, rank_ref, *refs):
    lefts, weights = refs[:count], refs[count : 2 * count]
    outs = refs[2 * count :]
    width = weights[0].shape[0] // parts
    for r in range(parts):
        owner = jnp.bitwise_xor(rank_ref[0], r)
        rows = pl.ds(pl.multiple_of(owner * width, width), width)
        total = None
        for left, weight in zip(lefts, weights):
            product = dot(left[...], weight[rows, :], NT)
            total = product if total is None else total + product
        place = r // 2 * width
        outs[r % 2][:, place : place + width] = total.astype(BF16)


def project_split(rank, lefts, weights, axis, after):
    count = len(lefts)
    parts = lax.axis_size(axis)
    tok_rows, inner = lefts[0].shape
    width = weights[0].shape[0]
    return run(
        functools.partial(split_body, count, parts),
        [rank, *lefts, *weights],
        after,
        in_specs=[pl.BlockSpec(memory_space=pltpu.SMEM)]
        + [pl.BlockSpec(memory_space=pltpu.VMEM)] * (2 * count),
        out_shape=[shape(tok_rows, width // 2)] * 2,
        compiler_params=params(5),
        cost_estimate=cost(1.0),
    )


def exchange(block, axis, distance):
    count = lax.axis_size(axis)
    return lax.ppermute(block, axis, [(i, i ^ distance) for i in range(count)])


def add(left, right):
    return (left.astype(F32) + right.astype(F32)).astype(BF16)


def term_half_body(chunk_ref, into_ref, out_ref):
    rows = slice(0, out_ref.shape[0])
    out_ref[...] = (chunk_ref[rows, :].astype(F32) + into_ref[rows, :].astype(F32)).astype(BF16)


def half_sum(chunk, into, rows, weight, after):
    return run(
        term_half_body,
        [chunk, into],
        after,
        out_shape=shape(rows, chunk.shape[1]),
        compiler_params=params(3),
        cost_estimate=cost(weight),
    )


def scatter_body(pieces, keep_ref, into_ref, even_ref, odd_ref):
    width = keep_ref.shape[1] // pieces
    for i in range(pieces):
        here = slice(i * width, (i + 1) * width)
        place = slice(i // 2 * width, (i // 2 + 1) * width)
        total = keep_ref[:, here].astype(F32) + into_ref[:, here].astype(F32)
        (even_ref, odd_ref)[i % 2][:, place] = total.astype(BF16)


def last_body(left_ref, right_ref, token_ref, out_ref):
    token_ref[...] = jnp.zeros_like(token_ref)
    out_ref[...] = (left_ref[...].astype(F32) + right_ref[...].astype(F32)).astype(BF16)


def last_sum(left, right, after):
    return run(
        last_body,
        [left, right],
        after,
        out_shape=[shape(8, 128, F32), shape(*left.shape)],
        compiler_params=params(3),
        cost_estimate=cost(0.9),
    )


def scatter_step(keep, into, pieces, after):
    rows, width = keep.shape
    return run(
        functools.partial(scatter_body, pieces),
        [keep, into],
        after,
        out_shape=[shape(rows, width // 2)] * 2,
        compiler_params=params(4),
        cost_estimate=cost(0.2),
    )


def turn_body(end_ref, half_ref, across_ref, chunk_ref, total_ref, send_ref):
    total = (half_ref[...].astype(F32) + across_ref[...].astype(F32)).astype(BF16)
    total_ref[...] = total

    @pl.when(end_ref[0] == 1)
    def _():
        send_ref[...] = chunk_ref[...]

    @pl.when(end_ref[0] == 0)
    def _():
        send_ref[...] = total


def turn(end, half, across, chunk, weight, after):
    return run(
        turn_body,
        [end, half, across, chunk],
        after,
        in_specs=[pl.BlockSpec(memory_space=pltpu.SMEM)]
        + [pl.BlockSpec(memory_space=pltpu.VMEM)] * 3,
        out_shape=[shape(*half.shape)] * 2,
        compiler_params=params(2),
        cost_estimate=cost(weight),
    )


def output_body(count, end_ref, *refs):
    totals, ends, (token_ref, out_ref) = refs[:count], refs[count : 2 * count], refs[2 * count :]
    token_ref[...] = jnp.zeros_like(token_ref)
    rows = totals[0].shape[0]

    for flag, sources in ((0, totals), (1, ends)):

        @pl.when(end_ref[0] == flag)
        def _():
            for i, ref in enumerate(sources):
                out_ref[i * rows : (i + 1) * rows, :] = ref[...]


def output(end, totals, ends, after):
    count = len(totals)
    rows, width = totals[0].shape
    return run(
        functools.partial(output_body, count),
        [end, *totals, *ends],
        after,
        in_specs=[pl.BlockSpec(memory_space=pltpu.SMEM)]
        + [pl.BlockSpec(memory_space=pltpu.VMEM)] * (2 * count),
        out_shape=[shape(8, 128, F32), shape(count * rows, width)],
        compiler_params=params(4),
        cost_estimate=cost(0.9),
    )


def relay_body(source_ref, target_ref):
    target_ref[...] = source_ref[...]


def relay(block, after):
    return run(
        relay_body,
        [block],
        after,
        out_shape=shape(*block.shape),
        compiler_params=params(3),
        cost_estimate=cost(0.2),
    )


class Line:
    lag = 3
    half_weights = (3.0, 3.0, 3.0, 3.0, 3.0, 3.0, 3.0, 0.5)
    turn_weights = (4.0, 4.0, 3.0, 3.0, 4.0, 2.0, 0.5, 0.5)

    def __init__(self, axis, other, end, step):
        self.axis, self.axes, self.step = axis, (axis, other), step
        self.count = lax.axis_size(axis)
        self.end = end
        width = lax.axis_size(other)
        self.across = []
        for place in range(self.count):
            for seat in range(width):
                target = (place, seat ^ 1 if width > 1 else seat)
                if place & 3 in (1, 2):
                    target = (place ^ 3, seat)
                self.across.append((place * width + seat, target[0] * width + target[1]))
        self.chunks, self.into, self.halves, self.crossed, self.totals = [], [], [], [], []

    def enter(self, chunk):
        self.chunks.append(chunk)
        self.into.append(exchange(chunk, self.axis, 1))

    def meet(self, rows):
        k = len(self.halves)
        weight = self.half_weights[k]
        half = self.step(half_sum, self.chunks[k], self.into[k], rows, weight)
        self.halves.append(half)
        self.crossed.append(lax.ppermute(half, self.axes, self.across))

    def turn(self, chunk):
        old = len(self.totals)
        half, crossed = self.halves[old], self.crossed[old]
        weight = self.turn_weights[old]
        total, send = self.step(turn, self.end, half, crossed, chunk, weight)
        self.totals.append(total)
        self.chunks.append(chunk)
        self.into.append(exchange(send, self.axis, 1))

    def leave(self):
        old = len(self.totals)
        half = self.halves[old]
        weight = self.turn_weights[old]
        total = self.step(half_sum, half, self.crossed[old], half.shape[0], weight)
        self.totals.append(total)
        self.into.append(exchange(total, self.axis, 1))

    def output(self, first, count):
        ends = self.into[first + self.lag : first + self.lag + count]
        _, result = self.step(output, self.end, self.totals[first : first + count], ends)
        distance = 4
        while distance < self.count:
            result = add(result, exchange(result, self.axis, distance))
            distance *= 2
        return result


class Scatter:
    def __init__(self, parts, axis, step):
        self.axis, self.step = axis, step
        self.pieces = lax.axis_size(axis) // 2
        self.keep, send = parts
        self.distance = 1
        self.into = exchange(send, axis, 1)

    def advance(self):
        while self.pieces > 1:
            self.keep, send = self.step(scatter_step, self.keep, self.into, self.pieces)
            self.distance *= 2
            self.pieces //= 2
            self.into = exchange(send, self.axis, self.distance)

    def result(self):
        return self.step(last_sum, self.keep, self.into)[1]


def per_device(tokens, w_query, w_key, w_value, w_out, cotangent):
    tok_rows = tokens.shape[0]
    inner = w_query.shape[1]
    local_levels = (tok_rows // BLOCK).bit_length() - 1
    count = lax.axis_size("seq")
    far_levels = count.bit_length() - 1
    far_bits = [d.bit_length() - 1 for d in range(1, count)]

    last = []

    def step(kernel, *operands):
        made = kernel(*operands, list(last))
        last[:] = made[:1] if isinstance(made, (list, tuple)) else [made]
        return made

    place = jnp.bitwise_and(lax.axis_index("seq"), 3)
    end = jnp.reshape((place == 0) | (place == 3), (1,)).astype(jnp.int32)
    rank = jnp.reshape(lax.axis_index("head"), (1,)).astype(jnp.int32)
    parts = key_value(tokens, w_key, w_value, local_levels, far_levels, [end, rank])
    levels, tops = parts[:local_levels], parts[local_levels:]
    fars = [exchange(tops[bit], "seq", d) for d, bit in enumerate(far_bits, 1)]
    query = step(project, tokens, w_query)
    powers, near = step(near_powers, query, levels)
    grad = step(project, cotangent, w_out)
    attended, attended_t, stats = step(forward, query, powers, near, levels, fars, far_bits)

    line = Line("seq", "head", end, step)
    pieces = 2
    rows = tokens.shape[1] // pieces
    line.enter(step(weight_terms, attended_t, cotangent, inner, 0, 0, pieces))
    line.enter(step(weight_terms, attended_t, cotangent, inner, 0, 1, pieces))
    parts = step(project_split, rank, [attended], [w_out], "head")
    mixed = Scatter(parts, "head", step)
    dquery, dkv, query_first, query_second, *away = step(
        backward, query, grad, attended_t, stats, tokens, levels, fars, far_bits, pieces
    )
    backs = [exchange(piece, "seq", d) for d, piece in enumerate(away, 1)]
    line.meet(rows)
    mixed.advance()
    line.meet(rows)
    dkey, dvalue, dkv_t = step(close_keys, dkv, backs, far_bits, local_levels)
    line.enter(step(relay, query_first))
    key_first = step(weight_terms, dkv_t, tokens, inner, 0, 0, pieces)
    line.turn(query_second)
    key_second = step(weight_terms, dkv_t, tokens, inner, 0, 1, pieces)
    line.meet(rows)
    line.turn(key_first)
    keep, send = step(project_split, rank, [dquery, dkey, dvalue], [w_query, w_key, w_value], "head")
    line.meet(rows)
    value_first = step(weight_terms, dkv_t, tokens, inner, 1, 0, pieces)
    line.turn(key_second)
    line.meet(rows)
    tokens_grad = Scatter([keep, step(relay, send)], "head", step)
    line.turn(value_first)
    mixed = mixed.result()
    value_second = step(weight_terms, dkv_t, tokens, inner, 1, 1, pieces)
    line.meet(rows)
    line.turn(value_second)
    out_grad = line.output(0, pieces)
    line.meet(rows)
    tokens_grad.advance()
    line.leave()
    line.meet(rows)
    query_grad = line.output(2, pieces)
    line.leave()
    key_grad = line.output(4, pieces)
    line.leave()
    tokens_grad = tokens_grad.result()
    value_grad = line.output(6, pieces)
    return mixed, tokens_grad, query_grad, key_grad, value_grad, out_grad


def solution(mesh):
    return jax.shard_map(
        per_device,
        mesh=mesh,
        in_specs=(
            P(("groups", "seq"), None),
            P(None, "head"),
            P(None, "head"),
            P(None, "head"),
            P(None, "head"),
            P(("groups", "seq"), None),
        ),
        out_specs=(
            P(("groups", "seq"), "head"),
            P(("groups", "seq"), "head"),
            P("groups", "head"),
            P("groups", "head"),
            P("groups", "head"),
            P("groups", "head"),
        ),
        check_vma=False,
    )
```

```python
import functools
import math

import jax
import jax.numpy as jnp
from jax import lax
from jax.experimental import pallas as pl
from jax.experimental.pallas import tpu as pltpu
from jax.sharding import PartitionSpec as P

HEAD_DIM = 128
BLOCK = 128
BF16 = jnp.bfloat16
F32 = jnp.float32
MIB = 1024 * 1024

NN = (((1,), (0,)), ((), ()))
NT = (((1,), (1,)), ((), ()))
TN = (((0,), (0,)), ((), ()))


def dot(left, right, dims=NN):
    return lax.dot_general(left, right, dims, preferred_element_type=F32)


def params(mib):
    return pltpu.CompilerParams(vmem_limit_bytes=mib * MIB)


def cost(microseconds):
    return pl.CostEstimate(flops=int(microseconds * 1150e6) + 1, bytes_accessed=1, transcendentals=0)


def run(body, ready, after=(), in_specs=None, **options):
    count, extra = len(ready), len(after)

    def kernel(*refs):
        body(*refs[:count], *refs[count + extra :])

    in_specs = in_specs or [pl.BlockSpec(memory_space=pltpu.VMEM)] * count
    in_specs = in_specs + [pl.BlockSpec(memory_space=pl.ANY)] * extra
    return pl.pallas_call(kernel, in_specs=in_specs, **options)(*ready, *after)


def shape(rows, cols, dtype=BF16):
    return jax.ShapeDtypeStruct((rows, cols), dtype)


def whole(rows, cols):
    return pl.BlockSpec((rows, cols), lambda *_: (0, 0))


def pool_matrix(rows):
    row = lax.broadcasted_iota(jnp.int32, (rows // 2, rows), 0)
    col = lax.broadcasted_iota(jnp.int32, (rows // 2, rows), 1)
    return jnp.where(jnp.right_shift(col, 1) == row, 0.5, 0.0).astype(BF16)


def spread_matrix(rows, step_bits, offset, cols, weight):
    row = lax.broadcasted_iota(jnp.int32, (rows, cols), 0) + offset
    col = lax.broadcasted_iota(jnp.int32, (rows, cols), 1)
    return jnp.where(jnp.right_shift(row, step_bits) == col, weight, 0.0).astype(BF16)


def key_value_body(local_levels, far_levels, parts, tok_hbm, wk_hbm, wv_hbm, *refs):
    out_hbm = refs[:local_levels]
    far = refs[local_levels : local_levels + far_levels]
    refs = refs[local_levels + far_levels :]
    tok_ref, wk_ref, wv_ref = refs[:3]
    levels = refs[3 : 3 + local_levels]
    in_sems, out_sems = refs[3 + local_levels :]
    part = tok_ref.shape[0] // parts

    def fetch(source, target, i):
        copy = pltpu.make_async_copy(source, target, in_sems.at[i])
        copy.start()
        return copy

    def flush(i):
        copy = pltpu.make_async_copy(levels[i], out_hbm[i], out_sems.at[i])
        copy.start()
        return copy

    weights = [fetch(wk_hbm, wk_ref, 0), fetch(wv_hbm, wv_ref, 1)]
    tiles = []
    for p in range(parts):
        rows = pl.ds(p * part, part)
        tiles.append(fetch(tok_hbm.at[rows], tok_ref.at[rows], 2 + p))
    for copy in weights:
        copy.wait()
    for p in range(parts):
        tiles[p].wait()
        here = slice(p * part, (p + 1) * part)
        x = tok_ref[here, :]
        both = jnp.concatenate([dot(x, wk_ref[...]), dot(x, wv_ref[...])], axis=1)
        levels[0][here, :] = both.astype(BF16)
    flushes = [flush(0)]
    pool = pool_matrix(part)
    for i in range(1, local_levels):
        source = levels[i - 1]
        for low in range(0, source.shape[0], part):
            mean = dot(pool, source[low : low + part, :])
            levels[i][low // 2 : (low + part) // 2, :] = mean.astype(BF16)
        flushes.append(flush(i))
    rows = dot(pool, levels[-1][...]).astype(BF16)
    for i in range(far_levels):
        if i:
            rows = dot(pool_matrix(rows.shape[0]), rows).astype(BF16)
        far[i][...] = rows
    for copy in flushes:
        copy.wait()


def key_value(tokens, w_key, w_value, local_levels, far_levels, after):
    tok_rows, width = tokens.shape
    inner = w_key.shape[1]
    parts = tok_rows // (2 * BLOCK)
    held = [(tok_rows >> i, 2 * inner) for i in range(local_levels)]
    tops = [(BLOCK >> i, 2 * inner) for i in range(far_levels)]
    return run(
        functools.partial(key_value_body, local_levels, far_levels, parts),
        [tokens, w_key, w_value],
        after,
        in_specs=[pl.BlockSpec(memory_space=pl.ANY)] * 3,
        out_specs=[pl.BlockSpec(memory_space=pl.ANY)] * len(held)
        + [pl.BlockSpec(memory_space=pltpu.VMEM)] * len(tops),
        out_shape=[shape(*dims) for dims in held + tops],
        scratch_shapes=[pltpu.VMEM((tok_rows, width), BF16)]
        + [pltpu.VMEM((width, inner), BF16)] * 2
        + [pltpu.VMEM(dims, BF16) for dims in held]
        + [pltpu.SemaphoreType.DMA((parts + 2,)), pltpu.SemaphoreType.DMA((len(held),))],
        compiler_params=params(56),
        cost_estimate=cost(5.0),
    )


def project_body(left_ref, weight_ref, out_ref):
    out_ref[...] = dot(left_ref[...], weight_ref[...]).astype(BF16)


def project(left, weight, after):
    tok_rows, width = left.shape
    inner = weight.shape[1]
    return run(
        project_body,
        [left, weight],
        after,
        out_shape=shape(tok_rows, inner),
        compiler_params=params(4),
        cost_estimate=cost(0.7),
    )


class KeySet:
    def __init__(self, far_rows, far_bits, local_levels):
        mids = local_levels - 1
        self.sizes = [2 * BLOCK] + [BLOCK] * mids + list(far_rows)
        self.bounds = [sum(self.sizes[:i]) for i in range(len(self.sizes) + 1)]
        steps = [0] + list(range(1, local_levels)) + [local_levels + b for b in far_bits]
        self.biases = [float(step) for step in steps]
        self.mids = mids
        self.far_start = self.bounds[1 + mids]
        self.factor = math.log2(math.e) / math.sqrt(HEAD_DIM)

    def here(self, m):
        return pl.ds(pl.multiple_of(m * 2 * BLOCK, 2 * BLOCK), 2 * BLOCK)

    def seats(self, m):
        for i in range(self.mids):
            sibling = jnp.bitwise_xor(jnp.right_shift(m, i), 1)
            yield pl.ds(pl.multiple_of(sibling * BLOCK, BLOCK), BLOCK)

    def near(self, m, level_refs, cols):
        rows = [level_refs[0][self.here(m), cols]]
        rows += [ref[seat, cols] for ref, seat in zip(level_refs[1:], self.seats(m))]
        return rows

    def far(self, far_refs, cols):
        return [ref[:, cols] for ref in far_refs]

    def pieces(self, array, first=0, count=None):
        base = self.bounds[first]
        ends = self.bounds[first:] if count is None else self.bounds[first : first + count + 1]
        return [array[a - base : b - base] for a, b in zip(ends, ends[1:])]

    def top(self, pieces, first=0):
        tops = [
            jnp.max(piece, axis=0, keepdims=True) * self.factor + bias
            for piece, bias in zip(pieces, self.biases[first:])
        ]
        return functools.reduce(jnp.maximum, tops)

    def powers(self, pieces, top, first=0):
        return jnp.concatenate(
            [
                jnp.exp2(piece * self.factor + (bias - top))
                for piece, bias in zip(pieces, self.biases[first:])
            ],
            axis=0,
        )


def head_columns(h, inner):
    low = h * HEAD_DIM
    return slice(low, low + HEAD_DIM), slice(inner + low, inner + low + HEAD_DIM)


def near_body(local_levels, q_ref, *refs):
    level_refs = refs[:local_levels]
    power_ref, stat_ref = refs[local_levels:]
    tok_rows, inner = q_ref.shape
    heads = inner // HEAD_DIM
    keyset = KeySet([], [], local_levels)
    rows = keyset.far_start

    def step(m, carry):
        here = keyset.here(m)
        for h in range(heads):
            cols, _ = head_columns(h, inner)
            keys = jnp.concatenate(keyset.near(m, level_refs, cols), axis=0)
            pieces = keyset.pieces(dot(keys, q_ref[here, cols], NT))
            top = keyset.top(pieces)
            powers = keyset.powers(pieces, top)
            stat_ref[h : h + 1, here] = top
            stat_ref[heads + h : heads + h + 1, here] = jnp.sum(powers, axis=0, keepdims=True)
            power_ref[pl.ds(pl.multiple_of((m * heads + h) * rows, rows), rows), :] = powers
        return carry

    lax.fori_loop(0, tok_rows // (2 * BLOCK), step, 0)


def near_powers(query, levels, after):
    tok_rows, inner = query.shape
    heads = inner // HEAD_DIM
    pairs = tok_rows // (2 * BLOCK)
    rows = (len(levels) + 1) * BLOCK
    return run(
        functools.partial(near_body, len(levels)),
        [query, *levels],
        after,
        out_shape=[shape(pairs * heads * rows, 2 * BLOCK, F32), shape(2 * heads, tok_rows, F32)],
        compiler_params=params(6),
        cost_estimate=cost(2.3),
    )


def forward_body(local_levels, far_bits, *refs):
    fars = len(far_bits)
    q_ref, power_ref, near_ref = refs[:3]
    level_refs = refs[3 : 3 + local_levels]
    far_refs = refs[3 + local_levels : 3 + local_levels + fars]
    att_ref, att_t_ref, stat_ref = refs[3 + local_levels + fars :]
    tok_rows, inner = q_ref.shape
    heads = inner // HEAD_DIM
    keyset = KeySet([r.shape[0] for r in far_refs], far_bits, local_levels)
    rows = keyset.far_start

    def step(m, carry):
        here = keyset.here(m)
        for h in range(heads):
            cols, vcols = head_columns(h, inner)
            second = heads + h
            keys = jnp.concatenate(keyset.far(far_refs, cols), axis=0)
            values = keyset.near(m, level_refs, vcols) + keyset.far(far_refs, vcols)
            values = jnp.concatenate(values, axis=0)
            first = local_levels
            pieces = keyset.pieces(dot(keys, q_ref[here, cols], NT), first)
            near_top = near_ref[h : h + 1, here]
            top = jnp.maximum(near_top, keyset.top(pieces, first))
            shrink = jnp.exp2(near_top - top)
            powers = keyset.powers(pieces, top, first)
            total = near_ref[second : second + 1, here] * shrink
            total = total + jnp.sum(powers, axis=0, keepdims=True)
            inverse = 1.0 / total
            place = pl.ds(pl.multiple_of((m * heads + h) * rows, rows), rows)
            near_probs = (power_ref[place, :] * (shrink * inverse)).astype(BF16)
            far_probs = (powers * inverse).astype(BF16)
            probs_b = jnp.concatenate([near_probs, far_probs], axis=0)
            att_t = dot(values, probs_b, TN).astype(BF16)
            att_t_ref[cols, here] = att_t
            att_ref[here, cols] = att_t.T
            stat_ref[h : h + 1, here] = top
            stat_ref[second : second + 1, here] = inverse
        return carry

    lax.fori_loop(0, tok_rows // (2 * BLOCK), step, 0)


def forward(query, powers, near, levels, fars, far_bits, after):
    tok_rows, inner = query.shape
    heads = inner // HEAD_DIM
    set_rows = (len(levels) + 1) * BLOCK + sum(f.shape[0] for f in fars)
    return run(
        functools.partial(forward_body, len(levels), far_bits),
        [query, powers, near, *levels, *fars],
        after,
        out_shape=[
            shape(tok_rows, inner),
            shape(inner, tok_rows),
            shape(2 * heads, tok_rows, F32),
        ],
        compiler_params=params(6),
        cost_estimate=cost(4.0),
    )


def backward_body(h, heads, local_levels, far_bits, pieces, *refs):
    mids = local_levels - 1
    fars = len(far_bits)
    closing = h == heads - 1
    q_ref, g_ref, att_t_ref, stat_ref = refs[:4]
    level_refs = refs[4 : 4 + local_levels]
    far_refs = refs[4 + local_levels : 4 + local_levels + fars]
    refs = refs[4 + local_levels + fars :]
    if closing:
        tok_ref, *earlier = refs[: 1 + 3 * h]
        refs = refs[1 + 3 * h :]
        dq_ref, dkv_ref = refs[:2]
        term_refs = refs[2 : 2 + pieces]
        dfar_refs = refs[2 + pieces : 2 + pieces + fars]
        scratch = refs[2 + pieces + fars :]
        dq_t_ref = scratch[-1]
        place = slice(h * HEAD_DIM, (h + 1) * HEAD_DIM)
    else:
        dq_ref, dkv_ref, dq_t_ref, out_ref = refs[:4]
        scratch = refs[4:]
        place = slice(0, HEAD_DIM)
    dmid_refs = scratch[:mids]
    acc_ref = scratch[mids]
    tok_rows, inner = q_ref.shape
    score_scale = 1.0 / math.sqrt(HEAD_DIM)
    keyset = KeySet([r.shape[0] for r in far_refs], far_bits, local_levels)
    cols, vcols = head_columns(h, inner)
    parts = (slice(0, HEAD_DIM), slice(HEAD_DIM, 2 * HEAD_DIM))

    for ref in (*dmid_refs, acc_ref):
        ref[...] = jnp.zeros_like(ref)

    def unit(m):
        here = keyset.here(m)
        keys, values = (
            jnp.concatenate(keyset.near(m, level_refs, c) + keyset.far(far_refs, c), axis=0)
            for c in (cols, vcols)
        )
        q = q_ref[here, cols]
        g = g_ref[here, cols]
        top = stat_ref[h : h + 1, here]
        inverse = stat_ref[heads + h : heads + h + 1, here]
        probs = keyset.powers(keyset.pieces(dot(keys, q, NT)), top) * inverse
        att_t = att_t_ref[cols, here].astype(F32)
        delta = jnp.sum(g.T.astype(F32) * att_t, axis=0, keepdims=True)
        grads = (probs * (dot(values, g, NT) - delta) * score_scale).astype(BF16)
        dq_t = dot(keys, grads, TN).astype(BF16)
        dq_t_ref[place, here] = dq_t
        dq_ref[here, place] = dq_t.T
        for part, half in zip((dot(grads, q), dot(probs.astype(BF16), g)), parts):
            own, *sides = keyset.pieces(part)
            dkv_ref[here, half] = own
            for ref, seat, side in zip(dmid_refs, keyset.seats(m), sides):
                ref[seat, half] += side
            acc_ref[:, half] += part[keyset.far_start :]

    pairs = tok_rows // (2 * BLOCK)
    stride = 2 if pairs % 2 == 0 else 1

    def step(i, carry):
        for u in range(stride):
            unit(i * stride + u)
        return carry

    lax.fori_loop(0, pairs // stride, step, 0)
    fan = spread_matrix(2 * BLOCK, 1, 0, BLOCK, 0.5)
    targets = (dkv_ref, *dmid_refs)
    for i in reversed(range(mids)):
        for t in range(dmid_refs[i].shape[0] // BLOCK):
            part = dmid_refs[i][t * BLOCK : (t + 1) * BLOCK, :]
            high = part.astype(BF16)
            low = (part - high.astype(F32)).astype(BF16)
            rows = slice(2 * t * BLOCK, 2 * (t + 1) * BLOCK)
            targets[i][rows, :] += dot(fan, high) + dot(fan, low)
    away = acc_ref[...].astype(BF16)
    if not closing:
        out_ref[...] = away
        return
    aways = []
    for e in range(h):
        dq_e, dq_t_e, away_e = earlier[3 * e : 3 * e + 3]
        here = slice(e * HEAD_DIM, (e + 1) * HEAD_DIM)
        dq_ref[:, here] = dq_e[...]
        dq_t_ref[here, :] = dq_t_e[...]
        aways.append(away_e[...])
    aways.append(away)
    away = jnp.concatenate([x[:, half] for half in parts for x in aways], axis=1)
    width = term_refs[0].shape[0]
    low = 0
    for ref in dfar_refs:
        ref[...] = away[low : low + ref.shape[0]]
        low += ref.shape[0]
    for i, ref in enumerate(term_refs):
        part = dot(dq_t_ref[...], tok_ref[:, i * width : (i + 1) * width])
        ref[...] = part.astype(BF16).T


def backward_scratch(levels, fars):
    mids = [pltpu.VMEM((level.shape[0], 2 * HEAD_DIM), F32) for level in levels[1:]]
    return mids + [pltpu.VMEM((sum(f.shape[0] for f in fars), 2 * HEAD_DIM), F32)]


def backward_first(h, query, grad, attended_t, stats, levels, fars, far_bits, after):
    tok_rows, inner = query.shape
    return run(
        functools.partial(
            backward_body, h, inner // HEAD_DIM, len(levels), far_bits, 0
        ),
        [query, grad, attended_t, stats, *levels, *fars],
        after,
        out_shape=[
            shape(tok_rows, HEAD_DIM),
            shape(tok_rows, 2 * HEAD_DIM, F32),
            shape(HEAD_DIM, tok_rows),
            shape(sum(f.shape[0] for f in fars), 2 * HEAD_DIM),
        ],
        scratch_shapes=backward_scratch(levels, fars),
        compiler_params=params(10),
        cost_estimate=cost(4.0),
    )


def backward_last(earlier, query, grad, attended_t, stats, tokens, levels, fars, far_bits, pieces, after):
    tok_rows, inner = query.shape
    h = len(earlier)
    ready = [query, grad, attended_t, stats, *levels, *fars, tokens]
    for dq, _, dq_t, away in earlier:
        ready += [dq, dq_t, away]
    return run(
        functools.partial(
            backward_body, h, inner // HEAD_DIM, len(levels), far_bits, pieces
        ),
        ready,
        after,
        out_shape=[shape(tok_rows, inner), shape(tok_rows, 2 * HEAD_DIM, F32)]
        + [shape(tokens.shape[1] // pieces, inner)] * pieces
        + [shape(*f.shape) for f in fars],
        scratch_shapes=backward_scratch(levels, fars) + [pltpu.VMEM((inner, tok_rows), BF16)],
        compiler_params=params(10),
        cost_estimate=cost(4.0),
    )


def term_body(which, low, left_ref, right_ref, out_ref):
    width, inner = out_ref.shape
    left = left_ref[which * inner : (which + 1) * inner, :]
    out_ref[...] = dot(left, right_ref[:, low : low + width]).astype(BF16).T


def weight_terms(left_t, right, inner, which, part, parts, after):
    tok_rows = left_t.shape[1]
    width = right.shape[1] // parts
    return run(
        functools.partial(term_body, which, part * width),
        [left_t, right],
        after,
        out_shape=shape(width, inner),
        compiler_params=params(3),
        cost_estimate=cost(0.2),
    )


def close_body(local_levels, far_bits, heads, *refs):
    dkv_refs = refs[:heads]
    backs = [ref[...] for ref in refs[heads : heads + len(far_bits)]]
    dk_ref, dv_ref, dkv_t_ref = refs[heads + len(far_bits) :]
    inner = dk_ref.shape[1]
    tile = 2 * BLOCK
    halves = (slice(0, HEAD_DIM), slice(HEAD_DIM, 2 * HEAD_DIM))
    for t in range(dk_ref.shape[0] // tile):
        here = slice(t * tile, (t + 1) * tile)
        total = jnp.concatenate([ref[here, half] for half in halves for ref in dkv_refs], axis=1)
        for back, bit in zip(backs, far_bits):
            weight = 0.5 ** (local_levels + bit)
            fan = spread_matrix(tile, local_levels + bit, t * tile, back.shape[0], weight)
            total = total + dot(fan, back)
        final = total.astype(BF16)
        dk_ref[here, :] = final[:, :inner]
        dv_ref[here, :] = final[:, inner:]
        dkv_t_ref[:, here] = final.T


def close_keys(dkvs, backs, far_bits, local_levels, after):
    tok_rows = dkvs[0].shape[0]
    inner = len(dkvs) * HEAD_DIM
    double = 2 * inner
    return run(
        functools.partial(close_body, local_levels, far_bits, len(dkvs)),
        [*dkvs, *backs],
        after,
        out_shape=[shape(tok_rows, inner), shape(tok_rows, inner), shape(double, tok_rows)],
        compiler_params=params(5),
        cost_estimate=cost(0.2),
    )


def split_body(count, parts, rank_ref, *refs):
    lefts, weights = refs[:count], refs[count : 2 * count]
    outs = refs[2 * count :]
    width = weights[0].shape[0] // parts
    for r in range(parts):
        owner = jnp.bitwise_xor(rank_ref[0], r)
        rows = pl.ds(pl.multiple_of(owner * width, width), width)
        total = None
        for left, weight in zip(lefts, weights):
            product = dot(left[...], weight[rows, :], NT)
            total = product if total is None else total + product
        place = r // 2 * width
        outs[r % 2][:, place : place + width] = total.astype(BF16)


def project_split(rank, lefts, weights, axis, after):
    count = len(lefts)
    parts = lax.axis_size(axis)
    tok_rows, inner = lefts[0].shape
    width = weights[0].shape[0]
    return run(
        functools.partial(split_body, count, parts),
        [rank, *lefts, *weights],
        after,
        in_specs=[pl.BlockSpec(memory_space=pltpu.SMEM)]
        + [pl.BlockSpec(memory_space=pltpu.VMEM)] * (2 * count),
        out_shape=[shape(tok_rows, width // 2)] * 2,
        compiler_params=params(5),
        cost_estimate=cost(1.0),
    )


def exchange(block, axis, distance):
    count = lax.axis_size(axis)
    return lax.ppermute(block, axis, [(i, i ^ distance) for i in range(count)])


def add(left, right):
    return (left.astype(F32) + right.astype(F32)).astype(BF16)


def term_half_body(chunk_ref, into_ref, out_ref):
    rows = slice(0, out_ref.shape[0])
    out_ref[...] = (chunk_ref[rows, :].astype(F32) + into_ref[rows, :].astype(F32)).astype(BF16)


def half_sum(chunk, into, rows, weight, after):
    return run(
        term_half_body,
        [chunk, into],
        after,
        out_shape=shape(rows, chunk.shape[1]),
        compiler_params=params(3),
        cost_estimate=cost(weight),
    )


def scatter_body(pieces, keep_ref, into_ref, even_ref, odd_ref):
    width = keep_ref.shape[1] // pieces
    for i in range(pieces):
        here = slice(i * width, (i + 1) * width)
        place = slice(i // 2 * width, (i // 2 + 1) * width)
        total = keep_ref[:, here].astype(F32) + into_ref[:, here].astype(F32)
        (even_ref, odd_ref)[i % 2][:, place] = total.astype(BF16)


def last_body(left_ref, right_ref, token_ref, out_ref):
    token_ref[...] = jnp.zeros_like(token_ref)
    out_ref[...] = (left_ref[...].astype(F32) + right_ref[...].astype(F32)).astype(BF16)


def last_sum(left, right, after):
    return run(
        last_body,
        [left, right],
        after,
        out_shape=[shape(8, 128, F32), shape(*left.shape)],
        compiler_params=params(3),
        cost_estimate=cost(0.9),
    )


def scatter_step(keep, into, pieces, after):
    rows, width = keep.shape
    return run(
        functools.partial(scatter_body, pieces),
        [keep, into],
        after,
        out_shape=[shape(rows, width // 2)] * 2,
        compiler_params=params(4),
        cost_estimate=cost(0.2),
    )


def turn_body(end_ref, half_ref, across_ref, chunk_ref, total_ref, send_ref):
    total = (half_ref[...].astype(F32) + across_ref[...].astype(F32)).astype(BF16)
    total_ref[...] = total

    @pl.when(end_ref[0] == 1)
    def _():
        send_ref[...] = chunk_ref[...]

    @pl.when(end_ref[0] == 0)
    def _():
        send_ref[...] = total


def turn(end, half, across, chunk, weight, after):
    return run(
        turn_body,
        [end, half, across, chunk],
        after,
        in_specs=[pl.BlockSpec(memory_space=pltpu.SMEM)]
        + [pl.BlockSpec(memory_space=pltpu.VMEM)] * 3,
        out_shape=[shape(*half.shape)] * 2,
        compiler_params=params(2),
        cost_estimate=cost(weight),
    )


def output_body(count, end_ref, *refs):
    totals, ends, (token_ref, out_ref) = refs[:count], refs[count : 2 * count], refs[2 * count :]
    token_ref[...] = jnp.zeros_like(token_ref)
    rows = totals[0].shape[0]

    for flag, sources in ((0, totals), (1, ends)):

        @pl.when(end_ref[0] == flag)
        def _():
            for i, ref in enumerate(sources):
                out_ref[i * rows : (i + 1) * rows, :] = ref[...]


def output(end, totals, ends, after):
    count = len(totals)
    rows, width = totals[0].shape
    return run(
        functools.partial(output_body, count),
        [end, *totals, *ends],
        after,
        in_specs=[pl.BlockSpec(memory_space=pltpu.SMEM)]
        + [pl.BlockSpec(memory_space=pltpu.VMEM)] * (2 * count),
        out_shape=[shape(8, 128, F32), shape(count * rows, width)],
        compiler_params=params(4),
        cost_estimate=cost(0.9),
    )


def relay_body(source_ref, target_ref):
    target_ref[...] = source_ref[...]


def relay(block, after):
    return run(
        relay_body,
        [block],
        after,
        out_shape=shape(*block.shape),
        compiler_params=params(3),
        cost_estimate=cost(0.2),
    )


class Line:
    lag = 3
    half_weights = (3.0, 5.0, 3.0, 3.0, 3.0, 3.0, 3.0, 0.5)
    turn_weights = (4.0, 4.0, 3.0, 3.0, 4.0, 2.0, 0.5, 0.5)

    def __init__(self, axis, other, end, step):
        self.axis, self.axes, self.step = axis, (axis, other), step
        self.count = lax.axis_size(axis)
        self.end = end
        width = lax.axis_size(other)
        self.across = []
        for place in range(self.count):
            for seat in range(width):
                target = (place, seat ^ 1 if width > 1 else seat)
                if place & 3 in (1, 2):
                    target = (place ^ 3, seat)
                self.across.append((place * width + seat, target[0] * width + target[1]))
        self.chunks, self.into, self.halves, self.crossed, self.totals = [], [], [], [], []

    def enter(self, chunk):
        self.chunks.append(chunk)
        self.into.append(exchange(chunk, self.axis, 1))

    def meet(self, rows):
        k = len(self.halves)
        weight = self.half_weights[k]
        half = self.step(half_sum, self.chunks[k], self.into[k], rows, weight)
        self.halves.append(half)
        self.crossed.append(lax.ppermute(half, self.axes, self.across))

    def turn(self, chunk):
        old = len(self.totals)
        half, crossed = self.halves[old], self.crossed[old]
        weight = self.turn_weights[old]
        total, send = self.step(turn, self.end, half, crossed, chunk, weight)
        self.totals.append(total)
        self.chunks.append(chunk)
        self.into.append(exchange(send, self.axis, 1))

    def leave(self):
        old = len(self.totals)
        half = self.halves[old]
        weight = self.turn_weights[old]
        total = self.step(half_sum, half, self.crossed[old], half.shape[0], weight)
        self.totals.append(total)
        self.into.append(exchange(total, self.axis, 1))

    def output(self, first, count):
        ends = self.into[first + self.lag : first + self.lag + count]
        _, result = self.step(output, self.end, self.totals[first : first + count], ends)
        distance = 4
        while distance < self.count:
            result = add(result, exchange(result, self.axis, distance))
            distance *= 2
        return result


class Scatter:
    def __init__(self, parts, axis, step):
        self.axis, self.step = axis, step
        self.pieces = lax.axis_size(axis) // 2
        self.keep, send = parts
        self.distance = 1
        self.into = exchange(send, axis, 1)

    def advance(self):
        while self.pieces > 1:
            self.keep, send = self.step(scatter_step, self.keep, self.into, self.pieces)
            self.distance *= 2
            self.pieces //= 2
            self.into = exchange(send, self.axis, self.distance)

    def result(self):
        return self.step(last_sum, self.keep, self.into)[1]


def per_device(tokens, w_query, w_key, w_value, w_out, cotangent):
    tok_rows = tokens.shape[0]
    inner = w_query.shape[1]
    local_levels = (tok_rows // BLOCK).bit_length() - 1
    count = lax.axis_size("seq")
    far_levels = count.bit_length() - 1
    far_bits = [d.bit_length() - 1 for d in range(1, count)]

    last = []

    def step(kernel, *operands):
        made = kernel(*operands, list(last))
        last[:] = made[:1] if isinstance(made, (list, tuple)) else [made]
        return made

    place = jnp.bitwise_and(lax.axis_index("seq"), 3)
    end = jnp.reshape((place == 0) | (place == 3), (1,)).astype(jnp.int32)
    rank = jnp.reshape(lax.axis_index("head"), (1,)).astype(jnp.int32)
    parts = key_value(tokens, w_key, w_value, local_levels, far_levels, [end, rank])
    levels, tops = parts[:local_levels], parts[local_levels:]
    fars = [exchange(tops[bit], "seq", d) for d, bit in enumerate(far_bits, 1)]
    query = step(project, tokens, w_query)
    powers, near = step(near_powers, query, levels)
    grad = step(project, cotangent, w_out)
    attended, attended_t, stats = step(forward, query, powers, near, levels, fars, far_bits)

    line = Line("seq", "head", end, step)
    pieces = 2
    rows = tokens.shape[1] // pieces
    line.enter(step(weight_terms, attended_t, cotangent, inner, 0, 0, pieces))
    earlier = [
        step(backward_first, h, query, grad, attended_t, stats, levels, fars, far_bits)
        for h in range(inner // HEAD_DIM - 1)
    ]
    line.enter(step(weight_terms, attended_t, cotangent, inner, 0, 1, pieces))
    line.meet(rows)
    parts = step(project_split, rank, [attended], [w_out], "head")
    mixed = Scatter(parts, "head", step)
    dquery, dkv, query_first, query_second, *away = step(
        backward_last, earlier, query, grad, attended_t, stats, tokens, levels, fars, far_bits, pieces
    )
    dkvs = [made[1] for made in earlier] + [dkv]
    backs = [exchange(piece, "seq", d) for d, piece in enumerate(away, 1)]
    line.meet(rows)
    mixed.advance()
    line.enter(step(relay, query_first))
    line.turn(query_second)
    dkey, dvalue, dkv_t = step(close_keys, dkvs, backs, far_bits, local_levels)
    key_first = step(weight_terms, dkv_t, tokens, inner, 0, 0, pieces)
    key_second = step(weight_terms, dkv_t, tokens, inner, 0, 1, pieces)
    line.meet(rows)
    line.turn(key_first)
    keep, send = step(project_split, rank, [dquery, dkey, dvalue], [w_query, w_key, w_value], "head")
    line.meet(rows)
    value_first = step(weight_terms, dkv_t, tokens, inner, 1, 0, pieces)
    line.turn(key_second)
    line.meet(rows)
    tokens_grad = Scatter([keep, step(relay, send)], "head", step)
    line.turn(value_first)
    mixed = mixed.result()
    value_second = step(weight_terms, dkv_t, tokens, inner, 1, 1, pieces)
    line.meet(rows)
    line.turn(value_second)
    out_grad = line.output(0, pieces)
    line.meet(rows)
    tokens_grad.advance()
    line.leave()
    line.meet(rows)
    query_grad = line.output(2, pieces)
    line.leave()
    key_grad = line.output(4, pieces)
    line.leave()
    tokens_grad = tokens_grad.result()
    value_grad = line.output(6, pieces)
    return mixed, tokens_grad, query_grad, key_grad, value_grad, out_grad


def solution(mesh):
    return jax.shard_map(
        per_device,
        mesh=mesh,
        in_specs=(
            P(("groups", "seq"), None),
            P(None, "head"),
            P(None, "head"),
            P(None, "head"),
            P(None, "head"),
            P(("groups", "seq"), None),
        ),
        out_specs=(
            P(("groups", "seq"), "head"),
            P(("groups", "seq"), "head"),
            P("groups", "head"),
            P("groups", "head"),
            P("groups", "head"),
            P("groups", "head"),
        ),
        check_vma=False,
    )
```

```python
import functools
import math

import jax
import jax.numpy as jnp
from jax import lax
from jax.experimental import pallas as pl
from jax.experimental.pallas import tpu as pltpu
from jax.sharding import PartitionSpec as P

HEAD_DIM = 128
BLOCK = 128
BF16 = jnp.bfloat16
F32 = jnp.float32
MIB = 1024 * 1024

NN = (((1,), (0,)), ((), ()))
NT = (((1,), (1,)), ((), ()))
TN = (((0,), (0,)), ((), ()))


def dot(left, right, dims=NN):
    return lax.dot_general(left, right, dims, preferred_element_type=F32)


def params(mib):
    return pltpu.CompilerParams(vmem_limit_bytes=mib * MIB)


def cost(microseconds):
    return pl.CostEstimate(flops=int(microseconds * 1150e6) + 1, bytes_accessed=1, transcendentals=0)


def run(body, ready, after=(), in_specs=None, **options):
    count, extra = len(ready), len(after)

    def kernel(*refs):
        body(*refs[:count], *refs[count + extra :])

    in_specs = in_specs or [pl.BlockSpec(memory_space=pltpu.VMEM)] * count
    in_specs = in_specs + [pl.BlockSpec(memory_space=pl.ANY)] * extra
    return pl.pallas_call(kernel, in_specs=in_specs, **options)(*ready, *after)


def shape(rows, cols, dtype=BF16):
    return jax.ShapeDtypeStruct((rows, cols), dtype)


def whole(rows, cols):
    return pl.BlockSpec((rows, cols), lambda *_: (0, 0))


def pool_matrix(rows):
    row = lax.broadcasted_iota(jnp.int32, (rows // 2, rows), 0)
    col = lax.broadcasted_iota(jnp.int32, (rows // 2, rows), 1)
    return jnp.where(jnp.right_shift(col, 1) == row, 0.5, 0.0).astype(BF16)


def spread_matrix(rows, step_bits, offset, cols, weight):
    row = lax.broadcasted_iota(jnp.int32, (rows, cols), 0) + offset
    col = lax.broadcasted_iota(jnp.int32, (rows, cols), 1)
    return jnp.where(jnp.right_shift(row, step_bits) == col, weight, 0.0).astype(BF16)


def key_value_body(local_levels, far_levels, parts, tok_hbm, wk_hbm, wv_hbm, *refs):
    out_hbm = refs[:local_levels]
    far = refs[local_levels : local_levels + far_levels]
    refs = refs[local_levels + far_levels :]
    tok_ref, wk_ref, wv_ref = refs[:3]
    levels = refs[3 : 3 + local_levels]
    in_sems, out_sems = refs[3 + local_levels :]
    part = tok_ref.shape[0] // parts

    def fetch(source, target, i):
        copy = pltpu.make_async_copy(source, target, in_sems.at[i])
        copy.start()
        return copy

    def flush(i):
        copy = pltpu.make_async_copy(levels[i], out_hbm[i], out_sems.at[i])
        copy.start()
        return copy

    weights = [fetch(wk_hbm, wk_ref, 0), fetch(wv_hbm, wv_ref, 1)]
    tiles = []
    for p in range(parts):
        rows = pl.ds(p * part, part)
        tiles.append(fetch(tok_hbm.at[rows], tok_ref.at[rows], 2 + p))
    for copy in weights:
        copy.wait()
    for p in range(parts):
        tiles[p].wait()
        here = slice(p * part, (p + 1) * part)
        x = tok_ref[here, :]
        both = jnp.concatenate([dot(x, wk_ref[...]), dot(x, wv_ref[...])], axis=1)
        levels[0][here, :] = both.astype(BF16)
    flushes = [flush(0)]
    pool = pool_matrix(part)
    for i in range(1, local_levels):
        source = levels[i - 1]
        for low in range(0, source.shape[0], part):
            mean = dot(pool, source[low : low + part, :])
            levels[i][low // 2 : (low + part) // 2, :] = mean.astype(BF16)
        flushes.append(flush(i))
    rows = dot(pool, levels[-1][...]).astype(BF16)
    for i in range(far_levels):
        if i:
            rows = dot(pool_matrix(rows.shape[0]), rows).astype(BF16)
        far[i][...] = rows
    for copy in flushes:
        copy.wait()


def key_value(tokens, w_key, w_value, local_levels, far_levels, after):
    tok_rows, width = tokens.shape
    inner = w_key.shape[1]
    parts = tok_rows // (2 * BLOCK)
    held = [(tok_rows >> i, 2 * inner) for i in range(local_levels)]
    tops = [(BLOCK >> i, 2 * inner) for i in range(far_levels)]
    return run(
        functools.partial(key_value_body, local_levels, far_levels, parts),
        [tokens, w_key, w_value],
        after,
        in_specs=[pl.BlockSpec(memory_space=pl.ANY)] * 3,
        out_specs=[pl.BlockSpec(memory_space=pl.ANY)] * len(held)
        + [pl.BlockSpec(memory_space=pltpu.VMEM)] * len(tops),
        out_shape=[shape(*dims) for dims in held + tops],
        scratch_shapes=[pltpu.VMEM((tok_rows, width), BF16)]
        + [pltpu.VMEM((width, inner), BF16)] * 2
        + [pltpu.VMEM(dims, BF16) for dims in held]
        + [pltpu.SemaphoreType.DMA((parts + 2,)), pltpu.SemaphoreType.DMA((len(held),))],
        compiler_params=params(56),
        cost_estimate=cost(5.0),
    )


def project_body(left_ref, weight_ref, out_ref):
    out_ref[...] = dot(left_ref[...], weight_ref[...]).astype(BF16)


def project(left, weight, after):
    tok_rows, width = left.shape
    inner = weight.shape[1]
    return run(
        project_body,
        [left, weight],
        after,
        out_shape=shape(tok_rows, inner),
        compiler_params=params(4),
        cost_estimate=cost(0.7),
    )


class KeySet:
    def __init__(self, far_rows, far_bits, local_levels):
        mids = local_levels - 1
        self.sizes = [2 * BLOCK] + [BLOCK] * mids + list(far_rows)
        self.bounds = [sum(self.sizes[:i]) for i in range(len(self.sizes) + 1)]
        steps = [0] + list(range(1, local_levels)) + [local_levels + b for b in far_bits]
        self.biases = [float(step) for step in steps]
        self.mids = mids
        self.far_start = self.bounds[1 + mids]
        self.factor = math.log2(math.e) / math.sqrt(HEAD_DIM)

    def here(self, m):
        return pl.ds(pl.multiple_of(m * 2 * BLOCK, 2 * BLOCK), 2 * BLOCK)

    def seats(self, m):
        for i in range(self.mids):
            sibling = jnp.bitwise_xor(jnp.right_shift(m, i), 1)
            yield pl.ds(pl.multiple_of(sibling * BLOCK, BLOCK), BLOCK)

    def near(self, m, level_refs, cols):
        rows = [level_refs[0][self.here(m), cols]]
        rows += [ref[seat, cols] for ref, seat in zip(level_refs[1:], self.seats(m))]
        return rows

    def far(self, far_refs, cols):
        return [ref[:, cols] for ref in far_refs]

    def pieces(self, array, first=0, count=None):
        base = self.bounds[first]
        ends = self.bounds[first:] if count is None else self.bounds[first : first + count + 1]
        return [array[a - base : b - base] for a, b in zip(ends, ends[1:])]

    def top(self, pieces, first=0):
        tops = [
            jnp.max(piece, axis=0, keepdims=True) * self.factor + bias
            for piece, bias in zip(pieces, self.biases[first:])
        ]
        return functools.reduce(jnp.maximum, tops)

    def powers(self, pieces, top, first=0):
        return jnp.concatenate(
            [
                jnp.exp2(piece * self.factor + (bias - top))
                for piece, bias in zip(pieces, self.biases[first:])
            ],
            axis=0,
        )


def head_columns(h, inner):
    low = h * HEAD_DIM
    return slice(low, low + HEAD_DIM), slice(inner + low, inner + low + HEAD_DIM)


def near_body(local_levels, q_ref, *refs):
    level_refs = refs[:local_levels]
    power_ref, stat_ref = refs[local_levels:]
    tok_rows, inner = q_ref.shape
    heads = inner // HEAD_DIM
    keyset = KeySet([], [], local_levels)
    rows = keyset.far_start

    def step(m, carry):
        here = keyset.here(m)
        for h in range(heads):
            cols, _ = head_columns(h, inner)
            keys = jnp.concatenate(keyset.near(m, level_refs, cols), axis=0)
            pieces = keyset.pieces(dot(keys, q_ref[here, cols], NT))
            top = keyset.top(pieces)
            powers = keyset.powers(pieces, top)
            stat_ref[h : h + 1, here] = top
            stat_ref[heads + h : heads + h + 1, here] = jnp.sum(powers, axis=0, keepdims=True)
            power_ref[pl.ds(pl.multiple_of((m * heads + h) * rows, rows), rows), :] = powers
        return carry

    lax.fori_loop(0, tok_rows // (2 * BLOCK), step, 0)


def near_powers(query, levels, after):
    tok_rows, inner = query.shape
    heads = inner // HEAD_DIM
    pairs = tok_rows // (2 * BLOCK)
    rows = (len(levels) + 1) * BLOCK
    return run(
        functools.partial(near_body, len(levels)),
        [query, *levels],
        after,
        out_shape=[shape(pairs * heads * rows, 2 * BLOCK, F32), shape(2 * heads, tok_rows, F32)],
        compiler_params=params(6),
        cost_estimate=cost(2.3),
    )


def forward_body(local_levels, far_bits, *refs):
    fars = len(far_bits)
    q_ref, power_ref, near_ref = refs[:3]
    level_refs = refs[3 : 3 + local_levels]
    far_refs = refs[3 + local_levels : 3 + local_levels + fars]
    att_ref, att_t_ref, stat_ref = refs[3 + local_levels + fars :]
    tok_rows, inner = q_ref.shape
    heads = inner // HEAD_DIM
    keyset = KeySet([r.shape[0] for r in far_refs], far_bits, local_levels)
    rows = keyset.far_start

    def step(m, carry):
        here = keyset.here(m)
        for h in range(heads):
            cols, vcols = head_columns(h, inner)
            second = heads + h
            keys = jnp.concatenate(keyset.far(far_refs, cols), axis=0)
            values = keyset.near(m, level_refs, vcols) + keyset.far(far_refs, vcols)
            values = jnp.concatenate(values, axis=0)
            first = local_levels
            pieces = keyset.pieces(dot(keys, q_ref[here, cols], NT), first)
            near_top = near_ref[h : h + 1, here]
            top = jnp.maximum(near_top, keyset.top(pieces, first))
            shrink = jnp.exp2(near_top - top)
            powers = keyset.powers(pieces, top, first)
            total = near_ref[second : second + 1, here] * shrink
            total = total + jnp.sum(powers, axis=0, keepdims=True)
            inverse = 1.0 / total
            place = pl.ds(pl.multiple_of((m * heads + h) * rows, rows), rows)
            near_probs = (power_ref[place, :] * (shrink * inverse)).astype(BF16)
            far_probs = (powers * inverse).astype(BF16)
            probs_b = jnp.concatenate([near_probs, far_probs], axis=0)
            att_t = dot(values, probs_b, TN).astype(BF16)
            att_t_ref[cols, here] = att_t
            att_ref[here, cols] = att_t.T
            stat_ref[h : h + 1, here] = top
            stat_ref[second : second + 1, here] = inverse
        return carry

    lax.fori_loop(0, tok_rows // (2 * BLOCK), step, 0)


def forward(query, powers, near, levels, fars, far_bits, after):
    tok_rows, inner = query.shape
    heads = inner // HEAD_DIM
    set_rows = (len(levels) + 1) * BLOCK + sum(f.shape[0] for f in fars)
    return run(
        functools.partial(forward_body, len(levels), far_bits),
        [query, powers, near, *levels, *fars],
        after,
        out_shape=[
            shape(tok_rows, inner),
            shape(inner, tok_rows),
            shape(2 * heads, tok_rows, F32),
        ],
        compiler_params=params(6),
        cost_estimate=cost(4.0),
    )


def backward_body(local_levels, far_bits, pieces, *refs):
    mids = local_levels - 1
    fars = len(far_bits)
    q_ref, g_ref, att_t_ref, stat_ref, tok_ref = refs[:5]
    level_refs = refs[5 : 5 + local_levels]
    far_refs = refs[5 + local_levels : 5 + local_levels + fars]
    outs = refs[5 + local_levels + fars :]
    dq_ref, dkv_ref = outs[:2]
    term_refs = outs[2 : 2 + pieces]
    dfar_refs = outs[2 + pieces : 2 + pieces + fars]
    dmid_refs = outs[2 + pieces + fars : 2 + pieces + fars + mids]
    dq_t_ref, acc_ref = outs[-2:]
    tok_rows, inner = q_ref.shape
    heads = inner // HEAD_DIM
    score_scale = 1.0 / math.sqrt(HEAD_DIM)
    keyset = KeySet([r.shape[0] for r in far_refs], far_bits, local_levels)

    for ref in (*dmid_refs, acc_ref):
        ref[...] = jnp.zeros_like(ref)

    def step(m, carry):
        here = keyset.here(m)
        for h in range(heads):
            cols, vcols = head_columns(h, inner)
            keys, values = (
                jnp.concatenate(keyset.near(m, level_refs, c) + keyset.far(far_refs, c), axis=0)
                for c in (cols, vcols)
            )
            q = q_ref[here, cols]
            g = g_ref[here, cols]
            top = stat_ref[h : h + 1, here]
            inverse = stat_ref[heads + h : heads + h + 1, here]
            probs = keyset.powers(keyset.pieces(dot(keys, q, NT)), top) * inverse
            att_t = att_t_ref[cols, here].astype(F32)
            delta = jnp.sum(g.T.astype(F32) * att_t, axis=0, keepdims=True)
            grads = (probs * (dot(values, g, NT) - delta) * score_scale).astype(BF16)
            dq_t = dot(keys, grads, TN).astype(BF16)
            dq_t_ref[cols, here] = dq_t
            dq_ref[here, cols] = dq_t.T
            for part, place in ((dot(grads, q), cols), (dot(probs.astype(BF16), g), vcols)):
                own, *sides = keyset.pieces(part)
                dkv_ref[here, place] = own
                for ref, seat, side in zip(dmid_refs, keyset.seats(m), sides):
                    ref[seat, place] += side
                acc_ref[:, place] += part[keyset.far_start :]
        return carry

    lax.fori_loop(0, tok_rows // (2 * BLOCK), step, 0)
    width = term_refs[-1].shape[0]
    low = 0
    for ref in dfar_refs:
        ref[...] = acc_ref[low : low + ref.shape[0]].astype(BF16)
        low += ref.shape[0]
    for i, ref in enumerate(term_refs):
        part = dot(dq_t_ref[...], tok_ref[:, i * width : (i + 1) * width])
        ref[...] = part.astype(BF16).T
    fan = spread_matrix(2 * BLOCK, 1, 0, BLOCK, 0.5)
    targets = (dkv_ref, *dmid_refs)
    for i in reversed(range(mids)):
        for t in range(dmid_refs[i].shape[0] // BLOCK):
            part = dmid_refs[i][t * BLOCK : (t + 1) * BLOCK, :]
            high = part.astype(BF16)
            low = (part - high.astype(F32)).astype(BF16)
            rows = slice(2 * t * BLOCK, 2 * (t + 1) * BLOCK)
            targets[i][rows, :] += dot(fan, high) + dot(fan, low)


def backward(query, grad, attended_t, stats, tokens, levels, fars, far_bits, pieces, after):
    tok_rows, inner = query.shape
    far_rows = sum(f.shape[0] for f in fars)
    set_rows = (len(levels) + 1) * BLOCK + far_rows
    return run(
        functools.partial(backward_body, len(levels), far_bits, pieces),
        [query, grad, attended_t, stats, tokens, *levels, *fars],
        after,
        out_shape=[shape(tok_rows, inner), shape(tok_rows, 2 * inner, F32)]
        + [shape(tokens.shape[1] // pieces, inner)] * pieces
        + [shape(*f.shape) for f in fars],
        scratch_shapes=[pltpu.VMEM(level.shape, F32) for level in levels[1:]]
        + [pltpu.VMEM((inner, tok_rows), BF16), pltpu.VMEM((far_rows, 2 * inner), F32)],
        compiler_params=params(10),
        cost_estimate=cost(8.0),
    )


def term_body(which, low, left_ref, right_ref, out_ref):
    width, inner = out_ref.shape
    left = left_ref[which * inner : (which + 1) * inner, :]
    out_ref[...] = dot(left, right_ref[:, low : low + width]).astype(BF16).T


def weight_terms(left_t, right, inner, which, part, parts, after):
    tok_rows = left_t.shape[1]
    width = right.shape[1] // parts
    return run(
        functools.partial(term_body, which, part * width),
        [left_t, right],
        after,
        out_shape=shape(width, inner),
        compiler_params=params(3),
        cost_estimate=cost(0.2),
    )


def close_body(local_levels, far_bits, dkv_ref, *refs):
    backs = [ref[...] for ref in refs[: len(far_bits)]]
    dk_ref, dv_ref, dkv_t_ref = refs[len(far_bits) :]
    inner = dk_ref.shape[1]
    tile = 2 * BLOCK
    for t in range(dkv_ref.shape[0] // tile):
        here = slice(t * tile, (t + 1) * tile)
        total = dkv_ref[here, :]
        for back, bit in zip(backs, far_bits):
            weight = 0.5 ** (local_levels + bit)
            fan = spread_matrix(tile, local_levels + bit, t * tile, back.shape[0], weight)
            total = total + dot(fan, back)
        final = total.astype(BF16)
        dk_ref[here, :] = final[:, :inner]
        dv_ref[here, :] = final[:, inner:]
        dkv_t_ref[:, here] = final.T


def close_keys(dkv, backs, far_bits, local_levels, after):
    tok_rows, double = dkv.shape
    inner = double // 2
    return run(
        functools.partial(close_body, local_levels, far_bits),
        [dkv, *backs],
        after,
        out_shape=[shape(tok_rows, inner), shape(tok_rows, inner), shape(double, tok_rows)],
        compiler_params=params(5),
        cost_estimate=cost(0.2),
    )


def split_body(count, parts, rank_ref, *refs):
    lefts, weights = refs[:count], refs[count : 2 * count]
    outs = refs[2 * count :]
    width = weights[0].shape[0] // parts
    for r in range(parts):
        owner = jnp.bitwise_xor(rank_ref[0], r)
        rows = pl.ds(pl.multiple_of(owner * width, width), width)
        total = None
        for left, weight in zip(lefts, weights):
            product = dot(left[...], weight[rows, :], NT)
            total = product if total is None else total + product
        place = r // 2 * width
        outs[r % 2][:, place : place + width] = total.astype(BF16)


def project_split(rank, lefts, weights, axis, after):
    count = len(lefts)
    parts = lax.axis_size(axis)
    tok_rows, inner = lefts[0].shape
    width = weights[0].shape[0]
    return run(
        functools.partial(split_body, count, parts),
        [rank, *lefts, *weights],
        after,
        in_specs=[pl.BlockSpec(memory_space=pltpu.SMEM)]
        + [pl.BlockSpec(memory_space=pltpu.VMEM)] * (2 * count),
        out_shape=[shape(tok_rows, width // 2)] * 2,
        compiler_params=params(5),
        cost_estimate=cost(1.0),
    )


def exchange(block, axis, distance):
    count = lax.axis_size(axis)
    return lax.ppermute(block, axis, [(i, i ^ distance) for i in range(count)])


def add(left, right):
    return (left.astype(F32) + right.astype(F32)).astype(BF16)


def term_half_body(chunk_ref, into_ref, out_ref):
    rows = slice(0, out_ref.shape[0])
    out_ref[...] = (chunk_ref[rows, :].astype(F32) + into_ref[rows, :].astype(F32)).astype(BF16)


def half_sum(chunk, into, rows, weight, after):
    return run(
        term_half_body,
        [chunk, into],
        after,
        out_shape=shape(rows, chunk.shape[1]),
        compiler_params=params(3),
        cost_estimate=cost(weight),
    )


def scatter_body(pieces, keep_ref, into_ref, even_ref, odd_ref):
    width = keep_ref.shape[1] // pieces
    for i in range(pieces):
        here = slice(i * width, (i + 1) * width)
        place = slice(i // 2 * width, (i // 2 + 1) * width)
        total = keep_ref[:, here].astype(F32) + into_ref[:, here].astype(F32)
        (even_ref, odd_ref)[i % 2][:, place] = total.astype(BF16)


def last_body(left_ref, right_ref, token_ref, out_ref):
    token_ref[...] = jnp.zeros_like(token_ref)
    out_ref[...] = (left_ref[...].astype(F32) + right_ref[...].astype(F32)).astype(BF16)


def last_sum(left, right, after):
    return run(
        last_body,
        [left, right],
        after,
        out_shape=[shape(8, 128, F32), shape(*left.shape)],
        compiler_params=params(3),
        cost_estimate=cost(0.9),
    )


def scatter_step(keep, into, pieces, after):
    rows, width = keep.shape
    return run(
        functools.partial(scatter_body, pieces),
        [keep, into],
        after,
        out_shape=[shape(rows, width // 2)] * 2,
        compiler_params=params(4),
        cost_estimate=cost(0.2),
    )


def turn_body(end_ref, half_ref, across_ref, chunk_ref, total_ref, send_ref):
    total = (half_ref[...].astype(F32) + across_ref[...].astype(F32)).astype(BF16)
    total_ref[...] = total

    @pl.when(end_ref[0] == 1)
    def _():
        send_ref[...] = chunk_ref[...]

    @pl.when(end_ref[0] == 0)
    def _():
        send_ref[...] = total


def turn(end, half, across, chunk, weight, after):
    return run(
        turn_body,
        [end, half, across, chunk],
        after,
        in_specs=[pl.BlockSpec(memory_space=pltpu.SMEM)]
        + [pl.BlockSpec(memory_space=pltpu.VMEM)] * 3,
        out_shape=[shape(*half.shape)] * 2,
        compiler_params=params(2),
        cost_estimate=cost(weight),
    )


def output_body(count, end_ref, *refs):
    totals, ends, (token_ref, out_ref) = refs[:count], refs[count : 2 * count], refs[2 * count :]
    token_ref[...] = jnp.zeros_like(token_ref)
    rows = totals[0].shape[0]

    for flag, sources in ((0, totals), (1, ends)):

        @pl.when(end_ref[0] == flag)
        def _():
            for i, ref in enumerate(sources):
                out_ref[i * rows : (i + 1) * rows, :] = ref[...]


def output(end, totals, ends, after):
    count = len(totals)
    rows, width = totals[0].shape
    return run(
        functools.partial(output_body, count),
        [end, *totals, *ends],
        after,
        in_specs=[pl.BlockSpec(memory_space=pltpu.SMEM)]
        + [pl.BlockSpec(memory_space=pltpu.VMEM)] * (2 * count),
        out_shape=[shape(8, 128, F32), shape(count * rows, width)],
        compiler_params=params(4),
        cost_estimate=cost(0.9),
    )


def relay_body(source_ref, target_ref):
    target_ref[...] = source_ref[...]


def relay(block, after):
    return run(
        relay_body,
        [block],
        after,
        out_shape=shape(*block.shape),
        compiler_params=params(3),
        cost_estimate=cost(0.2),
    )


def relay_all_body(*refs):
    count = len(refs) // 2
    for source, target in zip(refs[:count], refs[count:]):
        target[...] = source[...]


def relay_all(blocks, after):
    return run(
        relay_all_body,
        list(blocks),
        after,
        out_shape=[shape(*block.shape) for block in blocks],
        compiler_params=params(3),
        cost_estimate=cost(0.2),
    )


class Line:
    lag = 3
    half_weights = (3.0, 3.0, 3.0, 3.0, 3.0, 3.0, 3.0, 0.5)
    turn_weights = (4.0, 4.0, 3.0, 3.0, 4.0, 2.0, 0.5, 0.5)

    def __init__(self, axis, other, end, step):
        self.axis, self.axes, self.step = axis, (axis, other), step
        self.count = lax.axis_size(axis)
        self.end = end
        width = lax.axis_size(other)
        self.across = []
        for place in range(self.count):
            for seat in range(width):
                target = (place, seat ^ 1 if width > 1 else seat)
                if place & 3 in (1, 2):
                    target = (place ^ 3, seat)
                self.across.append((place * width + seat, target[0] * width + target[1]))
        self.chunks, self.into, self.halves, self.crossed, self.totals = [], [], [], [], []

    def enter(self, chunk):
        self.chunks.append(chunk)
        self.into.append(exchange(chunk, self.axis, 1))

    def meet(self, rows):
        k = len(self.halves)
        weight = self.half_weights[k]
        half = self.step(half_sum, self.chunks[k], self.into[k], rows, weight)
        self.halves.append(half)
        self.crossed.append(lax.ppermute(half, self.axes, self.across))

    def turn(self, chunk):
        old = len(self.totals)
        half, crossed = self.halves[old], self.crossed[old]
        weight = self.turn_weights[old]
        total, send = self.step(turn, self.end, half, crossed, chunk, weight)
        self.totals.append(total)
        self.chunks.append(chunk)
        self.into.append(exchange(send, self.axis, 1))

    def leave(self):
        old = len(self.totals)
        half = self.halves[old]
        weight = self.turn_weights[old]
        total = self.step(half_sum, half, self.crossed[old], half.shape[0], weight)
        self.totals.append(total)
        self.into.append(exchange(total, self.axis, 1))

    def output(self, first, count):
        ends = self.into[first + self.lag : first + self.lag + count]
        _, result = self.step(output, self.end, self.totals[first : first + count], ends)
        distance = 4
        while distance < self.count:
            result = add(result, exchange(result, self.axis, distance))
            distance *= 2
        return result


class Scatter:
    def __init__(self, parts, axis, step):
        self.axis, self.step = axis, step
        self.pieces = lax.axis_size(axis) // 2
        self.keep, send = parts
        self.distance = 1
        self.into = exchange(send, axis, 1)

    def advance(self):
        while self.pieces > 1:
            self.keep, send = self.step(scatter_step, self.keep, self.into, self.pieces)
            self.distance *= 2
            self.pieces //= 2
            self.into = exchange(send, self.axis, self.distance)

    def result(self):
        return self.step(last_sum, self.keep, self.into)[1]


def per_device(tokens, w_query, w_key, w_value, w_out, cotangent):
    tok_rows = tokens.shape[0]
    inner = w_query.shape[1]
    local_levels = (tok_rows // BLOCK).bit_length() - 1
    count = lax.axis_size("seq")
    far_levels = count.bit_length() - 1
    far_bits = [d.bit_length() - 1 for d in range(1, count)]

    last = []

    def step(kernel, *operands):
        made = kernel(*operands, list(last))
        last[:] = made[:1] if isinstance(made, (list, tuple)) else [made]
        return made

    place = jnp.bitwise_and(lax.axis_index("seq"), 3)
    end = jnp.reshape((place == 0) | (place == 3), (1,)).astype(jnp.int32)
    rank = jnp.reshape(lax.axis_index("head"), (1,)).astype(jnp.int32)
    parts = key_value(tokens, w_key, w_value, local_levels, far_levels, [end, rank])
    levels, tops = parts[:local_levels], parts[local_levels:]
    fars = [exchange(tops[bit], "seq", d) for d, bit in enumerate(far_bits, 1)]
    query = step(project, tokens, w_query)
    powers, near = step(near_powers, query, levels)
    grad = step(project, cotangent, w_out)
    attended, attended_t, stats = step(forward, query, powers, near, levels, fars, far_bits)

    line = Line("seq", "head", end, step)
    pieces = 2
    rows = tokens.shape[1] // pieces
    line.enter(step(weight_terms, attended_t, cotangent, inner, 0, 0, pieces))
    line.enter(step(weight_terms, attended_t, cotangent, inner, 0, 1, pieces))
    parts = step(project_split, rank, [attended], [w_out], "head")
    mixed = Scatter(parts, "head", step)
    dquery, dkv, query_first, query_second, *away = step(
        backward, query, grad, attended_t, stats, tokens, levels, fars, far_bits, pieces
    )
    line.meet(rows)
    mixed.advance()
    away = step(relay_all, away)
    backs = [exchange(piece, "seq", d) for d, piece in enumerate(away, 1)]
    line.meet(rows)
    dkey, dvalue, dkv_t = step(close_keys, dkv, backs, far_bits, local_levels)
    line.enter(step(relay, query_first))
    key_first = step(weight_terms, dkv_t, tokens, inner, 0, 0, pieces)
    line.turn(query_second)
    key_second = step(weight_terms, dkv_t, tokens, inner, 0, 1, pieces)
    line.meet(rows)
    line.turn(key_first)
    keep, send = step(project_split, rank, [dquery, dkey, dvalue], [w_query, w_key, w_value], "head")
    line.meet(rows)
    value_first = step(weight_terms, dkv_t, tokens, inner, 1, 0, pieces)
    line.turn(key_second)
    line.meet(rows)
    tokens_grad = Scatter([keep, step(relay, send)], "head", step)
    line.turn(value_first)
    mixed = mixed.result()
    value_second = step(weight_terms, dkv_t, tokens, inner, 1, 1, pieces)
    line.meet(rows)
    line.turn(value_second)
    out_grad = line.output(0, pieces)
    line.meet(rows)
    tokens_grad.advance()
    line.leave()
    line.meet(rows)
    query_grad = line.output(2, pieces)
    line.leave()
    key_grad = line.output(4, pieces)
    line.leave()
    tokens_grad = tokens_grad.result()
    value_grad = line.output(6, pieces)
    return mixed, tokens_grad, query_grad, key_grad, value_grad, out_grad


def solution(mesh):
    return jax.shard_map(
        per_device,
        mesh=mesh,
        in_specs=(
            P(("groups", "seq"), None),
            P(None, "head"),
            P(None, "head"),
            P(None, "head"),
            P(None, "head"),
            P(("groups", "seq"), None),
        ),
        out_specs=(
            P(("groups", "seq"), "head"),
            P(("groups", "seq"), "head"),
            P("groups", "head"),
            P("groups", "head"),
            P("groups", "head"),
            P("groups", "head"),
        ),
        check_vma=False,
    )
```

```python
import functools
import math

import jax
import jax.numpy as jnp
from jax import lax
from jax.experimental import pallas as pl
from jax.experimental.pallas import tpu as pltpu
from jax.sharding import PartitionSpec as P

HEAD_DIM = 128
BLOCK = 128
BF16 = jnp.bfloat16
F32 = jnp.float32
MIB = 1024 * 1024

NN = (((1,), (0,)), ((), ()))
NT = (((1,), (1,)), ((), ()))
TN = (((0,), (0,)), ((), ()))


def dot(left, right, dims=NN):
    return lax.dot_general(left, right, dims, preferred_element_type=F32)


def params(mib):
    return pltpu.CompilerParams(vmem_limit_bytes=mib * MIB)


def cost(microseconds):
    return pl.CostEstimate(flops=int(microseconds * 1150e6) + 1, bytes_accessed=1, transcendentals=0)


def run(body, ready, after=(), in_specs=None, **options):
    count, extra = len(ready), len(after)

    def kernel(*refs):
        body(*refs[:count], *refs[count + extra :])

    in_specs = in_specs or [pl.BlockSpec(memory_space=pltpu.VMEM)] * count
    in_specs = in_specs + [pl.BlockSpec(memory_space=pl.ANY)] * extra
    return pl.pallas_call(kernel, in_specs=in_specs, **options)(*ready, *after)


def shape(rows, cols, dtype=BF16):
    return jax.ShapeDtypeStruct((rows, cols), dtype)


def whole(rows, cols):
    return pl.BlockSpec((rows, cols), lambda *_: (0, 0))


def pool_matrix(rows):
    row = lax.broadcasted_iota(jnp.int32, (rows // 2, rows), 0)
    col = lax.broadcasted_iota(jnp.int32, (rows // 2, rows), 1)
    return jnp.where(jnp.right_shift(col, 1) == row, 0.5, 0.0).astype(BF16)


def spread_matrix(rows, step_bits, offset, cols, weight):
    row = lax.broadcasted_iota(jnp.int32, (rows, cols), 0) + offset
    col = lax.broadcasted_iota(jnp.int32, (rows, cols), 1)
    return jnp.where(jnp.right_shift(row, step_bits) == col, weight, 0.0).astype(BF16)


def key_value_body(local_levels, far_levels, parts, tok_hbm, wk_hbm, wv_hbm, *refs):
    out_hbm = refs[:local_levels]
    far = refs[local_levels : local_levels + far_levels]
    refs = refs[local_levels + far_levels :]
    tok_ref, wk_ref, wv_ref = refs[:3]
    levels = refs[3 : 3 + local_levels]
    in_sems, out_sems = refs[3 + local_levels :]
    part = tok_ref.shape[0] // parts

    def fetch(source, target, i):
        copy = pltpu.make_async_copy(source, target, in_sems.at[i])
        copy.start()
        return copy

    def flush(i):
        copy = pltpu.make_async_copy(levels[i], out_hbm[i], out_sems.at[i])
        copy.start()
        return copy

    weights = [fetch(wk_hbm, wk_ref, 0), fetch(wv_hbm, wv_ref, 1)]
    tiles = []
    for p in range(parts):
        rows = pl.ds(p * part, part)
        tiles.append(fetch(tok_hbm.at[rows], tok_ref.at[rows], 2 + p))
    for copy in weights:
        copy.wait()
    for p in range(parts):
        tiles[p].wait()
        here = slice(p * part, (p + 1) * part)
        x = tok_ref[here, :]
        both = jnp.concatenate([dot(x, wk_ref[...]), dot(x, wv_ref[...])], axis=1)
        levels[0][here, :] = both.astype(BF16)
    flushes = [flush(0)]
    pool = pool_matrix(part)
    for i in range(1, local_levels):
        source = levels[i - 1]
        for low in range(0, source.shape[0], part):
            mean = dot(pool, source[low : low + part, :])
            levels[i][low // 2 : (low + part) // 2, :] = mean.astype(BF16)
        flushes.append(flush(i))
    rows = dot(pool, levels[-1][...]).astype(BF16)
    for i in range(far_levels):
        if i:
            rows = dot(pool_matrix(rows.shape[0]), rows).astype(BF16)
        far[i][...] = rows
    for copy in flushes:
        copy.wait()


def key_value(tokens, w_key, w_value, local_levels, far_levels, after):
    tok_rows, width = tokens.shape
    inner = w_key.shape[1]
    parts = tok_rows // (2 * BLOCK)
    held = [(tok_rows >> i, 2 * inner) for i in range(local_levels)]
    tops = [(BLOCK >> i, 2 * inner) for i in range(far_levels)]
    return run(
        functools.partial(key_value_body, local_levels, far_levels, parts),
        [tokens, w_key, w_value],
        after,
        in_specs=[pl.BlockSpec(memory_space=pl.ANY)] * 3,
        out_specs=[pl.BlockSpec(memory_space=pl.ANY)] * len(held)
        + [pl.BlockSpec(memory_space=pltpu.VMEM)] * len(tops),
        out_shape=[shape(*dims) for dims in held + tops],
        scratch_shapes=[pltpu.VMEM((tok_rows, width), BF16)]
        + [pltpu.VMEM((width, inner), BF16)] * 2
        + [pltpu.VMEM(dims, BF16) for dims in held]
        + [pltpu.SemaphoreType.DMA((parts + 2,)), pltpu.SemaphoreType.DMA((len(held),))],
        compiler_params=params(56),
        cost_estimate=cost(5.0),
    )


def project_body(left_ref, weight_ref, out_ref):
    out_ref[...] = dot(left_ref[...], weight_ref[...]).astype(BF16)


def project(left, weight, after):
    tok_rows, width = left.shape
    inner = weight.shape[1]
    return run(
        project_body,
        [left, weight],
        after,
        out_shape=shape(tok_rows, inner),
        compiler_params=params(4),
        cost_estimate=cost(0.7),
    )


class KeySet:
    def __init__(self, far_rows, far_bits, local_levels):
        mids = local_levels - 1
        self.sizes = [2 * BLOCK] + [BLOCK] * mids + list(far_rows)
        self.bounds = [sum(self.sizes[:i]) for i in range(len(self.sizes) + 1)]
        steps = [0] + list(range(1, local_levels)) + [local_levels + b for b in far_bits]
        self.biases = [float(step) for step in steps]
        self.mids = mids
        self.far_start = self.bounds[1 + mids]
        self.factor = math.log2(math.e) / math.sqrt(HEAD_DIM)

    def here(self, m):
        return pl.ds(pl.multiple_of(m * 2 * BLOCK, 2 * BLOCK), 2 * BLOCK)

    def seats(self, m):
        for i in range(self.mids):
            sibling = jnp.bitwise_xor(jnp.right_shift(m, i), 1)
            yield pl.ds(pl.multiple_of(sibling * BLOCK, BLOCK), BLOCK)

    def near(self, m, level_refs, cols):
        rows = [level_refs[0][self.here(m), cols]]
        rows += [ref[seat, cols] for ref, seat in zip(level_refs[1:], self.seats(m))]
        return rows

    def far(self, far_refs, cols):
        return [ref[:, cols] for ref in far_refs]

    def pieces(self, array, first=0, count=None):
        base = self.bounds[first]
        ends = self.bounds[first:] if count is None else self.bounds[first : first + count + 1]
        return [array[a - base : b - base] for a, b in zip(ends, ends[1:])]

    def top(self, pieces, first=0):
        tops = [
            jnp.max(piece, axis=0, keepdims=True) * self.factor + bias
            for piece, bias in zip(pieces, self.biases[first:])
        ]
        return functools.reduce(jnp.maximum, tops)

    def powers(self, pieces, top, first=0):
        return jnp.concatenate(
            [
                jnp.exp2(piece * self.factor + (bias - top))
                for piece, bias in zip(pieces, self.biases[first:])
            ],
            axis=0,
        )


def head_columns(h, inner):
    low = h * HEAD_DIM
    return slice(low, low + HEAD_DIM), slice(inner + low, inner + low + HEAD_DIM)


def near_body(local_levels, q_ref, *refs):
    level_refs = refs[:local_levels]
    power_ref, stat_ref = refs[local_levels:]
    tok_rows, inner = q_ref.shape
    heads = inner // HEAD_DIM
    keyset = KeySet([], [], local_levels)
    rows = keyset.far_start

    def step(m, carry):
        here = keyset.here(m)
        for h in range(heads):
            cols, _ = head_columns(h, inner)
            keys = jnp.concatenate(keyset.near(m, level_refs, cols), axis=0)
            pieces = keyset.pieces(dot(keys, q_ref[here, cols], NT))
            top = keyset.top(pieces)
            powers = keyset.powers(pieces, top)
            stat_ref[h : h + 1, here] = top
            stat_ref[heads + h : heads + h + 1, here] = jnp.sum(powers, axis=0, keepdims=True)
            power_ref[pl.ds(pl.multiple_of((m * heads + h) * rows, rows), rows), :] = powers
        return carry

    lax.fori_loop(0, tok_rows // (2 * BLOCK), step, 0)


def near_powers(query, levels, after):
    tok_rows, inner = query.shape
    heads = inner // HEAD_DIM
    pairs = tok_rows // (2 * BLOCK)
    rows = (len(levels) + 1) * BLOCK
    return run(
        functools.partial(near_body, len(levels)),
        [query, *levels],
        after,
        out_shape=[shape(pairs * heads * rows, 2 * BLOCK, F32), shape(2 * heads, tok_rows, F32)],
        compiler_params=params(6),
        cost_estimate=cost(2.3),
    )


def forward_body(local_levels, far_bits, *refs):
    fars = len(far_bits)
    q_ref, power_ref, near_ref = refs[:3]
    level_refs = refs[3 : 3 + local_levels]
    far_refs = refs[3 + local_levels : 3 + local_levels + fars]
    att_ref, att_t_ref, stat_ref = refs[3 + local_levels + fars :]
    tok_rows, inner = q_ref.shape
    heads = inner // HEAD_DIM
    keyset = KeySet([r.shape[0] for r in far_refs], far_bits, local_levels)
    rows = keyset.far_start

    def step(m, carry):
        here = keyset.here(m)
        for h in range(heads):
            cols, vcols = head_columns(h, inner)
            second = heads + h
            keys = jnp.concatenate(keyset.far(far_refs, cols), axis=0)
            values = keyset.near(m, level_refs, vcols) + keyset.far(far_refs, vcols)
            values = jnp.concatenate(values, axis=0)
            first = local_levels
            pieces = keyset.pieces(dot(keys, q_ref[here, cols], NT), first)
            near_top = near_ref[h : h + 1, here]
            top = jnp.maximum(near_top, keyset.top(pieces, first))
            shrink = jnp.exp2(near_top - top)
            powers = keyset.powers(pieces, top, first)
            total = near_ref[second : second + 1, here] * shrink
            total = total + jnp.sum(powers, axis=0, keepdims=True)
            inverse = 1.0 / total
            place = pl.ds(pl.multiple_of((m * heads + h) * rows, rows), rows)
            near_probs = (power_ref[place, :] * (shrink * inverse)).astype(BF16)
            far_probs = (powers * inverse).astype(BF16)
            probs_b = jnp.concatenate([near_probs, far_probs], axis=0)
            att_t = dot(values, probs_b, TN).astype(BF16)
            att_t_ref[cols, here] = att_t
            att_ref[here, cols] = att_t.T
            stat_ref[h : h + 1, here] = top
            stat_ref[second : second + 1, here] = inverse
        return carry

    lax.fori_loop(0, tok_rows // (2 * BLOCK), step, 0)


def forward(query, powers, near, levels, fars, far_bits, after):
    tok_rows, inner = query.shape
    heads = inner // HEAD_DIM
    set_rows = (len(levels) + 1) * BLOCK + sum(f.shape[0] for f in fars)
    return run(
        functools.partial(forward_body, len(levels), far_bits),
        [query, powers, near, *levels, *fars],
        after,
        out_shape=[
            shape(tok_rows, inner),
            shape(inner, tok_rows),
            shape(2 * heads, tok_rows, F32),
        ],
        compiler_params=params(6),
        cost_estimate=cost(4.0),
    )


def backward_body(local_levels, far_bits, pieces, *refs):
    mids = local_levels - 1
    fars = len(far_bits)
    q_ref, g_ref, att_t_ref, stat_ref, tok_ref = refs[:5]
    level_refs = refs[5 : 5 + local_levels]
    far_refs = refs[5 + local_levels : 5 + local_levels + fars]
    outs = refs[5 + local_levels + fars :]
    dq_ref, dkv_ref = outs[:2]
    term_refs = outs[2 : 2 + pieces]
    dfar_refs = outs[2 + pieces : 2 + pieces + fars]
    dmid_refs = outs[2 + pieces + fars : 2 + pieces + fars + mids]
    dq_t_ref, acc_ref = outs[-2:]
    tok_rows, inner = q_ref.shape
    heads = inner // HEAD_DIM
    score_scale = 1.0 / math.sqrt(HEAD_DIM)
    keyset = KeySet([r.shape[0] for r in far_refs], far_bits, local_levels)

    for ref in (*dmid_refs, acc_ref):
        ref[...] = jnp.zeros_like(ref)

    def step(m, carry):
        here = keyset.here(m)
        for h in range(heads):
            cols, vcols = head_columns(h, inner)
            keys, values = (
                jnp.concatenate(keyset.near(m, level_refs, c) + keyset.far(far_refs, c), axis=0)
                for c in (cols, vcols)
            )
            q = q_ref[here, cols]
            g = g_ref[here, cols]
            top = stat_ref[h : h + 1, here]
            inverse = stat_ref[heads + h : heads + h + 1, here]
            probs = keyset.powers(keyset.pieces(dot(keys, q, NT)), top) * inverse
            att_t = att_t_ref[cols, here].astype(F32)
            delta = jnp.sum(g.T.astype(F32) * att_t, axis=0, keepdims=True)
            grads = (probs * (dot(values, g, NT) - delta) * score_scale).astype(BF16)
            dq_t = dot(keys, grads, TN).astype(BF16)
            dq_t_ref[cols, here] = dq_t
            dq_ref[here, cols] = dq_t.T
            for part, place in ((dot(grads, q), cols), (dot(probs.astype(BF16), g), vcols)):
                own, *sides = keyset.pieces(part)
                dkv_ref[here, place] = own
                for ref, seat, side in zip(dmid_refs, keyset.seats(m), sides):
                    ref[seat, place] += side
                acc_ref[:, place] += part[keyset.far_start :]
        return carry

    lax.fori_loop(0, tok_rows // (2 * BLOCK), step, 0)
    width = term_refs[-1].shape[0]
    low = 0
    for ref in dfar_refs:
        ref[...] = acc_ref[low : low + ref.shape[0]].astype(BF16)
        low += ref.shape[0]
    for i, ref in enumerate(term_refs):
        part = dot(dq_t_ref[...], tok_ref[:, i * width : (i + 1) * width])
        ref[...] = part.astype(BF16).T
    fan = spread_matrix(2 * BLOCK, 1, 0, BLOCK, 0.5)
    targets = (dkv_ref, *dmid_refs)
    for i in reversed(range(mids)):
        for t in range(dmid_refs[i].shape[0] // BLOCK):
            part = dmid_refs[i][t * BLOCK : (t + 1) * BLOCK, :]
            high = part.astype(BF16)
            low = (part - high.astype(F32)).astype(BF16)
            rows = slice(2 * t * BLOCK, 2 * (t + 1) * BLOCK)
            targets[i][rows, :] += dot(fan, high) + dot(fan, low)


def backward(query, grad, attended_t, stats, tokens, levels, fars, far_bits, pieces, after):
    tok_rows, inner = query.shape
    far_rows = sum(f.shape[0] for f in fars)
    set_rows = (len(levels) + 1) * BLOCK + far_rows
    return run(
        functools.partial(backward_body, len(levels), far_bits, pieces),
        [query, grad, attended_t, stats, tokens, *levels, *fars],
        after,
        out_shape=[shape(tok_rows, inner), shape(tok_rows, 2 * inner, F32)]
        + [shape(tokens.shape[1] // pieces, inner)] * pieces
        + [shape(*f.shape) for f in fars],
        scratch_shapes=[pltpu.VMEM(level.shape, F32) for level in levels[1:]]
        + [pltpu.VMEM((inner, tok_rows), BF16), pltpu.VMEM((far_rows, 2 * inner), F32)],
        compiler_params=params(10),
        cost_estimate=cost(8.0),
    )


def term_body(which, low, left_ref, right_ref, out_ref):
    width, inner = out_ref.shape
    left = left_ref[which * inner : (which + 1) * inner, :]
    out_ref[...] = dot(left, right_ref[:, low : low + width]).astype(BF16).T


def weight_terms(left_t, right, inner, which, part, parts, after):
    tok_rows = left_t.shape[1]
    width = right.shape[1] // parts
    return run(
        functools.partial(term_body, which, part * width),
        [left_t, right],
        after,
        out_shape=shape(width, inner),
        compiler_params=params(3),
        cost_estimate=cost(0.2),
    )


def close_body(local_levels, far_bits, dkv_ref, *refs):
    backs = [ref[...] for ref in refs[: len(far_bits)]]
    dk_ref, dv_ref, dkv_t_ref = refs[len(far_bits) :]
    inner = dk_ref.shape[1]
    tile = 2 * BLOCK
    for t in range(dkv_ref.shape[0] // tile):
        here = slice(t * tile, (t + 1) * tile)
        total = dkv_ref[here, :]
        for back, bit in zip(backs, far_bits):
            weight = 0.5 ** (local_levels + bit)
            fan = spread_matrix(tile, local_levels + bit, t * tile, back.shape[0], weight)
            total = total + dot(fan, back)
        final = total.astype(BF16)
        dk_ref[here, :] = final[:, :inner]
        dv_ref[here, :] = final[:, inner:]
        dkv_t_ref[:, here] = final.T


def close_keys(dkv, backs, far_bits, local_levels, after):
    tok_rows, double = dkv.shape
    inner = double // 2
    return run(
        functools.partial(close_body, local_levels, far_bits),
        [dkv, *backs],
        after,
        out_shape=[shape(tok_rows, inner), shape(tok_rows, inner), shape(double, tok_rows)],
        compiler_params=params(5),
        cost_estimate=cost(0.2),
    )


def split_body(count, parts, rank_ref, *refs):
    lefts, weights = refs[:count], refs[count : 2 * count]
    outs = refs[2 * count :]
    width = weights[0].shape[0] // parts
    for r in range(parts):
        owner = jnp.bitwise_xor(rank_ref[0], r)
        rows = pl.ds(pl.multiple_of(owner * width, width), width)
        total = None
        for left, weight in zip(lefts, weights):
            product = dot(left[...], weight[rows, :], NT)
            total = product if total is None else total + product
        place = r // 2 * width
        outs[r % 2][:, place : place + width] = total.astype(BF16)


def project_split(rank, lefts, weights, axis, after):
    count = len(lefts)
    parts = lax.axis_size(axis)
    tok_rows, inner = lefts[0].shape
    width = weights[0].shape[0]
    return run(
        functools.partial(split_body, count, parts),
        [rank, *lefts, *weights],
        after,
        in_specs=[pl.BlockSpec(memory_space=pltpu.SMEM)]
        + [pl.BlockSpec(memory_space=pltpu.VMEM)] * (2 * count),
        out_shape=[shape(tok_rows, width // 2)] * 2,
        compiler_params=params(5),
        cost_estimate=cost(1.0),
    )


def exchange(block, axis, distance):
    count = lax.axis_size(axis)
    return lax.ppermute(block, axis, [(i, i ^ distance) for i in range(count)])


def add(left, right):
    return (left.astype(F32) + right.astype(F32)).astype(BF16)


def term_half_body(chunk_ref, into_ref, out_ref):
    rows = slice(0, out_ref.shape[0])
    out_ref[...] = (chunk_ref[rows, :].astype(F32) + into_ref[rows, :].astype(F32)).astype(BF16)


def half_sum(chunk, into, rows, weight, after):
    return run(
        term_half_body,
        [chunk, into],
        after,
        out_shape=shape(rows, chunk.shape[1]),
        compiler_params=params(3),
        cost_estimate=cost(weight),
    )


def scatter_body(pieces, keep_ref, into_ref, even_ref, odd_ref):
    width = keep_ref.shape[1] // pieces
    for i in range(pieces):
        here = slice(i * width, (i + 1) * width)
        place = slice(i // 2 * width, (i // 2 + 1) * width)
        total = keep_ref[:, here].astype(F32) + into_ref[:, here].astype(F32)
        (even_ref, odd_ref)[i % 2][:, place] = total.astype(BF16)


def last_body(left_ref, right_ref, token_ref, out_ref):
    token_ref[...] = jnp.zeros_like(token_ref)
    out_ref[...] = (left_ref[...].astype(F32) + right_ref[...].astype(F32)).astype(BF16)


def last_sum(left, right, after):
    return run(
        last_body,
        [left, right],
        after,
        out_shape=[shape(8, 128, F32), shape(*left.shape)],
        compiler_params=params(3),
        cost_estimate=cost(0.9),
    )


def scatter_step(keep, into, pieces, after):
    rows, width = keep.shape
    return run(
        functools.partial(scatter_body, pieces),
        [keep, into],
        after,
        out_shape=[shape(rows, width // 2)] * 2,
        compiler_params=params(4),
        cost_estimate=cost(0.2),
    )


def turn_body(end_ref, half_ref, across_ref, chunk_ref, total_ref, send_ref):
    total = (half_ref[...].astype(F32) + across_ref[...].astype(F32)).astype(BF16)
    total_ref[...] = total

    @pl.when(end_ref[0] == 1)
    def _():
        send_ref[...] = chunk_ref[...]

    @pl.when(end_ref[0] == 0)
    def _():
        send_ref[...] = total


def turn(end, half, across, chunk, weight, after):
    return run(
        turn_body,
        [end, half, across, chunk],
        after,
        in_specs=[pl.BlockSpec(memory_space=pltpu.SMEM)]
        + [pl.BlockSpec(memory_space=pltpu.VMEM)] * 3,
        out_shape=[shape(*half.shape)] * 2,
        compiler_params=params(2),
        cost_estimate=cost(weight),
    )


def output_body(count, end_ref, *refs):
    totals, ends, (token_ref, out_ref) = refs[:count], refs[count : 2 * count], refs[2 * count :]
    token_ref[...] = jnp.zeros_like(token_ref)
    rows = totals[0].shape[0]

    for flag, sources in ((0, totals), (1, ends)):

        @pl.when(end_ref[0] == flag)
        def _():
            for i, ref in enumerate(sources):
                out_ref[i * rows : (i + 1) * rows, :] = ref[...]


def output(end, totals, ends, after):
    count = len(totals)
    rows, width = totals[0].shape
    return run(
        functools.partial(output_body, count),
        [end, *totals, *ends],
        after,
        in_specs=[pl.BlockSpec(memory_space=pltpu.SMEM)]
        + [pl.BlockSpec(memory_space=pltpu.VMEM)] * (2 * count),
        out_shape=[shape(8, 128, F32), shape(count * rows, width)],
        compiler_params=params(4),
        cost_estimate=cost(0.9),
    )


def relay_body(source_ref, target_ref):
    target_ref[...] = source_ref[...]


def relay(block, after):
    return run(
        relay_body,
        [block],
        after,
        out_shape=shape(*block.shape),
        compiler_params=params(3),
        cost_estimate=cost(0.2),
    )


class Line:
    lag = 3
    half_weights = (3.0, 3.0, 3.0, 3.0, 3.0, 3.0, 3.0, 0.5)
    turn_weights = (4.0, 4.0, 3.0, 3.0, 4.0, 2.0, 0.5, 0.5)

    def __init__(self, axis, other, end, step):
        self.axis, self.axes, self.step = axis, (axis, other), step
        self.count = lax.axis_size(axis)
        self.end = end
        width = lax.axis_size(other)
        self.across = []
        for place in range(self.count):
            for seat in range(width):
                target = (place, seat ^ 1 if width > 1 else seat)
                if place & 3 in (1, 2):
                    target = (place ^ 3, seat)
                self.across.append((place * width + seat, target[0] * width + target[1]))
        self.chunks, self.into, self.halves, self.crossed, self.totals = [], [], [], [], []

    def enter(self, chunk):
        self.chunks.append(chunk)
        self.into.append(exchange(chunk, self.axis, 1))

    def meet(self, rows):
        k = len(self.halves)
        weight = self.half_weights[k]
        half = self.step(half_sum, self.chunks[k], self.into[k], rows, weight)
        self.halves.append(half)
        self.crossed.append(lax.ppermute(half, self.axes, self.across))

    def turn(self, chunk):
        old = len(self.totals)
        half, crossed = self.halves[old], self.crossed[old]
        weight = self.turn_weights[old]
        total, send = self.step(turn, self.end, half, crossed, chunk, weight)
        self.totals.append(total)
        self.chunks.append(chunk)
        self.into.append(exchange(send, self.axis, 1))

    def leave(self):
        old = len(self.totals)
        half = self.halves[old]
        weight = self.turn_weights[old]
        total = self.step(half_sum, half, self.crossed[old], half.shape[0], weight)
        self.totals.append(total)
        self.into.append(exchange(total, self.axis, 1))

    def output(self, first, count):
        ends = self.into[first + self.lag : first + self.lag + count]
        _, result = self.step(output, self.end, self.totals[first : first + count], ends)
        distance = 4
        while distance < self.count:
            result = add(result, exchange(result, self.axis, distance))
            distance *= 2
        return result


class Scatter:
    def __init__(self, parts, axis, step):
        self.axis, self.step = axis, step
        self.pieces = lax.axis_size(axis) // 2
        self.keep, send = parts
        self.distance = 1
        self.into = exchange(send, axis, 1)

    def advance(self):
        while self.pieces > 1:
            self.keep, send = self.step(scatter_step, self.keep, self.into, self.pieces)
            self.distance *= 2
            self.pieces //= 2
            self.into = exchange(send, self.axis, self.distance)

    def result(self):
        return self.step(last_sum, self.keep, self.into)[1]


def per_device(tokens, w_query, w_key, w_value, w_out, cotangent):
    tok_rows = tokens.shape[0]
    inner = w_query.shape[1]
    local_levels = (tok_rows // BLOCK).bit_length() - 1
    count = lax.axis_size("seq")
    far_levels = count.bit_length() - 1
    far_bits = [d.bit_length() - 1 for d in range(1, count)]

    last = []

    def step(kernel, *operands):
        made = kernel(*operands, list(last))
        last[:] = made[:1] if isinstance(made, (list, tuple)) else [made]
        return made

    place = jnp.bitwise_and(lax.axis_index("seq"), 3)
    end = jnp.reshape((place == 0) | (place == 3), (1,)).astype(jnp.int32)
    rank = jnp.reshape(lax.axis_index("head"), (1,)).astype(jnp.int32)
    parts = key_value(tokens, w_key, w_value, local_levels, far_levels, [end, rank])
    levels, tops = parts[:local_levels], parts[local_levels:]
    fars = [exchange(tops[bit], "seq", d) for d, bit in enumerate(far_bits, 1)]
    query = step(project, tokens, w_query)
    powers, near = step(near_powers, query, levels)
    grad = step(project, cotangent, w_out)
    attended, attended_t, stats = step(forward, query, powers, near, levels, fars, far_bits)

    line = Line("seq", "head", end, step)
    pieces = 2
    rows = tokens.shape[1] // pieces
    line.enter(step(weight_terms, attended_t, cotangent, inner, 0, 0, pieces))
    line.enter(step(weight_terms, attended_t, cotangent, inner, 0, 1, pieces))
    parts = step(project_split, rank, [attended], [w_out], "head")
    mixed = Scatter(parts, "head", step)
    dquery, dkv, query_first, query_second, *away = step(
        backward, query, grad, attended_t, stats, tokens, levels, fars, far_bits, pieces
    )
    backs = [exchange(piece, "seq", d) for d, piece in enumerate(away, 1)]
    line.meet(rows)
    mixed.advance()
    line.enter(step(relay, query_first))
    dkey, dvalue, dkv_t = step(close_keys, dkv, backs, far_bits, local_levels)
    line.meet(rows)
    key_first = step(weight_terms, dkv_t, tokens, inner, 0, 0, pieces)
    line.turn(query_second)
    key_second = step(weight_terms, dkv_t, tokens, inner, 0, 1, pieces)
    line.turn(key_first)
    line.meet(rows)
    keep, send = step(project_split, rank, [dquery, dkey, dvalue], [w_query, w_key, w_value], "head")
    line.meet(rows)
    value_first = step(weight_terms, dkv_t, tokens, inner, 1, 0, pieces)
    line.turn(key_second)
    line.meet(rows)
    tokens_grad = Scatter([keep, step(relay, send)], "head", step)
    line.turn(value_first)
    mixed = mixed.result()
    value_second = step(weight_terms, dkv_t, tokens, inner, 1, 1, pieces)
    line.meet(rows)
    line.turn(value_second)
    out_grad = line.output(0, pieces)
    line.meet(rows)
    tokens_grad.advance()
    line.leave()
    line.meet(rows)
    query_grad = line.output(2, pieces)
    line.leave()
    key_grad = line.output(4, pieces)
    line.leave()
    tokens_grad = tokens_grad.result()
    value_grad = line.output(6, pieces)
    return mixed, tokens_grad, query_grad, key_grad, value_grad, out_grad


def solution(mesh):
    return jax.shard_map(
        per_device,
        mesh=mesh,
        in_specs=(
            P(("groups", "seq"), None),
            P(None, "head"),
            P(None, "head"),
            P(None, "head"),
            P(None, "head"),
            P(("groups", "seq"), None),
        ),
        out_specs=(
            P(("groups", "seq"), "head"),
            P(("groups", "seq"), "head"),
            P("groups", "head"),
            P("groups", "head"),
            P("groups", "head"),
            P("groups", "head"),
        ),
        check_vma=False,
    )
```

```python
import functools
import math

import jax
import jax.numpy as jnp
from jax import lax
from jax.experimental import pallas as pl
from jax.experimental.pallas import tpu as pltpu
from jax.sharding import PartitionSpec as P

HEAD_DIM = 128
BLOCK = 128
BF16 = jnp.bfloat16
F32 = jnp.float32
MIB = 1024 * 1024

NN = (((1,), (0,)), ((), ()))
NT = (((1,), (1,)), ((), ()))
TN = (((0,), (0,)), ((), ()))


def dot(left, right, dims=NN):
    return lax.dot_general(left, right, dims, preferred_element_type=F32)


def params(mib):
    return pltpu.CompilerParams(vmem_limit_bytes=mib * MIB)


def cost(microseconds):
    return pl.CostEstimate(flops=int(microseconds * 1150e6) + 1, bytes_accessed=1, transcendentals=0)


def run(body, ready, after=(), in_specs=None, **options):
    count, extra = len(ready), len(after)

    def kernel(*refs):
        body(*refs[:count], *refs[count + extra :])

    in_specs = in_specs or [pl.BlockSpec(memory_space=pltpu.VMEM)] * count
    in_specs = in_specs + [pl.BlockSpec(memory_space=pl.ANY)] * extra
    return pl.pallas_call(kernel, in_specs=in_specs, **options)(*ready, *after)


def shape(rows, cols, dtype=BF16):
    return jax.ShapeDtypeStruct((rows, cols), dtype)


def whole(rows, cols):
    return pl.BlockSpec((rows, cols), lambda *_: (0, 0))


def pool_matrix(rows):
    row = lax.broadcasted_iota(jnp.int32, (rows // 2, rows), 0)
    col = lax.broadcasted_iota(jnp.int32, (rows // 2, rows), 1)
    return jnp.where(jnp.right_shift(col, 1) == row, 0.5, 0.0).astype(BF16)


def spread_matrix(rows, step_bits, offset, cols, weight):
    row = lax.broadcasted_iota(jnp.int32, (rows, cols), 0) + offset
    col = lax.broadcasted_iota(jnp.int32, (rows, cols), 1)
    return jnp.where(jnp.right_shift(row, step_bits) == col, weight, 0.0).astype(BF16)


def key_value_body(local_levels, far_levels, parts, tok_hbm, wk_hbm, wv_hbm, *refs):
    out_hbm = refs[:local_levels]
    far = refs[local_levels : local_levels + far_levels]
    refs = refs[local_levels + far_levels :]
    tok_ref, wk_ref, wv_ref = refs[:3]
    levels = refs[3 : 3 + local_levels]
    in_sems, out_sems = refs[3 + local_levels :]
    part = tok_ref.shape[0] // parts

    def fetch(source, target, i):
        copy = pltpu.make_async_copy(source, target, in_sems.at[i])
        copy.start()
        return copy

    def flush(i):
        copy = pltpu.make_async_copy(levels[i], out_hbm[i], out_sems.at[i])
        copy.start()
        return copy

    weights = [fetch(wk_hbm, wk_ref, 0), fetch(wv_hbm, wv_ref, 1)]
    tiles = []
    for p in range(parts):
        rows = pl.ds(p * part, part)
        tiles.append(fetch(tok_hbm.at[rows], tok_ref.at[rows], 2 + p))
    for copy in weights:
        copy.wait()
    for p in range(parts):
        tiles[p].wait()
        here = slice(p * part, (p + 1) * part)
        x = tok_ref[here, :]
        both = jnp.concatenate([dot(x, wk_ref[...]), dot(x, wv_ref[...])], axis=1)
        levels[0][here, :] = both.astype(BF16)
    flushes = [flush(0)]
    pool = pool_matrix(part)
    for i in range(1, local_levels):
        source = levels[i - 1]
        for low in range(0, source.shape[0], part):
            mean = dot(pool, source[low : low + part, :])
            levels[i][low // 2 : (low + part) // 2, :] = mean.astype(BF16)
        flushes.append(flush(i))
    rows = dot(pool, levels[-1][...]).astype(BF16)
    for i in range(far_levels):
        if i:
            rows = dot(pool_matrix(rows.shape[0]), rows).astype(BF16)
        far[i][...] = rows
    for copy in flushes:
        copy.wait()


def key_value(tokens, w_key, w_value, local_levels, far_levels, after):
    tok_rows, width = tokens.shape
    inner = w_key.shape[1]
    parts = tok_rows // (2 * BLOCK)
    held = [(tok_rows >> i, 2 * inner) for i in range(local_levels)]
    tops = [(BLOCK >> i, 2 * inner) for i in range(far_levels)]
    return run(
        functools.partial(key_value_body, local_levels, far_levels, parts),
        [tokens, w_key, w_value],
        after,
        in_specs=[pl.BlockSpec(memory_space=pl.ANY)] * 3,
        out_specs=[pl.BlockSpec(memory_space=pl.ANY)] * len(held)
        + [pl.BlockSpec(memory_space=pltpu.VMEM)] * len(tops),
        out_shape=[shape(*dims) for dims in held + tops],
        scratch_shapes=[pltpu.VMEM((tok_rows, width), BF16)]
        + [pltpu.VMEM((width, inner), BF16)] * 2
        + [pltpu.VMEM(dims, BF16) for dims in held]
        + [pltpu.SemaphoreType.DMA((parts + 2,)), pltpu.SemaphoreType.DMA((len(held),))],
        compiler_params=params(56),
        cost_estimate=cost(5.0),
    )


def project_body(left_ref, weight_ref, out_ref):
    out_ref[...] = dot(left_ref[...], weight_ref[...]).astype(BF16)


def project(left, weight, after):
    tok_rows, width = left.shape
    inner = weight.shape[1]
    return run(
        project_body,
        [left, weight],
        after,
        out_shape=shape(tok_rows, inner),
        compiler_params=params(4),
        cost_estimate=cost(0.7),
    )


class KeySet:
    def __init__(self, far_rows, far_bits, local_levels):
        mids = local_levels - 1
        self.sizes = [2 * BLOCK] + [BLOCK] * mids + list(far_rows)
        self.bounds = [sum(self.sizes[:i]) for i in range(len(self.sizes) + 1)]
        steps = [0] + list(range(1, local_levels)) + [local_levels + b for b in far_bits]
        self.biases = [float(step) for step in steps]
        self.mids = mids
        self.far_start = self.bounds[1 + mids]
        self.factor = math.log2(math.e) / math.sqrt(HEAD_DIM)

    def here(self, m):
        return pl.ds(pl.multiple_of(m * 2 * BLOCK, 2 * BLOCK), 2 * BLOCK)

    def seats(self, m):
        for i in range(self.mids):
            sibling = jnp.bitwise_xor(jnp.right_shift(m, i), 1)
            yield pl.ds(pl.multiple_of(sibling * BLOCK, BLOCK), BLOCK)

    def near(self, m, level_refs, cols):
        rows = [level_refs[0][self.here(m), cols]]
        rows += [ref[seat, cols] for ref, seat in zip(level_refs[1:], self.seats(m))]
        return rows

    def far(self, far_refs, cols):
        return [ref[:, cols] for ref in far_refs]

    def pieces(self, array, first=0, count=None):
        base = self.bounds[first]
        ends = self.bounds[first:] if count is None else self.bounds[first : first + count + 1]
        return [array[a - base : b - base] for a, b in zip(ends, ends[1:])]

    def top(self, pieces, first=0):
        tops = [
            jnp.max(piece, axis=0, keepdims=True) * self.factor + bias
            for piece, bias in zip(pieces, self.biases[first:])
        ]
        return functools.reduce(jnp.maximum, tops)

    def powers(self, pieces, top, first=0):
        return jnp.concatenate(
            [
                jnp.exp2(piece * self.factor + (bias - top))
                for piece, bias in zip(pieces, self.biases[first:])
            ],
            axis=0,
        )


def head_columns(h, inner):
    low = h * HEAD_DIM
    return slice(low, low + HEAD_DIM), slice(inner + low, inner + low + HEAD_DIM)


def near_body(local_levels, q_ref, *refs):
    level_refs = refs[:local_levels]
    power_ref, stat_ref = refs[local_levels:]
    tok_rows, inner = q_ref.shape
    heads = inner // HEAD_DIM
    keyset = KeySet([], [], local_levels)
    rows = keyset.far_start

    def step(m, carry):
        here = keyset.here(m)
        for h in range(heads):
            cols, _ = head_columns(h, inner)
            keys = jnp.concatenate(keyset.near(m, level_refs, cols), axis=0)
            pieces = keyset.pieces(dot(keys, q_ref[here, cols], NT))
            top = keyset.top(pieces)
            powers = keyset.powers(pieces, top)
            stat_ref[h : h + 1, here] = top
            stat_ref[heads + h : heads + h + 1, here] = jnp.sum(powers, axis=0, keepdims=True)
            power_ref[pl.ds(pl.multiple_of((m * heads + h) * rows, rows), rows), :] = powers
        return carry

    lax.fori_loop(0, tok_rows // (2 * BLOCK), step, 0)


def near_powers(query, levels, after):
    tok_rows, inner = query.shape
    heads = inner // HEAD_DIM
    pairs = tok_rows // (2 * BLOCK)
    rows = (len(levels) + 1) * BLOCK
    return run(
        functools.partial(near_body, len(levels)),
        [query, *levels],
        after,
        out_shape=[shape(pairs * heads * rows, 2 * BLOCK, F32), shape(2 * heads, tok_rows, F32)],
        compiler_params=params(6),
        cost_estimate=cost(2.3),
    )


def forward_body(local_levels, far_bits, *refs):
    fars = len(far_bits)
    q_ref, power_ref, near_ref = refs[:3]
    level_refs = refs[3 : 3 + local_levels]
    far_refs = refs[3 + local_levels : 3 + local_levels + fars]
    att_ref, att_t_ref, stat_ref = refs[3 + local_levels + fars :]
    tok_rows, inner = q_ref.shape
    heads = inner // HEAD_DIM
    keyset = KeySet([r.shape[0] for r in far_refs], far_bits, local_levels)
    rows = keyset.far_start

    def step(m, carry):
        here = keyset.here(m)
        for h in range(heads):
            cols, vcols = head_columns(h, inner)
            second = heads + h
            keys = jnp.concatenate(keyset.far(far_refs, cols), axis=0)
            values = keyset.near(m, level_refs, vcols) + keyset.far(far_refs, vcols)
            values = jnp.concatenate(values, axis=0)
            first = local_levels
            pieces = keyset.pieces(dot(keys, q_ref[here, cols], NT), first)
            near_top = near_ref[h : h + 1, here]
            top = jnp.maximum(near_top, keyset.top(pieces, first))
            shrink = jnp.exp2(near_top - top)
            powers = keyset.powers(pieces, top, first)
            total = near_ref[second : second + 1, here] * shrink
            total = total + jnp.sum(powers, axis=0, keepdims=True)
            inverse = 1.0 / total
            place = pl.ds(pl.multiple_of((m * heads + h) * rows, rows), rows)
            near_probs = (power_ref[place, :] * (shrink * inverse)).astype(BF16)
            far_probs = (powers * inverse).astype(BF16)
            probs_b = jnp.concatenate([near_probs, far_probs], axis=0)
            att_t = dot(values, probs_b, TN).astype(BF16)
            att_t_ref[cols, here] = att_t
            att_ref[here, cols] = att_t.T
            stat_ref[h : h + 1, here] = top
            stat_ref[second : second + 1, here] = inverse
        return carry

    lax.fori_loop(0, tok_rows // (2 * BLOCK), step, 0)


def forward(query, powers, near, levels, fars, far_bits, after):
    tok_rows, inner = query.shape
    heads = inner // HEAD_DIM
    set_rows = (len(levels) + 1) * BLOCK + sum(f.shape[0] for f in fars)
    return run(
        functools.partial(forward_body, len(levels), far_bits),
        [query, powers, near, *levels, *fars],
        after,
        out_shape=[
            shape(tok_rows, inner),
            shape(inner, tok_rows),
            shape(2 * heads, tok_rows, F32),
        ],
        compiler_params=params(6),
        cost_estimate=cost(4.0),
    )


def backward_body(local_levels, far_bits, pieces, *refs):
    mids = local_levels - 1
    fars = len(far_bits)
    q_ref, g_ref, att_t_ref, stat_ref, tok_ref = refs[:5]
    level_refs = refs[5 : 5 + local_levels]
    far_refs = refs[5 + local_levels : 5 + local_levels + fars]
    outs = refs[5 + local_levels + fars :]
    dq_ref, dkv_ref = outs[:2]
    term_refs = outs[2 : 2 + pieces]
    dfar_refs = outs[2 + pieces : 2 + pieces + fars]
    dmid_refs = outs[2 + pieces + fars : 2 + pieces + fars + mids]
    dq_t_ref, acc_ref = outs[-2:]
    tok_rows, inner = q_ref.shape
    heads = inner // HEAD_DIM
    score_scale = 1.0 / math.sqrt(HEAD_DIM)
    keyset = KeySet([r.shape[0] for r in far_refs], far_bits, local_levels)

    for ref in (*dmid_refs, acc_ref):
        ref[...] = jnp.zeros_like(ref)

    def step(m, carry):
        here = keyset.here(m)
        for h in range(heads):
            cols, vcols = head_columns(h, inner)
            keys, values = (
                jnp.concatenate(keyset.near(m, level_refs, c) + keyset.far(far_refs, c), axis=0)
                for c in (cols, vcols)
            )
            q = q_ref[here, cols]
            g = g_ref[here, cols]
            top = stat_ref[h : h + 1, here]
            inverse = stat_ref[heads + h : heads + h + 1, here]
            probs = keyset.powers(keyset.pieces(dot(keys, q, NT)), top) * inverse
            att_t = att_t_ref[cols, here].astype(F32)
            delta = jnp.sum(g.T.astype(F32) * att_t, axis=0, keepdims=True)
            grads = (probs * (dot(values, g, NT) - delta) * score_scale).astype(BF16)
            dq_t = dot(keys, grads, TN).astype(BF16)
            dq_t_ref[cols, here] = dq_t
            dq_ref[here, cols] = dq_t.T
            for part, place in ((dot(grads, q), cols), (dot(probs.astype(BF16), g), vcols)):
                own, *sides = keyset.pieces(part)
                dkv_ref[here, place] = own
                for ref, seat, side in zip(dmid_refs, keyset.seats(m), sides):
                    ref[seat, place] += side
                acc_ref[:, place] += part[keyset.far_start :]
        return carry

    lax.fori_loop(0, tok_rows // (2 * BLOCK), step, 0)
    width = term_refs[-1].shape[0]
    low = 0
    for ref in dfar_refs:
        ref[...] = acc_ref[low : low + ref.shape[0]].astype(BF16)
        low += ref.shape[0]
    for i, ref in enumerate(term_refs):
        part = dot(dq_t_ref[...], tok_ref[:, i * width : (i + 1) * width])
        ref[...] = part.astype(BF16).T
    fan = spread_matrix(2 * BLOCK, 1, 0, BLOCK, 0.5)
    targets = (dkv_ref, *dmid_refs)
    for i in reversed(range(mids)):
        for t in range(dmid_refs[i].shape[0] // BLOCK):
            part = dmid_refs[i][t * BLOCK : (t + 1) * BLOCK, :]
            high = part.astype(BF16)
            low = (part - high.astype(F32)).astype(BF16)
            rows = slice(2 * t * BLOCK, 2 * (t + 1) * BLOCK)
            targets[i][rows, :] += dot(fan, high) + dot(fan, low)


def backward(query, grad, attended_t, stats, tokens, levels, fars, far_bits, pieces, after):
    tok_rows, inner = query.shape
    far_rows = sum(f.shape[0] for f in fars)
    set_rows = (len(levels) + 1) * BLOCK + far_rows
    return run(
        functools.partial(backward_body, len(levels), far_bits, pieces),
        [query, grad, attended_t, stats, tokens, *levels, *fars],
        after,
        out_shape=[shape(tok_rows, inner), shape(tok_rows, 2 * inner, F32)]
        + [shape(tokens.shape[1] // pieces, inner)] * pieces
        + [shape(*f.shape) for f in fars],
        scratch_shapes=[pltpu.VMEM(level.shape, F32) for level in levels[1:]]
        + [pltpu.VMEM((inner, tok_rows), BF16), pltpu.VMEM((far_rows, 2 * inner), F32)],
        compiler_params=params(10),
        cost_estimate=cost(8.0),
    )


def term_body(which, low, left_ref, right_ref, out_ref):
    width, inner = out_ref.shape
    left = left_ref[which * inner : (which + 1) * inner, :]
    out_ref[...] = dot(left, right_ref[:, low : low + width]).astype(BF16).T


def weight_terms(left_t, right, inner, which, part, parts, after):
    tok_rows = left_t.shape[1]
    width = right.shape[1] // parts
    return run(
        functools.partial(term_body, which, part * width),
        [left_t, right],
        after,
        out_shape=shape(width, inner),
        compiler_params=params(3),
        cost_estimate=cost(0.2),
    )


def close_body(local_levels, far_bits, dkv_ref, *refs):
    backs = [ref[...] for ref in refs[: len(far_bits)]]
    dk_ref, dv_ref, dkv_t_ref = refs[len(far_bits) :]
    inner = dk_ref.shape[1]
    tile = 2 * BLOCK
    for t in range(dkv_ref.shape[0] // tile):
        here = slice(t * tile, (t + 1) * tile)
        total = dkv_ref[here, :]
        for back, bit in zip(backs, far_bits):
            weight = 0.5 ** (local_levels + bit)
            fan = spread_matrix(tile, local_levels + bit, t * tile, back.shape[0], weight)
            total = total + dot(fan, back)
        final = total.astype(BF16)
        dk_ref[here, :] = final[:, :inner]
        dv_ref[here, :] = final[:, inner:]
        dkv_t_ref[:, here] = final.T


def close_keys(dkv, backs, far_bits, local_levels, after):
    tok_rows, double = dkv.shape
    inner = double // 2
    return run(
        functools.partial(close_body, local_levels, far_bits),
        [dkv, *backs],
        after,
        out_shape=[shape(tok_rows, inner), shape(tok_rows, inner), shape(double, tok_rows)],
        compiler_params=params(5),
        cost_estimate=cost(0.2),
    )


def split_body(count, parts, rank_ref, *refs):
    lefts, weights = refs[:count], refs[count : 2 * count]
    outs = refs[2 * count :]
    width = weights[0].shape[0] // parts
    for r in range(parts):
        owner = jnp.bitwise_xor(rank_ref[0], r)
        rows = pl.ds(pl.multiple_of(owner * width, width), width)
        total = None
        for left, weight in zip(lefts, weights):
            product = dot(left[...], weight[rows, :], NT)
            total = product if total is None else total + product
        place = r // 2 * width
        outs[r % 2][:, place : place + width] = total.astype(BF16)


def project_split(rank, lefts, weights, axis, after):
    count = len(lefts)
    parts = lax.axis_size(axis)
    tok_rows, inner = lefts[0].shape
    width = weights[0].shape[0]
    return run(
        functools.partial(split_body, count, parts),
        [rank, *lefts, *weights],
        after,
        in_specs=[pl.BlockSpec(memory_space=pltpu.SMEM)]
        + [pl.BlockSpec(memory_space=pltpu.VMEM)] * (2 * count),
        out_shape=[shape(tok_rows, width // 2)] * 2,
        compiler_params=params(5),
        cost_estimate=cost(1.0),
    )


def exchange(block, axis, distance):
    count = lax.axis_size(axis)
    return lax.ppermute(block, axis, [(i, i ^ distance) for i in range(count)])


def add(left, right):
    return (left.astype(F32) + right.astype(F32)).astype(BF16)


def term_half_body(chunk_ref, into_ref, out_ref):
    rows = slice(0, out_ref.shape[0])
    out_ref[...] = (chunk_ref[rows, :].astype(F32) + into_ref[rows, :].astype(F32)).astype(BF16)


def half_sum(chunk, into, rows, weight, after):
    return run(
        term_half_body,
        [chunk, into],
        after,
        out_shape=shape(rows, chunk.shape[1]),
        compiler_params=params(3),
        cost_estimate=cost(weight),
    )


def scatter_body(pieces, keep_ref, into_ref, even_ref, odd_ref):
    width = keep_ref.shape[1] // pieces
    for i in range(pieces):
        here = slice(i * width, (i + 1) * width)
        place = slice(i // 2 * width, (i // 2 + 1) * width)
        total = keep_ref[:, here].astype(F32) + into_ref[:, here].astype(F32)
        (even_ref, odd_ref)[i % 2][:, place] = total.astype(BF16)


def last_body(left_ref, right_ref, token_ref, out_ref):
    token_ref[...] = jnp.zeros_like(token_ref)
    out_ref[...] = (left_ref[...].astype(F32) + right_ref[...].astype(F32)).astype(BF16)


def last_sum(left, right, after):
    return run(
        last_body,
        [left, right],
        after,
        out_shape=[shape(8, 128, F32), shape(*left.shape)],
        compiler_params=params(3),
        cost_estimate=cost(0.9),
    )


def scatter_step(keep, into, pieces, after):
    rows, width = keep.shape
    return run(
        functools.partial(scatter_body, pieces),
        [keep, into],
        after,
        out_shape=[shape(rows, width // 2)] * 2,
        compiler_params=params(4),
        cost_estimate=cost(0.2),
    )


def turn_body(end_ref, half_ref, across_ref, chunk_ref, total_ref, send_ref):
    total = (half_ref[...].astype(F32) + across_ref[...].astype(F32)).astype(BF16)
    total_ref[...] = total

    @pl.when(end_ref[0] == 1)
    def _():
        send_ref[...] = chunk_ref[...]

    @pl.when(end_ref[0] == 0)
    def _():
        send_ref[...] = total


def turn(end, half, across, chunk, weight, after):
    return run(
        turn_body,
        [end, half, across, chunk],
        after,
        in_specs=[pl.BlockSpec(memory_space=pltpu.SMEM)]
        + [pl.BlockSpec(memory_space=pltpu.VMEM)] * 3,
        out_shape=[shape(*half.shape)] * 2,
        compiler_params=params(2),
        cost_estimate=cost(weight),
    )


def output_body(count, end_ref, *refs):
    totals, ends, (token_ref, out_ref) = refs[:count], refs[count : 2 * count], refs[2 * count :]
    token_ref[...] = jnp.zeros_like(token_ref)
    rows = totals[0].shape[0]

    for flag, sources in ((0, totals), (1, ends)):

        @pl.when(end_ref[0] == flag)
        def _():
            for i, ref in enumerate(sources):
                out_ref[i * rows : (i + 1) * rows, :] = ref[...]


def output(end, totals, ends, after):
    count = len(totals)
    rows, width = totals[0].shape
    return run(
        functools.partial(output_body, count),
        [end, *totals, *ends],
        after,
        in_specs=[pl.BlockSpec(memory_space=pltpu.SMEM)]
        + [pl.BlockSpec(memory_space=pltpu.VMEM)] * (2 * count),
        out_shape=[shape(8, 128, F32), shape(count * rows, width)],
        compiler_params=params(4),
        cost_estimate=cost(0.9),
    )


def relay_body(source_ref, target_ref):
    target_ref[...] = source_ref[...]


def relay(block, after):
    return run(
        relay_body,
        [block],
        after,
        out_shape=shape(*block.shape),
        compiler_params=params(3),
        cost_estimate=cost(0.2),
    )


def relay_all_body(*refs):
    count = len(refs) // 2
    for source, target in zip(refs[:count], refs[count:]):
        target[...] = source[...]


def relay_all(blocks, after):
    return run(
        relay_all_body,
        list(blocks),
        after,
        out_shape=[shape(*block.shape) for block in blocks],
        compiler_params=params(3),
        cost_estimate=cost(0.2),
    )


class Line:
    lag = 3
    half_weights = (3.0, 4.0, 3.0, 3.0, 3.0, 3.0, 3.0, 0.5)
    turn_weights = (3.0, 4.0, 3.0, 3.0, 4.0, 2.0, 0.5, 0.5)

    def __init__(self, axis, other, end, step):
        self.axis, self.axes, self.step = axis, (axis, other), step
        self.count = lax.axis_size(axis)
        self.end = end
        width = lax.axis_size(other)
        self.across = []
        for place in range(self.count):
            for seat in range(width):
                target = (place, seat ^ 1 if width > 1 else seat)
                if place & 3 in (1, 2):
                    target = (place ^ 3, seat)
                self.across.append((place * width + seat, target[0] * width + target[1]))
        self.chunks, self.into, self.halves, self.crossed, self.totals = [], [], [], [], []

    def enter(self, chunk):
        self.chunks.append(chunk)
        self.into.append(exchange(chunk, self.axis, 1))

    def meet(self, rows):
        k = len(self.halves)
        weight = self.half_weights[k]
        half = self.step(half_sum, self.chunks[k], self.into[k], rows, weight)
        self.halves.append(half)
        self.crossed.append(lax.ppermute(half, self.axes, self.across))

    def turn(self, chunk):
        old = len(self.totals)
        half, crossed = self.halves[old], self.crossed[old]
        weight = self.turn_weights[old]
        total, send = self.step(turn, self.end, half, crossed, chunk, weight)
        self.totals.append(total)
        self.chunks.append(chunk)
        self.into.append(exchange(send, self.axis, 1))

    def leave(self):
        old = len(self.totals)
        half = self.halves[old]
        weight = self.turn_weights[old]
        total = self.step(half_sum, half, self.crossed[old], half.shape[0], weight)
        self.totals.append(total)
        self.into.append(exchange(total, self.axis, 1))

    def output(self, first, count):
        ends = self.into[first + self.lag : first + self.lag + count]
        _, result = self.step(output, self.end, self.totals[first : first + count], ends)
        distance = 4
        while distance < self.count:
            result = add(result, exchange(result, self.axis, distance))
            distance *= 2
        return result


class Scatter:
    def __init__(self, parts, axis, step):
        self.axis, self.step = axis, step
        self.pieces = lax.axis_size(axis) // 2
        self.keep, send = parts
        self.distance = 1
        self.into = exchange(send, axis, 1)

    def advance(self):
        while self.pieces > 1:
            self.keep, send = self.step(scatter_step, self.keep, self.into, self.pieces)
            self.distance *= 2
            self.pieces //= 2
            self.into = exchange(send, self.axis, self.distance)

    def result(self):
        return self.step(last_sum, self.keep, self.into)[1]


def per_device(tokens, w_query, w_key, w_value, w_out, cotangent):
    tok_rows = tokens.shape[0]
    inner = w_query.shape[1]
    local_levels = (tok_rows // BLOCK).bit_length() - 1
    count = lax.axis_size("seq")
    far_levels = count.bit_length() - 1
    far_bits = [d.bit_length() - 1 for d in range(1, count)]

    last = []

    def step(kernel, *operands):
        made = kernel(*operands, list(last))
        last[:] = made[:1] if isinstance(made, (list, tuple)) else [made]
        return made

    place = jnp.bitwise_and(lax.axis_index("seq"), 3)
    end = jnp.reshape((place == 0) | (place == 3), (1,)).astype(jnp.int32)
    rank = jnp.reshape(lax.axis_index("head"), (1,)).astype(jnp.int32)
    parts = key_value(tokens, w_key, w_value, local_levels, far_levels, [end, rank])
    levels, tops = parts[:local_levels], parts[local_levels:]
    fars = [exchange(tops[bit], "seq", d) for d, bit in enumerate(far_bits, 1)]
    query = step(project, tokens, w_query)
    powers, near = step(near_powers, query, levels)
    grad = step(project, cotangent, w_out)
    attended, attended_t, stats = step(forward, query, powers, near, levels, fars, far_bits)

    line = Line("seq", "head", end, step)
    pieces = 2
    rows = tokens.shape[1] // pieces
    line.enter(step(weight_terms, attended_t, cotangent, inner, 0, 0, pieces))
    line.enter(step(weight_terms, attended_t, cotangent, inner, 0, 1, pieces))
    parts = step(project_split, rank, [attended], [w_out], "head")
    mixed = Scatter(parts, "head", step)
    dquery, dkv, query_first, query_second, *away = step(
        backward, query, grad, attended_t, stats, tokens, levels, fars, far_bits, pieces
    )
    line.meet(rows)
    mixed.advance()
    away = step(relay_all, away)
    backs = [exchange(piece, "seq", d) for d, piece in enumerate(away, 1)]
    line.meet(rows)
    line.enter(step(relay, query_first))
    line.turn(query_second)
    dkey, dvalue, dkv_t = step(close_keys, dkv, backs, far_bits, local_levels)
    key_first = step(weight_terms, dkv_t, tokens, inner, 0, 0, pieces)
    line.meet(rows)
    line.turn(key_first)
    key_second = step(weight_terms, dkv_t, tokens, inner, 0, 1, pieces)
    keep, send = step(project_split, rank, [dquery, dkey, dvalue], [w_query, w_key, w_value], "head")
    line.meet(rows)
    value_first = step(weight_terms, dkv_t, tokens, inner, 1, 0, pieces)
    line.turn(key_second)
    line.meet(rows)
    tokens_grad = Scatter([keep, step(relay, send)], "head", step)
    line.turn(value_first)
    mixed = mixed.result()
    value_second = step(weight_terms, dkv_t, tokens, inner, 1, 1, pieces)
    line.meet(rows)
    line.turn(value_second)
    out_grad = line.output(0, pieces)
    line.meet(rows)
    tokens_grad.advance()
    line.leave()
    line.meet(rows)
    query_grad = line.output(2, pieces)
    line.leave()
    key_grad = line.output(4, pieces)
    line.leave()
    tokens_grad = tokens_grad.result()
    value_grad = line.output(6, pieces)
    return mixed, tokens_grad, query_grad, key_grad, value_grad, out_grad


def solution(mesh):
    return jax.shard_map(
        per_device,
        mesh=mesh,
        in_specs=(
            P(("groups", "seq"), None),
            P(None, "head"),
            P(None, "head"),
            P(None, "head"),
            P(None, "head"),
            P(("groups", "seq"), None),
        ),
        out_specs=(
            P(("groups", "seq"), "head"),
            P(("groups", "seq"), "head"),
            P("groups", "head"),
            P("groups", "head"),
            P("groups", "head"),
            P("groups", "head"),
        ),
        check_vma=False,
    )
```

```python
import functools
import math

import jax
import jax.numpy as jnp
from jax import lax
from jax.experimental import pallas as pl
from jax.experimental.pallas import tpu as pltpu
from jax.sharding import PartitionSpec as P

HEAD_DIM = 128
BLOCK = 128
BF16 = jnp.bfloat16
F32 = jnp.float32
MIB = 1024 * 1024

NN = (((1,), (0,)), ((), ()))
NT = (((1,), (1,)), ((), ()))
TN = (((0,), (0,)), ((), ()))


def dot(left, right, dims=NN):
    return lax.dot_general(left, right, dims, preferred_element_type=F32)


def params(mib):
    return pltpu.CompilerParams(vmem_limit_bytes=mib * MIB)


def cost(microseconds):
    return pl.CostEstimate(flops=int(microseconds * 1150e6) + 1, bytes_accessed=1, transcendentals=0)


def run(body, ready, after=(), in_specs=None, **options):
    count, extra = len(ready), len(after)

    def kernel(*refs):
        body(*refs[:count], *refs[count + extra :])

    in_specs = in_specs or [pl.BlockSpec(memory_space=pltpu.VMEM)] * count
    in_specs = in_specs + [pl.BlockSpec(memory_space=pl.ANY)] * extra
    return pl.pallas_call(kernel, in_specs=in_specs, **options)(*ready, *after)


def shape(rows, cols, dtype=BF16):
    return jax.ShapeDtypeStruct((rows, cols), dtype)


def whole(rows, cols):
    return pl.BlockSpec((rows, cols), lambda *_: (0, 0))


def pool_matrix(rows):
    row = lax.broadcasted_iota(jnp.int32, (rows // 2, rows), 0)
    col = lax.broadcasted_iota(jnp.int32, (rows // 2, rows), 1)
    return jnp.where(jnp.right_shift(col, 1) == row, 0.5, 0.0).astype(BF16)


def spread_matrix(rows, step_bits, offset, cols, weight):
    row = lax.broadcasted_iota(jnp.int32, (rows, cols), 0) + offset
    col = lax.broadcasted_iota(jnp.int32, (rows, cols), 1)
    return jnp.where(jnp.right_shift(row, step_bits) == col, weight, 0.0).astype(BF16)


def key_value_body(local_levels, far_levels, parts, tok_hbm, wk_hbm, wv_hbm, *refs):
    out_hbm = refs[:local_levels]
    far = refs[local_levels : local_levels + far_levels]
    refs = refs[local_levels + far_levels :]
    tok_ref, wk_ref, wv_ref = refs[:3]
    levels = refs[3 : 3 + local_levels]
    in_sems, out_sems = refs[3 + local_levels :]
    part = tok_ref.shape[0] // parts

    def fetch(source, target, i):
        copy = pltpu.make_async_copy(source, target, in_sems.at[i])
        copy.start()
        return copy

    def flush(i):
        copy = pltpu.make_async_copy(levels[i], out_hbm[i], out_sems.at[i])
        copy.start()
        return copy

    weights = [fetch(wk_hbm, wk_ref, 0), fetch(wv_hbm, wv_ref, 1)]
    tiles = []
    for p in range(parts):
        rows = pl.ds(p * part, part)
        tiles.append(fetch(tok_hbm.at[rows], tok_ref.at[rows], 2 + p))
    for copy in weights:
        copy.wait()
    for p in range(parts):
        tiles[p].wait()
        here = slice(p * part, (p + 1) * part)
        x = tok_ref[here, :]
        both = jnp.concatenate([dot(x, wk_ref[...]), dot(x, wv_ref[...])], axis=1)
        levels[0][here, :] = both.astype(BF16)
    flushes = [flush(0)]
    pool = pool_matrix(part)
    for i in range(1, local_levels):
        source = levels[i - 1]
        for low in range(0, source.shape[0], part):
            mean = dot(pool, source[low : low + part, :])
            levels[i][low // 2 : (low + part) // 2, :] = mean.astype(BF16)
        flushes.append(flush(i))
    rows = dot(pool, levels[-1][...]).astype(BF16)
    for i in range(far_levels):
        if i:
            rows = dot(pool_matrix(rows.shape[0]), rows).astype(BF16)
        far[i][...] = rows
    for copy in flushes:
        copy.wait()


def key_value(tokens, w_key, w_value, local_levels, far_levels, after):
    tok_rows, width = tokens.shape
    inner = w_key.shape[1]
    parts = tok_rows // (2 * BLOCK)
    held = [(tok_rows >> i, 2 * inner) for i in range(local_levels)]
    tops = [(BLOCK >> i, 2 * inner) for i in range(far_levels)]
    return run(
        functools.partial(key_value_body, local_levels, far_levels, parts),
        [tokens, w_key, w_value],
        after,
        in_specs=[pl.BlockSpec(memory_space=pl.ANY)] * 3,
        out_specs=[pl.BlockSpec(memory_space=pl.ANY)] * len(held)
        + [pl.BlockSpec(memory_space=pltpu.VMEM)] * len(tops),
        out_shape=[shape(*dims) for dims in held + tops],
        scratch_shapes=[pltpu.VMEM((tok_rows, width), BF16)]
        + [pltpu.VMEM((width, inner), BF16)] * 2
        + [pltpu.VMEM(dims, BF16) for dims in held]
        + [pltpu.SemaphoreType.DMA((parts + 2,)), pltpu.SemaphoreType.DMA((len(held),))],
        compiler_params=params(56),
        cost_estimate=cost(5.0),
    )


def project_body(left_ref, weight_ref, out_ref):
    out_ref[...] = dot(left_ref[...], weight_ref[...]).astype(BF16)


def project(left, weight, after):
    tok_rows, width = left.shape
    inner = weight.shape[1]
    return run(
        project_body,
        [left, weight],
        after,
        out_shape=shape(tok_rows, inner),
        compiler_params=params(4),
        cost_estimate=cost(0.7),
    )


class KeySet:
    def __init__(self, far_rows, far_bits, local_levels):
        mids = local_levels - 1
        self.sizes = [2 * BLOCK] + [BLOCK] * mids + list(far_rows)
        self.bounds = [sum(self.sizes[:i]) for i in range(len(self.sizes) + 1)]
        steps = [0] + list(range(1, local_levels)) + [local_levels + b for b in far_bits]
        self.biases = [float(step) for step in steps]
        self.mids = mids
        self.far_start = self.bounds[1 + mids]
        self.factor = math.log2(math.e) / math.sqrt(HEAD_DIM)

    def here(self, m):
        return pl.ds(pl.multiple_of(m * 2 * BLOCK, 2 * BLOCK), 2 * BLOCK)

    def seats(self, m):
        for i in range(self.mids):
            sibling = jnp.bitwise_xor(jnp.right_shift(m, i), 1)
            yield pl.ds(pl.multiple_of(sibling * BLOCK, BLOCK), BLOCK)

    def near(self, m, level_refs, cols):
        rows = [level_refs[0][self.here(m), cols]]
        rows += [ref[seat, cols] for ref, seat in zip(level_refs[1:], self.seats(m))]
        return rows

    def far(self, far_refs, cols):
        return [ref[:, cols] for ref in far_refs]

    def pieces(self, array, first=0, count=None):
        base = self.bounds[first]
        ends = self.bounds[first:] if count is None else self.bounds[first : first + count + 1]
        return [array[a - base : b - base] for a, b in zip(ends, ends[1:])]

    def top(self, pieces, first=0):
        tops = [
            jnp.max(piece, axis=0, keepdims=True) * self.factor + bias
            for piece, bias in zip(pieces, self.biases[first:])
        ]
        return functools.reduce(jnp.maximum, tops)

    def powers(self, pieces, top, first=0):
        return jnp.concatenate(
            [
                jnp.exp2(piece * self.factor + (bias - top))
                for piece, bias in zip(pieces, self.biases[first:])
            ],
            axis=0,
        )


def head_columns(h, inner):
    low = h * HEAD_DIM
    return slice(low, low + HEAD_DIM), slice(inner + low, inner + low + HEAD_DIM)


def near_body(local_levels, q_ref, *refs):
    level_refs = refs[:local_levels]
    power_ref, stat_ref = refs[local_levels:]
    tok_rows, inner = q_ref.shape
    heads = inner // HEAD_DIM
    keyset = KeySet([], [], local_levels)
    rows = keyset.far_start

    def step(m, carry):
        here = keyset.here(m)
        for h in range(heads):
            cols, _ = head_columns(h, inner)
            keys = jnp.concatenate(keyset.near(m, level_refs, cols), axis=0)
            pieces = keyset.pieces(dot(keys, q_ref[here, cols], NT))
            top = keyset.top(pieces)
            powers = keyset.powers(pieces, top)
            stat_ref[h : h + 1, here] = top
            stat_ref[heads + h : heads + h + 1, here] = jnp.sum(powers, axis=0, keepdims=True)
            power_ref[pl.ds(pl.multiple_of((m * heads + h) * rows, rows), rows), :] = powers
        return carry

    lax.fori_loop(0, tok_rows // (2 * BLOCK), step, 0)


def near_powers(query, levels, after):
    tok_rows, inner = query.shape
    heads = inner // HEAD_DIM
    pairs = tok_rows // (2 * BLOCK)
    rows = (len(levels) + 1) * BLOCK
    return run(
        functools.partial(near_body, len(levels)),
        [query, *levels],
        after,
        out_shape=[shape(pairs * heads * rows, 2 * BLOCK, F32), shape(2 * heads, tok_rows, F32)],
        compiler_params=params(6),
        cost_estimate=cost(2.3),
    )


def forward_body(local_levels, far_bits, *refs):
    fars = len(far_bits)
    q_ref, power_ref, near_ref = refs[:3]
    level_refs = refs[3 : 3 + local_levels]
    far_refs = refs[3 + local_levels : 3 + local_levels + fars]
    att_ref, att_t_ref, stat_ref = refs[3 + local_levels + fars :]
    tok_rows, inner = q_ref.shape
    heads = inner // HEAD_DIM
    keyset = KeySet([r.shape[0] for r in far_refs], far_bits, local_levels)
    rows = keyset.far_start

    def step(m, carry):
        here = keyset.here(m)
        for h in range(heads):
            cols, vcols = head_columns(h, inner)
            second = heads + h
            keys = jnp.concatenate(keyset.far(far_refs, cols), axis=0)
            values = keyset.near(m, level_refs, vcols) + keyset.far(far_refs, vcols)
            values = jnp.concatenate(values, axis=0)
            first = local_levels
            pieces = keyset.pieces(dot(keys, q_ref[here, cols], NT), first)
            near_top = near_ref[h : h + 1, here]
            top = jnp.maximum(near_top, keyset.top(pieces, first))
            shrink = jnp.exp2(near_top - top)
            powers = keyset.powers(pieces, top, first)
            total = near_ref[second : second + 1, here] * shrink
            total = total + jnp.sum(powers, axis=0, keepdims=True)
            inverse = 1.0 / total
            place = pl.ds(pl.multiple_of((m * heads + h) * rows, rows), rows)
            near_probs = (power_ref[place, :] * (shrink * inverse)).astype(BF16)
            far_probs = (powers * inverse).astype(BF16)
            probs_b = jnp.concatenate([near_probs, far_probs], axis=0)
            att_t = dot(values, probs_b, TN).astype(BF16)
            att_t_ref[cols, here] = att_t
            att_ref[here, cols] = att_t.T
            stat_ref[h : h + 1, here] = top
            stat_ref[second : second + 1, here] = inverse
        return carry

    lax.fori_loop(0, tok_rows // (2 * BLOCK), step, 0)


def forward(query, powers, near, levels, fars, far_bits, after):
    tok_rows, inner = query.shape
    heads = inner // HEAD_DIM
    set_rows = (len(levels) + 1) * BLOCK + sum(f.shape[0] for f in fars)
    return run(
        functools.partial(forward_body, len(levels), far_bits),
        [query, powers, near, *levels, *fars],
        after,
        out_shape=[
            shape(tok_rows, inner),
            shape(inner, tok_rows),
            shape(2 * heads, tok_rows, F32),
        ],
        compiler_params=params(6),
        cost_estimate=cost(4.0),
    )


def backward_body(local_levels, far_bits, pieces, *refs):
    mids = local_levels - 1
    fars = len(far_bits)
    q_ref, g_ref, att_t_ref, stat_ref, tok_ref = refs[:5]
    level_refs = refs[5 : 5 + local_levels]
    far_refs = refs[5 + local_levels : 5 + local_levels + fars]
    outs = refs[5 + local_levels + fars :]
    dq_ref, dkv_ref = outs[:2]
    term_refs = outs[2 : 2 + pieces]
    dfar_refs = outs[2 + pieces : 1 + pieces + fars]
    dmid_refs = outs[1 + pieces + fars : 1 + pieces + fars + mids]
    dq_t_ref, acc_ref = outs[-2:]
    tok_rows, inner = q_ref.shape
    heads = inner // HEAD_DIM
    score_scale = 1.0 / math.sqrt(HEAD_DIM)
    keyset = KeySet([r.shape[0] for r in far_refs], far_bits, local_levels)

    for ref in (*dmid_refs, acc_ref):
        ref[...] = jnp.zeros_like(ref)

    def step(m, carry):
        here = keyset.here(m)
        for h in range(heads):
            cols, vcols = head_columns(h, inner)
            keys, values = (
                jnp.concatenate(keyset.near(m, level_refs, c) + keyset.far(far_refs, c), axis=0)
                for c in (cols, vcols)
            )
            q = q_ref[here, cols]
            g = g_ref[here, cols]
            top = stat_ref[h : h + 1, here]
            inverse = stat_ref[heads + h : heads + h + 1, here]
            probs = keyset.powers(keyset.pieces(dot(keys, q, NT)), top) * inverse
            att_t = att_t_ref[cols, here].astype(F32)
            delta = jnp.sum(g.T.astype(F32) * att_t, axis=0, keepdims=True)
            grads = (probs * (dot(values, g, NT) - delta) * score_scale).astype(BF16)
            dq_t = dot(keys, grads, TN).astype(BF16)
            dq_t_ref[cols, here] = dq_t
            dq_ref[here, cols] = dq_t.T
            for part, place in ((dot(grads, q), cols), (dot(probs.astype(BF16), g), vcols)):
                own, *sides = keyset.pieces(part)
                dkv_ref[here, place] = own
                for ref, seat, side in zip(dmid_refs, keyset.seats(m), sides):
                    ref[seat, place] += side
                acc_ref[:, place] += part[keyset.far_start :]
        return carry

    lax.fori_loop(0, tok_rows // (2 * BLOCK), step, 0)
    width = term_refs[-1].shape[0]
    first = acc_ref[:BLOCK].astype(BF16)
    term_refs[0][width : width + BLOCK, :] = first[:, :inner]
    term_refs[0][width + BLOCK :, :] = first[:, inner:]
    low = BLOCK
    for ref in dfar_refs:
        ref[...] = acc_ref[low : low + ref.shape[0]].astype(BF16)
        low += ref.shape[0]
    for i, ref in enumerate(term_refs):
        part = dot(dq_t_ref[...], tok_ref[:, i * width : (i + 1) * width])
        ref[:width, :] = part.astype(BF16).T
    fan = spread_matrix(2 * BLOCK, 1, 0, BLOCK, 0.5)
    targets = (dkv_ref, *dmid_refs)
    for i in reversed(range(mids)):
        for t in range(dmid_refs[i].shape[0] // BLOCK):
            part = dmid_refs[i][t * BLOCK : (t + 1) * BLOCK, :]
            high = part.astype(BF16)
            low = (part - high.astype(F32)).astype(BF16)
            rows = slice(2 * t * BLOCK, 2 * (t + 1) * BLOCK)
            targets[i][rows, :] += dot(fan, high) + dot(fan, low)


def backward(query, grad, attended_t, stats, tokens, levels, fars, far_bits, pieces, after):
    tok_rows, inner = query.shape
    far_rows = sum(f.shape[0] for f in fars)
    set_rows = (len(levels) + 1) * BLOCK + far_rows
    return run(
        functools.partial(backward_body, len(levels), far_bits, pieces),
        [query, grad, attended_t, stats, tokens, *levels, *fars],
        after,
        out_shape=[shape(tok_rows, inner), shape(tok_rows, 2 * inner, F32)]
        + [shape(tokens.shape[1] // pieces + 2 * BLOCK, inner)]
        + [shape(tokens.shape[1] // pieces, inner)] * (pieces - 1)
        + [shape(*f.shape) for f in fars[1:]],
        scratch_shapes=[pltpu.VMEM(level.shape, F32) for level in levels[1:]]
        + [pltpu.VMEM((inner, tok_rows), BF16), pltpu.VMEM((far_rows, 2 * inner), F32)],
        compiler_params=params(10),
        cost_estimate=cost(8.0),
    )


def term_body(which, low, left_ref, right_ref, out_ref):
    width, inner = out_ref.shape
    left = left_ref[which * inner : (which + 1) * inner, :]
    out_ref[...] = dot(left, right_ref[:, low : low + width]).astype(BF16).T


def weight_terms(left_t, right, inner, which, part, parts, after):
    tok_rows = left_t.shape[1]
    width = right.shape[1] // parts
    return run(
        functools.partial(term_body, which, part * width),
        [left_t, right],
        after,
        out_shape=shape(width, inner),
        compiler_params=params(3),
        cost_estimate=cost(0.2),
    )


def close_body(local_levels, far_bits, dkv_ref, *refs):
    joined_ref, *back_refs = refs[: len(far_bits)]
    dk_ref, dv_ref, dkv_t_ref = refs[len(far_bits) :]
    inner = dk_ref.shape[1]
    tile = 2 * BLOCK
    low = joined_ref.shape[0] - 2 * BLOCK
    joined = [joined_ref[low : low + BLOCK, :], joined_ref[low + BLOCK :, :]]
    backs = [jnp.concatenate(joined, axis=1)] + [ref[...] for ref in back_refs]
    for t in range(dkv_ref.shape[0] // tile):
        here = slice(t * tile, (t + 1) * tile)
        total = dkv_ref[here, :]
        for back, bit in zip(backs, far_bits):
            weight = 0.5 ** (local_levels + bit)
            fan = spread_matrix(tile, local_levels + bit, t * tile, back.shape[0], weight)
            total = total + dot(fan, back)
        final = total.astype(BF16)
        dk_ref[here, :] = final[:, :inner]
        dv_ref[here, :] = final[:, inner:]
        dkv_t_ref[:, here] = final.T


def close_keys(dkv, backs, far_bits, local_levels, after):
    tok_rows, double = dkv.shape
    inner = double // 2
    return run(
        functools.partial(close_body, local_levels, far_bits),
        [dkv, *backs],
        after,
        out_shape=[shape(tok_rows, inner), shape(tok_rows, inner), shape(double, tok_rows)],
        compiler_params=params(5),
        cost_estimate=cost(0.2),
    )


def split_body(count, parts, rank_ref, *refs):
    lefts, weights = refs[:count], refs[count : 2 * count]
    outs = refs[2 * count :]
    width = weights[0].shape[0] // parts
    for r in range(parts):
        owner = jnp.bitwise_xor(rank_ref[0], r)
        rows = pl.ds(pl.multiple_of(owner * width, width), width)
        total = None
        for left, weight in zip(lefts, weights):
            product = dot(left[...], weight[rows, :], NT)
            total = product if total is None else total + product
        place = r // 2 * width
        outs[r % 2][:, place : place + width] = total.astype(BF16)


def project_split(rank, lefts, weights, axis, after):
    count = len(lefts)
    parts = lax.axis_size(axis)
    tok_rows, inner = lefts[0].shape
    width = weights[0].shape[0]
    return run(
        functools.partial(split_body, count, parts),
        [rank, *lefts, *weights],
        after,
        in_specs=[pl.BlockSpec(memory_space=pltpu.SMEM)]
        + [pl.BlockSpec(memory_space=pltpu.VMEM)] * (2 * count),
        out_shape=[shape(tok_rows, width // 2)] * 2,
        compiler_params=params(5),
        cost_estimate=cost(1.0),
    )


def exchange(block, axis, distance):
    count = lax.axis_size(axis)
    return lax.ppermute(block, axis, [(i, i ^ distance) for i in range(count)])


def add(left, right):
    return (left.astype(F32) + right.astype(F32)).astype(BF16)


def term_half_body(chunk_ref, into_ref, out_ref):
    rows = slice(0, out_ref.shape[0])
    out_ref[...] = (chunk_ref[rows, :].astype(F32) + into_ref[rows, :].astype(F32)).astype(BF16)


def half_sum(chunk, into, rows, weight, after):
    return run(
        term_half_body,
        [chunk, into],
        after,
        out_shape=shape(rows, chunk.shape[1]),
        compiler_params=params(3),
        cost_estimate=cost(weight),
    )


def scatter_body(pieces, keep_ref, into_ref, even_ref, odd_ref):
    width = keep_ref.shape[1] // pieces
    for i in range(pieces):
        here = slice(i * width, (i + 1) * width)
        place = slice(i // 2 * width, (i // 2 + 1) * width)
        total = keep_ref[:, here].astype(F32) + into_ref[:, here].astype(F32)
        (even_ref, odd_ref)[i % 2][:, place] = total.astype(BF16)


def last_body(left_ref, right_ref, token_ref, out_ref):
    token_ref[...] = jnp.zeros_like(token_ref)
    out_ref[...] = (left_ref[...].astype(F32) + right_ref[...].astype(F32)).astype(BF16)


def last_sum(left, right, after):
    return run(
        last_body,
        [left, right],
        after,
        out_shape=[shape(8, 128, F32), shape(*left.shape)],
        compiler_params=params(3),
        cost_estimate=cost(0.9),
    )


def scatter_step(keep, into, pieces, after):
    rows, width = keep.shape
    return run(
        functools.partial(scatter_body, pieces),
        [keep, into],
        after,
        out_shape=[shape(rows, width // 2)] * 2,
        compiler_params=params(4),
        cost_estimate=cost(0.2),
    )


def turn_body(end_ref, half_ref, across_ref, chunk_ref, total_ref, send_ref):
    total = (half_ref[...].astype(F32) + across_ref[...].astype(F32)).astype(BF16)
    total_ref[...] = total

    @pl.when(end_ref[0] == 1)
    def _():
        send_ref[...] = chunk_ref[...]

    @pl.when(end_ref[0] == 0)
    def _():
        send_ref[...] = total


def turn(end, half, across, chunk, weight, after):
    return run(
        turn_body,
        [end, half, across, chunk],
        after,
        in_specs=[pl.BlockSpec(memory_space=pltpu.SMEM)]
        + [pl.BlockSpec(memory_space=pltpu.VMEM)] * 3,
        out_shape=[shape(*half.shape)] * 2,
        compiler_params=params(2),
        cost_estimate=cost(weight),
    )


def output_body(count, end_ref, *refs):
    totals, ends, (token_ref, out_ref) = refs[:count], refs[count : 2 * count], refs[2 * count :]
    token_ref[...] = jnp.zeros_like(token_ref)
    rows = totals[0].shape[0]

    for flag, sources in ((0, totals), (1, ends)):

        @pl.when(end_ref[0] == flag)
        def _():
            for i, ref in enumerate(sources):
                out_ref[i * rows : (i + 1) * rows, :] = ref[...]


def output(end, totals, ends, after):
    count = len(totals)
    rows, width = totals[0].shape
    return run(
        functools.partial(output_body, count),
        [end, *totals, *ends],
        after,
        in_specs=[pl.BlockSpec(memory_space=pltpu.SMEM)]
        + [pl.BlockSpec(memory_space=pltpu.VMEM)] * (2 * count),
        out_shape=[shape(8, 128, F32), shape(count * rows, width)],
        compiler_params=params(4),
        cost_estimate=cost(0.9),
    )


def relay_body(source_ref, target_ref):
    target_ref[...] = source_ref[...]


def relay(block, after):
    return run(
        relay_body,
        [block],
        after,
        out_shape=shape(*block.shape),
        compiler_params=params(3),
        cost_estimate=cost(0.2),
    )


class Line:
    lag = 3
    half_weights = (3.0, 3.0, 3.0, 3.0, 3.0, 3.0, 1.0, 0.5)
    turn_weights = (3.0, 3.0, 3.0, 3.0, 3.0, 0.5, 0.5, 0.5)

    def __init__(self, axis, other, end, step):
        self.axis, self.axes, self.step = axis, (axis, other), step
        self.count = lax.axis_size(axis)
        self.end = end
        width = lax.axis_size(other)
        self.across = []
        for place in range(self.count):
            for seat in range(width):
                target = (place, seat ^ 1 if width > 1 else seat)
                if place & 3 in (1, 2):
                    target = (place ^ 3, seat)
                self.across.append((place * width + seat, target[0] * width + target[1]))
        self.chunks, self.into, self.halves, self.crossed, self.totals = [], [], [], [], []

    def enter(self, chunk):
        self.chunks.append(chunk)
        self.into.append(exchange(chunk, self.axis, 1))

    def meet(self, rows):
        k = len(self.halves)
        weight = self.half_weights[k]
        half = self.step(half_sum, self.chunks[k], self.into[k], rows, weight)
        self.halves.append(half)
        self.crossed.append(lax.ppermute(half, self.axes, self.across))

    def turn(self, chunk):
        old = len(self.totals)
        half, crossed = self.halves[old], self.crossed[old]
        weight = self.turn_weights[old]
        total, send = self.step(turn, self.end, half, crossed, chunk, weight)
        self.totals.append(total)
        self.chunks.append(chunk)
        self.into.append(exchange(send, self.axis, 1))

    def leave(self):
        old = len(self.totals)
        half = self.halves[old]
        weight = self.turn_weights[old]
        total = self.step(half_sum, half, self.crossed[old], half.shape[0], weight)
        self.totals.append(total)
        self.into.append(exchange(total, self.axis, 1))

    def output(self, first, count):
        ends = self.into[first + self.lag : first + self.lag + count]
        _, result = self.step(output, self.end, self.totals[first : first + count], ends)
        distance = 4
        while distance < self.count:
            result = add(result, exchange(result, self.axis, distance))
            distance *= 2
        return result


class Scatter:
    def __init__(self, parts, axis, step):
        self.axis, self.step = axis, step
        self.pieces = lax.axis_size(axis) // 2
        self.keep, send = parts
        self.distance = 1
        self.into = exchange(send, axis, 1)

    def advance(self):
        while self.pieces > 1:
            self.keep, send = self.step(scatter_step, self.keep, self.into, self.pieces)
            self.distance *= 2
            self.pieces //= 2
            self.into = exchange(send, self.axis, self.distance)

    def result(self):
        return self.step(last_sum, self.keep, self.into)[1]


def per_device(tokens, w_query, w_key, w_value, w_out, cotangent):
    tok_rows = tokens.shape[0]
    inner = w_query.shape[1]
    local_levels = (tok_rows // BLOCK).bit_length() - 1
    count = lax.axis_size("seq")
    far_levels = count.bit_length() - 1
    far_bits = [d.bit_length() - 1 for d in range(1, count)]

    last = []

    def step(kernel, *operands):
        made = kernel(*operands, list(last))
        last[:] = made[:1] if isinstance(made, (list, tuple)) else [made]
        return made

    place = jnp.bitwise_and(lax.axis_index("seq"), 3)
    end = jnp.reshape((place == 0) | (place == 3), (1,)).astype(jnp.int32)
    rank = jnp.reshape(lax.axis_index("head"), (1,)).astype(jnp.int32)
    parts = key_value(tokens, w_key, w_value, local_levels, far_levels, [end, rank])
    levels, tops = parts[:local_levels], parts[local_levels:]
    fars = [exchange(tops[bit], "seq", d) for d, bit in enumerate(far_bits, 1)]
    query = step(project, tokens, w_query)
    powers, near = step(near_powers, query, levels)
    grad = step(project, cotangent, w_out)
    attended, attended_t, stats = step(forward, query, powers, near, levels, fars, far_bits)

    line = Line("seq", "head", end, step)
    pieces = 2
    rows = tokens.shape[1] // pieces
    line.enter(step(weight_terms, attended_t, cotangent, inner, 0, 0, pieces))
    line.enter(step(weight_terms, attended_t, cotangent, inner, 0, 1, pieces))
    dquery, dkv, query_first, query_second, *away = step(
        backward, query, grad, attended_t, stats, tokens, levels, fars, far_bits, pieces
    )
    line.enter(query_first)
    backs = [exchange(piece, "seq", d) for d, piece in enumerate(away, 2)]
    line.meet(rows)
    line.meet(rows)
    line.turn(query_second)
    dkey, dvalue, dkv_t = step(
        close_keys, dkv, [line.into[2], *backs], far_bits, local_levels
    )
    key_first = step(weight_terms, dkv_t, tokens, inner, 0, 0, pieces)
    line.meet(rows)
    parts = step(project_split, rank, [attended], [w_out], "head")
    mixed = Scatter(parts, "head", step)
    line.turn(key_first)
    line.meet(rows)
    key_second = step(weight_terms, dkv_t, tokens, inner, 0, 1, pieces)
    line.turn(key_second)
    value_first = step(weight_terms, dkv_t, tokens, inner, 1, 0, pieces)
    keep, send = step(project_split, rank, [dquery, dkey, dvalue], [w_query, w_key, w_value], "head")
    line.meet(rows)
    tokens_grad = Scatter([keep, step(relay, send)], "head", step)
    line.turn(value_first)
    mixed.advance()
    value_second = step(weight_terms, dkv_t, tokens, inner, 1, 1, pieces)
    line.meet(rows)
    line.turn(value_second)
    out_grad = line.output(0, pieces)
    line.meet(rows)
    line.leave()
    tokens_grad.advance()
    line.meet(rows)
    query_grad = line.output(2, pieces)
    line.leave()
    mixed = mixed.result()
    key_grad = line.output(4, pieces)
    line.leave()
    tokens_grad = tokens_grad.result()
    value_grad = line.output(6, pieces)
    return mixed, tokens_grad, query_grad, key_grad, value_grad, out_grad


def solution(mesh):
    return jax.shard_map(
        per_device,
        mesh=mesh,
        in_specs=(
            P(("groups", "seq"), None),
            P(None, "head"),
            P(None, "head"),
            P(None, "head"),
            P(None, "head"),
            P(("groups", "seq"), None),
        ),
        out_specs=(
            P(("groups", "seq"), "head"),
            P(("groups", "seq"), "head"),
            P("groups", "head"),
            P("groups", "head"),
            P("groups", "head"),
            P("groups", "head"),
        ),
        check_vma=False,
    )
```
